32 devices in a mesh: seq: 8 (over z, x), batch: 4 (over y, core).
Axes of the slice: x: 2, y: 2, z: 4, core: 2. Of those that a mesh axis runs over, the one named last changes fastest.
Arguments:
- tokens: bfloat16 [4, 4096, 768], P('batch', 'seq'), may hold values from -6 to 6
- global_states: bfloat16 [4, 128, 768], P('batch'), may hold values from -6 to 6
- token_seg: int32 [4, 4096], P('batch', 'seq'), may hold values from 0 to 2, as said below
- global_seg: int32 [4, 128], P('batch'), may hold values from 0 to 2, as said below
- attn_gain: float32 [768], replicated, may hold values from 0.1 to 1.9
- attn_shift: float32 [768], replicated, may hold values from -4 to 4
- glob_gain: float32 [768], replicated, may hold values from 0.1 to 1.9
- glob_shift: float32 [768], replicated, may hold values from -4 to 4
- w_qkv: bfloat16 [768, 2304], replicated, may hold values from -0.21875 to 0.21875
- w_out: bfloat16 [768, 768], replicated, may hold values from -2.5 to 2.5
- ffn_gain: float32 [768], replicated, may hold values from 0.1 to 1.9
- ffn_shift: float32 [768], replicated, may hold values from -4 to 4
- w_up: bfloat16 [768, 3072], replicated, may hold values from -0.21875 to 0.21875
- up_bias: float32 [3072], replicated, may hold values from -6 to 6
- w_down: bfloat16 [3072, 768], replicated, may hold values from -0.109375 to 0.109375
- down_bias: float32 [768], replicated, may hold values from -4 to 4
- out_cotangent: bfloat16 [4, 4096, 768], P('batch', 'seq'), may hold values from -6 to 6
- global_cotangent: bfloat16 [4, 128, 768], P('batch'), may hold values from -6 to 6
Outputs:
- staggered_out: bfloat16 [4, 4096, 768], P('batch', 'seq')
- global_out: bfloat16 [4, 128, 768], P('batch')
- token_grad: bfloat16 [4, 4096, 768], P('batch', 'seq')
- global_grad: bfloat16 [4, 128, 768], P('batch')
- grad_attn_gain: float32 [768], P('seq')
- grad_attn_shift: float32 [768], P('seq')
- grad_glob_gain: float32 [768], P('seq')
- grad_glob_shift: float32 [768], P('seq')
- grad_w_qkv: float32 [768, 2304], P('seq', 'batch')
- grad_w_out: float32 [768, 768], P('seq', 'batch')
- grad_ffn_gain: float32 [768], P('seq')
- grad_ffn_shift: float32 [768], P('seq')
- grad_w_up: float32 [768, 3072], P('seq', 'batch')
- grad_up_bias: float32 [3072], P('seq')
- grad_w_down: float32 [3072, 768], P('seq', 'batch')
- grad_down_bias: float32 [768], P('seq')
The draws below stay inside these ranges and needn't reach their ends.
Inputs may be any that keep to these rules, and one draw needn't show every extreme that they name: `token_seg`: in input order each row holds three documents with ids 0, 1, 2 in turn; document 1 begins within the row's first 256 tokens and ends within its last 256; entry p holds the id of input position (p + 256) mod 4096. `global_seg`: the document that each global slot serves.
All inputs are finite; a program needn't handle non-finite values.
Results may differ from the reference program's by a relative error of at most 0.014.
Values may be sent and summed in bfloat16 or wider, within the bound.
A program may use at most 192 MiB of HBM per device.

```python
import jax
import jax.numpy as jnp
from jax import lax

D = 768
HEADS = 12
HEAD_DIM = 64
FF = 3072
BLOCK = 512
GLOB = 128
HALF = 256
LEN = 4096
ROWS = 4


def draw_token_seg(key, part):
    key = jax.random.fold_in(key, 11)
    start_key, tail_key = jax.random.split(key)
    start = jax.random.randint(start_key, (ROWS, 1), 1, HALF + 1)
    tail = jax.random.randint(tail_key, (ROWS, 1), 1, HALF + 1)
    position = lax.broadcasted_iota(jnp.int32, (ROWS, LEN), 1)
    unshifted = (position + HALF) % LEN
    return (unshifted >= start).astype(jnp.int32) + (unshifted >= LEN - tail).astype(jnp.int32)


def draw_global_seg(key, part):
    key = jax.random.fold_in(key, 23)
    picked = jax.random.randint(key, (ROWS, GLOB), 0, 4)
    return jnp.where(picked == 0, 0, jnp.where(picked == 3, 2, 1)).astype(jnp.int32)


def block_levels(rng, shape, cuts, smallest, largest):
    def one(axis_at, blocks):
        heights = jax.random.uniform(jax.random.fold_in(jax.random.fold_in(rng, 6), axis_at), (blocks,), jnp.float32, smallest / len(cuts), largest / len(cuts))
        return jnp.repeat(jnp.exp(heights), shape[axis_at] // blocks).reshape((-1,) + (1,) * (len(shape) - axis_at - 1))

    factor_of = one(*cuts[0])
    for cut in cuts[1:]:
        factor_of = factor_of * one(*cut)
    return factor_of


def normal_values(own_key, shape, scale, most, cuts=(), kind=jnp.bfloat16):
    drawn = jax.random.normal(own_key, shape, jnp.float32) * scale
    if len(cuts) > 0:
        drawn = block_levels(own_key, shape, cuts, -0.22, 0.18) * drawn
    return jnp.clip(drawn, min=-most, max=most).astype(kind)


def setup_inputs(seed: int = 0) -> dict:
    keys = jax.random.split(jax.random.key(seed), 19)
    return {
        "tokens": normal_values(keys[0], (ROWS, LEN, D), 1.0, 6.0, ((0, 4), (1, 8))),
        "global_states": normal_values(keys[1], (ROWS, GLOB, D), 1.0, 6.0, ((0, 4),)),
        "token_seg": draw_token_seg(jax.random.fold_in(keys[18], 71), 0),
        "global_seg": draw_global_seg(jax.random.fold_in(keys[18], 71), 0),
        "attn_gain": jnp.clip(1.0 + 0.18 * jax.random.normal(keys[4], (D,), jnp.float32), 0.1, 1.9),
        "attn_shift": normal_values(keys[5], (D,), 0.3, 4.0, (), jnp.float32),
        "glob_gain": jnp.clip(1.0 + 0.18 * jax.random.normal(keys[6], (D,), jnp.float32), 0.1, 1.9),
        "glob_shift": normal_values(keys[7], (D,), 0.3, 4.0, (), jnp.float32),
        "w_qkv": normal_values(keys[8], (D, 3 * D), D ** -0.5, 0.21875),
        "w_out": normal_values(keys[9], (D, D), (max(D // 128, 1)) ** -0.5, 2.5),
        "ffn_gain": jnp.clip(1.0 + 0.18 * jax.random.normal(keys[10], (D,), jnp.float32), 0.1, 1.9),
        "ffn_shift": normal_values(keys[11], (D,), 0.3, 4.0, (), jnp.float32),
        "w_up": normal_values(keys[12], (D, FF), D ** -0.5, 0.21875),
        "up_bias": normal_values(keys[13], (FF,), 0.5, 6.0, (), jnp.float32),
        "w_down": normal_values(keys[14], (FF, D), FF ** -0.5, 0.109375),
        "down_bias": normal_values(keys[15], (D,), 0.3, 4.0, (), jnp.float32),
        "out_cotangent": normal_values(keys[16], (ROWS, LEN, D), 1.0, 6.0, ((0, 4), (1, 8))),
        "global_cotangent": normal_values(keys[17], (ROWS, GLOB, D), 1.0, 6.0, ((0, 4),)),
    }


@jax.custom_vjp
def low(v):
    return lax.optimization_barrier(v.astype(jnp.bfloat16)).astype(jnp.float32)

@jax.custom_vjp
def low_back(v):
    return v

def low_keep(v):
    return (low(v), None)

def low_pass(kept, grad):
    return (grad,)

def back_keep(v):
    return (v, None)

def back_low(kept, grad):
    return (low(grad),)
low.defvjp(low_keep, low_pass)
low_back.defvjp(back_keep, back_low)
EPS = 1e-05
NEGATIVE = -1e+30

def norm_rows(source, scaling, offset):
    center = lax.optimization_barrier(jnp.mean(source, axis=-1, keepdims=True))
    spread = source - center
    variance = lax.optimization_barrier(jnp.mean(spread * spread, axis=-1, keepdims=True))
    return spread * lax.rsqrt(variance + EPS) * scaling + offset

def product(former, latter):
    return jnp.dot(former, latter, precision=lax.Precision.HIGHEST)

def attend(queries, key_rows, value_rows, query_seg, key_seg):
    scores = jnp.einsum('qhd,khd->hqk', queries, key_rows, precision=lax.Precision.HIGHEST)
    scores = low_back(scores * HEAD_DIM ** (-0.5))
    allowed = (query_seg[:, None] == key_seg[None, :])[None]
    scores = jnp.where(allowed, scores, NEGATIVE)
    maxima = lax.optimization_barrier(jnp.max(scores, axis=-1, keepdims=True))
    raised = jnp.exp(scores - maxima)
    weights = low(raised / lax.optimization_barrier(jnp.sum(raised, axis=-1, keepdims=True)))
    return jnp.einsum('hqk,khd->qhd', weights, value_rows, precision=lax.Precision.HIGHEST)

def feed_forward(state, params):
    normed = low(norm_rows(state, params[6], params[7]))
    hidden = low_back(product(normed, params[8]) + params[9])
    active = low(jax.nn.gelu(hidden, approximate=False))
    return state + product(active, params[10]) + params[11]

def encoder_layer(params, tok_row, glob_row, seg_row, gseg_row):
    sectioned = jnp.roll(tok_row, -HALF, axis=0)
    normed = low(norm_rows(sectioned, params[0], params[1]))
    glob_normed = low(norm_rows(glob_row, params[2], params[3]))
    projected = low(low_back(product(normed, params[4]))).reshape(LEN, 3, HEADS, HEAD_DIM)
    glob_proj = low(low_back(product(glob_normed, params[4]))).reshape(GLOB, 3, HEADS, HEAD_DIM)
    block_count = LEN // BLOCK
    block_shape = (block_count, BLOCK, HEADS, HEAD_DIM)
    glob_keys = glob_proj[:, 1]
    glob_values = glob_proj[:, 2]

    def one_block(pieces):
        queries, key_rows, value_rows, seg_block = pieces
        return attend(queries, jnp.concatenate([key_rows, glob_keys], axis=0), jnp.concatenate([value_rows, glob_values], axis=0), seg_block, jnp.concatenate([seg_block, gseg_row], axis=0))
    local_out = lax.map(jax.checkpoint(one_block), (projected[:, 0].reshape(block_shape), projected[:, 1].reshape(block_shape), projected[:, 2].reshape(block_shape), seg_row.reshape(block_count, BLOCK)))
    attended = low(low_back(local_out.reshape(LEN, D)))
    glob_out = jax.checkpoint(attend)(glob_proj[:, 0], jnp.concatenate([glob_keys, projected[:, 1]], axis=0), jnp.concatenate([glob_values, projected[:, 2]], axis=0), gseg_row, jnp.concatenate([gseg_row, seg_row], axis=0))
    glob_attended = low(low_back(glob_out.reshape(GLOB, D)))
    attn_sum = sectioned + low_back(product(attended, params[5]))
    glob_sum = glob_row + low_back(product(glob_attended, params[5]))
    return (feed_forward(attn_sum, params), feed_forward(glob_sum, params))

def add_pair(former, latter):
    return former + latter

def reference(tokens, global_states, token_seg, global_seg, attn_gain, attn_shift, glob_gain, glob_shift, w_qkv, w_out, ffn_gain, ffn_shift, w_up, up_bias, w_down, down_bias, out_cotangent, global_cotangent):
    params = tuple((weight_arr.astype(jnp.float32) for weight_arr in (attn_gain, attn_shift, glob_gain, glob_shift, w_qkv, w_out, ffn_gain, ffn_shift, w_up, up_bias, w_down, down_bias)))

    def one_row(summed, row_data):
        tok_row, glob_row, seg_row, gseg_row, cot_row, gcot_row = row_data

        def forward(weights, tok_in, glob_in):
            return encoder_layer(weights, tok_in, glob_in, seg_row, gseg_row)
        outputs, pullback = jax.vjp(forward, params, tok_row.astype(jnp.float32), glob_row.astype(jnp.float32))
        weight_grads, tok_grad, glob_grad = pullback((cot_row.astype(jnp.float32), gcot_row.astype(jnp.float32)))
        summed = jax.tree.map(add_pair, summed, weight_grads)
        return (summed, (outputs[0].astype(jnp.bfloat16), outputs[1].astype(jnp.bfloat16), tok_grad.astype(jnp.bfloat16), glob_grad.astype(jnp.bfloat16)))
    empty_sums = jax.tree.map(jnp.zeros_like, params)
    summed, stacked = lax.scan(one_row, empty_sums, (tokens, global_states, token_seg, global_seg, out_cotangent, global_cotangent))
    return (stacked[0], stacked[1], stacked[2], stacked[3], summed[0], summed[1], summed[2], summed[3], summed[4], summed[5], summed[6], summed[7], summed[8], summed[9], summed[10], summed[11])
```

```python
import functools

import jax
import jax.numpy as jnp
from jax import lax
from jax.experimental import pallas as pl
from jax.experimental.pallas import tpu as pltpu
from jax.sharding import PartitionSpec as P

HEADS = 12
HEAD_DIM = 64
BLOCK = 512


EPS = 1e-05
NEGATIVE = -1e30


def from_behind(block, axis, distance):
    devices = range(lax.axis_size(axis))
    route = [((i - distance) % len(devices), i) for i in devices]
    return lax.ppermute(block, axis, route)


def norm_rows(source, scaling, offset):
    center = jnp.mean(source, axis=-1, keepdims=True)
    spread = source - center
    variance = jnp.mean(spread * spread, axis=-1, keepdims=True)
    return spread * lax.rsqrt(variance + EPS) * scaling + offset


def norm_back(source, scaling, offset, upstream):
    _, pullback = jax.vjp(norm_rows, source, scaling, offset)
    return pullback(upstream)


def project(former, latter):
    return jnp.einsum("rsd,de->rse", former, latter, preferred_element_type=jnp.float32)


def project_back(former, latter):
    return jnp.einsum("rse,de->rsd", former, latter, preferred_element_type=jnp.float32)


def outer_sum(former, latter):
    return jnp.einsum("rsd,rse->de", former, latter, preferred_element_type=jnp.float32)


def gelu_exact(hidden):
    return jax.nn.gelu(hidden, approximate=False)


def ffn_forward(state, ffn_gain, ffn_shift, w_up, up_bias, w_down, down_bias):
    normed = norm_rows(state, ffn_gain, ffn_shift).astype(jnp.bfloat16)
    hidden = project(normed, w_up) + up_bias
    active = gelu_exact(hidden).astype(jnp.bfloat16)
    result = state + project(active, w_down) + down_bias
    return (result, (normed, hidden, active))


def ffn_backward(state, stored, upstream, ffn_gain, ffn_shift, w_up, w_down):
    normed, hidden, active = stored
    upstream_low = upstream.astype(jnp.bfloat16)
    grad_down = outer_sum(active, upstream_low)
    grad_down_bias = jnp.sum(upstream, axis=(0, 1))
    grad_active = project_back(upstream_low, w_down)
    _, gelu_pull = jax.vjp(gelu_exact, hidden)
    grad_hidden = gelu_pull(grad_active)[0].astype(jnp.bfloat16)
    grad_up = outer_sum(normed, grad_hidden)
    grad_up_bias = jnp.sum(grad_hidden.astype(jnp.float32), axis=(0, 1))
    grad_normed = project_back(grad_hidden, w_up)
    grad_state, grad_gain, grad_shift = norm_back(state, ffn_gain, ffn_shift, grad_normed)
    return (
        upstream + grad_state,
        (grad_gain, grad_shift, grad_up, grad_up_bias, grad_down, grad_down_bias),
    )


def local_scores(queries, keys_near, seg_near, keys_far, seg_far):
    scaling = HEAD_DIM ** (-0.5)
    near_scores = (
        jnp.einsum("rnqhd,rnkhd->rnhqk", queries, keys_near, preferred_element_type=jnp.float32)
        * scaling
    )
    far_scores = (
        jnp.einsum("rnqhd,rghd->rnhqg", queries, keys_far, preferred_element_type=jnp.float32)
        * scaling
    )
    near_open = (seg_near[:, :, :, None] == seg_near[:, :, None, :])[:, :, None]
    far_open = (seg_near[:, :, :, None] == seg_far[:, None, None, :])[:, :, None]
    return (jnp.where(near_open, near_scores, NEGATIVE), jnp.where(far_open, far_scores, NEGATIVE))


def local_forward(queries, keys_near, values_near, seg_near, keys_far, values_far, seg_far):
    near_scores, far_scores = local_scores(queries, keys_near, seg_near, keys_far, seg_far)
    maxima = jnp.maximum(jnp.max(near_scores, axis=-1), jnp.max(far_scores, axis=-1))
    near_exp = jnp.exp(near_scores - maxima[..., None])
    far_exp = jnp.exp(far_scores - maxima[..., None])
    totals = jnp.sum(near_exp, axis=-1) + jnp.sum(far_exp, axis=-1)
    near_weights = (near_exp / totals[..., None]).astype(jnp.bfloat16)
    far_weights = (far_exp / totals[..., None]).astype(jnp.bfloat16)
    mixed_out = jnp.einsum(
        "rnhqk,rnkhd->rnqhd", near_weights, values_near, preferred_element_type=jnp.float32
    )
    mixed_out = mixed_out + jnp.einsum(
        "rnhqg,rghd->rnqhd", far_weights, values_far, preferred_element_type=jnp.float32
    )
    return (mixed_out, maxima + jnp.log(totals))


def local_backward(
    queries, keys_near, values_near, seg_near, keys_far, values_far, seg_far, logsum, upstream
):
    scaling = HEAD_DIM ** (-0.5)
    near_scores, far_scores = local_scores(queries, keys_near, seg_near, keys_far, seg_far)
    near_weights = jnp.exp(near_scores - logsum[..., None])
    far_weights = jnp.exp(far_scores - logsum[..., None])
    near_grad = jnp.einsum(
        "rnqhd,rnkhd->rnhqk", upstream, values_near, preferred_element_type=jnp.float32
    )
    far_grad = jnp.einsum(
        "rnqhd,rghd->rnhqg", upstream, values_far, preferred_element_type=jnp.float32
    )
    row_inner = jnp.sum(near_weights * near_grad, axis=-1) + jnp.sum(
        far_weights * far_grad, axis=-1
    )
    near_score_grad = (near_weights * (near_grad - row_inner[..., None])).astype(jnp.bfloat16)
    far_score_grad = (far_weights * (far_grad - row_inner[..., None])).astype(jnp.bfloat16)
    grad_queries = jnp.einsum(
        "rnhqk,rnkhd->rnqhd", near_score_grad, keys_near, preferred_element_type=jnp.float32
    )
    grad_queries = scaling * (
        grad_queries
        + jnp.einsum(
            "rnhqg,rghd->rnqhd", far_score_grad, keys_far, preferred_element_type=jnp.float32
        )
    )
    grad_keys = scaling * jnp.einsum(
        "rnhqk,rnqhd->rnkhd", near_score_grad, queries, preferred_element_type=jnp.float32
    )
    grad_values = jnp.einsum(
        "rnhqk,rnqhd->rnkhd",
        near_weights.astype(jnp.bfloat16),
        upstream,
        preferred_element_type=jnp.float32,
    )
    grad_keys_far = scaling * jnp.einsum(
        "rnhqg,rnqhd->rghd", far_score_grad, queries, preferred_element_type=jnp.float32
    )
    grad_values_far = jnp.einsum(
        "rnhqg,rnqhd->rghd",
        far_weights.astype(jnp.bfloat16),
        upstream,
        preferred_element_type=jnp.float32,
    )
    return (grad_queries, grad_keys, grad_values, grad_keys_far, grad_values_far)


def global_scores(glob_queries, glob_keys, glob_seg, key_rows, seg_tokens):
    scaling = HEAD_DIM ** (-0.5)
    remote_scores = (
        jnp.einsum("rghd,rshd->rhgs", glob_queries, key_rows, preferred_element_type=jnp.float32)
        * scaling
    )
    own_scores = (
        jnp.einsum("rghd,rjhd->rhgj", glob_queries, glob_keys, preferred_element_type=jnp.float32)
        * scaling
    )
    remote_open = glob_seg[:, None, :, None] == seg_tokens[:, None, None, :]
    own_open = glob_seg[:, None, :, None] == glob_seg[:, None, None, :]
    return (
        jnp.where(remote_open, remote_scores, NEGATIVE),
        jnp.where(own_open, own_scores, NEGATIVE),
    )


def general(
    tokens,
    global_states,
    token_seg,
    global_seg,
    attn_gain,
    attn_shift,
    glob_gain,
    glob_shift,
    w_qkv,
    w_out,
    ffn_gain,
    ffn_shift,
    w_up,
    up_bias,
    w_down,
    down_bias,
    out_cotangent,
    global_cotangent,
):
    row_count, tok_count, model_width = tokens.shape
    glob_count = global_states.shape[1]
    half_block = BLOCK // 2
    block_count = tok_count // BLOCK
    seq_devices = lax.axis_size("seq")
    scaling = HEAD_DIM ** (-0.5)
    low_type = jnp.bfloat16
    arrived = from_behind(tokens[:, :half_block], "seq", -1)
    sectioned = jnp.concatenate([tokens[:, half_block:], arrived], axis=1).astype(jnp.float32)
    glob_state = global_states.astype(jnp.float32)
    normed = norm_rows(sectioned, attn_gain, attn_shift).astype(low_type)
    glob_normed = norm_rows(glob_state, glob_gain, glob_shift).astype(low_type)
    projected = (
        project(normed, w_qkv).astype(low_type).reshape(row_count, tok_count, 3, HEADS, HEAD_DIM)
    )
    glob_proj = (
        project(glob_normed, w_qkv)
        .astype(low_type)
        .reshape(row_count, glob_count, 3, HEADS, HEAD_DIM)
    )
    queries = projected[:, :, 0]
    key_rows = projected[:, :, 1]
    value_rows = projected[:, :, 2]
    glob_queries = glob_proj[:, :, 0]
    glob_keys = glob_proj[:, :, 1]
    glob_values = glob_proj[:, :, 2]
    block_shape = (row_count, block_count, BLOCK, HEADS, HEAD_DIM)
    block_queries = queries.reshape(block_shape)
    block_keys = key_rows.reshape(block_shape)
    block_values = value_rows.reshape(block_shape)
    block_seg = token_seg.reshape(row_count, block_count, BLOCK)
    local_out, local_logsum = local_forward(
        block_queries, block_keys, block_values, block_seg, glob_keys, glob_values, global_seg
    )
    remote_scores, own_scores = global_scores(
        glob_queries, glob_keys, global_seg, key_rows, token_seg
    )
    maxima = jnp.maximum(
        lax.pmax(jnp.max(remote_scores, axis=-1), "seq"), jnp.max(own_scores, axis=-1)
    )
    remote_total = jnp.sum(jnp.exp(remote_scores - maxima[..., None]), axis=-1)
    totals = lax.psum(remote_total, "seq") + jnp.sum(
        jnp.exp(own_scores - maxima[..., None]), axis=-1
    )
    remote_weights = (jnp.exp(remote_scores - maxima[..., None]) / totals[..., None]).astype(
        low_type
    )
    own_weights = (jnp.exp(own_scores - maxima[..., None]) / totals[..., None]).astype(low_type)
    remote_part = jnp.einsum(
        "rhgs,rshd->rghd", remote_weights, value_rows, preferred_element_type=jnp.float32
    )
    glob_out = lax.psum(remote_part, "seq")
    glob_out = glob_out + jnp.einsum(
        "rhgj,rjhd->rghd", own_weights, glob_values, preferred_element_type=jnp.float32
    )
    glob_logsum = maxima + jnp.log(totals)
    attended = local_out.reshape(row_count, tok_count, model_width).astype(low_type)
    glob_attended = glob_out.reshape(row_count, glob_count, model_width).astype(low_type)
    attn_sum = sectioned + project(attended, w_out)
    glob_sum = glob_state + project(glob_attended, w_out)
    result, stored = ffn_forward(attn_sum, ffn_gain, ffn_shift, w_up, up_bias, w_down, down_bias)
    glob_result, glob_stored = ffn_forward(
        glob_sum, ffn_gain, ffn_shift, w_up, up_bias, w_down, down_bias
    )
    grad_attn_sum, tok_ffn = ffn_backward(
        attn_sum, stored, out_cotangent.astype(jnp.float32), ffn_gain, ffn_shift, w_up, w_down
    )
    grad_glob_sum, glob_ffn = ffn_backward(
        glob_sum,
        glob_stored,
        global_cotangent.astype(jnp.float32),
        ffn_gain,
        ffn_shift,
        w_up,
        w_down,
    )
    branch_low = grad_attn_sum.astype(low_type)
    glob_branch_low = grad_glob_sum.astype(low_type)
    grad_out_all = (
        outer_sum(attended, branch_low) + outer_sum(glob_attended, glob_branch_low) / seq_devices
    )
    upstream_mix = project_back(branch_low, w_out).astype(low_type).reshape(block_shape)
    glob_upstream = (
        project_back(glob_branch_low, w_out)
        .astype(low_type)
        .reshape(row_count, glob_count, HEADS, HEAD_DIM)
    )
    remote_exact = jnp.exp(remote_scores - glob_logsum[..., None])
    own_exact = jnp.exp(own_scores - glob_logsum[..., None])
    remote_grad = jnp.einsum(
        "rghd,rshd->rhgs", glob_upstream, value_rows, preferred_element_type=jnp.float32
    )
    own_grad = jnp.einsum(
        "rghd,rjhd->rhgj", glob_upstream, glob_values, preferred_element_type=jnp.float32
    )
    row_inner = lax.psum(jnp.sum(remote_exact * remote_grad, axis=-1), "seq")
    row_inner = row_inner + jnp.sum(own_exact * own_grad, axis=-1)
    remote_score_grad = (remote_exact * (remote_grad - row_inner[..., None])).astype(low_type)
    own_score_grad = (own_exact * (own_grad - row_inner[..., None])).astype(low_type)
    remote_queries = scaling * jnp.einsum(
        "rhgs,rshd->rghd", remote_score_grad, key_rows, preferred_element_type=jnp.float32
    )
    tok_keys_extra = scaling * jnp.einsum(
        "rhgs,rghd->rshd", remote_score_grad, glob_queries, preferred_element_type=jnp.float32
    )
    tok_values_extra = jnp.einsum(
        "rhgs,rghd->rshd",
        remote_exact.astype(low_type),
        glob_upstream,
        preferred_element_type=jnp.float32,
    )
    own_queries = scaling * jnp.einsum(
        "rhgj,rjhd->rghd", own_score_grad, glob_keys, preferred_element_type=jnp.float32
    )
    own_keys = scaling * jnp.einsum(
        "rhgj,rghd->rjhd", own_score_grad, glob_queries, preferred_element_type=jnp.float32
    )
    own_values = jnp.einsum(
        "rhgj,rghd->rjhd",
        own_exact.astype(low_type),
        glob_upstream,
        preferred_element_type=jnp.float32,
    )
    grad_queries, grad_keys, grad_values, grad_keys_far, grad_values_far = local_backward(
        block_queries,
        block_keys,
        block_values,
        block_seg,
        glob_keys,
        glob_values,
        global_seg,
        local_logsum,
        upstream_mix,
    )
    far_grads = lax.psum((remote_queries, grad_keys_far, grad_values_far), "seq")
    head_shape = (row_count, tok_count, HEADS, HEAD_DIM)
    grad_projected = jnp.stack(
        [
            grad_queries.reshape(head_shape),
            grad_keys.reshape(head_shape) + tok_keys_extra,
            grad_values.reshape(head_shape) + tok_values_extra,
        ],
        axis=2,
    )
    grad_projected = grad_projected.reshape(row_count, tok_count, 3 * model_width).astype(low_type)
    glob_grad_projected = jnp.stack(
        [far_grads[0] + own_queries, far_grads[1] + own_keys, far_grads[2] + own_values], axis=2
    )
    glob_grad_projected = glob_grad_projected.reshape(
        row_count, glob_count, 3 * model_width
    ).astype(low_type)
    grad_qkv_all = (
        outer_sum(normed, grad_projected)
        + outer_sum(glob_normed, glob_grad_projected) / seq_devices
    )
    grad_normed = project_back(grad_projected, w_qkv)
    glob_grad_normed = project_back(glob_grad_projected, w_qkv)
    grad_sectioned, attn_gain_grad, attn_shift_grad = norm_back(
        sectioned, attn_gain, attn_shift, grad_normed
    )
    grad_sectioned = grad_sectioned + grad_attn_sum
    glob_grad_state, glob_gain_grad, glob_shift_grad = norm_back(
        glob_state, glob_gain, glob_shift, glob_grad_normed
    )
    global_grad = (glob_grad_state + grad_glob_sum).astype(low_type)
    grad_low = grad_sectioned.astype(low_type)
    returned = from_behind(grad_low[:, tok_count - half_block :], "seq", 1)
    token_grad = jnp.concatenate([returned, grad_low[:, : tok_count - half_block]], axis=1)
    ffn_gain_all = tok_ffn[0] + glob_ffn[0] / seq_devices
    ffn_shift_all = tok_ffn[1] + glob_ffn[1] / seq_devices
    up_all = tok_ffn[2] + glob_ffn[2] / seq_devices
    up_bias_all = tok_ffn[3] + glob_ffn[3] / seq_devices
    down_all = tok_ffn[4] + glob_ffn[4] / seq_devices
    down_bias_all = tok_ffn[5] + glob_ffn[5] / seq_devices
    glob_gain_all = glob_gain_grad / seq_devices
    glob_shift_all = glob_shift_grad / seq_devices
    mat_sums = (
        lax.psum_scatter(
            grad_qkv_all.astype(jnp.bfloat16), "batch", scatter_dimension=1, tiled=True
        ).astype(jnp.float32),
        lax.psum_scatter(
            grad_out_all.astype(jnp.bfloat16), "batch", scatter_dimension=1, tiled=True
        ).astype(jnp.float32),
        lax.psum_scatter(
            up_all.astype(jnp.bfloat16), "batch", scatter_dimension=1, tiled=True
        ).astype(jnp.float32),
        lax.psum_scatter(
            down_all.astype(jnp.bfloat16), "batch", scatter_dimension=1, tiled=True
        ).astype(jnp.float32),
    )
    vec_sums = (
        lax.psum(attn_gain_grad.astype(jnp.bfloat16), "batch").astype(jnp.float32),
        lax.psum(attn_shift_grad.astype(jnp.bfloat16), "batch").astype(jnp.float32),
        lax.psum(glob_gain_all.astype(jnp.bfloat16), "batch").astype(jnp.float32),
        lax.psum(glob_shift_all.astype(jnp.bfloat16), "batch").astype(jnp.float32),
        lax.psum(ffn_gain_all.astype(jnp.bfloat16), "batch").astype(jnp.float32),
        lax.psum(ffn_shift_all.astype(jnp.bfloat16), "batch").astype(jnp.float32),
        lax.psum(up_bias_all.astype(jnp.bfloat16), "batch").astype(jnp.float32),
        lax.psum(down_bias_all.astype(jnp.bfloat16), "batch").astype(jnp.float32),
    )
    shares = (
        lax.psum_scatter(vec_sums[0], "seq", scatter_dimension=0, tiled=True),
        lax.psum_scatter(vec_sums[1], "seq", scatter_dimension=0, tiled=True),
        lax.psum_scatter(vec_sums[2], "seq", scatter_dimension=0, tiled=True),
        lax.psum_scatter(vec_sums[3], "seq", scatter_dimension=0, tiled=True),
        lax.psum_scatter(mat_sums[0], "seq", scatter_dimension=0, tiled=True),
        lax.psum_scatter(mat_sums[1], "seq", scatter_dimension=0, tiled=True),
        lax.psum_scatter(vec_sums[4], "seq", scatter_dimension=0, tiled=True),
        lax.psum_scatter(vec_sums[5], "seq", scatter_dimension=0, tiled=True),
        lax.psum_scatter(mat_sums[2], "seq", scatter_dimension=0, tiled=True),
        lax.psum_scatter(vec_sums[6], "seq", scatter_dimension=0, tiled=True),
        lax.psum_scatter(mat_sums[3], "seq", scatter_dimension=0, tiled=True),
        lax.psum_scatter(vec_sums[7], "seq", scatter_dimension=0, tiled=True),
    )
    matrices = (shares[4], shares[5], shares[8], shares[10])
    vectors = (
        shares[0],
        shares[1],
        shares[2],
        shares[3],
        shares[6],
        shares[7],
        shares[9],
        shares[11],
    )
    return (
        result.astype(low_type),
        glob_result.astype(low_type),
        token_grad,
        global_grad,
        vectors[0],
        vectors[1],
        vectors[2],
        vectors[3],
        matrices[0],
        matrices[1],
        vectors[4],
        vectors[5],
        matrices[2],
        vectors[6],
        matrices[3],
        vectors[7],
    )


MESH = pl.DeviceIdType.MESH
BF = jnp.bfloat16
F32 = jnp.float32


def dot_nn(left, right):
    return lax.dot_general(left, right, (((1,), (0,)), ((), ())), preferred_element_type=F32)


def dot_nt(left, right):
    return lax.dot_general(left, right, (((1,), (1,)), ((), ())), preferred_element_type=F32)


def lanes_of(shape):
    return lax.broadcasted_iota(jnp.int32, shape, len(shape) - 1)


def two_parts(value):
    high = value.astype(BF)
    return high, (value - high.astype(F32)).astype(BF)


def norm_stats(value):
    center = jnp.mean(value, axis=-1, keepdims=True)
    spread = value - center
    variance = jnp.mean(spread * spread, axis=-1, keepdims=True)
    return spread, lax.rsqrt(variance + EPS)


def norm_pull(value, gain, upstream):
    spread, scale = norm_stats(value)
    unit = spread * scale
    scaled = upstream * gain
    first = jnp.mean(scaled, axis=-1, keepdims=True)
    second = jnp.mean(scaled * unit, axis=-1, keepdims=True)
    grad = scale * (scaled - first - unit * second)
    return (
        grad,
        jnp.sum(upstream * unit, axis=0, keepdims=True),
        jnp.sum(upstream, axis=0, keepdims=True),
    )


def gelu_pair(hidden):
    size = jnp.abs(hidden) * 0.7071067811865476
    step = 1.0 / (1.0 + 0.3275911 * size)
    bell = jnp.exp(-(size * size))
    series = 1.061405429 * 0.5
    for term in (-1.453152027, 1.421413741, -0.284496736, 0.254829592):
        series = series * step + term * 0.5
    tail = series * step * bell
    mass = jnp.where(hidden < 0.0, tail, 1.0 - tail)
    return hidden * mass, mass + hidden * (bell * 0.3989422804014327)


def layer_kernel(
    tokens, gstates, tseg, gseg, attn_gain, attn_shift, glob_gain, glob_shift, w_qkv, w_out,
    ffn_gain, ffn_shift, w_up, up_bias, w_down, down_bias, cotan, gcotan,
    o_out, o_gout, o_tgrad, o_ggrad, o_qkv, o_wout, o_up, o_down, o_vec, o_ub,
    sec, nrm, proj, kvt, probs, att_t, att, x2, n2, n2t, ct, ct_t, acc, gn2, gatt, qaug, kaug,
    wq, wo, wus, wds,
    lse_t, rl_t, og_t, msg1, rcv1, cx, rcv2, rcv3, vec, rvec, rll,
    gd, r0d, r1d, r2d, r3d, r4d, gu, r0u, r1u, r2u, r3u, r4u, r0q, r1qx, r1qy, r2q, r3q, r4q,
    loc, wsem, hs, hr, m1s, m1r, m2s, m2r, m3s, m3r, gos, gor, ggs_s, ggs_r, vs, vr,
    d0s, d0r, d1s, d1r, d2s, d2r, d3s, d3r, d4s, d4r,
    u0s, u0r, u1s, u1r, u2s, u2r, u3s, u3r, u4s, u4r,
    q0s, q0r, q1s, q1r, q2s, q2r, q3s, q3r, q4s, q4r,
    hs2, hr2, osem,
):
    tok, width = tokens.shape
    glob = gstates.shape[0]
    rows = tok + glob
    n_seq = lax.axis_size("seq")
    slots = glob // n_seq
    wide = tok + slots
    half = tok // 2
    pairs = HEADS // 2
    chunk = wus.shape[2]
    n_chunk = up_bias.shape[1] // chunk
    tail = 128

    s = lax.axis_index("seq")
    b = lax.axis_index("batch")
    x, zl, zh = s % 2, (s // 2) % 2, s // 4
    c, y = b % 2, b // 2
    dev_c, dev_y = (s, b + 1 - 2 * c), (s, b + 2 - 4 * y)
    dev_x, dev_1, dev_2 = (s + 1 - 2 * x, b), (s + 2 - 4 * zl, b), (s + 4 - 8 * zh, b)

    def flip(k):
        other = s
        if k & 1:
            other = other + 1 - 2 * x
        if k & 2:
            other = other + 2 - 4 * zl
        if k & 4:
            other = other + 4 - 8 * zh
        return other

    def remote(src, dst, ss, rs, dev):
        return pltpu.make_async_remote_copy(
            src_ref=src, dst_ref=dst, send_sem=ss, recv_sem=rs, device_id=dev, device_id_type=MESH
        )

    peers = tuple(range(1, n_seq))

    my_slots = pl.multiple_of(s * slots, slots)
    loads = [
        (tokens.at[pl.ds(half, half)], sec.at[pl.ds(0, half)]),
        (gstates, sec.at[pl.ds(tok, glob)]),
        (w_qkv, wq),
        (cotan, ct.at[pl.ds(0, tok)]),
        (gcotan.at[pl.ds(my_slots, slots)], ct.at[pl.ds(tok, slots)]),
        (w_out, wo),
    ]
    loads = [pltpu.make_async_copy(a, d, loc.at[i]) for i, (a, d) in enumerate(loads)]
    for load in loads:
        load.start()

    def stream(i, slot):
        at = pl.multiple_of(i * chunk, chunk)
        return (
            pltpu.make_async_copy(w_up.at[:, pl.ds(at, chunk)], wus.at[slot], wsem.at[0, slot]),
            pltpu.make_async_copy(w_down.at[pl.ds(at, chunk)], wds.at[slot], wsem.at[1, slot]),
        )

    for i in range(2):
        for copy in stream(i, i):
            copy.start()

    bar = pltpu.get_barrier_semaphore()
    for k in peers:
        pl.semaphore_signal(bar, inc=1, device_id=(flip(k), b), device_id_type=MESH)
    pl.semaphore_signal(bar, inc=1, device_id=dev_c, device_id_type=MESH)
    pl.semaphore_signal(bar, inc=1, device_id=dev_y, device_id_type=MESH)
    pl.semaphore_wait(bar, len(peers) + 2)
    halo = remote(
        tokens.at[pl.ds(0, half)], sec.at[pl.ds(half, half)], hs.at[0], hr.at[0],
        (lax.rem(s + n_seq - 1, n_seq), b),
    )
    halo.start()

    seg_row = jnp.concatenate([tseg[...], gseg[...]], axis=1)
    which = lax.broadcasted_iota(jnp.int32, (128, rows), 0)
    col = lanes_of((128, rows))
    is_glob = col >= tok
    same = which == seg_row
    q_t = jnp.where(which < 3, jnp.where(same, 1.0, 0.0), jnp.where((which == 3) & is_glob, 1.0, 0.0))
    far = jnp.where(s == 0, 0.0, NEGATIVE)
    k_t = jnp.where(which < 3, jnp.where(same, 0.0, NEGATIVE), jnp.where((which == 3) & is_glob, far, 0.0))
    qaug[...] = jnp.transpose(q_t).astype(BF)
    kaug[...] = jnp.transpose(k_t).astype(BF)

    def norm_to(first, count, gain, shift):
        for r in range(first, first + count, 128):
            spread, scale = norm_stats(sec[pl.ds(r, 128), :].astype(F32))
            nrm[pl.ds(r, 128), :] = (spread * scale * gain[...] + shift[...]).astype(BF)

    def project_rows(first, count):
        def step(i, carry):
            at = pl.multiple_of(i * width, width)
            proj[pl.ds(first, count), pl.ds(at, width)] = dot_nn(
                nrm[pl.ds(first, count), :], wq[:, pl.ds(at, width)]
            ).astype(BF)
            return carry

        lax.fori_loop(0, 3, step, 0)

    loads[1].wait()
    norm_to(tok, glob, glob_gain, glob_shift)
    loads[0].wait()
    norm_to(0, half, attn_gain, attn_shift)
    loads[2].wait()
    project_rows(tok, glob)
    project_rows(0, half)
    loads[3].wait()
    loads[4].wait()
    ct_t[:, pl.ds(0, wide)] = jnp.transpose(ct[...])
    halo.wait()
    norm_to(half, half, attn_gain, attn_shift)
    project_rows(half, half)

    kvt[...] = jnp.transpose(proj[:, pl.ds(2 * width, width)])
    lane_p = lanes_of((1, 128))
    even = jnp.where(lane_p < HEAD_DIM, HEAD_DIM ** (-0.5), 0.0).astype(BF)
    odd = jnp.where(lane_p < HEAD_DIM, 0.0, HEAD_DIM ** (-0.5)).astype(BF)
    even_one = jnp.where(lane_p < HEAD_DIM, 1.0, 0.0).astype(BF)
    odd_one = jnp.where(lane_p < HEAD_DIM, 0.0, 1.0).astype(BF)
    first_head = lax.broadcasted_iota(jnp.int32, (128, 128), 0) < HEAD_DIM
    lse_t[...] = jnp.zeros_like(lse_t)
    rl_t[...] = jnp.zeros_like(rl_t)

    def glob_forward(p, carry):
        at = pl.multiple_of(p * 128, 128)
        keys = jnp.concatenate([proj[:, pl.ds(width + at, 128)], kaug[...]], axis=1)
        qg = proj[pl.ds(tok, glob), pl.ds(at, 128)]
        qa = qaug[pl.ds(tok, glob), :]
        queries = jnp.concatenate(
            [jnp.concatenate([qg * even, qa], axis=1), jnp.concatenate([qg * odd, qa], axis=1)], axis=0
        )
        scores = dot_nt(keys, queries)
        top = jnp.max(scores, axis=0, keepdims=True)
        raised = jnp.exp(scores - top)
        total = jnp.sum(raised, axis=0, keepdims=True)
        weights = (raised * (1.0 / total)).astype(BF)
        probs[p, :, pl.ds(2 * tok, 2 * glob)] = weights
        mixed = dot_nn(kvt[pl.ds(at, 128), :], weights)
        og_t[pl.ds(at, 128), :] = jnp.where(first_head, mixed[:, :glob], mixed[:, glob:])
        logsum = top + jnp.log(total)
        lse_t[pl.ds(2 * p, 1), :] = logsum[:, :glob]
        lse_t[pl.ds(2 * p + 1, 1), :] = logsum[:, glob:]
        return carry

    lax.fori_loop(0, pairs, glob_forward, 0)

    lse = jnp.transpose(lse_t[...])
    in_heads = lanes_of((glob, 128)) < HEADS
    lse = jnp.where(in_heads, lse, 0.0)
    part_a, rest = two_parts(lse)
    rest = lse - part_a.astype(F32)
    part_b = rest.astype(BF)
    part_c = rest - part_b.astype(F32)
    packed = part_a.astype(F32) + pltpu.roll(part_b.astype(F32), 16, 1) + pltpu.roll(part_c, 32, 1)
    msg1[:, pl.ds(0, width)] = jnp.transpose(og_t[...]).astype(BF)
    msg1[:, pl.ds(width, 128)] = packed.astype(BF)
    sends1 = []
    for k in peers:
        other = flip(k)
        at = pl.multiple_of(other * slots, slots)
        copy = remote(msg1.at[pl.ds(at, slots)], rcv1.at[k], m1s.at[k], m1r.at[k], (other, b))
        copy.start()
        sends1.append(copy)
    rcv1[0] = msg1[pl.ds(my_slots, slots), :]

    def local_forward_pair(p, carry):
        at = pl.multiple_of(p * 128, 128)
        keys = jnp.concatenate([proj[:, pl.ds(width + at, 128)], kaug[...]], axis=1)
        qp = proj[pl.ds(0, tok), pl.ds(at, 128)]
        for e, mask in ((0, even), (1, odd)):
            queries = jnp.concatenate([qp * mask, qaug[pl.ds(0, tok), :]], axis=1)
            scores = dot_nt(keys, queries)
            top = jnp.max(scores, axis=0, keepdims=True)
            raised = jnp.exp(scores - top)
            inverse = 1.0 / jnp.sum(raised, axis=0, keepdims=True)
            weights = raised.astype(BF)
            probs[p, :, pl.ds(e * tok, tok)] = weights
            rl_t[pl.ds(2 * p + e, 1), :] = inverse
            here = pl.multiple_of(at + e * HEAD_DIM, HEAD_DIM)
            mixed = dot_nn(kvt[pl.ds(here, HEAD_DIM), :], weights)
            att_t[pl.ds(here, HEAD_DIM), pl.ds(0, tok)] = (mixed * inverse).astype(BF)
        return carry

    lax.fori_loop(0, pairs, local_forward_pair, 0)
    att[pl.ds(0, tok), :] = jnp.transpose(att_t[:, pl.ds(0, tok)])

    head_of = lanes_of((128, width)) // HEAD_DIM
    spread_heads = jnp.where(head_of == lax.broadcasted_iota(jnp.int32, (128, width), 0), 1.0, 0.0).astype(BF)
    for copy in sends1:
        copy.wait()
    logs = []
    for k in range(n_seq):
        packed = rcv1[k, :, pl.ds(width, 128)].astype(F32)
        logs.append(packed + pltpu.roll(packed, 112, 1) + pltpu.roll(packed, 96, 1))
    high = functools.reduce(jnp.maximum, logs)
    raised = [jnp.exp(one - high) for one in logs]
    total = functools.reduce(jnp.add, raised)
    in_heads = lanes_of((slots, 128)) < HEADS
    shares = jnp.concatenate([jnp.where(in_heads, one / total, 0.0) for one in raised], axis=0)
    share_a, share_b = two_parts(shares)
    shares = dot_nn(share_a, spread_heads) + dot_nn(share_b, spread_heads)
    cx[...] = shares
    mixed = jnp.zeros((slots, width), F32)
    for k in range(n_seq):
        mixed = mixed + shares[k * slots : (k + 1) * slots] * rcv1[k, :, pl.ds(0, width)].astype(F32)
    att[pl.ds(tok, slots), :] = mixed.astype(BF)
    att_t[:, pl.ds(tok, tail)] = jnp.transpose(
        jnp.concatenate([mixed, jnp.zeros((tail - slots, width), F32)], axis=0)
    ).astype(BF)

    loads[5].wait()
    x2[...] = dot_nn(att[...], wo[...])
    x2[pl.ds(0, tok), :] += sec[pl.ds(0, tok), :].astype(F32)
    x2[pl.ds(tok, slots), :] += sec[pl.ds(pl.multiple_of(tok + my_slots, slots), slots), :].astype(F32)

    def second_norm(first, count):
        spread, scale = norm_stats(x2[pl.ds(first, count), :])
        n2[pl.ds(first, count), :] = (spread * scale * ffn_gain[...] + ffn_shift[...]).astype(BF)

    for r in range(0, tok, 128):
        second_norm(r, 128)
    second_norm(tok, slots)
    n2t[:, pl.ds(0, wide)] = jnp.transpose(n2[...])

    def d_core(i):
        return remote(gd.at[i, :, 1 - c], r0d.at[i], d0s.at[i], d0r.at[i], dev_c)

    def d_y(i):
        return remote(r0d.at[i, 1 - y], r1d.at[i], d1s.at[i], d1r.at[i], dev_y)

    def d_x(z):
        return remote(r1d.at[2 * z + 1 - x], r2d.at[z], d2s.at[z], d2r.at[z], dev_x)

    def d_1(h):
        return remote(r2d.at[2 * h + 1 - zl], r3d.at[h], d3s.at[h], d3r.at[h], dev_1)

    def d_2():
        return remote(r3d.at[1 - zh], r4d, d4s.at[0], d4r.at[0], dev_2)

    def do_d_y(i):
        d_core(i).wait_recv()
        r0d[i] = r0d[i] + gd[i, :, c]
        d_y(i).start()

    def do_d_x(z):
        for o in range(2):
            d_y(2 * z + o).wait_recv()
            r1d[2 * z + o] = r1d[2 * z + o] + r0d[2 * z + o, y]
        d_x(z).start()

    def do_d_1(h):
        for o in range(2):
            d_x(2 * h + o).wait_recv()
            r2d[2 * h + o] = r2d[2 * h + o] + r1d[2 * (2 * h + o) + x]
        d_1(h).start()

    def do_d_2():
        for h in range(2):
            d_1(h).wait_recv()
            r3d[h] = r3d[h] + r2d[2 * h + zl]
        d_2().start()

    def u_core(yy, j):
        return remote(gu.at[yy, 1 - c, j], r0u.at[yy, j], u0s.at[yy * 2 + j], u0r.at[yy * 2 + j], dev_c)

    def u_x(yy, j):
        return remote(r0u.at[yy, j, :, :, 1 - x], r1u.at[yy, j], u1s.at[yy * 2 + j], u1r.at[yy * 2 + j], dev_x)

    def u_y(j):
        return remote(r1u.at[1 - y, j], r2u.at[j], u2s.at[j], u2r.at[j], dev_y)

    def u_1():
        return remote(r2u.at[:, :, 1 - zl], r3u, u3s.at[0], u3r.at[0], dev_1)

    def u_2():
        return remote(r3u.at[:, 1 - zh], r4u, u4s.at[0], u4r.at[0], dev_2)

    def do_u_x(yy, j):
        u_core(yy, j).wait_recv()
        r0u[yy, j] = r0u[yy, j] + gu[yy, c, j]
        u_x(yy, j).start()

    def do_u_y(j):
        for yy in range(2):
            u_x(yy, j).wait_recv()
            r1u[yy, j] = r1u[yy, j] + r0u[yy, j, :, :, x]
        u_y(j).start()

    def do_u_1():
        for j in range(2):
            u_y(j).wait_recv()
            r2u[j] = r2u[j] + r1u[y, j]
        u_1().start()

    def do_u_2():
        u_1().wait_recv()
        r3u[...] = r3u[...] + r2u[:, :, zl]
        u_2().start()

    acc[...] = jnp.zeros_like(acc)
    gn2[...] = jnp.zeros_like(gn2)

    def ffn_step(i, carry):
        slot = lax.rem(i, 2)
        for copy in stream(i, slot):
            copy.wait()
        at = pl.multiple_of(i * chunk, chunk)
        hidden = dot_nn(n2[...], wus[slot]) + up_bias[:, pl.ds(at, chunk)]
        active, slope = gelu_pair(hidden)
        active = active.astype(BF)
        gd[i] = dot_nn(ct_t[:, pl.ds(0, wide)], active).astype(BF).reshape(gd.shape[1:])
        d_core(i).start()
        grad_hidden = (slope * dot_nt(ct[...], wds[slot])).astype(BF)
        gu[i // 4, (i // 2) % 2, i % 2] = (
            dot_nn(n2t[:, pl.ds(0, wide)], grad_hidden).astype(BF).reshape(gu.shape[3:])
        )

        @pl.when((i // 2) % 2 != c)
        def _():
            u_core(i // 4, i % 2).start()

        rll[pl.ds(i, 1), :] = jnp.sum(grad_hidden.astype(F32), axis=0, keepdims=True)
        acc[...] += dot_nn(active, wds[slot])
        gn2[...] += dot_nt(grad_hidden, wus[slot])

        @pl.when(i + 2 < n_chunk)
        def _():
            for copy in stream(i + 2, slot):
                copy.start()

        @pl.when(i >= 2)
        def _():
            do_d_y(i - 2)

        @pl.when((i >= 2) & (((i - 2) // 2) % 2 == c))
        def _():
            do_u_x((i - 2) // 4, i % 2)

        return carry

    lax.fori_loop(0, n_chunk, ffn_step, 0)

    vec[...] = jnp.zeros_like(vec)
    for i in range(n_chunk):
        vec[pl.ds(8 + i // 2, 1), pl.ds((i % 2) * chunk, chunk)] = rll[pl.ds(i, 1), :]

    def second_pull(first, count):
        grad, gain_term, shift_term = norm_pull(
            x2[pl.ds(first, count), :], ffn_gain[...], gn2[pl.ds(first, count), :]
        )
        upstream = ct[pl.ds(first, count), :].astype(F32)
        total = upstream + grad
        acc[pl.ds(first, count), :] += x2[pl.ds(first, count), :] + down_bias[...]
        x2[pl.ds(first, count), :] = total
        n2[pl.ds(first, count), :] = total.astype(BF)
        vec[pl.ds(4, 1), :] += gain_term
        vec[pl.ds(5, 1), :] += shift_term
        vec[pl.ds(6, 1), :] += jnp.sum(upstream, axis=0, keepdims=True)

    for r in range(0, tok, 128):
        second_pull(r, 128)
    second_pull(tok, slots)
    do_d_y(n_chunk - 2)
    do_d_y(n_chunk - 1)

    @pl.when(c == 1)
    def _():
        do_u_x(1, 0)
        do_u_x(1, 1)

    gatt[...] = dot_nt(n2[...], wo[...]).astype(BF)

    slot_grad = gatt[pl.ds(tok, slots), :].astype(F32)
    slot_att = att[pl.ds(tok, slots), :].astype(F32)
    head_sel = lanes_of((1, 128)) < HEADS

    def inner_aug(upstream, values):
        high, low = two_parts(upstream.astype(F32) * values)
        inner = dot_nt(high, spread_heads) + dot_nt(low, spread_heads)
        high, low = two_parts(jnp.where(head_sel, inner, 0.0))
        return (high.astype(F32) + pltpu.roll(low.astype(F32), 16, 1)).astype(BF)

    scaled = jnp.concatenate(
        [(cx[pl.ds(k * slots, slots), :] * slot_grad).astype(BF) for k in range(n_seq)], axis=0
    )
    msg1[:, pl.ds(0, width)] = scaled
    msg1[:, pl.ds(width, 128)] = inner_aug(scaled, jnp.concatenate([slot_att] * n_seq, axis=0))
    sends2 = []
    for k in peers:
        copy = remote(
            msg1.at[pl.ds(k * slots, slots)], rcv2.at[pl.ds(my_slots, slots)], m2s.at[k], m2r.at[k],
            (flip(k), b),
        )
        copy.start()
        sends2.append(copy)
    rcv2[pl.ds(my_slots, slots), :] = msg1[pl.ds(0, slots), :]

    n2t[:, pl.ds(0, tok)] = jnp.transpose(nrm[pl.ds(0, tok), :])
    mine = nrm[pl.ds(pl.multiple_of(tok + my_slots, slots), slots), :].astype(F32)
    n2t[:, pl.ds(tok, tail)] = jnp.transpose(
        jnp.concatenate([mine, jnp.zeros((tail - slots, width), F32)], axis=0)
    ).astype(BF)

    outs = nrm
    outs[pl.ds(0, wide), :] = acc[...].astype(BF)
    out_copy = pltpu.make_async_copy(outs.at[pl.ds(0, tok)], o_out, osem.at[0])
    out_copy.start()
    own_out = pltpu.make_async_copy(
        outs.at[pl.ds(tok, slots)], o_gout.at[pl.ds(my_slots, slots)], osem.at[1]
    )
    own_out.start()
    sends_o = []
    for k in peers:
        copy = remote(
            outs.at[pl.ds(tok, slots)], o_gout.at[pl.ds(my_slots, slots)], gos.at[k], gor.at[k], (flip(k), b)
        )
        copy.start()
        sends_o.append(copy)

    scale_c = jnp.transpose(
        jnp.concatenate([rl_t[...], jnp.zeros((128 - rl_t.shape[0], tok), F32)], axis=0)
    )
    scale_a, scale_b = two_parts(scale_c)
    for r in range(0, tok, 128):
        wider = dot_nn(scale_a[r : r + 128], spread_heads) + dot_nn(scale_b[r : r + 128], spread_heads)
        scaled = (gatt[pl.ds(r, 128), :].astype(F32) * wider).astype(BF)
        gatt[pl.ds(r, 128), :] = scaled
        qaug[pl.ds(r, 128), :] = inner_aug(scaled, att[pl.ds(r, 128), :].astype(F32))
    kvt[...] = jnp.transpose(proj[:, pl.ds(width, width)])
    for i in range(4):
        do_d_x(i)
    do_u_y(0)
    do_u_y(1)
    for copy in sends2:
        copy.wait()

    minus = jnp.where(lanes_of((rows, 128)) < 32, -1.0, 0.0).astype(BF)

    def chosen(head):
        lane = lanes_of((1, 128))
        return jnp.where((lane == head) | (lane == head + 16), 1.0, 0.0).astype(BF)

    def attention_back(p, carry):
        at = pl.multiple_of(p * 128, 128)
        qp = proj[pl.ds(0, tok), pl.ds(at, 128)]
        qg = proj[pl.ds(tok, glob), pl.ds(at, 128)]
        gp = gatt[pl.ds(0, tok), pl.ds(at, 128)]
        gg = rcv2[:, pl.ds(at, 128)]
        dg = rcv2[:, pl.ds(width, 128)]
        values = jnp.concatenate([proj[:, pl.ds(2 * width + at, 128)], minus], axis=1)
        ups = jnp.concatenate([gp * even_one, gp * odd_one, gg * even_one, gg * odd_one], axis=0)
        dd = qaug[pl.ds(0, tok), :]
        sel_e, sel_o = chosen(2 * p), chosen(2 * p + 1)
        inner = jnp.concatenate([dd * sel_e, dd * sel_o, dg * sel_e, dg * sel_o], axis=0)
        qs = jnp.concatenate([qp * even, qp * odd, qg * even, qg * odd], axis=0)
        grad_v = dot_nn(probs[p], ups)
        for first, count in ((0, tok), (tok, tok), (2 * tok, 2 * glob)):
            right = jnp.concatenate([ups[first : first + count], inner[first : first + count]], axis=1)
            grad_w = dot_nt(values, right)
            here = probs[p, :, pl.ds(first, count)].astype(F32)
            probs[p, :, pl.ds(first, count)] = (here * grad_w).astype(BF)
        grad_k = dot_nn(probs[p], qs)
        factor = HEAD_DIM ** (-0.5)
        low = dot_nn(kvt[pl.ds(at, HEAD_DIM), :], probs[p, :, pl.ds(0, tok)])
        upper = dot_nn(
            kvt[pl.ds(pl.multiple_of(at + HEAD_DIM, HEAD_DIM), HEAD_DIM), :], probs[p, :, pl.ds(tok, tok)]
        )
        grad_q = jnp.concatenate([low, upper], axis=0) * factor
        own = dot_nn(kvt[pl.ds(at, 128), :], probs[p, :, pl.ds(2 * tok, 2 * glob)])
        own = jnp.where(first_head, own[:, :glob], own[:, glob:]) * factor
        proj[pl.ds(0, tok), pl.ds(at, 128)] = jnp.transpose(grad_q).astype(BF)
        proj[pl.ds(tok, glob), pl.ds(at, 128)] = jnp.transpose(own).astype(BF)
        proj[:, pl.ds(width + at, 128)] = grad_k.astype(BF)
        proj[:, pl.ds(2 * width + at, 128)] = grad_v.astype(BF)

        @pl.when(p == 2)
        def _():
            do_d_1(0)
            do_d_1(1)

        @pl.when(p == 3)
        def _():
            do_u_1()

        @pl.when(p == 4)
        def _():
            do_d_2()

        @pl.when(p == 5)
        def _():
            do_u_2()

        return carry

    lax.fori_loop(0, pairs, attention_back, 0)

    sends3 = []
    for k in peers:
        other = flip(k)
        at = pl.multiple_of(tok + other * slots, slots)
        copy = remote(proj.at[pl.ds(at, slots)], rcv3.at[k - 1], m3s.at[k], m3r.at[k], (other, b))
        copy.start()
        sends3.append(copy)

    total3 = proj[pl.ds(pl.multiple_of(tok + my_slots, slots), slots), :].astype(F32)
    for copy in sends3:
        copy.wait()
    for k in peers:
        total3 = total3 + rcv3[k - 1].astype(F32)
    proj[pl.ds(tok, slots), :] = total3.astype(BF)

    for yy in range(2):
        for j in range(2):
            u_core(yy, j).wait_send()

    def q_block(yy, cc):
        bb = 2 * yy + cc
        odd_b = cc == 1
        at = pl.multiple_of(bb * 576 - 64 * cc, 128)
        window = proj[pl.ds(0, wide), pl.ds(at, 640)].astype(F32)
        window = jnp.where(odd_b, pltpu.roll(window, 576, 1), window).astype(BF)
        at = pl.multiple_of(bb * 192 - 64 * cc, 128)
        branch = n2[:, pl.ds(at, 256)].astype(F32)
        branch = jnp.where(odd_b, branch, pltpu.roll(branch, 64, 1)).astype(BF)
        first = dot_nn(n2t[:, pl.ds(0, wide)], window[:, :384])
        second = dot_nn(n2t[:, pl.ds(0, wide)], window[:, 384:])
        third = dot_nn(att_t[:, pl.ds(0, wide)], branch)
        middle = jnp.where(lanes_of((width, 128)) < 64, second[:, 128:], third[:, :128])
        return first, jnp.concatenate([second[:, :128], middle, third[:, 128:]], axis=1)

    def q_core(yy, j):
        return remote(gu.at[yy, 1 - c, j], r0q.at[yy, j], q0s.at[yy * 2 + j], q0r.at[yy * 2 + j], dev_c)

    def q_first(yy, carry):
        for j, block in enumerate(q_block(yy, 1 - c)):
            gu[yy, 1 - c, j] = block.astype(BF).reshape(gu.shape[3:])
            q_core(yy, j).start()
        return carry

    lax.fori_loop(0, 2, q_first, 0)

    gn2[...] = dot_nt(proj[pl.ds(0, wide), :], wq[...])

    def q_x0(yy):
        return remote(r0q.at[yy, 0, :, :, 1 - x], r1qx.at[yy], q1s.at[yy], q1r.at[yy], dev_x)

    def q_y0():
        return remote(r1qx.at[1 - y], r2q.at[0], q2s.at[0], q2r.at[0], dev_y)

    def q_y1():
        return remote(r0q.at[1 - y, 1], r1qy, q1s.at[2], q1r.at[2], dev_y)

    def q_x1():
        return remote(r1qy.at[:, :, 1 - x], r2q.at[1], q2s.at[1], q2r.at[1], dev_x)

    def q_1():
        return remote(r2q.at[:, :, 1 - zl], r3q, q3s.at[0], q3r.at[0], dev_1)

    def q_2():
        return remote(r3q.at[:, 1 - zh], r4q, q4s.at[0], q4r.at[0], dev_2)

    def q_second(yy, carry):
        first, second = q_block(yy, c)
        q_core(yy, 0).wait_recv()
        r0q[yy, 0] = (r0q[yy, 0].astype(F32) + first.reshape(gu.shape[3:])).astype(BF)
        q_x0(yy).start()
        q_core(yy, 1).wait_recv()
        r0q[yy, 1] = (r0q[yy, 1].astype(F32) + second.reshape(gu.shape[3:])).astype(BF)
        return carry

    lax.fori_loop(0, 2, q_second, 0)
    q_y1().start()

    def first_pull(first):
        grad, gain_term, shift_term = norm_pull(
            sec[pl.ds(first, 128), :].astype(F32), attn_gain[...], gn2[pl.ds(first, 128), :]
        )
        n2[pl.ds(first, 128), :] = (grad + x2[pl.ds(first, 128), :]).astype(BF)
        vec[pl.ds(0, 1), :] += gain_term
        vec[pl.ds(1, 1), :] += shift_term

    for r in range(half, tok, 128):
        first_pull(r)
    back = remote(
        n2.at[pl.ds(half, half)], o_tgrad.at[pl.ds(0, half)], hs2.at[0], hr2.at[0],
        (lax.rem(s + 1, n_seq), b),
    )
    back.start()
    for r in range(0, half, 128):
        first_pull(r)
    keep = pltpu.make_async_copy(n2.at[pl.ds(0, half)], o_tgrad.at[pl.ds(half, half)], osem.at[2])
    keep.start()

    grad, gain_term, shift_term = norm_pull(
        sec[pl.ds(pl.multiple_of(tok + my_slots, slots), slots), :].astype(F32),
        glob_gain[...],
        gn2[pl.ds(tok, slots), :],
    )
    vec[pl.ds(2, 1), :] += gain_term
    vec[pl.ds(3, 1), :] += shift_term
    n2[pl.ds(tok, slots), :] = (grad + x2[pl.ds(tok, slots), :]).astype(BF)
    own_grad = pltpu.make_async_copy(
        n2.at[pl.ds(tok, slots)], o_ggrad.at[pl.ds(my_slots, slots)], osem.at[3]
    )
    own_grad.start()
    sends_g = []
    for k in peers:
        copy = remote(
            n2.at[pl.ds(tok, slots)], o_ggrad.at[pl.ds(my_slots, slots)], ggs_s.at[k], ggs_r.at[k],
            (flip(k), b),
        )
        copy.start()
        sends_g.append(copy)

    def vec_step(k, dev):
        return remote(vec, rvec.at[k], vs.at[k], vr.at[k], dev)

    def vec_add(k, dev):
        vec_step(k, dev).wait()
        vec[...] += rvec[k]

    vec_step(0, dev_c).start()
    d_2().wait_recv()
    o_down[...] = jnp.transpose(r4d[...].astype(F32) + r3d[zh].astype(F32))
    u_2().wait_recv()
    last = r4u[...].astype(F32) + r3u[:, zh].astype(F32)
    o_up[:, pl.ds(0, 384)] = last[0]
    o_up[:, pl.ds(384, 384)] = last[1]
    vec_add(0, dev_c)
    vec_step(1, dev_y).start()
    for yy in range(2):
        q_x0(yy).wait_recv()
        r1qx[yy] = r1qx[yy] + r0q[yy, 0, :, :, x]
    q_y0().start()
    vec_add(1, dev_y)
    vec_step(2, dev_x).start()
    q_y1().wait_recv()
    r1qy[...] = r1qy[...] + r0q[y, 1]
    q_x1().start()
    vec_add(2, dev_x)
    vec_step(3, dev_1).start()
    q_y0().wait_recv()
    r2q[0] = r2q[0] + r1qx[y]
    q_x1().wait_recv()
    r2q[1] = r2q[1] + r1qy[:, :, x]
    q_1().start()
    vec_add(3, dev_1)
    vec_step(4, dev_2).start()
    q_1().wait_recv()
    r3q[...] = r3q[...] + r2q[:, :, zl]
    q_2().start()
    vec_add(4, dev_2)
    share = vec.shape[1] // n_seq
    turned = pltpu.roll(vec[pl.ds(0, 8), :], lax.rem(vec.shape[1] - share * s, vec.shape[1]), 1)
    o_vec[...] = turned[:, :share]
    o_ub[...] = vec[pl.ds(8 + s // 2, 1), pl.ds(pl.multiple_of((s % 2) * chunk, chunk), chunk)]
    q_2().wait_recv()
    last = r4q[...].astype(F32) + r3q[:, zh].astype(F32)
    o_qkv[:, pl.ds(0, 384)] = last[0]
    o_qkv[:, pl.ds(384, 192)] = last[1][:, :192]
    o_wout[...] = last[1][:, 192:]

    for i in range(8):
        d_core(i).wait_send()
        d_y(i).wait_send()
    for i in range(4):
        d_x(i).wait_send()
    for i in range(2):
        d_1(i).wait_send()
    d_2().wait_send()
    for yy in range(2):
        for j in range(2):
            u_x(yy, j).wait_send()
            q_core(yy, j).wait_send()
        u_y(yy).wait_send()
        q_x0(yy).wait_send()
    u_1().wait_send()
    u_2().wait_send()
    q_y0().wait_send()
    q_y1().wait_send()
    q_x1().wait_send()
    q_1().wait_send()
    q_2().wait_send()
    back.wait()
    keep.wait()
    own_grad.wait()
    out_copy.wait()
    own_out.wait()
    for copy in sends_o + sends_g:
        copy.wait()


def fits(tokens, global_states, w_qkv, w_up):
    return (
        lax.axis_size("seq") == 8
        and lax.axis_size("batch") == 4
        and tokens.shape == (1, BLOCK, HEADS * HEAD_DIM)
        and global_states.shape == (1, 128, HEADS * HEAD_DIM)
        and w_qkv.shape == (HEADS * HEAD_DIM, 3 * HEADS * HEAD_DIM)
        and w_up.shape == (HEADS * HEAD_DIM, 3072)
    )


def fused(
    tokens, global_states, token_seg, global_seg, attn_gain, attn_shift, glob_gain, glob_shift, w_qkv, w_out,
    ffn_gain, ffn_shift, w_up, up_bias, w_down, down_bias, out_cotangent, global_cotangent,
):
    tok, width = tokens.shape[1:]
    glob = global_states.shape[1]
    hidden = w_up.shape[1]
    n_seq, n_batch = lax.axis_size("seq"), lax.axis_size("batch")
    rows, slots = tok + glob, glob // n_seq
    wide = tok + slots
    chunk, part, side = hidden // n_seq, width // n_seq, width // n_batch
    pairs = HEADS // 2
    dma = pltpu.SemaphoreType.DMA

    def any_space():
        return pl.BlockSpec(memory_space=pl.ANY)

    def vmem():
        return pl.BlockSpec(memory_space=pltpu.VMEM)

    def low(*shape):
        return pltpu.VMEM(shape, BF)

    def full(*shape):
        return pltpu.VMEM(shape, F32)

    scratch = [
        low(rows, width), low(rows, width), low(rows, 3 * width), low(width, rows),
        low(pairs, rows, 2 * tok + 2 * glob), low(width, tok + 128), low(wide, width), full(wide, width),
        low(wide, width), low(width, tok + 128), low(wide, width), low(width, tok + 128),
        full(wide, width), full(wide, width), low(wide, width), low(rows, 128), low(rows, 128),
        low(width, 3 * width), low(width, width), low(2, width, chunk), low(2, chunk, width),
        full(128, glob), full(16, tok), full(width, glob), low(glob, width + 128),
        low(n_seq, slots, width + 128), full(glob, width), low(glob, width + 128),
        low(n_seq - 1, slots, 3 * width),
        full(16, width), full(5, 16, width), full(8, chunk),
        low(8, 2, 2, side, chunk), low(8, 2, side, chunk), low(8, side, chunk), low(4, side, chunk),
        low(2, side, chunk), low(side, chunk),
        low(2, 2, 2, 2, 2, 2, part, chunk), low(2, 2, 2, 2, 2, part, chunk), low(2, 2, 2, 2, part, chunk),
        low(2, 2, 2, part, chunk), low(2, 2, part, chunk), low(2, part, chunk),
        low(2, 2, 2, 2, 2, part, chunk), low(2, 2, 2, part, chunk), low(2, 2, 2, part, chunk),
        low(2, 2, 2, part, chunk), low(2, 2, part, chunk), low(2, part, chunk),
        dma((8,)), dma((2, 2)), dma((1,)), dma((1,)),
        *[dma((8,)) for _ in range(10)], dma((5,)), dma((5,)),
        dma((8,)), dma((8,)), dma((8,)), dma((8,)), dma((4,)), dma((4,)), dma((2,)), dma((2,)), dma((1,)), dma((1,)),
        dma((4,)), dma((4,)), dma((4,)), dma((4,)), dma((2,)), dma((2,)), dma((1,)), dma((1,)), dma((1,)), dma((1,)),
        dma((4,)), dma((4,)), dma((3,)), dma((3,)), dma((2,)), dma((2,)), dma((1,)), dma((1,)), dma((1,)), dma((1,)),
        dma((1,)), dma((1,)), dma((4,)),
    ]

    def row(vector):
        return vector.reshape(1, -1)

    results = pl.pallas_call(
        layer_kernel,
        out_shape=[
            jax.ShapeDtypeStruct((tok, width), BF),
            jax.ShapeDtypeStruct((glob, width), BF),
            jax.ShapeDtypeStruct((tok, width), BF),
            jax.ShapeDtypeStruct((glob, width), BF),
            jax.ShapeDtypeStruct((part, 3 * side), F32),
            jax.ShapeDtypeStruct((part, side), F32),
            jax.ShapeDtypeStruct((part, 2 * chunk), F32),
            jax.ShapeDtypeStruct((chunk, side), F32),
            jax.ShapeDtypeStruct((8, part), F32),
            jax.ShapeDtypeStruct((1, chunk), F32),
        ],
        in_specs=[any_space(), any_space(), vmem(), vmem(), vmem(), vmem(), vmem(), vmem(), any_space(), any_space(),
                  vmem(), vmem(), any_space(), vmem(), any_space(), vmem(), any_space(), any_space()],
        out_specs=[any_space()] * 4 + [vmem()] * 6,
        scratch_shapes=scratch,
        compiler_params=pltpu.CompilerParams(
            collective_id=0, has_side_effects=True, vmem_limit_bytes=64 * 1024 * 1024
        ),
        name="layer",
    )(
        tokens[0], global_states[0], token_seg, global_seg, row(attn_gain), row(attn_shift), row(glob_gain),
        row(glob_shift), w_qkv, w_out, row(ffn_gain), row(ffn_shift), w_up, row(up_bias), w_down, row(down_bias),
        out_cotangent[0], global_cotangent[0],
    )
    out, gout, tgrad, ggrad, g_qkv, g_out, g_up, g_down, g_vec, g_ub = results
    return (
        out[None], gout[None], tgrad[None], ggrad[None], g_vec[0], g_vec[1], g_vec[2], g_vec[3], g_qkv, g_out,
        g_vec[4], g_vec[5], g_up, g_ub[0], g_down, g_vec[6],
    )


def local(tokens, global_states, token_seg, global_seg, *rest):
    w_qkv, w_up = rest[4], rest[8]
    way = fused if fits(tokens, global_states, w_qkv, w_up) else general
    return way(tokens, global_states, token_seg, global_seg, *rest)


def solution(mesh):
    placed = (
        P("batch", "seq", None),
        P("batch", None, None),
        P("batch", "seq"),
        P("batch", None),
        P(),
        P(),
        P(),
        P(),
        P(),
        P(),
        P(),
        P(),
        P(),
        P(),
        P(),
        P(),
        P("batch", "seq", None),
        P("batch", None, None),
    )
    return jax.shard_map(
        local,
        mesh=mesh,
        in_specs=placed,
        out_specs=(
            P("batch", "seq", None),
            P("batch", None, None),
            P("batch", "seq", None),
            P("batch", None, None),
            P("seq"),
            P("seq"),
            P("seq"),
            P("seq"),
            P("seq", "batch"),
            P("seq", "batch"),
            P("seq"),
            P("seq"),
            P("seq", "batch"),
            P("seq"),
            P("seq", "batch"),
            P("seq"),
        ),
        check_vma=False,
    )
```

```python
import functools

import jax
import jax.numpy as jnp
from jax import lax
from jax.experimental import pallas as pl
from jax.experimental.pallas import tpu as pltpu
from jax.sharding import PartitionSpec as P

HEADS = 12
HEAD_DIM = 64
BLOCK = 512


EPS = 1e-05
NEGATIVE = -1e30


def from_behind(block, axis, distance):
    devices = range(lax.axis_size(axis))
    route = [((i - distance) % len(devices), i) for i in devices]
    return lax.ppermute(block, axis, route)


def norm_rows(source, scaling, offset):
    center = jnp.mean(source, axis=-1, keepdims=True)
    spread = source - center
    variance = jnp.mean(spread * spread, axis=-1, keepdims=True)
    return spread * lax.rsqrt(variance + EPS) * scaling + offset


def norm_back(source, scaling, offset, upstream):
    _, pullback = jax.vjp(norm_rows, source, scaling, offset)
    return pullback(upstream)


def project(former, latter):
    return jnp.einsum("rsd,de->rse", former, latter, preferred_element_type=jnp.float32)


def project_back(former, latter):
    return jnp.einsum("rse,de->rsd", former, latter, preferred_element_type=jnp.float32)


def outer_sum(former, latter):
    return jnp.einsum("rsd,rse->de", former, latter, preferred_element_type=jnp.float32)


def gelu_exact(hidden):
    return jax.nn.gelu(hidden, approximate=False)


def ffn_forward(state, ffn_gain, ffn_shift, w_up, up_bias, w_down, down_bias):
    normed = norm_rows(state, ffn_gain, ffn_shift).astype(jnp.bfloat16)
    hidden = project(normed, w_up) + up_bias
    active = gelu_exact(hidden).astype(jnp.bfloat16)
    result = state + project(active, w_down) + down_bias
    return (result, (normed, hidden, active))


def ffn_backward(state, stored, upstream, ffn_gain, ffn_shift, w_up, w_down):
    normed, hidden, active = stored
    upstream_low = upstream.astype(jnp.bfloat16)
    grad_down = outer_sum(active, upstream_low)
    grad_down_bias = jnp.sum(upstream, axis=(0, 1))
    grad_active = project_back(upstream_low, w_down)
    _, gelu_pull = jax.vjp(gelu_exact, hidden)
    grad_hidden = gelu_pull(grad_active)[0].astype(jnp.bfloat16)
    grad_up = outer_sum(normed, grad_hidden)
    grad_up_bias = jnp.sum(grad_hidden.astype(jnp.float32), axis=(0, 1))
    grad_normed = project_back(grad_hidden, w_up)
    grad_state, grad_gain, grad_shift = norm_back(state, ffn_gain, ffn_shift, grad_normed)
    return (
        upstream + grad_state,
        (grad_gain, grad_shift, grad_up, grad_up_bias, grad_down, grad_down_bias),
    )


def local_scores(queries, keys_near, seg_near, keys_far, seg_far):
    scaling = HEAD_DIM ** (-0.5)
    near_scores = (
        jnp.einsum("rnqhd,rnkhd->rnhqk", queries, keys_near, preferred_element_type=jnp.float32)
        * scaling
    )
    far_scores = (
        jnp.einsum("rnqhd,rghd->rnhqg", queries, keys_far, preferred_element_type=jnp.float32)
        * scaling
    )
    near_open = (seg_near[:, :, :, None] == seg_near[:, :, None, :])[:, :, None]
    far_open = (seg_near[:, :, :, None] == seg_far[:, None, None, :])[:, :, None]
    return (jnp.where(near_open, near_scores, NEGATIVE), jnp.where(far_open, far_scores, NEGATIVE))


def local_forward(queries, keys_near, values_near, seg_near, keys_far, values_far, seg_far):
    near_scores, far_scores = local_scores(queries, keys_near, seg_near, keys_far, seg_far)
    maxima = jnp.maximum(jnp.max(near_scores, axis=-1), jnp.max(far_scores, axis=-1))
    near_exp = jnp.exp(near_scores - maxima[..., None])
    far_exp = jnp.exp(far_scores - maxima[..., None])
    totals = jnp.sum(near_exp, axis=-1) + jnp.sum(far_exp, axis=-1)
    near_weights = (near_exp / totals[..., None]).astype(jnp.bfloat16)
    far_weights = (far_exp / totals[..., None]).astype(jnp.bfloat16)
    mixed_out = jnp.einsum(
        "rnhqk,rnkhd->rnqhd", near_weights, values_near, preferred_element_type=jnp.float32
    )
    mixed_out = mixed_out + jnp.einsum(
        "rnhqg,rghd->rnqhd", far_weights, values_far, preferred_element_type=jnp.float32
    )
    return (mixed_out, maxima + jnp.log(totals))


def local_backward(
    queries, keys_near, values_near, seg_near, keys_far, values_far, seg_far, logsum, upstream
):
    scaling = HEAD_DIM ** (-0.5)
    near_scores, far_scores = local_scores(queries, keys_near, seg_near, keys_far, seg_far)
    near_weights = jnp.exp(near_scores - logsum[..., None])
    far_weights = jnp.exp(far_scores - logsum[..., None])
    near_grad = jnp.einsum(
        "rnqhd,rnkhd->rnhqk", upstream, values_near, preferred_element_type=jnp.float32
    )
    far_grad = jnp.einsum(
        "rnqhd,rghd->rnhqg", upstream, values_far, preferred_element_type=jnp.float32
    )
    row_inner = jnp.sum(near_weights * near_grad, axis=-1) + jnp.sum(
        far_weights * far_grad, axis=-1
    )
    near_score_grad = (near_weights * (near_grad - row_inner[..., None])).astype(jnp.bfloat16)
    far_score_grad = (far_weights * (far_grad - row_inner[..., None])).astype(jnp.bfloat16)
    grad_queries = jnp.einsum(
        "rnhqk,rnkhd->rnqhd", near_score_grad, keys_near, preferred_element_type=jnp.float32
    )
    grad_queries = scaling * (
        grad_queries
        + jnp.einsum(
            "rnhqg,rghd->rnqhd", far_score_grad, keys_far, preferred_element_type=jnp.float32
        )
    )
    grad_keys = scaling * jnp.einsum(
        "rnhqk,rnqhd->rnkhd", near_score_grad, queries, preferred_element_type=jnp.float32
    )
    grad_values = jnp.einsum(
        "rnhqk,rnqhd->rnkhd",
        near_weights.astype(jnp.bfloat16),
        upstream,
        preferred_element_type=jnp.float32,
    )
    grad_keys_far = scaling * jnp.einsum(
        "rnhqg,rnqhd->rghd", far_score_grad, queries, preferred_element_type=jnp.float32
    )
    grad_values_far = jnp.einsum(
        "rnhqg,rnqhd->rghd",
        far_weights.astype(jnp.bfloat16),
        upstream,
        preferred_element_type=jnp.float32,
    )
    return (grad_queries, grad_keys, grad_values, grad_keys_far, grad_values_far)


def global_scores(glob_queries, glob_keys, glob_seg, key_rows, seg_tokens):
    scaling = HEAD_DIM ** (-0.5)
    remote_scores = (
        jnp.einsum("rghd,rshd->rhgs", glob_queries, key_rows, preferred_element_type=jnp.float32)
        * scaling
    )
    own_scores = (
        jnp.einsum("rghd,rjhd->rhgj", glob_queries, glob_keys, preferred_element_type=jnp.float32)
        * scaling
    )
    remote_open = glob_seg[:, None, :, None] == seg_tokens[:, None, None, :]
    own_open = glob_seg[:, None, :, None] == glob_seg[:, None, None, :]
    return (
        jnp.where(remote_open, remote_scores, NEGATIVE),
        jnp.where(own_open, own_scores, NEGATIVE),
    )


def general(
    tokens,
    global_states,
    token_seg,
    global_seg,
    attn_gain,
    attn_shift,
    glob_gain,
    glob_shift,
    w_qkv,
    w_out,
    ffn_gain,
    ffn_shift,
    w_up,
    up_bias,
    w_down,
    down_bias,
    out_cotangent,
    global_cotangent,
):
    row_count, tok_count, model_width = tokens.shape
    glob_count = global_states.shape[1]
    half_block = BLOCK // 2
    block_count = tok_count // BLOCK
    seq_devices = lax.axis_size("seq")
    scaling = HEAD_DIM ** (-0.5)
    low_type = jnp.bfloat16
    arrived = from_behind(tokens[:, :half_block], "seq", -1)
    sectioned = jnp.concatenate([tokens[:, half_block:], arrived], axis=1).astype(jnp.float32)
    glob_state = global_states.astype(jnp.float32)
    normed = norm_rows(sectioned, attn_gain, attn_shift).astype(low_type)
    glob_normed = norm_rows(glob_state, glob_gain, glob_shift).astype(low_type)
    projected = (
        project(normed, w_qkv).astype(low_type).reshape(row_count, tok_count, 3, HEADS, HEAD_DIM)
    )
    glob_proj = (
        project(glob_normed, w_qkv)
        .astype(low_type)
        .reshape(row_count, glob_count, 3, HEADS, HEAD_DIM)
    )
    queries = projected[:, :, 0]
    key_rows = projected[:, :, 1]
    value_rows = projected[:, :, 2]
    glob_queries = glob_proj[:, :, 0]
    glob_keys = glob_proj[:, :, 1]
    glob_values = glob_proj[:, :, 2]
    block_shape = (row_count, block_count, BLOCK, HEADS, HEAD_DIM)
    block_queries = queries.reshape(block_shape)
    block_keys = key_rows.reshape(block_shape)
    block_values = value_rows.reshape(block_shape)
    block_seg = token_seg.reshape(row_count, block_count, BLOCK)
    local_out, local_logsum = local_forward(
        block_queries, block_keys, block_values, block_seg, glob_keys, glob_values, global_seg
    )
    remote_scores, own_scores = global_scores(
        glob_queries, glob_keys, global_seg, key_rows, token_seg
    )
    maxima = jnp.maximum(
        lax.pmax(jnp.max(remote_scores, axis=-1), "seq"), jnp.max(own_scores, axis=-1)
    )
    remote_total = jnp.sum(jnp.exp(remote_scores - maxima[..., None]), axis=-1)
    totals = lax.psum(remote_total, "seq") + jnp.sum(
        jnp.exp(own_scores - maxima[..., None]), axis=-1
    )
    remote_weights = (jnp.exp(remote_scores - maxima[..., None]) / totals[..., None]).astype(
        low_type
    )
    own_weights = (jnp.exp(own_scores - maxima[..., None]) / totals[..., None]).astype(low_type)
    remote_part = jnp.einsum(
        "rhgs,rshd->rghd", remote_weights, value_rows, preferred_element_type=jnp.float32
    )
    glob_out = lax.psum(remote_part, "seq")
    glob_out = glob_out + jnp.einsum(
        "rhgj,rjhd->rghd", own_weights, glob_values, preferred_element_type=jnp.float32
    )
    glob_logsum = maxima + jnp.log(totals)
    attended = local_out.reshape(row_count, tok_count, model_width).astype(low_type)
    glob_attended = glob_out.reshape(row_count, glob_count, model_width).astype(low_type)
    attn_sum = sectioned + project(attended, w_out)
    glob_sum = glob_state + project(glob_attended, w_out)
    result, stored = ffn_forward(attn_sum, ffn_gain, ffn_shift, w_up, up_bias, w_down, down_bias)
    glob_result, glob_stored = ffn_forward(
        glob_sum, ffn_gain, ffn_shift, w_up, up_bias, w_down, down_bias
    )
    grad_attn_sum, tok_ffn = ffn_backward(
        attn_sum, stored, out_cotangent.astype(jnp.float32), ffn_gain, ffn_shift, w_up, w_down
    )
    grad_glob_sum, glob_ffn = ffn_backward(
        glob_sum,
        glob_stored,
        global_cotangent.astype(jnp.float32),
        ffn_gain,
        ffn_shift,
        w_up,
        w_down,
    )
    branch_low = grad_attn_sum.astype(low_type)
    glob_branch_low = grad_glob_sum.astype(low_type)
    grad_out_all = (
        outer_sum(attended, branch_low) + outer_sum(glob_attended, glob_branch_low) / seq_devices
    )
    upstream_mix = project_back(branch_low, w_out).astype(low_type).reshape(block_shape)
    glob_upstream = (
        project_back(glob_branch_low, w_out)
        .astype(low_type)
        .reshape(row_count, glob_count, HEADS, HEAD_DIM)
    )
    remote_exact = jnp.exp(remote_scores - glob_logsum[..., None])
    own_exact = jnp.exp(own_scores - glob_logsum[..., None])
    remote_grad = jnp.einsum(
        "rghd,rshd->rhgs", glob_upstream, value_rows, preferred_element_type=jnp.float32
    )
    own_grad = jnp.einsum(
        "rghd,rjhd->rhgj", glob_upstream, glob_values, preferred_element_type=jnp.float32
    )
    row_inner = lax.psum(jnp.sum(remote_exact * remote_grad, axis=-1), "seq")
    row_inner = row_inner + jnp.sum(own_exact * own_grad, axis=-1)
    remote_score_grad = (remote_exact * (remote_grad - row_inner[..., None])).astype(low_type)
    own_score_grad = (own_exact * (own_grad - row_inner[..., None])).astype(low_type)
    remote_queries = scaling * jnp.einsum(
        "rhgs,rshd->rghd", remote_score_grad, key_rows, preferred_element_type=jnp.float32
    )
    tok_keys_extra = scaling * jnp.einsum(
        "rhgs,rghd->rshd", remote_score_grad, glob_queries, preferred_element_type=jnp.float32
    )
    tok_values_extra = jnp.einsum(
        "rhgs,rghd->rshd",
        remote_exact.astype(low_type),
        glob_upstream,
        preferred_element_type=jnp.float32,
    )
    own_queries = scaling * jnp.einsum(
        "rhgj,rjhd->rghd", own_score_grad, glob_keys, preferred_element_type=jnp.float32
    )
    own_keys = scaling * jnp.einsum(
        "rhgj,rghd->rjhd", own_score_grad, glob_queries, preferred_element_type=jnp.float32
    )
    own_values = jnp.einsum(
        "rhgj,rghd->rjhd",
        own_exact.astype(low_type),
        glob_upstream,
        preferred_element_type=jnp.float32,
    )
    grad_queries, grad_keys, grad_values, grad_keys_far, grad_values_far = local_backward(
        block_queries,
        block_keys,
        block_values,
        block_seg,
        glob_keys,
        glob_values,
        global_seg,
        local_logsum,
        upstream_mix,
    )
    far_grads = lax.psum((remote_queries, grad_keys_far, grad_values_far), "seq")
    head_shape = (row_count, tok_count, HEADS, HEAD_DIM)
    grad_projected = jnp.stack(
        [
            grad_queries.reshape(head_shape),
            grad_keys.reshape(head_shape) + tok_keys_extra,
            grad_values.reshape(head_shape) + tok_values_extra,
        ],
        axis=2,
    )
    grad_projected = grad_projected.reshape(row_count, tok_count, 3 * model_width).astype(low_type)
    glob_grad_projected = jnp.stack(
        [far_grads[0] + own_queries, far_grads[1] + own_keys, far_grads[2] + own_values], axis=2
    )
    glob_grad_projected = glob_grad_projected.reshape(
        row_count, glob_count, 3 * model_width
    ).astype(low_type)
    grad_qkv_all = (
        outer_sum(normed, grad_projected)
        + outer_sum(glob_normed, glob_grad_projected) / seq_devices
    )
    grad_normed = project_back(grad_projected, w_qkv)
    glob_grad_normed = project_back(glob_grad_projected, w_qkv)
    grad_sectioned, attn_gain_grad, attn_shift_grad = norm_back(
        sectioned, attn_gain, attn_shift, grad_normed
    )
    grad_sectioned = grad_sectioned + grad_attn_sum
    glob_grad_state, glob_gain_grad, glob_shift_grad = norm_back(
        glob_state, glob_gain, glob_shift, glob_grad_normed
    )
    global_grad = (glob_grad_state + grad_glob_sum).astype(low_type)
    grad_low = grad_sectioned.astype(low_type)
    returned = from_behind(grad_low[:, tok_count - half_block :], "seq", 1)
    token_grad = jnp.concatenate([returned, grad_low[:, : tok_count - half_block]], axis=1)
    ffn_gain_all = tok_ffn[0] + glob_ffn[0] / seq_devices
    ffn_shift_all = tok_ffn[1] + glob_ffn[1] / seq_devices
    up_all = tok_ffn[2] + glob_ffn[2] / seq_devices
    up_bias_all = tok_ffn[3] + glob_ffn[3] / seq_devices
    down_all = tok_ffn[4] + glob_ffn[4] / seq_devices
    down_bias_all = tok_ffn[5] + glob_ffn[5] / seq_devices
    glob_gain_all = glob_gain_grad / seq_devices
    glob_shift_all = glob_shift_grad / seq_devices
    mat_sums = (
        lax.psum_scatter(
            grad_qkv_all.astype(jnp.bfloat16), "batch", scatter_dimension=1, tiled=True
        ).astype(jnp.float32),
        lax.psum_scatter(
            grad_out_all.astype(jnp.bfloat16), "batch", scatter_dimension=1, tiled=True
        ).astype(jnp.float32),
        lax.psum_scatter(
            up_all.astype(jnp.bfloat16), "batch", scatter_dimension=1, tiled=True
        ).astype(jnp.float32),
        lax.psum_scatter(
            down_all.astype(jnp.bfloat16), "batch", scatter_dimension=1, tiled=True
        ).astype(jnp.float32),
    )
    vec_sums = (
        lax.psum(attn_gain_grad.astype(jnp.bfloat16), "batch").astype(jnp.float32),
        lax.psum(attn_shift_grad.astype(jnp.bfloat16), "batch").astype(jnp.float32),
        lax.psum(glob_gain_all.astype(jnp.bfloat16), "batch").astype(jnp.float32),
        lax.psum(glob_shift_all.astype(jnp.bfloat16), "batch").astype(jnp.float32),
        lax.psum(ffn_gain_all.astype(jnp.bfloat16), "batch").astype(jnp.float32),
        lax.psum(ffn_shift_all.astype(jnp.bfloat16), "batch").astype(jnp.float32),
        lax.psum(up_bias_all.astype(jnp.bfloat16), "batch").astype(jnp.float32),
        lax.psum(down_bias_all.astype(jnp.bfloat16), "batch").astype(jnp.float32),
    )
    shares = (
        lax.psum_scatter(vec_sums[0], "seq", scatter_dimension=0, tiled=True),
        lax.psum_scatter(vec_sums[1], "seq", scatter_dimension=0, tiled=True),
        lax.psum_scatter(vec_sums[2], "seq", scatter_dimension=0, tiled=True),
        lax.psum_scatter(vec_sums[3], "seq", scatter_dimension=0, tiled=True),
        lax.psum_scatter(mat_sums[0], "seq", scatter_dimension=0, tiled=True),
        lax.psum_scatter(mat_sums[1], "seq", scatter_dimension=0, tiled=True),
        lax.psum_scatter(vec_sums[4], "seq", scatter_dimension=0, tiled=True),
        lax.psum_scatter(vec_sums[5], "seq", scatter_dimension=0, tiled=True),
        lax.psum_scatter(mat_sums[2], "seq", scatter_dimension=0, tiled=True),
        lax.psum_scatter(vec_sums[6], "seq", scatter_dimension=0, tiled=True),
        lax.psum_scatter(mat_sums[3], "seq", scatter_dimension=0, tiled=True),
        lax.psum_scatter(vec_sums[7], "seq", scatter_dimension=0, tiled=True),
    )
    matrices = (shares[4], shares[5], shares[8], shares[10])
    vectors = (
        shares[0],
        shares[1],
        shares[2],
        shares[3],
        shares[6],
        shares[7],
        shares[9],
        shares[11],
    )
    return (
        result.astype(low_type),
        glob_result.astype(low_type),
        token_grad,
        global_grad,
        vectors[0],
        vectors[1],
        vectors[2],
        vectors[3],
        matrices[0],
        matrices[1],
        vectors[4],
        vectors[5],
        matrices[2],
        vectors[6],
        matrices[3],
        vectors[7],
    )


MESH = pl.DeviceIdType.MESH
BF = jnp.bfloat16
F32 = jnp.float32


def dot_nn(left, right):
    return lax.dot_general(left, right, (((1,), (0,)), ((), ())), preferred_element_type=F32)


def dot_nt(left, right):
    return lax.dot_general(left, right, (((1,), (1,)), ((), ())), preferred_element_type=F32)


def lanes_of(shape):
    return lax.broadcasted_iota(jnp.int32, shape, len(shape) - 1)


def two_parts(value):
    high = value.astype(BF)
    return high, (value - high.astype(F32)).astype(BF)


def norm_stats(value):
    center = jnp.mean(value, axis=-1, keepdims=True)
    spread = value - center
    variance = jnp.mean(spread * spread, axis=-1, keepdims=True)
    return spread, lax.rsqrt(variance + EPS)


def norm_pull(value, gain, upstream):
    spread, scale = norm_stats(value)
    unit = spread * scale
    scaled = upstream * gain
    first = jnp.mean(scaled, axis=-1, keepdims=True)
    second = jnp.mean(scaled * unit, axis=-1, keepdims=True)
    grad = scale * (scaled - first - unit * second)
    return (
        grad,
        jnp.sum(upstream * unit, axis=0, keepdims=True),
        jnp.sum(upstream, axis=0, keepdims=True),
    )


def gelu_pair(hidden):
    size = jnp.abs(hidden) * 0.7071067811865476
    step = 1.0 / (1.0 + 0.3275911 * size)
    bell = jnp.exp(-(size * size))
    series = 1.061405429 * 0.5
    for term in (-1.453152027, 1.421413741, -0.284496736, 0.254829592):
        series = series * step + term * 0.5
    tail = series * step * bell
    mass = jnp.where(hidden < 0.0, tail, 1.0 - tail)
    return hidden * mass, mass + hidden * (bell * 0.3989422804014327)


def layer_kernel(
    tokens, gstates, tseg, gseg, attn_gain, attn_shift, glob_gain, glob_shift, w_qkv, w_out,
    ffn_gain, ffn_shift, w_up, up_bias, w_down, down_bias, cotan, gcotan,
    o_out, o_gout, o_tgrad, o_ggrad, o_qkv, o_wout, o_up, o_down, o_vec, o_ub,
    sec, nrm, proj, kvt, probs, att_t, att, x2, n2, n2t, ct, ct_t, acc, gn2, gatt, qaug, kaug,
    wq, wo, wus, wds,
    lse_t, rl_t, cx, msg1, rcv1, rcv2, rcv3, vec, vmsg, vrcv, vsum, rll,
    gd, r0d, r1d, r2d, r3d, r4d, gu, r0u, r1u, r2u, r3u, r4u, r0q, r1q, r2q, r3q, r4q, both, ymsg, yrcv,
    loc, wsem, hs, hr, m1s, m1r, m2s, m2r, m3s, m3r, gos, gor, ggs_s, ggs_r, vs, vr,
    d0s, d0r, d1s, d1r, d2s, d2r, d3s, d3r, d4s, d4r,
    u0s, u0r, u1s, u1r, u2s, u2r, u3s, u3r, u4s, u4r,
    q0s, q0r, q1s, q1r, q2s, q2r, q3s, q3r, q4s, q4r,
    fs, fr, hs2, hr2, osem,
):
    tok, width = tokens.shape
    glob = gstates.shape[0]
    rows = tok + glob
    n_seq = lax.axis_size("seq")
    slots = glob // n_seq
    wide = tok + slots
    half = tok // 2
    pairs = HEADS // 2
    chunk = wus.shape[2]
    n_chunk = up_bias.shape[0] // chunk
    tail = 128

    s = lax.axis_index("seq")
    b = lax.axis_index("batch")
    x, zl, zh = s % 2, (s // 2) % 2, s // 4
    c, y = b % 2, b // 2
    dev_c, dev_y = (s, b + 1 - 2 * c), (s, b + 2 - 4 * y)
    dev_x, dev_1, dev_2 = (s + 1 - 2 * x, b), (s + 2 - 4 * zl, b), (s + 4 - 8 * zh, b)

    def flip(k):
        other = s
        if k & 1:
            other = other + 1 - 2 * x
        if k & 2:
            other = other + 2 - 4 * zl
        if k & 4:
            other = other + 4 - 8 * zh
        return other

    def remote(src, dst, ss, rs, dev):
        return pltpu.make_async_remote_copy(
            src_ref=src, dst_ref=dst, send_sem=ss, recv_sem=rs, device_id=dev, device_id_type=MESH
        )

    peers = tuple(range(1, n_seq))

    def as_row(vector):
        return vector[...].reshape(1, vector.shape[0])

    attn_gain, attn_shift, glob_gain, glob_shift, ffn_gain, ffn_shift, down_bias = (
        as_row(v) for v in (attn_gain, attn_shift, glob_gain, glob_shift, ffn_gain, ffn_shift, down_bias)
    )

    my_slots = pl.multiple_of(s * slots, slots)
    loads = [
        (tokens.at[pl.ds(half, half)], sec.at[pl.ds(0, half)]),
        (gstates, sec.at[pl.ds(tok, glob)]),
        (w_qkv, wq),
        (cotan, ct.at[pl.ds(0, tok)]),
        (gcotan.at[pl.ds(my_slots, slots)], ct.at[pl.ds(tok, slots)]),
        (w_out, wo),
    ]
    loads = [pltpu.make_async_copy(a, d, loc.at[i]) for i, (a, d) in enumerate(loads)]
    for load in loads:
        load.start()

    def stream(i, slot):
        at = pl.multiple_of(i * chunk, chunk)
        return (
            pltpu.make_async_copy(w_up.at[:, pl.ds(at, chunk)], wus.at[slot], wsem.at[0, slot]),
            pltpu.make_async_copy(w_down.at[pl.ds(at, chunk)], wds.at[slot], wsem.at[1, slot]),
        )

    for i in range(2):
        for copy in stream(i, i):
            copy.start()

    bar = pltpu.get_barrier_semaphore()
    for k in peers:
        pl.semaphore_signal(bar, inc=1, device_id=(flip(k), b), device_id_type=MESH)
    pl.semaphore_signal(bar, inc=1, device_id=dev_c, device_id_type=MESH)
    pl.semaphore_signal(bar, inc=1, device_id=dev_y, device_id_type=MESH)
    pl.semaphore_wait(bar, len(peers) + 2)
    halo = remote(
        tokens.at[pl.ds(0, half)], sec.at[pl.ds(half, half)], hs.at[0], hr.at[0],
        (lax.rem(s + n_seq - 1, n_seq), b),
    )
    halo.start()

    seg_row = jnp.concatenate([tseg[...], gseg[...]], axis=1)
    which = lax.broadcasted_iota(jnp.int32, (128, rows), 0)
    col = lanes_of((128, rows))
    is_glob = col >= tok
    same = which == seg_row
    q_t = jnp.where(which < 3, jnp.where(same, 1.0, 0.0), jnp.where((which == 3) & is_glob, 1.0, 0.0))
    far = jnp.where(s == 0, 0.0, NEGATIVE)
    k_t = jnp.where(which < 3, jnp.where(same, 0.0, NEGATIVE), jnp.where((which == 3) & is_glob, far, 0.0))
    qaug[...] = jnp.transpose(q_t).astype(BF)
    kaug[...] = jnp.transpose(k_t).astype(BF)

    def norm_to(first, count, gain, shift):
        for r in range(first, first + count, 128):
            spread, scale = norm_stats(sec[pl.ds(r, 128), :].astype(F32))
            nrm[pl.ds(r, 128), :] = (spread * scale * gain + shift).astype(BF)

    def project_rows(first, count):
        def step(i, carry):
            at = pl.multiple_of(i * width, width)
            proj[pl.ds(first, count), pl.ds(at, width)] = dot_nn(
                nrm[pl.ds(first, count), :], wq[:, pl.ds(at, width)]
            ).astype(BF)
            return carry

        lax.fori_loop(0, 3, step, 0)

    loads[1].wait()
    norm_to(tok, glob, glob_gain, glob_shift)
    loads[0].wait()
    norm_to(0, half, attn_gain, attn_shift)
    loads[2].wait()
    project_rows(tok, glob)
    project_rows(0, half)
    loads[3].wait()
    loads[4].wait()
    ct_t[:, pl.ds(0, wide)] = jnp.transpose(ct[...])
    halo.wait()
    norm_to(half, half, attn_gain, attn_shift)
    project_rows(half, half)

    kvt[...] = jnp.transpose(proj[:, pl.ds(2 * width, width)])
    lane_p = lanes_of((1, 128))
    even = jnp.where(lane_p < HEAD_DIM, HEAD_DIM ** (-0.5), 0.0).astype(BF)
    odd = jnp.where(lane_p < HEAD_DIM, 0.0, HEAD_DIM ** (-0.5)).astype(BF)
    even_one = jnp.where(lane_p < HEAD_DIM, 1.0, 0.0).astype(BF)
    odd_one = jnp.where(lane_p < HEAD_DIM, 0.0, 1.0).astype(BF)
    first_head = lax.broadcasted_iota(jnp.int32, (128, 128), 0) < HEAD_DIM
    lse_t[...] = jnp.zeros_like(lse_t)
    rl_t[...] = jnp.zeros_like(rl_t)

    def glob_forward(p, carry):
        at = pl.multiple_of(p * 128, 128)
        keys = jnp.concatenate([proj[:, pl.ds(width + at, 128)], kaug[...]], axis=1)
        qg = proj[pl.ds(tok, glob), pl.ds(at, 128)]
        qa = qaug[pl.ds(tok, glob), :]
        queries = jnp.concatenate(
            [jnp.concatenate([qg * even, qa], axis=1), jnp.concatenate([qg * odd, qa], axis=1)], axis=0
        )
        scores = dot_nt(keys, queries)
        top = jnp.max(scores, axis=0, keepdims=True)
        raised = jnp.exp(scores - top)
        total = jnp.sum(raised, axis=0, keepdims=True)
        weights = (raised * (1.0 / total)).astype(BF)
        probs[p, :, pl.ds(2 * tok, 2 * glob)] = weights
        mixed = dot_nn(kvt[pl.ds(at, 128), :], weights)
        cx[:, pl.ds(at, 128)] = jnp.transpose(jnp.where(first_head, mixed[:, :glob], mixed[:, glob:]))
        logsum = top + jnp.log(total)
        lse_t[pl.ds(2 * p, 1), :] = logsum[:, :glob]
        lse_t[pl.ds(2 * p + 1, 1), :] = logsum[:, glob:]
        return carry

    lax.fori_loop(0, pairs, glob_forward, 0)

    lse = jnp.transpose(lse_t[...])
    in_heads = lanes_of((glob, 128)) < HEADS
    lse = jnp.where(in_heads, lse, 0.0)
    part_a, rest = two_parts(lse)
    rest = lse - part_a.astype(F32)
    part_b = rest.astype(BF)
    part_c = rest - part_b.astype(F32)
    packed = part_a.astype(F32) + pltpu.roll(part_b.astype(F32), 16, 1) + pltpu.roll(part_c, 32, 1)
    msg1[:, pl.ds(0, width)] = cx[...].astype(BF)
    msg1[:, pl.ds(width, 128)] = packed.astype(BF)
    sends1 = []
    for k in peers:
        other = flip(k)
        at = pl.multiple_of(other * slots, slots)
        copy = remote(msg1.at[pl.ds(at, slots)], rcv1.at[k], m1s.at[k], m1r.at[k], (other, b))
        copy.start()
        sends1.append(copy)
    rcv1[0] = msg1[pl.ds(my_slots, slots), :]

    def local_forward_pair(p, carry):
        at = pl.multiple_of(p * 128, 128)
        keys = jnp.concatenate([proj[:, pl.ds(width + at, 128)], kaug[...]], axis=1)
        qp = proj[pl.ds(0, tok), pl.ds(at, 128)]
        for e, mask in ((0, even), (1, odd)):
            queries = jnp.concatenate([qp * mask, qaug[pl.ds(0, tok), :]], axis=1)
            scores = dot_nt(keys, queries)
            top = jnp.max(scores, axis=0, keepdims=True)
            raised = jnp.exp(scores - top)
            inverse = 1.0 / jnp.sum(raised, axis=0, keepdims=True)
            weights = raised.astype(BF)
            probs[p, :, pl.ds(e * tok, tok)] = weights
            rl_t[pl.ds(2 * p + e, 1), :] = inverse
            here = pl.multiple_of(at + e * HEAD_DIM, HEAD_DIM)
            mixed = dot_nn(kvt[pl.ds(here, HEAD_DIM), :], weights)
            att_t[pl.ds(here, HEAD_DIM), pl.ds(0, tok)] = (mixed * inverse).astype(BF)
        return carry

    lax.fori_loop(0, pairs, local_forward_pair, 0)
    att[pl.ds(0, tok), :] = jnp.transpose(att_t[:, pl.ds(0, tok)])

    head_of = lanes_of((128, width)) // HEAD_DIM
    spread_heads = jnp.where(head_of == lax.broadcasted_iota(jnp.int32, (128, width), 0), 1.0, 0.0).astype(BF)
    for copy in sends1:
        copy.wait()
    logs = []
    for k in range(n_seq):
        packed = rcv1[k, :, pl.ds(width, 128)].astype(F32)
        logs.append(packed + pltpu.roll(packed, 112, 1) + pltpu.roll(packed, 96, 1))
    high = functools.reduce(jnp.maximum, logs)
    raised = [jnp.exp(one - high) for one in logs]
    total = functools.reduce(jnp.add, raised)
    in_heads = lanes_of((slots, 128)) < HEADS
    shares = jnp.concatenate([jnp.where(in_heads, one / total, 0.0) for one in raised], axis=0)
    share_a, share_b = two_parts(shares)
    shares = dot_nn(share_a, spread_heads) + dot_nn(share_b, spread_heads)
    cx[...] = shares
    mixed = jnp.zeros((slots, width), F32)
    for k in range(n_seq):
        mixed = mixed + shares[k * slots : (k + 1) * slots] * rcv1[k, :, pl.ds(0, width)].astype(F32)
    att[pl.ds(tok, slots), :] = mixed.astype(BF)
    att_t[:, pl.ds(tok, tail)] = jnp.transpose(
        jnp.concatenate([mixed, jnp.zeros((tail - slots, width), F32)], axis=0)
    ).astype(BF)

    loads[5].wait()
    x2[...] = dot_nn(att[...], wo[...])
    x2[pl.ds(0, tok), :] += sec[pl.ds(0, tok), :].astype(F32)
    x2[pl.ds(tok, slots), :] += sec[pl.ds(pl.multiple_of(tok + my_slots, slots), slots), :].astype(F32)

    def second_norm(first, count):
        spread, scale = norm_stats(x2[pl.ds(first, count), :])
        n2[pl.ds(first, count), :] = (spread * scale * ffn_gain + ffn_shift).astype(BF)

    for r in range(0, tok, 128):
        second_norm(r, 128)
    second_norm(tok, slots)
    n2t[:, pl.ds(0, wide)] = jnp.transpose(n2[...])

    def d_core(i):
        return remote(gd.at[i, :, 1 - c], r0d.at[i], d0s.at[i], d0r.at[i], dev_c)

    def d_y(i):
        return remote(r0d.at[i, 1 - y], r1d.at[i], d1s.at[i], d1r.at[i], dev_y)

    def d_x(z):
        return remote(r1d.at[2 * z + 1 - x], r2d.at[z], d2s.at[z], d2r.at[z], dev_x)

    def d_1(h):
        return remote(r2d.at[2 * h + 1 - zl], r3d.at[h], d3s.at[h], d3r.at[h], dev_1)

    def d_2():
        return remote(r3d.at[1 - zh], r4d, d4s.at[0], d4r.at[0], dev_2)

    def do_d_y(i):
        d_core(i).wait_recv()
        r0d[i] = r0d[i] + gd[i, :, c]
        d_y(i).start()

    def do_d_x(z):
        for o in range(2):
            d_y(2 * z + o).wait_recv()
            r1d[2 * z + o] = r1d[2 * z + o] + r0d[2 * z + o, y]
        d_x(z).start()

    def do_d_1(h):
        for o in range(2):
            d_x(2 * h + o).wait_recv()
            r2d[2 * h + o] = r2d[2 * h + o] + r1d[2 * (2 * h + o) + x]
        d_1(h).start()

    def do_d_2():
        for h in range(2):
            d_1(h).wait_recv()
            r3d[h] = r3d[h] + r2d[2 * h + zl]
        d_2().start()

    def u_core(yy, j):
        return remote(gu.at[yy, 1 - c, j], r0u.at[yy, j], u0s.at[yy * 2 + j], u0r.at[yy * 2 + j], dev_c)

    def u_x(yy, j):
        return remote(r0u.at[yy, j, :, :, 1 - x], r1u.at[yy, j], u1s.at[yy * 2 + j], u1r.at[yy * 2 + j], dev_x)

    def u_y(j):
        return remote(r1u.at[1 - y, j], r2u.at[j], u2s.at[j], u2r.at[j], dev_y)

    def u_1():
        return remote(r2u.at[:, :, 1 - zl], r3u, u3s.at[0], u3r.at[0], dev_1)

    def u_2():
        return remote(r3u.at[:, 1 - zh], r4u, u4s.at[0], u4r.at[0], dev_2)

    def do_u_x(yy, j):
        u_core(yy, j).wait_recv()
        r0u[yy, j] = r0u[yy, j] + gu[yy, c, j]
        u_x(yy, j).start()

    def do_u_y(j):
        for yy in range(2):
            u_x(yy, j).wait_recv()
            r1u[yy, j] = r1u[yy, j] + r0u[yy, j, :, :, x]
        u_y(j).start()

    def do_u_1():
        for j in range(2):
            u_y(j).wait_recv()
            r2u[j] = r2u[j] + r1u[y, j]
        u_1().start()

    def do_u_2():
        u_1().wait_recv()
        r3u[...] = r3u[...] + r2u[:, :, zl]
        u_2().start()

    for i in range(n_chunk):
        rll[pl.ds(i, 1), :] = up_bias[pl.ds(i * chunk, chunk)].reshape(1, chunk)
    acc[...] = jnp.zeros_like(acc)
    gn2[...] = jnp.zeros_like(gn2)

    def ffn_step(i, carry):
        slot = lax.rem(i, 2)
        for copy in stream(i, slot):
            copy.wait()
        at = pl.multiple_of(i * chunk, chunk)
        hidden = dot_nn(n2[...], wus[slot]) + rll[pl.ds(i, 1), :]
        active, slope = gelu_pair(hidden)
        active = active.astype(BF)
        gd[i] = dot_nn(ct_t[:, pl.ds(0, wide)], active).astype(BF).reshape(gd.shape[1:])
        d_core(i).start()
        grad_hidden = (slope * dot_nt(ct[...], wds[slot])).astype(BF)
        gu[i // 4, (i // 2) % 2, i % 2] = (
            dot_nn(n2t[:, pl.ds(0, wide)], grad_hidden).astype(BF).reshape(gu.shape[3:])
        )

        @pl.when((i // 2) % 2 != c)
        def _():
            u_core(i // 4, i % 2).start()

        rll[pl.ds(i, 1), :] = jnp.sum(grad_hidden.astype(F32), axis=0, keepdims=True)
        acc[...] += dot_nn(active, wds[slot])
        gn2[...] += dot_nt(grad_hidden, wus[slot])

        @pl.when(i + 2 < n_chunk)
        def _():
            for copy in stream(i + 2, slot):
                copy.start()

        @pl.when(i >= 2)
        def _():
            do_d_y(i - 2)

        @pl.when((i >= 2) & (((i - 2) // 2) % 2 == c))
        def _():
            do_u_x((i - 2) // 4, i % 2)

        return carry

    lax.fori_loop(0, n_chunk, ffn_step, 0)

    vec[...] = jnp.zeros_like(vec)
    for i in range(n_chunk):
        vec[pl.ds(8 + i // 2, 1), pl.ds((i % 2) * chunk, chunk)] = rll[pl.ds(i, 1), :]

    def second_pull(first, count):
        grad, gain_term, shift_term = norm_pull(
            x2[pl.ds(first, count), :], ffn_gain, gn2[pl.ds(first, count), :]
        )
        upstream = ct[pl.ds(first, count), :].astype(F32)
        total = upstream + grad
        acc[pl.ds(first, count), :] += x2[pl.ds(first, count), :] + down_bias
        x2[pl.ds(first, count), :] = total
        n2[pl.ds(first, count), :] = total.astype(BF)
        vec[pl.ds(4, 1), :] += gain_term
        vec[pl.ds(5, 1), :] += shift_term
        vec[pl.ds(6, 1), :] += jnp.sum(upstream, axis=0, keepdims=True)

    for r in range(0, tok, 128):
        second_pull(r, 128)
    second_pull(tok, slots)
    do_d_y(n_chunk - 2)
    do_d_y(n_chunk - 1)

    @pl.when(c == 1)
    def _():
        do_u_x(1, 0)
        do_u_x(1, 1)

    gatt[...] = dot_nt(n2[...], wo[...]).astype(BF)

    slot_grad = gatt[pl.ds(tok, slots), :].astype(F32)
    slot_att = att[pl.ds(tok, slots), :].astype(F32)
    head_sel = lanes_of((1, 128)) < HEADS

    def inner_aug(upstream, values):
        high, low = two_parts(upstream.astype(F32) * values)
        inner = dot_nt(high, spread_heads) + dot_nt(low, spread_heads)
        high, low = two_parts(jnp.where(head_sel, inner, 0.0))
        return (high.astype(F32) + pltpu.roll(low.astype(F32), 16, 1)).astype(BF)

    scaled = jnp.concatenate(
        [(cx[pl.ds(k * slots, slots), :] * slot_grad).astype(BF) for k in range(n_seq)], axis=0
    )
    msg1[:, pl.ds(0, width)] = scaled
    msg1[:, pl.ds(width, 128)] = inner_aug(scaled, jnp.concatenate([slot_att] * n_seq, axis=0))
    sends2 = []
    for k in peers:
        copy = remote(
            msg1.at[pl.ds(k * slots, slots)], rcv2.at[pl.ds(my_slots, slots)], m2s.at[k], m2r.at[k],
            (flip(k), b),
        )
        copy.start()
        sends2.append(copy)
    rcv2[pl.ds(my_slots, slots), :] = msg1[pl.ds(0, slots), :]

    n2t[:, pl.ds(0, tok)] = jnp.transpose(nrm[pl.ds(0, tok), :])
    mine = nrm[pl.ds(pl.multiple_of(tok + my_slots, slots), slots), :].astype(F32)
    n2t[:, pl.ds(tok, tail)] = jnp.transpose(
        jnp.concatenate([mine, jnp.zeros((tail - slots, width), F32)], axis=0)
    ).astype(BF)

    outs = nrm
    outs[pl.ds(0, wide), :] = acc[...].astype(BF)
    out_copy = pltpu.make_async_copy(outs.at[pl.ds(0, tok)], o_out, osem.at[0])
    out_copy.start()
    own_out = pltpu.make_async_copy(
        outs.at[pl.ds(tok, slots)], o_gout.at[pl.ds(my_slots, slots)], osem.at[1]
    )
    own_out.start()
    sends_o = []
    for k in peers:
        copy = remote(
            outs.at[pl.ds(tok, slots)], o_gout.at[pl.ds(my_slots, slots)], gos.at[k], gor.at[k], (flip(k), b)
        )
        copy.start()
        sends_o.append(copy)

    scale_c = jnp.transpose(
        jnp.concatenate([rl_t[...], jnp.zeros((128 - rl_t.shape[0], tok), F32)], axis=0)
    )
    scale_a, scale_b = two_parts(scale_c)
    for r in range(0, tok, 128):
        wider = dot_nn(scale_a[r : r + 128], spread_heads) + dot_nn(scale_b[r : r + 128], spread_heads)
        scaled = (gatt[pl.ds(r, 128), :].astype(F32) * wider).astype(BF)
        gatt[pl.ds(r, 128), :] = scaled
        qaug[pl.ds(r, 128), :] = inner_aug(scaled, att[pl.ds(r, 128), :].astype(F32))
    kvt[...] = jnp.transpose(proj[:, pl.ds(width, width)])
    for i in range(4):
        do_d_x(i)
    do_u_y(0)
    do_u_y(1)
    for copy in sends2:
        copy.wait()

    def chunk_at(p):
        return gu.at[p // 4, lax.rem(p // 2, 2), lax.rem(p, 2)]

    def put_chunk(p, value):
        gu[p // 4, lax.rem(p // 2, 2), lax.rem(p, 2)] = value.astype(BF).reshape(gu.shape[3:])

    def q_core(p):
        i = p // 2
        return remote(chunk_at(p), r0q.at[i], q0s.at[i], q0r.at[i], dev_c)

    def q_a(i, first):
        src, dev = (r0q.at[i, :, :, 1 - x], dev_x) if first == "x" else (r0q.at[i, :, :, :, 1 - y], dev_y)
        return remote(src, r1q.at[i], q1s.at[i], q1r.at[i], dev)

    def q_b(i, first):
        side_bit, dev = (y, dev_y) if first == "x" else (x, dev_x)
        return remote(r1q.at[i, :, :, 1 - side_bit], r2q.at[i], q2s.at[i], q2r.at[i], dev)

    def q_1(i):
        return remote(r2q.at[i, :, 1 - zl], r3q.at[i], q3s.at[i], q3r.at[i], dev_1)

    def q_2(i):
        return remote(r3q.at[i, 1 - zh], r4q.at[i], q4s.at[i], q4r.at[i], dev_2)

    def by_order(i, act):
        if isinstance(i, int):
            act("x" if i % 2 else "y")
            return

        @pl.when(lax.rem(i, 2) == 1)
        def _():
            act("x")

        @pl.when(lax.rem(i, 2) == 0)
        def _():
            act("y")

    def do_q_a(p):
        i = p // 2
        q_core(p).wait_recv()
        r0q[i] = r0q[i] + chunk_at(p)[...].reshape(r0q.shape[1:])
        by_order(i, lambda first: q_a(i, first).start())

    def do_q_b(i):
        def act(first):
            q_a(i, first).wait_recv()
            if first == "x":
                r1q[i] = r1q[i] + r0q[i, :, :, x]
            else:
                r1q[i] = r1q[i] + r0q[i, :, :, :, y]
            q_b(i, first).start()

        by_order(i, act)

    def do_q_1(i):
        def act(first):
            q_b(i, first).wait_recv()
            r2q[i] = r2q[i] + r1q[i, :, :, y if first == "x" else x]

        by_order(i, act)
        q_1(i).start()

    def do_q_2(i):
        q_1(i).wait_recv()
        r3q[i] = r3q[i] + r2q[i, :, zl]
        q_2(i).start()

    def m3(p, k):
        other = flip(k)
        at = pl.multiple_of(p * glob + other * slots, slots)
        return remote(wus.at[0, pl.ds(at, slots)], rcv3.at[k - 1, p], m3s.at[p, k], m3r.at[p, k], (other, b))

    def q_chunk(p):
        own = wus[0, pl.ds(pl.multiple_of(p * glob + s * slots, slots), slots), :].astype(F32)
        for k in peers:
            m3(p, k).wait_recv()
        for k in peers:
            own = own + rcv3[k - 1, p].astype(F32)
        own = own.astype(BF)
        for w in range(3):
            proj[pl.ds(tok, slots), pl.ds(pl.multiple_of(w * width + p * 128, 128), 128)] = own[
                :, w * 128 : (w + 1) * 128
            ]
        right = jnp.concatenate(
            [proj[pl.ds(0, wide), pl.ds(pl.multiple_of(w * width + p * 128, 128), 128)] for w in range(3)], axis=1
        )
        put_chunk(p, dot_nn(n2t[:, pl.ds(0, wide)], right))
        send_chunk(p)

    def send_chunk(p):
        @pl.when(lax.rem(p, 2) != c)
        def _():
            q_core(p).start()

    def tick(p):
        for back, act in ((5, do_q_2), (4, do_q_1), (3, do_q_b), (2, do_q_a)):
            q = p - back
            if isinstance(p, int) and not 0 <= q < pairs:
                continue
            mine = lax.rem(q, 2) == c if isinstance(q, int) else (q >= 0) & (lax.rem(q, 2) == c)

            @pl.when(mine)
            def _(act=act, q=q):
                act(q if act is do_q_a else q // 2)

    for yy in range(2):
        for j in range(2):
            u_core(yy, j).wait_send()
    for h in range(2):
        put_chunk(pairs + h, dot_nn(att_t[:, pl.ds(0, wide)], n2[:, pl.ds(h * 384, 384)]))
        send_chunk(pairs + h)

    minus = jnp.where(lanes_of((rows, 128)) < 32, -1.0, 0.0).astype(BF)

    def chosen(head):
        lane = lanes_of((1, 128))
        return jnp.where((lane == head) | (lane == head + 16), 1.0, 0.0).astype(BF)

    def attention_back(p, carry):
        at = pl.multiple_of(p * 128, 128)
        qp = proj[pl.ds(0, tok), pl.ds(at, 128)]
        qg = proj[pl.ds(tok, glob), pl.ds(at, 128)]
        gp = gatt[pl.ds(0, tok), pl.ds(at, 128)]
        gg = rcv2[:, pl.ds(at, 128)]
        dg = rcv2[:, pl.ds(width, 128)]
        values = jnp.concatenate([proj[:, pl.ds(2 * width + at, 128)], minus], axis=1)
        ups = jnp.concatenate([gp * even_one, gp * odd_one, gg * even_one, gg * odd_one], axis=0)
        dd = qaug[pl.ds(0, tok), :]
        sel_e, sel_o = chosen(2 * p), chosen(2 * p + 1)
        inner = jnp.concatenate([dd * sel_e, dd * sel_o, dg * sel_e, dg * sel_o], axis=0)
        qs = jnp.concatenate([qp * even, qp * odd, qg * even, qg * odd], axis=0)
        grad_v = dot_nn(probs[p], ups)
        for first, count in ((0, tok), (tok, tok), (2 * tok, 2 * glob)):
            right = jnp.concatenate([ups[first : first + count], inner[first : first + count]], axis=1)
            grad_w = dot_nt(values, right)
            here = probs[p, :, pl.ds(first, count)].astype(F32)
            probs[p, :, pl.ds(first, count)] = (here * grad_w).astype(BF)
        grad_k = dot_nn(probs[p], qs)
        factor = HEAD_DIM ** (-0.5)
        low = dot_nn(kvt[pl.ds(at, HEAD_DIM), :], probs[p, :, pl.ds(0, tok)])
        upper = dot_nn(
            kvt[pl.ds(pl.multiple_of(at + HEAD_DIM, HEAD_DIM), HEAD_DIM), :], probs[p, :, pl.ds(tok, tok)]
        )
        grad_q = jnp.concatenate([low, upper], axis=0) * factor
        own = dot_nn(kvt[pl.ds(at, 128), :], probs[p, :, pl.ds(2 * tok, 2 * glob)])
        own = jnp.where(first_head, own[:, :glob], own[:, glob:]) * factor
        stage = pl.ds(pl.multiple_of(p * glob, glob), glob)
        wus[0, stage, pl.ds(0, 128)] = jnp.transpose(own).astype(BF)
        wus[0, stage, pl.ds(128, 128)] = grad_k[tok:].astype(BF)
        wus[0, stage, pl.ds(256, 128)] = grad_v[tok:].astype(BF)
        for k in peers:
            m3(p, k).start()
        proj[pl.ds(0, tok), pl.ds(at, 128)] = jnp.transpose(grad_q).astype(BF)
        proj[pl.ds(0, tok), pl.ds(width + at, 128)] = grad_k[:tok].astype(BF)
        proj[pl.ds(0, tok), pl.ds(2 * width + at, 128)] = grad_v[:tok].astype(BF)

        @pl.when(p == 0)
        def _():
            do_d_1(0)
            do_d_1(1)

        @pl.when(p == 1)
        def _():
            do_u_1()
            own_out_chunk(do_q_a, lambda: pairs + c)

        @pl.when(p == 2)
        def _():
            do_d_2()
            own_out_chunk(do_q_b, lambda: 3)

        @pl.when(p == 3)
        def _():
            do_u_2()
            own_out_chunk(do_q_1, lambda: 3)

        @pl.when(p == 4)
        def _():
            own_out_chunk(do_q_2, lambda: 3)

        @pl.when(p >= 1)
        def _():
            q_chunk(p - 1)

        tick(p)
        return carry

    def own_out_chunk(act, which):
        act(which())

    lax.fori_loop(0, pairs, attention_back, 0)

    def first_pull(first):
        grad, gain_term, shift_term = norm_pull(
            sec[pl.ds(first, 128), :].astype(F32), attn_gain, gn2[pl.ds(first, 128), :]
        )
        n2[pl.ds(first, 128), :] = (grad + x2[pl.ds(first, 128), :]).astype(BF)
        vec[pl.ds(0, 1), :] += gain_term
        vec[pl.ds(1, 1), :] += shift_term

    tick(6)
    gn2[pl.ds(half, half), :] = dot_nt(proj[pl.ds(half, half), :], wq[...])
    for r in range(half, tok, 128):
        first_pull(r)
    back = remote(
        n2.at[pl.ds(half, half)], o_tgrad.at[pl.ds(0, half)], hs2.at[0], hr2.at[0],
        (lax.rem(s + 1, n_seq), b),
    )
    back.start()

    q_chunk(pairs - 1)

    gn2[pl.ds(0, half), :] = dot_nt(proj[pl.ds(0, half), :], wq[...])
    for r in range(0, half, 128):
        first_pull(r)
    keep = pltpu.make_async_copy(n2.at[pl.ds(0, half)], o_tgrad.at[pl.ds(half, half)], osem.at[2])
    keep.start()
    tick(7)
    gn2[pl.ds(tok, slots), :] = dot_nt(proj[pl.ds(tok, slots), :], wq[...])
    grad, gain_term, shift_term = norm_pull(
        sec[pl.ds(pl.multiple_of(tok + my_slots, slots), slots), :].astype(F32),
        glob_gain,
        gn2[pl.ds(tok, slots), :],
    )
    vec[pl.ds(2, 1), :] += gain_term
    vec[pl.ds(3, 1), :] += shift_term
    n2[pl.ds(tok, slots), :] = (grad + x2[pl.ds(tok, slots), :]).astype(BF)
    own_grad = pltpu.make_async_copy(
        n2.at[pl.ds(tok, slots)], o_ggrad.at[pl.ds(my_slots, slots)], osem.at[3]
    )
    own_grad.start()
    sends_g = []
    for k in peers:
        copy = remote(
            n2.at[pl.ds(tok, slots)], o_ggrad.at[pl.ds(my_slots, slots)], ggs_s.at[k], ggs_r.at[k],
            (flip(k), b),
        )
        copy.start()
        sends_g.append(copy)

    share = vec.shape[1] // n_seq
    for j in range(n_seq):
        rolled = vec[pl.ds(0, 8), :]
        if j:
            rolled = pltpu.roll(rolled, vec.shape[1] - share * j, 1)
        vmsg[j, :, pl.ds(0, 128)] = rolled[:, :128]
        vmsg[j, :, pl.ds(128, chunk)] = jnp.broadcast_to(
            vec[pl.ds(8 + j // 2, 1), pl.ds((j % 2) * chunk, chunk)], (8, chunk)
        )
    sends_v = []
    for k in peers:
        copy = remote(vmsg.at[flip(k)], vrcv.at[k - 1], vs.at[k], vr.at[k], (flip(k), b))
        copy.start()
        sends_v.append(copy)

    d_2().wait_recv()
    o_down[...] = r4d[...].astype(F32) + r3d[zh].astype(F32)
    u_2().wait_recv()
    last = r4u[...].astype(F32) + r3u[:, zh].astype(F32)
    o_up[:, pl.ds(0, 384)] = last[0].reshape(96, 384)
    o_up[:, pl.ds(384, 384)] = last[1].reshape(96, 384)

    tick(8)
    for copy in sends_v:
        copy.wait()
    vsum[0] = vmsg[s]
    for k in peers:
        vsum[0] = vsum[0] + vrcv[k - 1]
    v_core = remote(vsum.at[0], vsum.at[1], vs.at[0], vr.at[0], dev_c)
    v_core.start()
    tick(9)
    v_core.wait()
    vsum[2] = vsum[0] + vsum[1]
    v_y = remote(vsum.at[2], vsum.at[3], vs.at[8], vr.at[8], dev_y)
    v_y.start()
    tick(10)
    v_y.wait()
    shared = vsum[2] + vsum[3]
    o_vec[...] = shared[:, :share]
    o_ub[...] = shared[0:1, 128:]

    for i in range(4):
        q_2(i).wait_recv()
        both[c, i] = r4q[i] + r3q[i, zh]
    f_core = remote(both.at[c], both.at[c], fs.at[0], fr.at[0], dev_c)
    f_core.start()
    f_core.wait()

    def columns_of(bb):
        tiles = []
        for n in range(5):
            tile = (bb * 576 - 64 * c) // 128 + n
            which, pair = tile // 6, lax.rem(tile, 6)
            tiles.append(both[lax.rem(pair, 2), pair // 2, :, pl.ds(pl.multiple_of(which * 128, 128), 128)])
        for n in range(2):
            tile = (bb * 192 - 64 * c) // 128 + n
            tiles.append(both[tile // 3, 3, :, pl.ds(pl.multiple_of(lax.rem(tile, 3) * 128, 128), 128)])
        return jnp.concatenate(tiles, axis=1)

    ymsg[...] = columns_of(b + 2 - 4 * y)
    f_y = remote(ymsg, yrcv, fs.at[1], fr.at[1], dev_y)
    f_y.start()

    def put_columns(yy, block):
        block = block.astype(F32)
        at = pl.multiple_of(yy * 48, 48)
        main = block[:, :640]
        o_qkv[pl.ds(at, 48), :] = jnp.where(c == 1, pltpu.roll(main, 576, 1), main)[:, :576]
        main = block[:, 640:]
        o_wout[pl.ds(at, 48), :] = jnp.where(c == 1, pltpu.roll(main, 192, 1), main)[:, :192]

    put_columns(y, columns_of(b))
    f_y.wait()
    put_columns(1 - y, yrcv[...])

    for i in range(8):
        d_core(i).wait_send()
        d_y(i).wait_send()
    for i in range(4):
        d_x(i).wait_send()
    for i in range(2):
        d_1(i).wait_send()
    d_2().wait_send()
    for yy in range(2):
        for j in range(2):
            u_x(yy, j).wait_send()
        u_y(yy).wait_send()
    u_1().wait_send()
    u_2().wait_send()
    for i in range(4):
        q_core(2 * i + 1 - c).wait_send()
        by_order(i, lambda first, i=i: (q_a(i, first).wait_send(), q_b(i, first).wait_send()))
        q_1(i).wait_send()
        q_2(i).wait_send()
    for p in range(pairs):
        for k in peers:
            m3(p, k).wait_send()
    back.wait()
    keep.wait()
    own_grad.wait()
    out_copy.wait()
    own_out.wait()
    for copy in sends_o + sends_g:
        copy.wait()


def fits(tokens, global_states, w_qkv, w_up):
    return (
        lax.axis_size("seq") == 8
        and lax.axis_size("batch") == 4
        and tokens.shape == (1, BLOCK, HEADS * HEAD_DIM)
        and global_states.shape == (1, 128, HEADS * HEAD_DIM)
        and w_qkv.shape == (HEADS * HEAD_DIM, 3 * HEADS * HEAD_DIM)
        and w_up.shape == (HEADS * HEAD_DIM, 3072)
    )


def finish_kernel(*refs):
    ins, outs = refs[:10], refs[10:]
    for i in range(8):
        outs[i][...] = ins[i][...]
    for i in range(7):
        outs[8 + i][...] = ins[8][i, :]
    outs[15][...] = ins[9][0, :]


def fused(
    tokens, global_states, token_seg, global_seg, attn_gain, attn_shift, glob_gain, glob_shift, w_qkv, w_out,
    ffn_gain, ffn_shift, w_up, up_bias, w_down, down_bias, out_cotangent, global_cotangent,
):
    tok, width = tokens.shape[1:]
    glob = global_states.shape[1]
    hidden = w_up.shape[1]
    n_seq, n_batch = lax.axis_size("seq"), lax.axis_size("batch")
    rows, slots = tok + glob, glob // n_seq
    wide = tok + slots
    chunk, part, side = hidden // n_seq, width // n_seq, width // n_batch
    pairs = HEADS // 2
    dma = pltpu.SemaphoreType.DMA

    def any_space():
        return pl.BlockSpec(memory_space=pl.ANY)

    def vmem():
        return pl.BlockSpec(memory_space=pltpu.VMEM)

    def low(*shape):
        return pltpu.VMEM(shape, BF)

    def full(*shape):
        return pltpu.VMEM(shape, F32)

    scratch = [
        low(rows, width), low(rows, width), low(rows, 3 * width), low(width, rows),
        low(pairs, rows, 2 * tok + 2 * glob), low(width, tok + 128), low(wide, width), full(wide, width),
        low(wide, width), low(width, tok + 128), low(wide, width), low(width, tok + 128),
        full(wide, width), full(wide, width), low(wide, width), low(rows, 128), low(rows, 128),
        low(width, 3 * width), low(width, width), low(2, width, chunk), low(2, chunk, width),
        full(128, glob), full(16, tok), full(glob, width), low(glob, width + 128),
        low(n_seq, slots, width + 128), low(glob, width + 128),
        low(n_seq - 1, pairs, slots, chunk),
        full(16, width), full(n_seq, 8, 128 + chunk), full(n_seq - 1, 8, 128 + chunk), full(4, 8, 128 + chunk), full(8, chunk),
        low(8, 2, 2, side, chunk), low(8, 2, side, chunk), low(8, side, chunk), low(4, side, chunk),
        low(2, side, chunk), low(side, chunk),
        *[low(*[2] * n, part // 2, chunk) for n in (7, 6, 5, 4, 3, 2)],
        low(4, 2, 2, 2, 2, part // 2, chunk), low(4, 2, 2, 2, part // 2, chunk), low(4, 2, 2, part // 2, chunk),
        low(4, 2, part // 2, chunk), low(4, part // 2, chunk), low(2, 4, part // 2, chunk),
        low(part // 2, 896), low(part // 2, 896),
        dma((8,)), dma((2, 2)), dma((1,)), dma((1,)),
        *[dma((8,)) for _ in range(4)], dma((pairs, 8)), dma((pairs, 8)), *[dma((8,)) for _ in range(4)], dma((9,)), dma((9,)),
        dma((8,)), dma((8,)), dma((8,)), dma((8,)), dma((4,)), dma((4,)), dma((2,)), dma((2,)), dma((1,)), dma((1,)),
        dma((4,)), dma((4,)), dma((4,)), dma((4,)), dma((2,)), dma((2,)), dma((1,)), dma((1,)), dma((1,)), dma((1,)),
        *[dma((4,)) for _ in range(10)],
        dma((2,)), dma((2,)), dma((1,)), dma((1,)), dma((4,)),
    ]

    results = pl.pallas_call(
        layer_kernel,
        out_shape=[
            jax.ShapeDtypeStruct((tok, width), BF),
            jax.ShapeDtypeStruct((glob, width), BF),
            jax.ShapeDtypeStruct((tok, width), BF),
            jax.ShapeDtypeStruct((glob, width), BF),
            jax.ShapeDtypeStruct((part, 3 * side), F32),
            jax.ShapeDtypeStruct((part, side), F32),
            jax.ShapeDtypeStruct((part, 2 * chunk), F32),
            jax.ShapeDtypeStruct((side, chunk), F32),
            jax.ShapeDtypeStruct((8, part), F32),
            jax.ShapeDtypeStruct((1, chunk), F32),
        ],
        in_specs=[any_space(), any_space(), vmem(), vmem(), vmem(), vmem(), vmem(), vmem(), any_space(), any_space(),
                  vmem(), vmem(), any_space(), vmem(), any_space(), vmem(), any_space(), any_space()],
        out_specs=[any_space()] * 4 + [vmem()] * 6,
        scratch_shapes=scratch,
        compiler_params=pltpu.CompilerParams(
            collective_id=0, has_side_effects=True, vmem_limit_bytes=64 * 1024 * 1024
        ),
        name="layer",
    )(
        tokens[0], global_states[0], token_seg, global_seg, attn_gain, attn_shift, glob_gain,
        glob_shift, w_qkv, w_out, ffn_gain, ffn_shift, w_up, up_bias, w_down, down_bias,
        out_cotangent[0], global_cotangent[0],
    )
    *large, vectors, ub = results
    results = pl.pallas_call(
        finish_kernel,
        out_shape=[jax.ShapeDtypeStruct(one.shape, one.dtype) for one in large]
        + [jax.ShapeDtypeStruct((part,), F32)] * 7
        + [jax.ShapeDtypeStruct((chunk,), F32)],
        in_specs=[vmem()] * 10,
        out_specs=[vmem()] * 16,
        name="results",
    )(*large, vectors, ub)
    out, gout, tgrad, ggrad, g_qkv, g_out, g_up, g_down, *g_vec, g_ub = results
    return (
        out[None], gout[None], tgrad[None], ggrad[None], g_vec[0], g_vec[1], g_vec[2], g_vec[3], g_qkv, g_out,
        g_vec[4], g_vec[5], g_up, g_ub, g_down.T, g_vec[6],
    )


def local(tokens, global_states, token_seg, global_seg, *rest):
    w_qkv, w_up = rest[4], rest[8]
    way = fused if fits(tokens, global_states, w_qkv, w_up) else general
    return way(tokens, global_states, token_seg, global_seg, *rest)


def solution(mesh):
    placed = (
        P("batch", "seq", None),
        P("batch", None, None),
        P("batch", "seq"),
        P("batch", None),
        P(),
        P(),
        P(),
        P(),
        P(),
        P(),
        P(),
        P(),
        P(),
        P(),
        P(),
        P(),
        P("batch", "seq", None),
        P("batch", None, None),
    )
    return jax.shard_map(
        local,
        mesh=mesh,
        in_specs=placed,
        out_specs=(
            P("batch", "seq", None),
            P("batch", None, None),
            P("batch", "seq", None),
            P("batch", None, None),
            P("seq"),
            P("seq"),
            P("seq"),
            P("seq"),
            P("seq", "batch"),
            P("seq", "batch"),
            P("seq"),
            P("seq"),
            P("seq", "batch"),
            P("seq"),
            P("seq", "batch"),
            P("seq"),
        ),
        check_vma=False,
    )
```

```python
import functools

import jax
import jax.numpy as jnp
from jax import lax
from jax.experimental import pallas as pl
from jax.experimental.pallas import tpu as pltpu
from jax.sharding import PartitionSpec as P

HEADS = 12
HEAD_DIM = 64
BLOCK = 512


EPS = 1e-05
NEGATIVE = -1e30


def from_behind(block, axis, distance):
    devices = range(lax.axis_size(axis))
    route = [((i - distance) % len(devices), i) for i in devices]
    return lax.ppermute(block, axis, route)


def norm_rows(source, scaling, offset):
    center = jnp.mean(source, axis=-1, keepdims=True)
    spread = source - center
    variance = jnp.mean(spread * spread, axis=-1, keepdims=True)
    return spread * lax.rsqrt(variance + EPS) * scaling + offset


def norm_back(source, scaling, offset, upstream):
    _, pullback = jax.vjp(norm_rows, source, scaling, offset)
    return pullback(upstream)


def project(former, latter):
    return jnp.einsum("rsd,de->rse", former, latter, preferred_element_type=jnp.float32)


def project_back(former, latter):
    return jnp.einsum("rse,de->rsd", former, latter, preferred_element_type=jnp.float32)


def outer_sum(former, latter):
    return jnp.einsum("rsd,rse->de", former, latter, preferred_element_type=jnp.float32)


def gelu_exact(hidden):
    return jax.nn.gelu(hidden, approximate=False)


def ffn_forward(state, ffn_gain, ffn_shift, w_up, up_bias, w_down, down_bias):
    normed = norm_rows(state, ffn_gain, ffn_shift).astype(jnp.bfloat16)
    hidden = project(normed, w_up) + up_bias
    active = gelu_exact(hidden).astype(jnp.bfloat16)
    result = state + project(active, w_down) + down_bias
    return (result, (normed, hidden, active))


def ffn_backward(state, stored, upstream, ffn_gain, ffn_shift, w_up, w_down):
    normed, hidden, active = stored
    upstream_low = upstream.astype(jnp.bfloat16)
    grad_down = outer_sum(active, upstream_low)
    grad_down_bias = jnp.sum(upstream, axis=(0, 1))
    grad_active = project_back(upstream_low, w_down)
    _, gelu_pull = jax.vjp(gelu_exact, hidden)
    grad_hidden = gelu_pull(grad_active)[0].astype(jnp.bfloat16)
    grad_up = outer_sum(normed, grad_hidden)
    grad_up_bias = jnp.sum(grad_hidden.astype(jnp.float32), axis=(0, 1))
    grad_normed = project_back(grad_hidden, w_up)
    grad_state, grad_gain, grad_shift = norm_back(state, ffn_gain, ffn_shift, grad_normed)
    return (
        upstream + grad_state,
        (grad_gain, grad_shift, grad_up, grad_up_bias, grad_down, grad_down_bias),
    )


def local_scores(queries, keys_near, seg_near, keys_far, seg_far):
    scaling = HEAD_DIM ** (-0.5)
    near_scores = (
        jnp.einsum("rnqhd,rnkhd->rnhqk", queries, keys_near, preferred_element_type=jnp.float32)
        * scaling
    )
    far_scores = (
        jnp.einsum("rnqhd,rghd->rnhqg", queries, keys_far, preferred_element_type=jnp.float32)
        * scaling
    )
    near_open = (seg_near[:, :, :, None] == seg_near[:, :, None, :])[:, :, None]
    far_open = (seg_near[:, :, :, None] == seg_far[:, None, None, :])[:, :, None]
    return (jnp.where(near_open, near_scores, NEGATIVE), jnp.where(far_open, far_scores, NEGATIVE))


def local_forward(queries, keys_near, values_near, seg_near, keys_far, values_far, seg_far):
    near_scores, far_scores = local_scores(queries, keys_near, seg_near, keys_far, seg_far)
    maxima = jnp.maximum(jnp.max(near_scores, axis=-1), jnp.max(far_scores, axis=-1))
    near_exp = jnp.exp(near_scores - maxima[..., None])
    far_exp = jnp.exp(far_scores - maxima[..., None])
    totals = jnp.sum(near_exp, axis=-1) + jnp.sum(far_exp, axis=-1)
    near_weights = (near_exp / totals[..., None]).astype(jnp.bfloat16)
    far_weights = (far_exp / totals[..., None]).astype(jnp.bfloat16)
    mixed_out = jnp.einsum(
        "rnhqk,rnkhd->rnqhd", near_weights, values_near, preferred_element_type=jnp.float32
    )
    mixed_out = mixed_out + jnp.einsum(
        "rnhqg,rghd->rnqhd", far_weights, values_far, preferred_element_type=jnp.float32
    )
    return (mixed_out, maxima + jnp.log(totals))


def local_backward(
    queries, keys_near, values_near, seg_near, keys_far, values_far, seg_far, logsum, upstream
):
    scaling = HEAD_DIM ** (-0.5)
    near_scores, far_scores = local_scores(queries, keys_near, seg_near, keys_far, seg_far)
    near_weights = jnp.exp(near_scores - logsum[..., None])
    far_weights = jnp.exp(far_scores - logsum[..., None])
    near_grad = jnp.einsum(
        "rnqhd,rnkhd->rnhqk", upstream, values_near, preferred_element_type=jnp.float32
    )
    far_grad = jnp.einsum(
        "rnqhd,rghd->rnhqg", upstream, values_far, preferred_element_type=jnp.float32
    )
    row_inner = jnp.sum(near_weights * near_grad, axis=-1) + jnp.sum(
        far_weights * far_grad, axis=-1
    )
    near_score_grad = (near_weights * (near_grad - row_inner[..., None])).astype(jnp.bfloat16)
    far_score_grad = (far_weights * (far_grad - row_inner[..., None])).astype(jnp.bfloat16)
    grad_queries = jnp.einsum(
        "rnhqk,rnkhd->rnqhd", near_score_grad, keys_near, preferred_element_type=jnp.float32
    )
    grad_queries = scaling * (
        grad_queries
        + jnp.einsum(
            "rnhqg,rghd->rnqhd", far_score_grad, keys_far, preferred_element_type=jnp.float32
        )
    )
    grad_keys = scaling * jnp.einsum(
        "rnhqk,rnqhd->rnkhd", near_score_grad, queries, preferred_element_type=jnp.float32
    )
    grad_values = jnp.einsum(
        "rnhqk,rnqhd->rnkhd",
        near_weights.astype(jnp.bfloat16),
        upstream,
        preferred_element_type=jnp.float32,
    )
    grad_keys_far = scaling * jnp.einsum(
        "rnhqg,rnqhd->rghd", far_score_grad, queries, preferred_element_type=jnp.float32
    )
    grad_values_far = jnp.einsum(
        "rnhqg,rnqhd->rghd",
        far_weights.astype(jnp.bfloat16),
        upstream,
        preferred_element_type=jnp.float32,
    )
    return (grad_queries, grad_keys, grad_values, grad_keys_far, grad_values_far)


def global_scores(glob_queries, glob_keys, glob_seg, key_rows, seg_tokens):
    scaling = HEAD_DIM ** (-0.5)
    remote_scores = (
        jnp.einsum("rghd,rshd->rhgs", glob_queries, key_rows, preferred_element_type=jnp.float32)
        * scaling
    )
    own_scores = (
        jnp.einsum("rghd,rjhd->rhgj", glob_queries, glob_keys, preferred_element_type=jnp.float32)
        * scaling
    )
    remote_open = glob_seg[:, None, :, None] == seg_tokens[:, None, None, :]
    own_open = glob_seg[:, None, :, None] == glob_seg[:, None, None, :]
    return (
        jnp.where(remote_open, remote_scores, NEGATIVE),
        jnp.where(own_open, own_scores, NEGATIVE),
    )


def general(
    tokens,
    global_states,
    token_seg,
    global_seg,
    attn_gain,
    attn_shift,
    glob_gain,
    glob_shift,
    w_qkv,
    w_out,
    ffn_gain,
    ffn_shift,
    w_up,
    up_bias,
    w_down,
    down_bias,
    out_cotangent,
    global_cotangent,
):
    row_count, tok_count, model_width = tokens.shape
    glob_count = global_states.shape[1]
    half_block = BLOCK // 2
    block_count = tok_count // BLOCK
    seq_devices = lax.axis_size("seq")
    scaling = HEAD_DIM ** (-0.5)
    low_type = jnp.bfloat16
    arrived = from_behind(tokens[:, :half_block], "seq", -1)
    sectioned = jnp.concatenate([tokens[:, half_block:], arrived], axis=1).astype(jnp.float32)
    glob_state = global_states.astype(jnp.float32)
    normed = norm_rows(sectioned, attn_gain, attn_shift).astype(low_type)
    glob_normed = norm_rows(glob_state, glob_gain, glob_shift).astype(low_type)
    projected = (
        project(normed, w_qkv).astype(low_type).reshape(row_count, tok_count, 3, HEADS, HEAD_DIM)
    )
    glob_proj = (
        project(glob_normed, w_qkv)
        .astype(low_type)
        .reshape(row_count, glob_count, 3, HEADS, HEAD_DIM)
    )
    queries = projected[:, :, 0]
    key_rows = projected[:, :, 1]
    value_rows = projected[:, :, 2]
    glob_queries = glob_proj[:, :, 0]
    glob_keys = glob_proj[:, :, 1]
    glob_values = glob_proj[:, :, 2]
    block_shape = (row_count, block_count, BLOCK, HEADS, HEAD_DIM)
    block_queries = queries.reshape(block_shape)
    block_keys = key_rows.reshape(block_shape)
    block_values = value_rows.reshape(block_shape)
    block_seg = token_seg.reshape(row_count, block_count, BLOCK)
    local_out, local_logsum = local_forward(
        block_queries, block_keys, block_values, block_seg, glob_keys, glob_values, global_seg
    )
    remote_scores, own_scores = global_scores(
        glob_queries, glob_keys, global_seg, key_rows, token_seg
    )
    maxima = jnp.maximum(
        lax.pmax(jnp.max(remote_scores, axis=-1), "seq"), jnp.max(own_scores, axis=-1)
    )
    remote_total = jnp.sum(jnp.exp(remote_scores - maxima[..., None]), axis=-1)
    totals = lax.psum(remote_total, "seq") + jnp.sum(
        jnp.exp(own_scores - maxima[..., None]), axis=-1
    )
    remote_weights = (jnp.exp(remote_scores - maxima[..., None]) / totals[..., None]).astype(
        low_type
    )
    own_weights = (jnp.exp(own_scores - maxima[..., None]) / totals[..., None]).astype(low_type)
    remote_part = jnp.einsum(
        "rhgs,rshd->rghd", remote_weights, value_rows, preferred_element_type=jnp.float32
    )
    glob_out = lax.psum(remote_part, "seq")
    glob_out = glob_out + jnp.einsum(
        "rhgj,rjhd->rghd", own_weights, glob_values, preferred_element_type=jnp.float32
    )
    glob_logsum = maxima + jnp.log(totals)
    attended = local_out.reshape(row_count, tok_count, model_width).astype(low_type)
    glob_attended = glob_out.reshape(row_count, glob_count, model_width).astype(low_type)
    attn_sum = sectioned + project(attended, w_out)
    glob_sum = glob_state + project(glob_attended, w_out)
    result, stored = ffn_forward(attn_sum, ffn_gain, ffn_shift, w_up, up_bias, w_down, down_bias)
    glob_result, glob_stored = ffn_forward(
        glob_sum, ffn_gain, ffn_shift, w_up, up_bias, w_down, down_bias
    )
    grad_attn_sum, tok_ffn = ffn_backward(
        attn_sum, stored, out_cotangent.astype(jnp.float32), ffn_gain, ffn_shift, w_up, w_down
    )
    grad_glob_sum, glob_ffn = ffn_backward(
        glob_sum,
        glob_stored,
        global_cotangent.astype(jnp.float32),
        ffn_gain,
        ffn_shift,
        w_up,
        w_down,
    )
    branch_low = grad_attn_sum.astype(low_type)
    glob_branch_low = grad_glob_sum.astype(low_type)
    grad_out_all = (
        outer_sum(attended, branch_low) + outer_sum(glob_attended, glob_branch_low) / seq_devices
    )
    upstream_mix = project_back(branch_low, w_out).astype(low_type).reshape(block_shape)
    glob_upstream = (
        project_back(glob_branch_low, w_out)
        .astype(low_type)
        .reshape(row_count, glob_count, HEADS, HEAD_DIM)
    )
    remote_exact = jnp.exp(remote_scores - glob_logsum[..., None])
    own_exact = jnp.exp(own_scores - glob_logsum[..., None])
    remote_grad = jnp.einsum(
        "rghd,rshd->rhgs", glob_upstream, value_rows, preferred_element_type=jnp.float32
    )
    own_grad = jnp.einsum(
        "rghd,rjhd->rhgj", glob_upstream, glob_values, preferred_element_type=jnp.float32
    )
    row_inner = lax.psum(jnp.sum(remote_exact * remote_grad, axis=-1), "seq")
    row_inner = row_inner + jnp.sum(own_exact * own_grad, axis=-1)
    remote_score_grad = (remote_exact * (remote_grad - row_inner[..., None])).astype(low_type)
    own_score_grad = (own_exact * (own_grad - row_inner[..., None])).astype(low_type)
    remote_queries = scaling * jnp.einsum(
        "rhgs,rshd->rghd", remote_score_grad, key_rows, preferred_element_type=jnp.float32
    )
    tok_keys_extra = scaling * jnp.einsum(
        "rhgs,rghd->rshd", remote_score_grad, glob_queries, preferred_element_type=jnp.float32
    )
    tok_values_extra = jnp.einsum(
        "rhgs,rghd->rshd",
        remote_exact.astype(low_type),
        glob_upstream,
        preferred_element_type=jnp.float32,
    )
    own_queries = scaling * jnp.einsum(
        "rhgj,rjhd->rghd", own_score_grad, glob_keys, preferred_element_type=jnp.float32
    )
    own_keys = scaling * jnp.einsum(
        "rhgj,rghd->rjhd", own_score_grad, glob_queries, preferred_element_type=jnp.float32
    )
    own_values = jnp.einsum(
        "rhgj,rghd->rjhd",
        own_exact.astype(low_type),
        glob_upstream,
        preferred_element_type=jnp.float32,
    )
    grad_queries, grad_keys, grad_values, grad_keys_far, grad_values_far = local_backward(
        block_queries,
        block_keys,
        block_values,
        block_seg,
        glob_keys,
        glob_values,
        global_seg,
        local_logsum,
        upstream_mix,
    )
    far_grads = lax.psum((remote_queries, grad_keys_far, grad_values_far), "seq")
    head_shape = (row_count, tok_count, HEADS, HEAD_DIM)
    grad_projected = jnp.stack(
        [
            grad_queries.reshape(head_shape),
            grad_keys.reshape(head_shape) + tok_keys_extra,
            grad_values.reshape(head_shape) + tok_values_extra,
        ],
        axis=2,
    )
    grad_projected = grad_projected.reshape(row_count, tok_count, 3 * model_width).astype(low_type)
    glob_grad_projected = jnp.stack(
        [far_grads[0] + own_queries, far_grads[1] + own_keys, far_grads[2] + own_values], axis=2
    )
    glob_grad_projected = glob_grad_projected.reshape(
        row_count, glob_count, 3 * model_width
    ).astype(low_type)
    grad_qkv_all = (
        outer_sum(normed, grad_projected)
        + outer_sum(glob_normed, glob_grad_projected) / seq_devices
    )
    grad_normed = project_back(grad_projected, w_qkv)
    glob_grad_normed = project_back(glob_grad_projected, w_qkv)
    grad_sectioned, attn_gain_grad, attn_shift_grad = norm_back(
        sectioned, attn_gain, attn_shift, grad_normed
    )
    grad_sectioned = grad_sectioned + grad_attn_sum
    glob_grad_state, glob_gain_grad, glob_shift_grad = norm_back(
        glob_state, glob_gain, glob_shift, glob_grad_normed
    )
    global_grad = (glob_grad_state + grad_glob_sum).astype(low_type)
    grad_low = grad_sectioned.astype(low_type)
    returned = from_behind(grad_low[:, tok_count - half_block :], "seq", 1)
    token_grad = jnp.concatenate([returned, grad_low[:, : tok_count - half_block]], axis=1)
    ffn_gain_all = tok_ffn[0] + glob_ffn[0] / seq_devices
    ffn_shift_all = tok_ffn[1] + glob_ffn[1] / seq_devices
    up_all = tok_ffn[2] + glob_ffn[2] / seq_devices
    up_bias_all = tok_ffn[3] + glob_ffn[3] / seq_devices
    down_all = tok_ffn[4] + glob_ffn[4] / seq_devices
    down_bias_all = tok_ffn[5] + glob_ffn[5] / seq_devices
    glob_gain_all = glob_gain_grad / seq_devices
    glob_shift_all = glob_shift_grad / seq_devices
    mat_sums = (
        lax.psum_scatter(
            grad_qkv_all.astype(jnp.bfloat16), "batch", scatter_dimension=1, tiled=True
        ).astype(jnp.float32),
        lax.psum_scatter(
            grad_out_all.astype(jnp.bfloat16), "batch", scatter_dimension=1, tiled=True
        ).astype(jnp.float32),
        lax.psum_scatter(
            up_all.astype(jnp.bfloat16), "batch", scatter_dimension=1, tiled=True
        ).astype(jnp.float32),
        lax.psum_scatter(
            down_all.astype(jnp.bfloat16), "batch", scatter_dimension=1, tiled=True
        ).astype(jnp.float32),
    )
    vec_sums = (
        lax.psum(attn_gain_grad.astype(jnp.bfloat16), "batch").astype(jnp.float32),
        lax.psum(attn_shift_grad.astype(jnp.bfloat16), "batch").astype(jnp.float32),
        lax.psum(glob_gain_all.astype(jnp.bfloat16), "batch").astype(jnp.float32),
        lax.psum(glob_shift_all.astype(jnp.bfloat16), "batch").astype(jnp.float32),
        lax.psum(ffn_gain_all.astype(jnp.bfloat16), "batch").astype(jnp.float32),
        lax.psum(ffn_shift_all.astype(jnp.bfloat16), "batch").astype(jnp.float32),
        lax.psum(up_bias_all.astype(jnp.bfloat16), "batch").astype(jnp.float32),
        lax.psum(down_bias_all.astype(jnp.bfloat16), "batch").astype(jnp.float32),
    )
    shares = (
        lax.psum_scatter(vec_sums[0], "seq", scatter_dimension=0, tiled=True),
        lax.psum_scatter(vec_sums[1], "seq", scatter_dimension=0, tiled=True),
        lax.psum_scatter(vec_sums[2], "seq", scatter_dimension=0, tiled=True),
        lax.psum_scatter(vec_sums[3], "seq", scatter_dimension=0, tiled=True),
        lax.psum_scatter(mat_sums[0], "seq", scatter_dimension=0, tiled=True),
        lax.psum_scatter(mat_sums[1], "seq", scatter_dimension=0, tiled=True),
        lax.psum_scatter(vec_sums[4], "seq", scatter_dimension=0, tiled=True),
        lax.psum_scatter(vec_sums[5], "seq", scatter_dimension=0, tiled=True),
        lax.psum_scatter(mat_sums[2], "seq", scatter_dimension=0, tiled=True),
        lax.psum_scatter(vec_sums[6], "seq", scatter_dimension=0, tiled=True),
        lax.psum_scatter(mat_sums[3], "seq", scatter_dimension=0, tiled=True),
        lax.psum_scatter(vec_sums[7], "seq", scatter_dimension=0, tiled=True),
    )
    matrices = (shares[4], shares[5], shares[8], shares[10])
    vectors = (
        shares[0],
        shares[1],
        shares[2],
        shares[3],
        shares[6],
        shares[7],
        shares[9],
        shares[11],
    )
    return (
        result.astype(low_type),
        glob_result.astype(low_type),
        token_grad,
        global_grad,
        vectors[0],
        vectors[1],
        vectors[2],
        vectors[3],
        matrices[0],
        matrices[1],
        vectors[4],
        vectors[5],
        matrices[2],
        vectors[6],
        matrices[3],
        vectors[7],
    )


MESH = pl.DeviceIdType.MESH
BF = jnp.bfloat16
F32 = jnp.float32


def dot_nn(left, right):
    return lax.dot_general(left, right, (((1,), (0,)), ((), ())), preferred_element_type=F32)


def dot_nt(left, right):
    return lax.dot_general(left, right, (((1,), (1,)), ((), ())), preferred_element_type=F32)


def lanes_of(shape):
    return lax.broadcasted_iota(jnp.int32, shape, len(shape) - 1)


def two_parts(value):
    high = value.astype(BF)
    return high, (value - high.astype(F32)).astype(BF)


def norm_stats(value):
    center = jnp.mean(value, axis=-1, keepdims=True)
    spread = value - center
    variance = jnp.mean(spread * spread, axis=-1, keepdims=True)
    return spread, lax.rsqrt(variance + EPS)


def norm_pull(value, gain, upstream):
    spread, scale = norm_stats(value)
    unit = spread * scale
    scaled = upstream * gain
    first = jnp.mean(scaled, axis=-1, keepdims=True)
    second = jnp.mean(scaled * unit, axis=-1, keepdims=True)
    grad = scale * (scaled - first - unit * second)
    return (
        grad,
        jnp.sum(upstream * unit, axis=0, keepdims=True),
        jnp.sum(upstream, axis=0, keepdims=True),
    )


def gelu_pair(hidden):
    size = jnp.abs(hidden) * 0.7071067811865476
    step = 1.0 / (1.0 + 0.3275911 * size)
    bell = jnp.exp(-(size * size))
    series = 1.061405429 * 0.5
    for term in (-1.453152027, 1.421413741, -0.284496736, 0.254829592):
        series = series * step + term * 0.5
    tail = series * step * bell
    mass = jnp.where(hidden < 0.0, tail, 1.0 - tail)
    return hidden * mass, mass + hidden * (bell * 0.3989422804014327)


def layer_kernel(
    tokens, gstates, tseg, gseg, attn_gain, attn_shift, glob_gain, glob_shift, w_qkv, w_out,
    ffn_gain, ffn_shift, w_up, up_bias, w_down, down_bias, cotan, gcotan,
    o_out, o_gout, o_tgrad, o_ggrad, o_qkv, o_wout, o_up, o_down, o_vec, o_ub,
    sec, nrm, proj, kvt, probs, att_t, att, x2, n2, n2t, ct, ct_t, acc, gn2, gatt, qaug, kaug,
    wq, wo, wu, wd,
    lse_t, rl_t, cx, msg1, rcv1, rcv2, rcv3, vec, vmsg, vrcv, vsum, ub,
    gd, r0d, r1d, r2d, r3d, r4d, gu, r0u, r1u, r2u, r3u, r4u, r0q, r1q, r2q, r3q, r4q, fmsg, frcv,
    loc, wsem, hs, hr, m1s, m1r, m2s, m2r, m3s, m3r, gos, gor, ggs_s, ggs_r, vs, vr,
    d0s, d0r, d1s, d1r, d2s, d2r, d3s, d3r, d4s, d4r,
    u0s, u0r, u1s, u1r, u2s, u2r, u3s, u3r, u4s, u4r,
    q0s, q0r, q1s, q1r, q2s, q2r, q3s, q3r, q4s, q4r,
    qps, qpr, qls, qlr, vbs, vbr, fs, fr, hs2, hr2, osem,
):
    tok, width = tokens.shape
    glob = gstates.shape[0]
    rows = tok + glob
    n_seq = lax.axis_size("seq")
    slots = glob // n_seq
    wide = tok + slots
    half = tok // 2
    pairs = HEADS // 2
    chunk = up_bias.shape[0] // n_seq
    n_chunk = up_bias.shape[0] // width
    side, part = width // 4, width // n_seq
    tail = 128

    s = lax.axis_index("seq")
    b = lax.axis_index("batch")
    x, zl, zh = s % 2, (s // 2) % 2, s // 4
    c, y = b % 2, b // 2
    dev_c, dev_y = (s, b + 1 - 2 * c), (s, b + 2 - 4 * y)
    dev_cy, dev_xy = (s, dev_y[1] + 1 - 2 * c), (s + 1 - 2 * x, dev_y[1])
    dev_x, dev_1, dev_2 = (s + 1 - 2 * x, b), (s + 2 - 4 * zl, b), (s + 4 - 8 * zh, b)

    def flip(k):
        other = s
        if k & 1:
            other = other + 1 - 2 * x
        if k & 2:
            other = other + 2 - 4 * zl
        if k & 4:
            other = other + 4 - 8 * zh
        return other

    def remote(src, dst, ss, rs, dev):
        return pltpu.make_async_remote_copy(
            src_ref=src, dst_ref=dst, send_sem=ss, recv_sem=rs, device_id=dev, device_id_type=MESH
        )

    peers = tuple(range(1, n_seq))

    def as_row(vector):
        return vector[...].reshape(1, vector.shape[0])

    attn_gain, attn_shift, glob_gain, glob_shift, ffn_gain, ffn_shift, down_bias = (
        as_row(v) for v in (attn_gain, attn_shift, glob_gain, glob_shift, ffn_gain, ffn_shift, down_bias)
    )

    my_slots = pl.multiple_of(s * slots, slots)
    loads = [
        (tokens.at[pl.ds(half, half)], sec.at[pl.ds(0, half)]),
        (gstates, sec.at[pl.ds(tok, glob)]),
        (w_qkv, wq),
        (cotan, ct.at[pl.ds(0, tok)]),
        (gcotan.at[pl.ds(my_slots, slots)], ct.at[pl.ds(tok, slots)]),
        (w_out, wo),
    ]
    loads = [pltpu.make_async_copy(a, d, loc.at[i]) for i, (a, d) in enumerate(loads)]
    for load in loads:
        load.start()

    def piece_of(i, o):
        return 4 * (i // 2) + 2 * o + i % 2

    def stream(i):
        copies = []
        for o in range(2):
            at = piece_of(i, o) * chunk
            at = at if isinstance(at, int) else pl.multiple_of(at, chunk)
            here = pl.ds(o * chunk, chunk)
            copies.append(pltpu.make_async_copy(w_up.at[:, pl.ds(at, chunk)], wu.at[:, here], wsem.at[0, o]))
            copies.append(pltpu.make_async_copy(w_down.at[pl.ds(at, chunk)], wd.at[here], wsem.at[1, o]))
        return copies

    for copy in stream(0):
        copy.start()

    bar = pltpu.get_barrier_semaphore()
    for k in peers:
        pl.semaphore_signal(bar, inc=1, device_id=(flip(k), b), device_id_type=MESH)
    pl.semaphore_signal(bar, inc=1, device_id=dev_c, device_id_type=MESH)
    for dev in (dev_y, dev_cy, dev_xy):
        pl.semaphore_signal(bar, inc=1, device_id=dev, device_id_type=MESH)
    pl.semaphore_wait(bar, len(peers) + 4)
    halo = remote(
        tokens.at[pl.ds(0, half)], sec.at[pl.ds(half, half)], hs.at[0], hr.at[0],
        (lax.rem(s + n_seq - 1, n_seq), b),
    )
    halo.start()

    seg_row = jnp.concatenate([tseg[...], gseg[...]], axis=1)
    which = lax.broadcasted_iota(jnp.int32, (128, rows), 0)
    col = lanes_of((128, rows))
    is_glob = col >= tok
    same = which == seg_row
    q_t = jnp.where(which < 3, jnp.where(same, 1.0, 0.0), jnp.where((which == 3) & is_glob, 1.0, 0.0))
    far = jnp.where(s == 0, 0.0, NEGATIVE)
    k_t = jnp.where(which < 3, jnp.where(same, 0.0, NEGATIVE), jnp.where((which == 3) & is_glob, far, 0.0))
    qaug[...] = jnp.transpose(q_t).astype(BF)
    kaug[...] = jnp.transpose(k_t).astype(BF)

    def norm_to(first, count, gain, shift):
        for r in range(first, first + count, 128):
            spread, scale = norm_stats(sec[pl.ds(r, 128), :].astype(F32))
            nrm[pl.ds(r, 128), :] = (spread * scale * gain + shift).astype(BF)

    def project_rows(first, count):
        def step(i, carry):
            at = pl.multiple_of(i * width, width)
            proj[pl.ds(first, count), pl.ds(at, width)] = dot_nn(
                nrm[pl.ds(first, count), :], wq[:, pl.ds(at, width)]
            ).astype(BF)
            return carry

        lax.fori_loop(0, 3, step, 0)

    loads[1].wait()
    norm_to(tok, glob, glob_gain, glob_shift)
    loads[0].wait()
    norm_to(0, half, attn_gain, attn_shift)
    loads[2].wait()
    project_rows(tok, glob)
    project_rows(0, half)
    loads[3].wait()
    loads[4].wait()
    ct_t[:, pl.ds(0, wide)] = jnp.transpose(ct[...])
    halo.wait()
    norm_to(half, half, attn_gain, attn_shift)
    project_rows(half, half)

    kvt[:, pl.ds(0, rows)] = jnp.transpose(proj[:, pl.ds(2 * width, width)])
    lane_p = lanes_of((1, 128))
    even = jnp.where(lane_p < HEAD_DIM, HEAD_DIM ** (-0.5), 0.0).astype(BF)
    odd = jnp.where(lane_p < HEAD_DIM, 0.0, HEAD_DIM ** (-0.5)).astype(BF)
    even_one = jnp.where(lane_p < HEAD_DIM, 1.0, 0.0).astype(BF)
    odd_one = jnp.where(lane_p < HEAD_DIM, 0.0, 1.0).astype(BF)
    first_head = lax.broadcasted_iota(jnp.int32, (128, 128), 0) < HEAD_DIM
    lse_t[...] = jnp.zeros_like(lse_t)
    rl_t[...] = jnp.zeros_like(rl_t)

    def glob_forward(p, carry):
        at = pl.multiple_of(p * 128, 128)
        keys = jnp.concatenate([proj[:, pl.ds(width + at, 128)], kaug[...]], axis=1)
        qg = proj[pl.ds(tok, glob), pl.ds(at, 128)]
        qa = qaug[pl.ds(tok, glob), :]
        queries = jnp.concatenate(
            [jnp.concatenate([qg * even, qa], axis=1), jnp.concatenate([qg * odd, qa], axis=1)], axis=0
        )
        scores = dot_nt(keys, queries)
        top = jnp.max(scores, axis=0, keepdims=True)
        raised = jnp.exp(scores - top)
        total = jnp.sum(raised, axis=0, keepdims=True)
        weights = (raised * (1.0 / total)).astype(BF)
        probs[p, :, pl.ds(2 * tok, 2 * glob)] = weights
        mixed = dot_nn(kvt[pl.ds(at, 128), pl.ds(0, rows)], weights)
        cx[:, pl.ds(at, 128)] = jnp.transpose(jnp.where(first_head, mixed[:, :glob], mixed[:, glob:]))
        logsum = top + jnp.log(total)
        lse_t[pl.ds(2 * p, 1), :] = logsum[:, :glob]
        lse_t[pl.ds(2 * p + 1, 1), :] = logsum[:, glob:]
        return carry

    lax.fori_loop(0, pairs, glob_forward, 0)

    lse = jnp.transpose(lse_t[...])
    in_heads = lanes_of((glob, 128)) < HEADS
    lse = jnp.where(in_heads, lse, 0.0)
    part_a, rest = two_parts(lse)
    rest = lse - part_a.astype(F32)
    part_b = rest.astype(BF)
    part_c = rest - part_b.astype(F32)
    packed = part_a.astype(F32) + pltpu.roll(part_b.astype(F32), 16, 1) + pltpu.roll(part_c, 32, 1)
    msg1[:, pl.ds(0, width)] = cx[...].astype(BF)
    msg1[:, pl.ds(width, 128)] = packed.astype(BF)
    sends1 = []
    for k in peers:
        other = flip(k)
        at = pl.multiple_of(other * slots, slots)
        copy = remote(msg1.at[pl.ds(at, slots)], rcv1.at[k], m1s.at[k], m1r.at[k], (other, b))
        copy.start()
        sends1.append(copy)
    rcv1[0] = msg1[pl.ds(my_slots, slots), :]

    def local_forward_pair(p, carry):
        at = pl.multiple_of(p * 128, 128)
        keys = jnp.concatenate([proj[:, pl.ds(width + at, 128)], kaug[...]], axis=1)
        qp = proj[pl.ds(0, tok), pl.ds(at, 128)]
        for e, mask in ((0, even), (1, odd)):
            queries = jnp.concatenate([qp * mask, qaug[pl.ds(0, tok), :]], axis=1)
            scores = dot_nt(keys, queries)
            top = jnp.max(scores, axis=0, keepdims=True)
            raised = jnp.exp(scores - top)
            inverse = 1.0 / jnp.sum(raised, axis=0, keepdims=True)
            weights = raised.astype(BF)
            probs[p, :, pl.ds(e * tok, tok)] = weights
            rl_t[pl.ds(2 * p + e, 1), :] = inverse
            here = pl.multiple_of(at + e * HEAD_DIM, HEAD_DIM)
            mixed = dot_nn(kvt[pl.ds(here, HEAD_DIM), pl.ds(0, rows)], weights)
            att_t[pl.ds(here, HEAD_DIM), pl.ds(0, tok)] = (mixed * inverse).astype(BF)
        return carry

    lax.fori_loop(0, pairs, local_forward_pair, 0)
    att[pl.ds(0, tok), :] = jnp.transpose(att_t[:, pl.ds(0, tok)])

    head_of = lanes_of((128, width)) // HEAD_DIM
    spread_heads = jnp.where(head_of == lax.broadcasted_iota(jnp.int32, (128, width), 0), 1.0, 0.0).astype(BF)
    for copy in sends1:
        copy.wait()
    logs = []
    for k in range(n_seq):
        packed = rcv1[k, :, pl.ds(width, 128)].astype(F32)
        logs.append(packed + pltpu.roll(packed, 112, 1) + pltpu.roll(packed, 96, 1))
    high = functools.reduce(jnp.maximum, logs)
    raised = [jnp.exp(one - high) for one in logs]
    total = functools.reduce(jnp.add, raised)
    in_heads = lanes_of((slots, 128)) < HEADS
    shares = jnp.concatenate([jnp.where(in_heads, one / total, 0.0) for one in raised], axis=0)
    share_a, share_b = two_parts(shares)
    shares = dot_nn(share_a, spread_heads) + dot_nn(share_b, spread_heads)
    cx[...] = shares
    mixed = jnp.zeros((slots, width), F32)
    for k in range(n_seq):
        mixed = mixed + shares[k * slots : (k + 1) * slots] * rcv1[k, :, pl.ds(0, width)].astype(F32)
    att[pl.ds(tok, slots), :] = mixed.astype(BF)
    att_t[:, pl.ds(tok, tail)] = jnp.transpose(
        jnp.concatenate([mixed, jnp.zeros((tail - slots, width), F32)], axis=0)
    ).astype(BF)

    loads[5].wait()
    x2[...] = dot_nn(att[...], wo[...])
    x2[pl.ds(0, tok), :] += sec[pl.ds(0, tok), :].astype(F32)
    x2[pl.ds(tok, slots), :] += sec[pl.ds(pl.multiple_of(tok + my_slots, slots), slots), :].astype(F32)

    def second_norm(first, count):
        spread, scale = norm_stats(x2[pl.ds(first, count), :])
        n2[pl.ds(first, count), :] = (spread * scale * ffn_gain + ffn_shift).astype(BF)

    for r in range(0, tok, 128):
        second_norm(r, 128)
    second_norm(tok, slots)
    n2t[:, pl.ds(0, wide)] = jnp.transpose(n2[...])

    def d_core(i):
        return remote(gd.at[i, :, :, 1 - c], r0d.at[i], d0s.at[i], d0r.at[i], dev_c)

    def d_y(i):
        return remote(r0d.at[i, :, 1 - y], r1d.at[i // 2, i % 2], d1s.at[i], d1r.at[i], dev_y)

    def d_x(h):
        return remote(r1d.at[h, 1 - x], r2d.at[h], d2s.at[h], d2r.at[h], dev_x)

    def d_1(h):
        return remote(r2d.at[h, 1 - zl], r3d.at[h], d3s.at[h], d3r.at[h], dev_1)

    def d_2():
        return remote(r3d.at[1 - zh], r4d, d4s.at[0], d4r.at[0], dev_2)

    def do_d_y(i):
        d_core(i).wait_recv()
        r0d[i] = r0d[i] + gd[i, :, :, c]
        d_y(i).start()

    def do_d_x(h):
        for j in range(2):
            d_y(2 * h + j).wait_recv()
            r1d[h, j] = r1d[h, j] + r0d[2 * h + j, :, y]
        d_x(h).start()

    def do_d_1(h):
        d_x(h).wait_recv()
        r2d[h] = r2d[h] + r1d[h, x]
        d_1(h).start()

    def do_d_2():
        for h in range(2):
            d_1(h).wait_recv()
            r3d[h] = r3d[h] + r2d[h, zl]
        d_2().start()

    def u_core(i):
        return remote(gu.at[i, 1 - c], r0u.at[i], u0s.at[i], u0r.at[i], dev_c)

    def u_1(i):
        return remote(r0u.at[i, :, 1 - zl], r1u.at[i], u1s.at[i], u1r.at[i], dev_1)

    def u_x(i):
        return remote(r1u.at[i, :, 1 - x], r2u.at[i // 2, i % 2], u2s.at[i], u2r.at[i], dev_x)

    def u_y():
        return remote(r2u.at[1 - y], r3u, u3s.at[0], u3r.at[0], dev_y)

    def u_2():
        return remote(r3u.at[:, 1 - zh], r4u, u4s.at[0], u4r.at[0], dev_2)

    def do_u_1(i):
        u_core(i).wait_recv()
        r0u[i] = r0u[i] + gu[i, c]
        u_1(i).start()

    def do_u_x(i):
        u_1(i).wait_recv()
        r1u[i] = r1u[i] + r0u[i, :, zl]
        u_x(i).start()

    def do_u_y():
        for i in range(4):
            u_x(i).wait_recv()
            r2u[i // 2, i % 2] = r2u[i // 2, i % 2] + r1u[i, :, x]
        u_y().start()

    def do_u_2():
        u_y().wait_recv()
        r3u[...] = r3u[...] + r2u[y]
        u_2().start()

    vec[...] = jnp.zeros_like(vec)
    for i in range(n_chunk):
        for o in range(2):
            ub[pl.ds(i, 1), pl.ds(o * chunk, chunk)] = up_bias[pl.ds(piece_of(i, o) * chunk, chunk)].reshape(1, chunk)
    acc[...] = jnp.zeros_like(acc)
    gn2[...] = jnp.zeros_like(gn2)

    act = gatt
    gh = kvt
    cuts = ((0, 256, ((0, 0, 0, 256),)), (256, 256, ((0, 256, 0, 128), (1, 0, 128, 128))), (512, 256, ((1, 128, 0, 256),)))

    def ffn_step(i, carry):
        for copy in stream(i):
            copy.wait()
        for first, count, _ in cuts:
            here = pl.ds(first, count)
            hidden = dot_nn(n2[...], wu[:, here]) + ub[pl.ds(i, 1), here]
            active, slope = gelu_pair(hidden)
            act[:, here] = active.astype(BF)
            grad_hidden = (slope * dot_nt(ct[...], wd[here, :])).astype(BF)
            gh[pl.ds(0, wide), here] = grad_hidden
            ub[pl.ds(i, 1), here] = jnp.sum(grad_hidden.astype(F32), axis=0, keepdims=True)

        @pl.when(i >= 1)
        def _():
            do_d_y(i - 1)
            do_u_1(i - 1)

        @pl.when(i >= 2)
        def _():
            do_u_x(i - 2)

        @pl.when(i == 3)
        def _():
            do_d_x(0)

        for first, count, _ in cuts:
            here = pl.ds(first, count)
            acc[:, here] += dot_nn(act[...], wd[:, here])
            gn2[:, here] += dot_nt(gh[pl.ds(0, wide), :], wu[here, :])

        @pl.when(i + 1 < n_chunk)
        def _():
            for copy in stream(i + 1):
                copy.start()

        for first, count, parts in cuts:
            block = dot_nn(ct_t[:, pl.ds(0, wide)], act[:, pl.ds(first, count)]).astype(BF)
            for o, at, start, size in parts:
                gd[i, o, :, :, :, pl.ds(at, size)] = block[:, start : start + size].reshape(2, 2, side, size)
        d_core(i).start()
        for first, count, parts in cuts:
            block = dot_nn(n2t[:, pl.ds(0, wide)], gh[pl.ds(0, wide), pl.ds(first, count)]).astype(BF)
            for o, at, start, size in parts:
                gu[i, o, :, :, :, :, :, pl.ds(at, size)] = block[:, start : start + size].reshape(
                    2, 2, 2, 2, part // 2, size
                )
        u_core(i).start()

        return carry

    lax.fori_loop(0, n_chunk, ffn_step, 0)

    for i in range(n_chunk):
        for o in range(2):
            block = piece_of(i, o)
            vec[pl.ds(8 + block // 2, 1), pl.ds(block % 2 * chunk, chunk)] = ub[pl.ds(i, 1), pl.ds(o * chunk, chunk)]


    def second_pull(first, count):
        grad, gain_term, shift_term = norm_pull(
            x2[pl.ds(first, count), :], ffn_gain, gn2[pl.ds(first, count), :]
        )
        upstream = ct[pl.ds(first, count), :].astype(F32)
        total = upstream + grad
        acc[pl.ds(first, count), :] += x2[pl.ds(first, count), :] + down_bias
        x2[pl.ds(first, count), :] = total
        n2[pl.ds(first, count), :] = total.astype(BF)
        vec[pl.ds(4, 1), :] += gain_term
        vec[pl.ds(5, 1), :] += shift_term
        vec[pl.ds(6, 1), :] += jnp.sum(upstream, axis=0, keepdims=True)

    for r in range(0, tok, 128):
        second_pull(r, 128)
    second_pull(tok, slots)
    gatt[...] = dot_nt(n2[...], wo[...]).astype(BF)

    slot_grad = gatt[pl.ds(tok, slots), :].astype(F32)
    slot_att = att[pl.ds(tok, slots), :].astype(F32)
    head_sel = lanes_of((1, 128)) < HEADS

    def inner_aug(upstream, values):
        high, low = two_parts(upstream.astype(F32) * values)
        inner = dot_nt(high, spread_heads) + dot_nt(low, spread_heads)
        high, low = two_parts(jnp.where(head_sel, inner, 0.0))
        return (high.astype(F32) + pltpu.roll(low.astype(F32), 16, 1)).astype(BF)

    scaled = jnp.concatenate(
        [(cx[pl.ds(k * slots, slots), :] * slot_grad).astype(BF) for k in range(n_seq)], axis=0
    )
    msg1[:, pl.ds(0, width)] = scaled
    msg1[:, pl.ds(width, 128)] = inner_aug(scaled, jnp.concatenate([slot_att] * n_seq, axis=0))
    sends2 = []
    for k in peers:
        copy = remote(
            msg1.at[pl.ds(k * slots, slots)], rcv2.at[pl.ds(my_slots, slots)], m2s.at[k], m2r.at[k],
            (flip(k), b),
        )
        copy.start()
        sends2.append(copy)
    rcv2[pl.ds(my_slots, slots), :] = msg1[pl.ds(0, slots), :]
    do_d_y(3)
    do_u_1(3)
    do_u_x(2)

    n2t[:, pl.ds(0, tok)] = jnp.transpose(nrm[pl.ds(0, tok), :])
    n2t[:, pl.ds(tok, glob)] = jnp.transpose(nrm[pl.ds(tok, glob), :])

    outs = nrm
    outs[pl.ds(0, wide), :] = acc[...].astype(BF)
    out_copy = pltpu.make_async_copy(outs.at[pl.ds(0, tok)], o_out, osem.at[0])
    out_copy.start()
    own_out = pltpu.make_async_copy(
        outs.at[pl.ds(tok, slots)], o_gout.at[pl.ds(my_slots, slots)], osem.at[1]
    )
    own_out.start()

    scale_c = jnp.transpose(
        jnp.concatenate([rl_t[...], jnp.zeros((128 - rl_t.shape[0], tok), F32)], axis=0)
    )
    scale_a, scale_b = two_parts(scale_c)
    for r in range(0, tok, 128):
        wider = dot_nn(scale_a[r : r + 128], spread_heads) + dot_nn(scale_b[r : r + 128], spread_heads)
        scaled = (gatt[pl.ds(r, 128), :].astype(F32) * wider).astype(BF)
        gatt[pl.ds(r, 128), :] = scaled
        qaug[pl.ds(r, 128), :] = inner_aug(scaled, att[pl.ds(r, 128), :].astype(F32))
    kvt[:, pl.ds(0, rows)] = jnp.transpose(proj[:, pl.ds(width, width)])

    def chunk_at(p):
        return gu.at[p // 2, lax.rem(p, 2)]

    def put_chunk(p, value):
        gu[p // 2, lax.rem(p, 2)] = value.astype(BF).reshape(gu.shape[2:])
        q_core(p).start()

    def q_core(p):
        return remote(chunk_at(p).at[:, 1 - c], r0q.at[p], q0s.at[p], q0r.at[p], dev_c)

    def x_first(p):
        return p % 2 == 1

    def q_a(p):
        src, dev = (r0q.at[p, :, 1 - x], dev_x) if x_first(p) else (r0q.at[p, :, :, 1 - y], dev_y)
        return remote(src, r1q.at[p], q1s.at[p], q1r.at[p], dev)

    def q_b(p):
        src, dev = (r1q.at[p, :, 1 - y], dev_y) if x_first(p) else (r1q.at[p, :, 1 - x], dev_x)
        return remote(src, r2q.at[p], q2s.at[p], q2r.at[p], dev)

    def q_1(p):
        return remote(r2q.at[p], r3q.at[p], q3s.at[p], q3r.at[p], dev_1)

    def q_2(p):
        return remote(r2q.at[p, 1 - zh], r4q.at[p], q4s.at[p], q4r.at[p], dev_2)

    def take_chunk(p):
        q_core(p).wait_recv()
        r0q[p] = r0q[p] + gu[p // 2, p % 2, :, c]

    def do_q_a(*which):
        for p in which:
            take_chunk(p)
            q_a(p).start()

    def do_q_b(*which):
        for p in which:
            q_a(p).wait_recv()
            r1q[p] = r1q[p] + (r0q[p, :, x] if x_first(p) else r0q[p, :, :, y])
            q_b(p).start()

    def do_q_1(*which):
        for p in which:
            q_b(p).wait_recv()
            r2q[p] = r2q[p] + r1q[p, :, y if x_first(p) else x]

            @pl.when(zl != c)
            def _(p=p):
                q_1(p).start()

    def do_q_2(*which):
        @pl.when(zl == c)
        def _():
            for p in which:
                q_1(p).wait_recv()
                r2q[p] = r2q[p] + r3q[p]
                q_2(p).start()

    def q_plane(n):
        src = (r0q.at[5, :, 1 - x, y], r0q.at[5, :, x, 1 - y], r0q.at[5, :, 1 - x, 1 - y])[n]
        dst = (r1q.at[5, :, 0], r1q.at[5, :, 1], r2q.at[5])[n]
        return remote(src, dst, qps.at[n], qpr.at[n], (dev_x, dev_y, dev_xy)[n])

    def q_line(n):
        src = (r0q.at[5, 1 - zh, x, y], r0q.at[5, zh, x, y], r0q.at[5, 1 - zh, x, y])[n]
        dst = (r3q.at[5, 0], r3q.at[5, 1], r4q.at[5])[n]
        return remote(src, dst, qls.at[n], qlr.at[n], (dev_2, dev_1, (flip(6), b))[n])

    def do_q_plane():
        take_chunk(5)
        for n in range(3):
            q_plane(n).start()

    def do_q_line():
        for n in range(3):
            q_plane(n).wait_recv()
        total = r0q[5, :, x, y].astype(F32) + r1q[5, :, 0].astype(F32) + r1q[5, :, 1].astype(F32) + r2q[5].astype(F32)
        r0q[5, :, x, y] = total.astype(BF)

        @pl.when(zl == c)
        def _():
            q_line(0).start()

        @pl.when(zl != c)
        def _():
            q_line(1).start()
            q_line(2).start()

    def q_chunk(p):
        right = jnp.concatenate(
            [proj[:, pl.ds(pl.multiple_of(w * width + p * 128, 128), 128)] for w in range(3)], axis=1
        )
        put_chunk(p, dot_nn(n2t[...], right))

    for i in range(4):
        u_core(i).wait_send()
    for h in range(2):
        put_chunk(pairs + h, dot_nn(att_t[:, pl.ds(0, wide)], n2[:, pl.ds(h * 384, 384)]))
    for copy in sends2:
        copy.wait()
    sends_o = []
    for k in peers:
        copy = remote(
            outs.at[pl.ds(tok, slots)], o_gout.at[pl.ds(my_slots, slots)], gos.at[k], gor.at[k], (flip(k), b)
        )
        copy.start()
        sends_o.append(copy)

    minus = jnp.where(lanes_of((rows, 128)) < 32, -1.0, 0.0).astype(BF)

    def chosen(head):
        lane = lanes_of((1, 128))
        return jnp.where((lane == head) | (lane == head + 16), 1.0, 0.0).astype(BF)

    def attention_back(p, carry):
        at = pl.multiple_of(p * 128, 128)
        qp = proj[pl.ds(0, tok), pl.ds(at, 128)]
        qg = proj[pl.ds(tok, glob), pl.ds(at, 128)]
        gp = gatt[pl.ds(0, tok), pl.ds(at, 128)]
        gg = rcv2[:, pl.ds(at, 128)]
        dg = rcv2[:, pl.ds(width, 128)]
        values = jnp.concatenate([proj[:, pl.ds(2 * width + at, 128)], minus], axis=1)
        ups = jnp.concatenate([gp * even_one, gp * odd_one, gg * even_one, gg * odd_one], axis=0)
        dd = qaug[pl.ds(0, tok), :]
        sel_e, sel_o = chosen(2 * p), chosen(2 * p + 1)
        inner = jnp.concatenate([dd * sel_e, dd * sel_o, dg * sel_e, dg * sel_o], axis=0)
        qs = jnp.concatenate([qp * even, qp * odd, qg * even, qg * odd], axis=0)
        grad_v = dot_nn(probs[p], ups)
        for first, count in ((0, tok), (tok, tok), (2 * tok, 2 * glob)):
            right = jnp.concatenate([ups[first : first + count], inner[first : first + count]], axis=1)
            grad_w = dot_nt(values, right)
            here = probs[p, :, pl.ds(first, count)].astype(F32)
            probs[p, :, pl.ds(first, count)] = (here * grad_w).astype(BF)
        grad_k = dot_nn(probs[p], qs)
        factor = HEAD_DIM ** (-0.5)
        low = dot_nn(kvt[pl.ds(at, HEAD_DIM), pl.ds(0, rows)], probs[p, :, pl.ds(0, tok)])
        upper = dot_nn(
            kvt[pl.ds(pl.multiple_of(at + HEAD_DIM, HEAD_DIM), HEAD_DIM), pl.ds(0, rows)], probs[p, :, pl.ds(tok, tok)]
        )
        grad_q = jnp.concatenate([low, upper], axis=0) * factor
        own = dot_nn(kvt[pl.ds(at, 128), pl.ds(0, rows)], probs[p, :, pl.ds(2 * tok, 2 * glob)])
        own = jnp.where(first_head, own[:, :glob], own[:, glob:]) * factor
        proj[pl.ds(tok, glob), pl.ds(at, 128)] = jnp.transpose(own).astype(BF)
        proj[pl.ds(0, tok), pl.ds(at, 128)] = jnp.transpose(grad_q).astype(BF)
        proj[:, pl.ds(width + at, 128)] = grad_k.astype(BF)
        proj[:, pl.ds(2 * width + at, 128)] = grad_v.astype(BF)

        q_chunk(p)
        for at_step, act in (
            (0, lambda: (do_d_x(1), do_u_x(3), do_q_a(6, 7))),
            (1, lambda: (do_d_1(0), do_d_1(1), do_u_y(), do_q_a(0))),
            (2, lambda: (do_d_2(), do_q_a(1))),
            (3, lambda: (do_u_2(), do_q_a(2), do_q_b(6, 7))),
            (4, lambda: (do_q_a(3), do_q_b(0))),
            (5, lambda: (do_q_a(4), do_q_b(1), do_q_1(6, 7))),
        ):

            @pl.when(p == at_step)
            def _(act=act):
                act()

        return carry

    lax.fori_loop(0, pairs, attention_back, 0)

    def first_pull(first):
        grad, gain_term, shift_term = norm_pull(
            sec[pl.ds(first, 128), :].astype(F32), attn_gain, gn2[pl.ds(first, 128), :]
        )
        n2[pl.ds(first, 128), :] = (grad + x2[pl.ds(first, 128), :]).astype(BF)
        vec[pl.ds(0, 1), :] += gain_term
        vec[pl.ds(1, 1), :] += shift_term

    gnm = wu
    gnm[pl.ds(0, glob), :] = dot_nt(proj[pl.ds(tok, glob), :], wq[...]).astype(BF)
    sends3 = []
    for k in peers:
        other = flip(k)
        at = pl.multiple_of(other * slots, slots)
        copy = remote(gnm.at[pl.ds(at, slots)], rcv3.at[k - 1], m3s.at[k], m3r.at[k], (other, b))
        copy.start()
        sends3.append(copy)
    do_q_plane()
    gn2[pl.ds(half, half), :] = dot_nt(proj[pl.ds(half, half), :], wq[...])
    for r in range(half, tok, 128):
        first_pull(r)
    do_q_b(2, 3)
    do_q_1(0, 1)
    do_q_2(6, 7)

    gn2[pl.ds(0, half), :] = dot_nt(proj[pl.ds(0, half), :], wq[...])
    for r in range(0, half, 128):
        first_pull(r)
    keep = pltpu.make_async_copy(n2.at[pl.ds(0, half)], o_tgrad.at[pl.ds(half, half)], osem.at[2])
    keep.start()
    do_q_b(4)
    do_q_line()

    grad_slots = gnm[pl.ds(my_slots, slots), :].astype(F32)
    for copy in sends3:
        copy.wait()
    for k in peers:
        grad_slots = grad_slots + rcv3[k - 1].astype(F32)
    grad, gain_term, shift_term = norm_pull(
        sec[pl.ds(pl.multiple_of(tok + my_slots, slots), slots), :].astype(F32),
        glob_gain,
        grad_slots,
    )
    vec[pl.ds(2, 1), :] += gain_term
    vec[pl.ds(3, 1), :] += shift_term
    n2[pl.ds(tok, slots), :] = (grad + x2[pl.ds(tok, slots), :]).astype(BF)
    own_grad = pltpu.make_async_copy(
        n2.at[pl.ds(tok, slots)], o_ggrad.at[pl.ds(my_slots, slots)], osem.at[3]
    )
    own_grad.start()

    share = vec.shape[1] // n_seq
    for j in range(n_seq):
        rolled = vec[pl.ds(0, 8), :]
        if j:
            rolled = pltpu.roll(rolled, vec.shape[1] - share * j, 1)
        vmsg[j, pl.ds(0, 8), :] = rolled[:, :128]
        for m in range(chunk // 128):
            vmsg[j, pl.ds(8 + m, 1), :] = vec[pl.ds(8 + j // 2, 1), pl.ds((j % 2) * chunk + m * 128, 128)]
    sends_v = []
    for k in peers:
        copy = remote(vmsg.at[flip(k)], vrcv.at[k - 1], vs.at[k], vr.at[k], (flip(k), b))
        copy.start()
        sends_v.append(copy)

    sends_g = []
    for k in peers:
        copy = remote(
            n2.at[pl.ds(tok, slots)], o_ggrad.at[pl.ds(my_slots, slots)], ggs_s.at[k], ggs_r.at[k],
            (flip(k), b),
        )
        copy.start()
        sends_g.append(copy)
    do_q_1(2, 3)
    do_q_2(0, 1)
    back = remote(
        n2.at[pl.ds(half, half)], o_tgrad.at[pl.ds(0, half)], hs2.at[0], hr2.at[0],
        (lax.rem(s + 1, n_seq), b),
    )
    back.start()

    d_2().wait_recv()
    o_down[...] = r4d[...].astype(F32) + r3d[zh].astype(F32)
    u_2().wait_recv()
    last = r4u[...].astype(F32) + r3u[:, zh].astype(F32)
    o_up[:, pl.ds(0, 384)] = last[0].reshape(96, 384)
    o_up[:, pl.ds(384, 384)] = last[1].reshape(96, 384)

    do_q_1(4)
    do_q_2(2, 3)

    for copy in sends_v:
        copy.wait()
    vsum[0] = vmsg[s]
    for k in peers:
        vsum[0] = vsum[0] + vrcv[k - 1]
    batch_peers = (dev_c, dev_y, dev_cy)
    sends_b = []
    for n, dev in enumerate(batch_peers):
        copy = remote(vsum.at[0], vsum.at[1 + n], vbs.at[n], vbr.at[n], dev)
        copy.start()
        sends_b.append(copy)

    do_q_2(4)

    def final(n, slot):
        return remote(fmsg.at[n], frcv.at[slot], fs.at[n], fr.at[n], (s, flip_b(n)))

    def flip_b(n):
        return (b, dev_c[1], dev_y[1], dev_cy[1])[n]

    @pl.when(zl == c)
    def _():
        for p in (6, 7, 0, 1, 2, 3, 4):
            q_2(p).wait_recv()
            r4q[p] = r4q[p] + r2q[p, zh]
        for n in range(3):
            q_line(n).wait_recv()
        r4q[5] = (
            r0q[5, zh, x, y].astype(F32) + r3q[5, 0].astype(F32) + r3q[5, 1].astype(F32) + r4q[5].astype(F32)
        ).astype(BF)

        def columns_of(bb):
            first = (bb * 576 - 64 * lax.rem(bb, 2)) // 128
            tiles = []
            for m in range(5):
                tile = first + m
                tiles.append(r4q[lax.rem(tile, 6), :, pl.ds(pl.multiple_of(tile // 6 * 128, 128), 128)])
            first = (bb * 192 - 64 * lax.rem(bb, 2)) // 128
            for m in range(2):
                tile = first + m
                tiles.append(r4q[pairs + tile // 3, :, pl.ds(pl.multiple_of(lax.rem(tile, 3) * 128, 128), 128)])
            return jnp.concatenate(tiles, axis=1)

        for n in (3, 2, 1):
            fmsg[n] = columns_of(flip_b(n))
            final(n, y).start()
        frcv[y] = columns_of(b)

    for copy in sends_b:
        copy.wait()
    shared = vsum[0] + vsum[1] + (vsum[2] + vsum[3])
    o_vec[...] = shared[0:8, :share]
    for m in range(chunk // 128):
        o_ub[:, pl.ds(m * 128, 128)] = shared[8 + m : 9 + m, :]

    @pl.when(zl == c)
    def _():
        final(2, 1 - y).wait_recv()

    @pl.when(zl != c)
    def _():
        final(1, y).wait_recv()
        final(3, 1 - y).wait_recv()

    for yy in range(2):
        block = frcv[yy].astype(F32)
        main = block[:, :640]
        o_qkv[pl.ds(yy * 48, 48), :] = jnp.where(c == 1, pltpu.roll(main, 576, 1), main)[:, :576]
        main = block[:, 640:]
        o_wout[pl.ds(yy * 48, 48), :] = jnp.where(c == 1, pltpu.roll(main, 192, 1), main)[:, :192]

    for i in range(4):
        d_core(i).wait_send()
        d_y(i).wait_send()
        u_1(i).wait_send()
        u_x(i).wait_send()
    for h in range(2):
        d_x(h).wait_send()
        d_1(h).wait_send()
    d_2().wait_send()
    u_y().wait_send()
    u_2().wait_send()
    for p in range(8):
        q_core(p).wait_send()
        if p != 5:
            q_a(p).wait_send()
            q_b(p).wait_send()
    for n in range(3):
        q_plane(n).wait_send()

    @pl.when(zl == c)
    def _():
        q_line(0).wait_send()
        for n in (1, 2, 3):
            final(n, y).wait_send()
        for p in (6, 7, 0, 1, 2, 3, 4):
            q_2(p).wait_send()

    @pl.when(zl != c)
    def _():
        for n in (1, 2):
            q_line(n).wait_send()
        for p in (6, 7, 0, 1, 2, 3, 4):
            q_1(p).wait_send()

    back.wait()
    keep.wait()
    own_grad.wait()
    out_copy.wait()
    own_out.wait()
    for copy in sends_o + sends_g:
        copy.wait()


def fits(tokens, global_states, w_qkv, w_up):
    return (
        lax.axis_size("seq") == 8
        and lax.axis_size("batch") == 4
        and tokens.shape == (1, BLOCK, HEADS * HEAD_DIM)
        and global_states.shape == (1, 128, HEADS * HEAD_DIM)
        and w_qkv.shape == (HEADS * HEAD_DIM, 3 * HEADS * HEAD_DIM)
        and w_up.shape == (HEADS * HEAD_DIM, 3072)
    )


def finish_kernel(*refs):
    ins, outs = refs[:10], refs[10:]
    for i in range(8):
        outs[i][...] = ins[i][...]
    for i in range(7):
        outs[8 + i][...] = ins[8][i, :]
    outs[15][...] = ins[9][0, :]


def fused(
    tokens, global_states, token_seg, global_seg, attn_gain, attn_shift, glob_gain, glob_shift, w_qkv, w_out,
    ffn_gain, ffn_shift, w_up, up_bias, w_down, down_bias, out_cotangent, global_cotangent,
):
    tok, width = tokens.shape[1:]
    glob = global_states.shape[1]
    hidden = w_up.shape[1]
    n_seq, n_batch = lax.axis_size("seq"), lax.axis_size("batch")
    rows, slots = tok + glob, glob // n_seq
    wide = tok + slots
    chunk, part, side = hidden // n_seq, width // n_seq, width // n_batch
    pairs = HEADS // 2
    eighth = (2, 2, 2)
    dma = pltpu.SemaphoreType.DMA

    def any_space():
        return pl.BlockSpec(memory_space=pl.ANY)

    def vmem():
        return pl.BlockSpec(memory_space=pltpu.VMEM)

    def low(*shape):
        return pltpu.VMEM(shape, BF)

    def full(*shape):
        return pltpu.VMEM(shape, F32)

    scratch = [
        low(rows, width), low(rows, width), low(rows, 3 * width), low(width, width),
        low(pairs, rows, 2 * tok + 2 * glob), low(width, tok + 128), low(wide, width), full(wide, width),
        low(wide, width), low(width, tok + 128), low(wide, width), low(width, tok + 128),
        full(wide, width), full(wide, width), low(wide, width), low(rows, 128), low(rows, 128),
        low(width, 3 * width), low(width, width), low(width, width), low(width, width),
        full(128, glob), full(16, tok), full(glob, width), low(glob, width + 128),
        low(n_seq, slots, width + 128), low(glob, width + 128),
        low(n_seq - 1, slots, width),
        full(16, width), full(n_seq, 16, 128), full(n_seq - 1, 16, 128), full(4, 16, 128), full(4, width),
        low(4, 2, 2, 2, side, chunk), low(4, 2, 2, side, chunk), low(2, 2, 2, side, chunk), low(2, 2, side, chunk),
        low(2, side, chunk), low(side, chunk),
        low(4, 2, *eighth, 2, part // 2, chunk), low(4, *eighth, 2, part // 2, chunk), low(4, 2, 2, 2, part // 2, chunk),
        low(2, 2, 2, 2, part // 2, chunk), low(2, 2, 2, part // 2, chunk), low(2, 2, part // 2, chunk),
        low(8, 2, 2, 2, part // 2, chunk), low(8, 2, 2, part // 2, chunk), low(8, 2, part // 2, chunk),
        low(8, 2, part // 2, chunk), low(8, part // 2, chunk),
        low(4, part // 2, 896), low(2, part // 2, 896),
        dma((8,)), dma((2, 2)), dma((1,)), dma((1,)),
        *[dma((8,)) for _ in range(10)], dma((9,)), dma((9,)),
        *[dma((4,)) for _ in range(10)], *[dma((4,)) for _ in range(10)], *[dma((8,)) for _ in range(10)],
        *[dma((3,)) for _ in range(6)], dma((4,)), dma((4,)), dma((1,)), dma((1,)), dma((4,)),
    ]

    results = pl.pallas_call(
        layer_kernel,
        out_shape=[
            jax.ShapeDtypeStruct((tok, width), BF),
            jax.ShapeDtypeStruct((glob, width), BF),
            jax.ShapeDtypeStruct((tok, width), BF),
            jax.ShapeDtypeStruct((glob, width), BF),
            jax.ShapeDtypeStruct((part, 3 * side), F32),
            jax.ShapeDtypeStruct((part, side), F32),
            jax.ShapeDtypeStruct((part, 2 * chunk), F32),
            jax.ShapeDtypeStruct((side, chunk), F32),
            jax.ShapeDtypeStruct((8, part), F32),
            jax.ShapeDtypeStruct((1, chunk), F32),
        ],
        in_specs=[any_space(), any_space(), vmem(), vmem(), vmem(), vmem(), vmem(), vmem(), any_space(), any_space(),
                  vmem(), vmem(), any_space(), vmem(), any_space(), vmem(), any_space(), any_space()],
        out_specs=[any_space()] * 4 + [vmem()] * 6,
        scratch_shapes=scratch,
        compiler_params=pltpu.CompilerParams(
            collective_id=0, has_side_effects=True, vmem_limit_bytes=64 * 1024 * 1024
        ),
        name="layer",
    )(
        tokens[0], global_states[0], token_seg, global_seg, attn_gain, attn_shift, glob_gain,
        glob_shift, w_qkv, w_out, ffn_gain, ffn_shift, w_up, up_bias, w_down, down_bias,
        out_cotangent[0], global_cotangent[0],
    )
    *large, vectors, ub = results
    results = pl.pallas_call(
        finish_kernel,
        out_shape=[jax.ShapeDtypeStruct(one.shape, one.dtype) for one in large]
        + [jax.ShapeDtypeStruct((part,), F32)] * 7
        + [jax.ShapeDtypeStruct((chunk,), F32)],
        in_specs=[vmem()] * 10,
        out_specs=[vmem()] * 16,
        name="results",
    )(*large, vectors, ub)
    out, gout, tgrad, ggrad, g_qkv, g_out, g_up, g_down, *g_vec, g_ub = results
    return (
        out[None], gout[None], tgrad[None], ggrad[None], g_vec[0], g_vec[1], g_vec[2], g_vec[3], g_qkv, g_out,
        g_vec[4], g_vec[5], g_up, g_ub, g_down.T, g_vec[6],
    )


def local(tokens, global_states, token_seg, global_seg, *rest):
    w_qkv, w_up = rest[4], rest[8]
    way = fused if fits(tokens, global_states, w_qkv, w_up) else general
    return way(tokens, global_states, token_seg, global_seg, *rest)


def solution(mesh):
    placed = (
        P("batch", "seq", None),
        P("batch", None, None),
        P("batch", "seq"),
        P("batch", None),
        P(),
        P(),
        P(),
        P(),
        P(),
        P(),
        P(),
        P(),
        P(),
        P(),
        P(),
        P(),
        P("batch", "seq", None),
        P("batch", None, None),
    )
    return jax.shard_map(
        local,
        mesh=mesh,
        in_specs=placed,
        out_specs=(
            P("batch", "seq", None),
            P("batch", None, None),
            P("batch", "seq", None),
            P("batch", None, None),
            P("seq"),
            P("seq"),
            P("seq"),
            P("seq"),
            P("seq", "batch"),
            P("seq", "batch"),
            P("seq"),
            P("seq"),
            P("seq", "batch"),
            P("seq"),
            P("seq", "batch"),
            P("seq"),
        ),
        check_vma=False,
    )
```

```python
import functools

import jax
import jax.numpy as jnp
from jax import lax
from jax.experimental import pallas as pl
from jax.experimental.pallas import tpu as pltpu
from jax.sharding import PartitionSpec as P

HEADS = 12
HEAD_DIM = 64
BLOCK = 512


EPS = 1e-05
NEGATIVE = -1e30


def from_behind(block, axis, distance):
    devices = range(lax.axis_size(axis))
    route = [((i - distance) % len(devices), i) for i in devices]
    return lax.ppermute(block, axis, route)


def norm_rows(source, scaling, offset):
    center = jnp.mean(source, axis=-1, keepdims=True)
    spread = source - center
    variance = jnp.mean(spread * spread, axis=-1, keepdims=True)
    return spread * lax.rsqrt(variance + EPS) * scaling + offset


def norm_back(source, scaling, offset, upstream):
    _, pullback = jax.vjp(norm_rows, source, scaling, offset)
    return pullback(upstream)


def project(former, latter):
    return jnp.einsum("rsd,de->rse", former, latter, preferred_element_type=jnp.float32)


def project_back(former, latter):
    return jnp.einsum("rse,de->rsd", former, latter, preferred_element_type=jnp.float32)


def outer_sum(former, latter):
    return jnp.einsum("rsd,rse->de", former, latter, preferred_element_type=jnp.float32)


def gelu_exact(hidden):
    return jax.nn.gelu(hidden, approximate=False)


def ffn_forward(state, ffn_gain, ffn_shift, w_up, up_bias, w_down, down_bias):
    normed = norm_rows(state, ffn_gain, ffn_shift).astype(jnp.bfloat16)
    hidden = project(normed, w_up) + up_bias
    active = gelu_exact(hidden).astype(jnp.bfloat16)
    result = state + project(active, w_down) + down_bias
    return (result, (normed, hidden, active))


def ffn_backward(state, stored, upstream, ffn_gain, ffn_shift, w_up, w_down):
    normed, hidden, active = stored
    upstream_low = upstream.astype(jnp.bfloat16)
    grad_down = outer_sum(active, upstream_low)
    grad_down_bias = jnp.sum(upstream, axis=(0, 1))
    grad_active = project_back(upstream_low, w_down)
    _, gelu_pull = jax.vjp(gelu_exact, hidden)
    grad_hidden = gelu_pull(grad_active)[0].astype(jnp.bfloat16)
    grad_up = outer_sum(normed, grad_hidden)
    grad_up_bias = jnp.sum(grad_hidden.astype(jnp.float32), axis=(0, 1))
    grad_normed = project_back(grad_hidden, w_up)
    grad_state, grad_gain, grad_shift = norm_back(state, ffn_gain, ffn_shift, grad_normed)
    return (
        upstream + grad_state,
        (grad_gain, grad_shift, grad_up, grad_up_bias, grad_down, grad_down_bias),
    )


def local_scores(queries, keys_near, seg_near, keys_far, seg_far):
    scaling = HEAD_DIM ** (-0.5)
    near_scores = (
        jnp.einsum("rnqhd,rnkhd->rnhqk", queries, keys_near, preferred_element_type=jnp.float32)
        * scaling
    )
    far_scores = (
        jnp.einsum("rnqhd,rghd->rnhqg", queries, keys_far, preferred_element_type=jnp.float32)
        * scaling
    )
    near_open = (seg_near[:, :, :, None] == seg_near[:, :, None, :])[:, :, None]
    far_open = (seg_near[:, :, :, None] == seg_far[:, None, None, :])[:, :, None]
    return (jnp.where(near_open, near_scores, NEGATIVE), jnp.where(far_open, far_scores, NEGATIVE))


def local_forward(queries, keys_near, values_near, seg_near, keys_far, values_far, seg_far):
    near_scores, far_scores = local_scores(queries, keys_near, seg_near, keys_far, seg_far)
    maxima = jnp.maximum(jnp.max(near_scores, axis=-1), jnp.max(far_scores, axis=-1))
    near_exp = jnp.exp(near_scores - maxima[..., None])
    far_exp = jnp.exp(far_scores - maxima[..., None])
    totals = jnp.sum(near_exp, axis=-1) + jnp.sum(far_exp, axis=-1)
    near_weights = (near_exp / totals[..., None]).astype(jnp.bfloat16)
    far_weights = (far_exp / totals[..., None]).astype(jnp.bfloat16)
    mixed_out = jnp.einsum(
        "rnhqk,rnkhd->rnqhd", near_weights, values_near, preferred_element_type=jnp.float32
    )
    mixed_out = mixed_out + jnp.einsum(
        "rnhqg,rghd->rnqhd", far_weights, values_far, preferred_element_type=jnp.float32
    )
    return (mixed_out, maxima + jnp.log(totals))


def local_backward(
    queries, keys_near, values_near, seg_near, keys_far, values_far, seg_far, logsum, upstream
):
    scaling = HEAD_DIM ** (-0.5)
    near_scores, far_scores = local_scores(queries, keys_near, seg_near, keys_far, seg_far)
    near_weights = jnp.exp(near_scores - logsum[..., None])
    far_weights = jnp.exp(far_scores - logsum[..., None])
    near_grad = jnp.einsum(
        "rnqhd,rnkhd->rnhqk", upstream, values_near, preferred_element_type=jnp.float32
    )
    far_grad = jnp.einsum(
        "rnqhd,rghd->rnhqg", upstream, values_far, preferred_element_type=jnp.float32
    )
    row_inner = jnp.sum(near_weights * near_grad, axis=-1) + jnp.sum(
        far_weights * far_grad, axis=-1
    )
    near_score_grad = (near_weights * (near_grad - row_inner[..., None])).astype(jnp.bfloat16)
    far_score_grad = (far_weights * (far_grad - row_inner[..., None])).astype(jnp.bfloat16)
    grad_queries = jnp.einsum(
        "rnhqk,rnkhd->rnqhd", near_score_grad, keys_near, preferred_element_type=jnp.float32
    )
    grad_queries = scaling * (
        grad_queries
        + jnp.einsum(
            "rnhqg,rghd->rnqhd", far_score_grad, keys_far, preferred_element_type=jnp.float32
        )
    )
    grad_keys = scaling * jnp.einsum(
        "rnhqk,rnqhd->rnkhd", near_score_grad, queries, preferred_element_type=jnp.float32
    )
    grad_values = jnp.einsum(
        "rnhqk,rnqhd->rnkhd",
        near_weights.astype(jnp.bfloat16),
        upstream,
        preferred_element_type=jnp.float32,
    )
    grad_keys_far = scaling * jnp.einsum(
        "rnhqg,rnqhd->rghd", far_score_grad, queries, preferred_element_type=jnp.float32
    )
    grad_values_far = jnp.einsum(
        "rnhqg,rnqhd->rghd",
        far_weights.astype(jnp.bfloat16),
        upstream,
        preferred_element_type=jnp.float32,
    )
    return (grad_queries, grad_keys, grad_values, grad_keys_far, grad_values_far)


def global_scores(glob_queries, glob_keys, glob_seg, key_rows, seg_tokens):
    scaling = HEAD_DIM ** (-0.5)
    remote_scores = (
        jnp.einsum("rghd,rshd->rhgs", glob_queries, key_rows, preferred_element_type=jnp.float32)
        * scaling
    )
    own_scores = (
        jnp.einsum("rghd,rjhd->rhgj", glob_queries, glob_keys, preferred_element_type=jnp.float32)
        * scaling
    )
    remote_open = glob_seg[:, None, :, None] == seg_tokens[:, None, None, :]
    own_open = glob_seg[:, None, :, None] == glob_seg[:, None, None, :]
    return (
        jnp.where(remote_open, remote_scores, NEGATIVE),
        jnp.where(own_open, own_scores, NEGATIVE),
    )


def general(
    tokens,
    global_states,
    token_seg,
    global_seg,
    attn_gain,
    attn_shift,
    glob_gain,
    glob_shift,
    w_qkv,
    w_out,
    ffn_gain,
    ffn_shift,
    w_up,
    up_bias,
    w_down,
    down_bias,
    out_cotangent,
    global_cotangent,
):
    row_count, tok_count, model_width = tokens.shape
    glob_count = global_states.shape[1]
    half_block = BLOCK // 2
    block_count = tok_count // BLOCK
    seq_devices = lax.axis_size("seq")
    scaling = HEAD_DIM ** (-0.5)
    low_type = jnp.bfloat16
    arrived = from_behind(tokens[:, :half_block], "seq", -1)
    sectioned = jnp.concatenate([tokens[:, half_block:], arrived], axis=1).astype(jnp.float32)
    glob_state = global_states.astype(jnp.float32)
    normed = norm_rows(sectioned, attn_gain, attn_shift).astype(low_type)
    glob_normed = norm_rows(glob_state, glob_gain, glob_shift).astype(low_type)
    projected = (
        project(normed, w_qkv).astype(low_type).reshape(row_count, tok_count, 3, HEADS, HEAD_DIM)
    )
    glob_proj = (
        project(glob_normed, w_qkv)
        .astype(low_type)
        .reshape(row_count, glob_count, 3, HEADS, HEAD_DIM)
    )
    queries = projected[:, :, 0]
    key_rows = projected[:, :, 1]
    value_rows = projected[:, :, 2]
    glob_queries = glob_proj[:, :, 0]
    glob_keys = glob_proj[:, :, 1]
    glob_values = glob_proj[:, :, 2]
    block_shape = (row_count, block_count, BLOCK, HEADS, HEAD_DIM)
    block_queries = queries.reshape(block_shape)
    block_keys = key_rows.reshape(block_shape)
    block_values = value_rows.reshape(block_shape)
    block_seg = token_seg.reshape(row_count, block_count, BLOCK)
    local_out, local_logsum = local_forward(
        block_queries, block_keys, block_values, block_seg, glob_keys, glob_values, global_seg
    )
    remote_scores, own_scores = global_scores(
        glob_queries, glob_keys, global_seg, key_rows, token_seg
    )
    maxima = jnp.maximum(
        lax.pmax(jnp.max(remote_scores, axis=-1), "seq"), jnp.max(own_scores, axis=-1)
    )
    remote_total = jnp.sum(jnp.exp(remote_scores - maxima[..., None]), axis=-1)
    totals = lax.psum(remote_total, "seq") + jnp.sum(
        jnp.exp(own_scores - maxima[..., None]), axis=-1
    )
    remote_weights = (jnp.exp(remote_scores - maxima[..., None]) / totals[..., None]).astype(
        low_type
    )
    own_weights = (jnp.exp(own_scores - maxima[..., None]) / totals[..., None]).astype(low_type)
    remote_part = jnp.einsum(
        "rhgs,rshd->rghd", remote_weights, value_rows, preferred_element_type=jnp.float32
    )
    glob_out = lax.psum(remote_part, "seq")
    glob_out = glob_out + jnp.einsum(
        "rhgj,rjhd->rghd", own_weights, glob_values, preferred_element_type=jnp.float32
    )
    glob_logsum = maxima + jnp.log(totals)
    attended = local_out.reshape(row_count, tok_count, model_width).astype(low_type)
    glob_attended = glob_out.reshape(row_count, glob_count, model_width).astype(low_type)
    attn_sum = sectioned + project(attended, w_out)
    glob_sum = glob_state + project(glob_attended, w_out)
    result, stored = ffn_forward(attn_sum, ffn_gain, ffn_shift, w_up, up_bias, w_down, down_bias)
    glob_result, glob_stored = ffn_forward(
        glob_sum, ffn_gain, ffn_shift, w_up, up_bias, w_down, down_bias
    )
    grad_attn_sum, tok_ffn = ffn_backward(
        attn_sum, stored, out_cotangent.astype(jnp.float32), ffn_gain, ffn_shift, w_up, w_down
    )
    grad_glob_sum, glob_ffn = ffn_backward(
        glob_sum,
        glob_stored,
        global_cotangent.astype(jnp.float32),
        ffn_gain,
        ffn_shift,
        w_up,
        w_down,
    )
    branch_low = grad_attn_sum.astype(low_type)
    glob_branch_low = grad_glob_sum.astype(low_type)
    grad_out_all = (
        outer_sum(attended, branch_low) + outer_sum(glob_attended, glob_branch_low) / seq_devices
    )
    upstream_mix = project_back(branch_low, w_out).astype(low_type).reshape(block_shape)
    glob_upstream = (
        project_back(glob_branch_low, w_out)
        .astype(low_type)
        .reshape(row_count, glob_count, HEADS, HEAD_DIM)
    )
    remote_exact = jnp.exp(remote_scores - glob_logsum[..., None])
    own_exact = jnp.exp(own_scores - glob_logsum[..., None])
    remote_grad = jnp.einsum(
        "rghd,rshd->rhgs", glob_upstream, value_rows, preferred_element_type=jnp.float32
    )
    own_grad = jnp.einsum(
        "rghd,rjhd->rhgj", glob_upstream, glob_values, preferred_element_type=jnp.float32
    )
    row_inner = lax.psum(jnp.sum(remote_exact * remote_grad, axis=-1), "seq")
    row_inner = row_inner + jnp.sum(own_exact * own_grad, axis=-1)
    remote_score_grad = (remote_exact * (remote_grad - row_inner[..., None])).astype(low_type)
    own_score_grad = (own_exact * (own_grad - row_inner[..., None])).astype(low_type)
    remote_queries = scaling * jnp.einsum(
        "rhgs,rshd->rghd", remote_score_grad, key_rows, preferred_element_type=jnp.float32
    )
    tok_keys_extra = scaling * jnp.einsum(
        "rhgs,rghd->rshd", remote_score_grad, glob_queries, preferred_element_type=jnp.float32
    )
    tok_values_extra = jnp.einsum(
        "rhgs,rghd->rshd",
        remote_exact.astype(low_type),
        glob_upstream,
        preferred_element_type=jnp.float32,
    )
    own_queries = scaling * jnp.einsum(
        "rhgj,rjhd->rghd", own_score_grad, glob_keys, preferred_element_type=jnp.float32
    )
    own_keys = scaling * jnp.einsum(
        "rhgj,rghd->rjhd", own_score_grad, glob_queries, preferred_element_type=jnp.float32
    )
    own_values = jnp.einsum(
        "rhgj,rghd->rjhd",
        own_exact.astype(low_type),
        glob_upstream,
        preferred_element_type=jnp.float32,
    )
    grad_queries, grad_keys, grad_values, grad_keys_far, grad_values_far = local_backward(
        block_queries,
        block_keys,
        block_values,
        block_seg,
        glob_keys,
        glob_values,
        global_seg,
        local_logsum,
        upstream_mix,
    )
    far_grads = lax.psum((remote_queries, grad_keys_far, grad_values_far), "seq")
    head_shape = (row_count, tok_count, HEADS, HEAD_DIM)
    grad_projected = jnp.stack(
        [
            grad_queries.reshape(head_shape),
            grad_keys.reshape(head_shape) + tok_keys_extra,
            grad_values.reshape(head_shape) + tok_values_extra,
        ],
        axis=2,
    )
    grad_projected = grad_projected.reshape(row_count, tok_count, 3 * model_width).astype(low_type)
    glob_grad_projected = jnp.stack(
        [far_grads[0] + own_queries, far_grads[1] + own_keys, far_grads[2] + own_values], axis=2
    )
    glob_grad_projected = glob_grad_projected.reshape(
        row_count, glob_count, 3 * model_width
    ).astype(low_type)
    grad_qkv_all = (
        outer_sum(normed, grad_projected)
        + outer_sum(glob_normed, glob_grad_projected) / seq_devices
    )
    grad_normed = project_back(grad_projected, w_qkv)
    glob_grad_normed = project_back(glob_grad_projected, w_qkv)
    grad_sectioned, attn_gain_grad, attn_shift_grad = norm_back(
        sectioned, attn_gain, attn_shift, grad_normed
    )
    grad_sectioned = grad_sectioned + grad_attn_sum
    glob_grad_state, glob_gain_grad, glob_shift_grad = norm_back(
        glob_state, glob_gain, glob_shift, glob_grad_normed
    )
    global_grad = (glob_grad_state + grad_glob_sum).astype(low_type)
    grad_low = grad_sectioned.astype(low_type)
    returned = from_behind(grad_low[:, tok_count - half_block :], "seq", 1)
    token_grad = jnp.concatenate([returned, grad_low[:, : tok_count - half_block]], axis=1)
    ffn_gain_all = tok_ffn[0] + glob_ffn[0] / seq_devices
    ffn_shift_all = tok_ffn[1] + glob_ffn[1] / seq_devices
    up_all = tok_ffn[2] + glob_ffn[2] / seq_devices
    up_bias_all = tok_ffn[3] + glob_ffn[3] / seq_devices
    down_all = tok_ffn[4] + glob_ffn[4] / seq_devices
    down_bias_all = tok_ffn[5] + glob_ffn[5] / seq_devices
    glob_gain_all = glob_gain_grad / seq_devices
    glob_shift_all = glob_shift_grad / seq_devices
    mat_sums = (
        lax.psum_scatter(
            grad_qkv_all.astype(jnp.bfloat16), "batch", scatter_dimension=1, tiled=True
        ).astype(jnp.float32),
        lax.psum_scatter(
            grad_out_all.astype(jnp.bfloat16), "batch", scatter_dimension=1, tiled=True
        ).astype(jnp.float32),
        lax.psum_scatter(
            up_all.astype(jnp.bfloat16), "batch", scatter_dimension=1, tiled=True
        ).astype(jnp.float32),
        lax.psum_scatter(
            down_all.astype(jnp.bfloat16), "batch", scatter_dimension=1, tiled=True
        ).astype(jnp.float32),
    )
    vec_sums = (
        lax.psum(attn_gain_grad.astype(jnp.bfloat16), "batch").astype(jnp.float32),
        lax.psum(attn_shift_grad.astype(jnp.bfloat16), "batch").astype(jnp.float32),
        lax.psum(glob_gain_all.astype(jnp.bfloat16), "batch").astype(jnp.float32),
        lax.psum(glob_shift_all.astype(jnp.bfloat16), "batch").astype(jnp.float32),
        lax.psum(ffn_gain_all.astype(jnp.bfloat16), "batch").astype(jnp.float32),
        lax.psum(ffn_shift_all.astype(jnp.bfloat16), "batch").astype(jnp.float32),
        lax.psum(up_bias_all.astype(jnp.bfloat16), "batch").astype(jnp.float32),
        lax.psum(down_bias_all.astype(jnp.bfloat16), "batch").astype(jnp.float32),
    )
    shares = (
        lax.psum_scatter(vec_sums[0], "seq", scatter_dimension=0, tiled=True),
        lax.psum_scatter(vec_sums[1], "seq", scatter_dimension=0, tiled=True),
        lax.psum_scatter(vec_sums[2], "seq", scatter_dimension=0, tiled=True),
        lax.psum_scatter(vec_sums[3], "seq", scatter_dimension=0, tiled=True),
        lax.psum_scatter(mat_sums[0], "seq", scatter_dimension=0, tiled=True),
        lax.psum_scatter(mat_sums[1], "seq", scatter_dimension=0, tiled=True),
        lax.psum_scatter(vec_sums[4], "seq", scatter_dimension=0, tiled=True),
        lax.psum_scatter(vec_sums[5], "seq", scatter_dimension=0, tiled=True),
        lax.psum_scatter(mat_sums[2], "seq", scatter_dimension=0, tiled=True),
        lax.psum_scatter(vec_sums[6], "seq", scatter_dimension=0, tiled=True),
        lax.psum_scatter(mat_sums[3], "seq", scatter_dimension=0, tiled=True),
        lax.psum_scatter(vec_sums[7], "seq", scatter_dimension=0, tiled=True),
    )
    matrices = (shares[4], shares[5], shares[8], shares[10])
    vectors = (
        shares[0],
        shares[1],
        shares[2],
        shares[3],
        shares[6],
        shares[7],
        shares[9],
        shares[11],
    )
    return (
        result.astype(low_type),
        glob_result.astype(low_type),
        token_grad,
        global_grad,
        vectors[0],
        vectors[1],
        vectors[2],
        vectors[3],
        matrices[0],
        matrices[1],
        vectors[4],
        vectors[5],
        matrices[2],
        vectors[6],
        matrices[3],
        vectors[7],
    )


MESH = pl.DeviceIdType.MESH
BF = jnp.bfloat16
F32 = jnp.float32


def dot_nn(left, right):
    return lax.dot_general(left, right, (((1,), (0,)), ((), ())), preferred_element_type=F32)


def dot_nt(left, right):
    return lax.dot_general(left, right, (((1,), (1,)), ((), ())), preferred_element_type=F32)


def lanes_of(shape):
    return lax.broadcasted_iota(jnp.int32, shape, len(shape) - 1)


def two_parts(value):
    high = value.astype(BF)
    return high, (value - high.astype(F32)).astype(BF)


def norm_stats(value):
    center = jnp.mean(value, axis=-1, keepdims=True)
    spread = value - center
    variance = jnp.mean(spread * spread, axis=-1, keepdims=True)
    return spread, lax.rsqrt(variance + EPS)


def norm_pull(value, gain, upstream):
    spread, scale = norm_stats(value)
    unit = spread * scale
    scaled = upstream * gain
    first = jnp.mean(scaled, axis=-1, keepdims=True)
    second = jnp.mean(scaled * unit, axis=-1, keepdims=True)
    grad = scale * (scaled - first - unit * second)
    return (
        grad,
        jnp.sum(upstream * unit, axis=0, keepdims=True),
        jnp.sum(upstream, axis=0, keepdims=True),
    )


def gelu_pair(hidden):
    size = jnp.abs(hidden) * 0.7071067811865476
    step = 1.0 / (1.0 + 0.3275911 * size)
    bell = jnp.exp(-(size * size))
    series = 1.061405429 * 0.5
    for term in (-1.453152027, 1.421413741, -0.284496736, 0.254829592):
        series = series * step + term * 0.5
    tail = series * step * bell
    mass = jnp.where(hidden < 0.0, tail, 1.0 - tail)
    return hidden * mass, mass + hidden * (bell * 0.3989422804014327)


def layer_kernel(
    tokens, gstates, tseg, gseg, attn_gain, attn_shift, glob_gain, glob_shift, w_qkv, w_out,
    ffn_gain, ffn_shift, w_up, up_bias, w_down, down_bias, cotan, gcotan,
    o_out, o_gout, o_tgrad, o_ggrad, o_qkv, o_wout, o_up, o_down, o_vec, o_ub,
    sec, nrm, proj, kvt, probs, att_t, att, x2, n2, n2t, ct, ct_t, acc_full, gn2_full, gatt, qaug, kaug,
    wq, wo, wu, wd,
    lse_t, rl_t, cx, msg1, rcv1, rcv2, rcv3, rcv3b, gsum, gall, vec, vmsg, vrcv, vsum, ub,
    gd, r0d, r1d, r2d, r3d, r4d, gu, r0u, r1u, r2u, r3u, r4u, r0q, r1q, r2q, r3q, r4q, fmsg, frcv, hid_a, hid_b,
    loc, wsem, hs, hr, m1s, m1r, m2s, m2r, m3s, m3r, gos, gor, ggs_s, ggs_r, vs, vr,
    d0s, d0r, d1s, d1r, d2s, d2r, d3s, d3r, d4s, d4r,
    u0s, u0r, u1s, u1r, u2s, u2r, u3s, u3r, u4s, u4r,
    q0s, q0r, q1s, q1r, q2s, q2r, q3s, q3r, q4s, q4r,
    qps, qpr, qls, qlr, vbs, vbr, fs, fr, hs2, hr2, osem, gsem,
):
    tok, width = tokens.shape
    glob = gstates.shape[0]
    rows = tok + glob
    n_seq = lax.axis_size("seq")
    slots = glob // n_seq
    wide = tok + slots
    half = tok // 2
    pairs = HEADS // 2
    chunk = up_bias.shape[0] // n_seq
    n_chunk = up_bias.shape[0] // width
    side, part = width // 4, width // n_seq
    tail = 128

    s = lax.axis_index("seq")
    b = lax.axis_index("batch")
    x, zl, zh = s % 2, (s // 2) % 2, s // 4
    c, y = b % 2, b // 2
    dev_c, dev_y = (s, b + 1 - 2 * c), (s, b + 2 - 4 * y)
    dev_cy, dev_xy = (s, dev_y[1] + 1 - 2 * c), (s + 1 - 2 * x, dev_y[1])
    dev_x, dev_1, dev_2 = (s + 1 - 2 * x, b), (s + 2 - 4 * zl, b), (s + 4 - 8 * zh, b)

    def flip(k):
        other = s
        if k & 1:
            other = other + 1 - 2 * x
        if k & 2:
            other = other + 2 - 4 * zl
        if k & 4:
            other = other + 4 - 8 * zh
        return other

    def remote(src, dst, ss, rs, dev):
        return pltpu.make_async_remote_copy(
            src_ref=src, dst_ref=dst, send_sem=ss, recv_sem=rs, device_id=dev, device_id_type=MESH
        )

    peers = tuple(range(1, n_seq))
    acc, gn2 = acc_full.at[pl.ds(0, wide)], gn2_full.at[pl.ds(0, wide)]
    score = (acc_full, gn2_full)

    def as_row(vector):
        return vector[...].reshape(1, vector.shape[0])

    attn_gain, attn_shift, glob_gain, glob_shift, ffn_gain, ffn_shift, down_bias = (
        as_row(v) for v in (attn_gain, attn_shift, glob_gain, glob_shift, ffn_gain, ffn_shift, down_bias)
    )

    my_slots = pl.multiple_of(s * slots, slots)
    loads = [
        (tokens.at[pl.ds(half, half)], sec.at[pl.ds(0, half)]),
        (gstates, sec.at[pl.ds(tok, glob)]),
        (w_qkv, wq),
        (cotan, ct.at[pl.ds(0, tok)]),
        (gcotan.at[pl.ds(my_slots, slots)], ct.at[pl.ds(tok, slots)]),
        (w_out, wo),
    ]
    loads = [pltpu.make_async_copy(a, d, loc.at[i]) for i, (a, d) in enumerate(loads)]
    for load in loads:
        load.start()

    def piece_of(i, o):
        return 4 * (i // 2) + 2 * o + i % 2

    def stream_up(i):
        copies = []
        for o in range(2):
            at = piece_of(i, o) * chunk
            at = at if isinstance(at, int) else pl.multiple_of(at, chunk)
            copies.append(
                pltpu.make_async_copy(w_up.at[:, pl.ds(at, chunk)], wu.at[:, pl.ds(o * chunk, chunk)], wsem.at[0, o])
            )
        return copies

    def stream_down(i, to, which):
        copies = []
        for o in range(2):
            at = piece_of(i, o) * chunk
            at = at if isinstance(at, int) else pl.multiple_of(at, chunk)
            copies.append(pltpu.make_async_copy(w_down.at[pl.ds(at, chunk)], to.at[pl.ds(o * chunk, chunk)], wsem.at[which, o]))
        return copies

    def stream(i):
        return stream_up(i) + stream_down(i, wd, 1)

    for i, to in ((0, wu), (1, wd)):
        for copy in stream_down(i, to, i):
            copy.start()

    bar = pltpu.get_barrier_semaphore()
    for k in peers:
        pl.semaphore_signal(bar, inc=1, device_id=(flip(k), b), device_id_type=MESH)
    pl.semaphore_signal(bar, inc=1, device_id=dev_c, device_id_type=MESH)
    for dev in (dev_y, dev_cy, dev_xy):
        pl.semaphore_signal(bar, inc=1, device_id=dev, device_id_type=MESH)
    pl.semaphore_wait(bar, len(peers) + 4)
    halo = remote(
        tokens.at[pl.ds(0, half)], sec.at[pl.ds(half, half)], hs.at[0], hr.at[0],
        (lax.rem(s + n_seq - 1, n_seq), b),
    )
    halo.start()

    seg_row = jnp.concatenate([tseg[...], gseg[...]], axis=1)
    which = lax.broadcasted_iota(jnp.int32, (128, rows), 0)
    col = lanes_of((128, rows))
    is_glob = col >= tok
    same = which == seg_row
    q_t = jnp.where(which < 3, jnp.where(same, 1.0, 0.0), jnp.where((which == 3) & is_glob, 1.0, 0.0))
    far = jnp.where(s == 0, 0.0, NEGATIVE)
    k_t = jnp.where(which < 3, jnp.where(same, 0.0, NEGATIVE), jnp.where((which == 3) & is_glob, far, 0.0))
    qaug[...] = jnp.transpose(q_t).astype(BF)
    kaug[...] = jnp.transpose(k_t).astype(BF)

    def norm_to(first, count, gain, shift):
        for r in range(first, first + count, 128):
            spread, scale = norm_stats(sec[pl.ds(r, 128), :].astype(F32))
            nrm[pl.ds(r, 128), :] = (spread * scale * gain + shift).astype(BF)

    def project_rows(first, count):
        def step(i, carry):
            at = pl.multiple_of(i * width, width)
            proj[pl.ds(first, count), pl.ds(at, width)] = dot_nn(
                nrm[pl.ds(first, count), :], wq[:, pl.ds(at, width)]
            ).astype(BF)
            return carry

        lax.fori_loop(0, 3, step, 0)

    loads[1].wait()
    norm_to(tok, glob, glob_gain, glob_shift)
    loads[0].wait()
    norm_to(0, half, attn_gain, attn_shift)
    loads[2].wait()
    project_rows(tok, glob)
    project_rows(0, half)
    loads[3].wait()
    loads[4].wait()
    ct_t[:, pl.ds(0, wide)] = jnp.transpose(ct[...])
    kept_rows = (((0,), 0, 384), ((1, 0, 0), 384, 96), ((1, 0, 1, 0), 480, 48))
    for i in range(n_chunk):
        to = (wu, wd)[i % 2]
        for copy in stream_down(i, to, i % 2):
            copy.wait()
        for o in range(2):
            grad_active = dot_nt(ct[...], to[pl.ds(o * chunk, chunk), :]).astype(BF)
            for where, first, count in kept_rows:
                kept = gu.at[(i, o) + where]
                kept[...] = grad_active[first : first + count].reshape(kept.shape)
        if i + 2 < n_chunk:
            for copy in stream_down(i + 2, to, i % 2):
                copy.start()
    for copy in stream(0):
        copy.start()
    halo.wait()
    norm_to(half, half, attn_gain, attn_shift)
    project_rows(half, half)

    kvt[:, pl.ds(0, rows)] = jnp.transpose(proj[:, pl.ds(2 * width, width)])
    lane_p = lanes_of((1, 128))
    even = jnp.where(lane_p < HEAD_DIM, HEAD_DIM ** (-0.5), 0.0).astype(BF)
    odd = jnp.where(lane_p < HEAD_DIM, 0.0, HEAD_DIM ** (-0.5)).astype(BF)
    even_one = jnp.where(lane_p < HEAD_DIM, 1.0, 0.0).astype(BF)
    odd_one = jnp.where(lane_p < HEAD_DIM, 0.0, 1.0).astype(BF)
    first_head = lax.broadcasted_iota(jnp.int32, (128, 128), 0) < HEAD_DIM
    lse_t[...] = jnp.zeros_like(lse_t)
    rl_t[...] = jnp.zeros_like(rl_t)

    def glob_forward(p, carry):
        at = pl.multiple_of(p * 128, 128)
        keys = jnp.concatenate([proj[:, pl.ds(width + at, 128)], kaug[...]], axis=1)
        qg = proj[pl.ds(tok, glob), pl.ds(at, 128)]
        qa = qaug[pl.ds(tok, glob), :]
        queries = jnp.concatenate(
            [jnp.concatenate([qg * even, qa], axis=1), jnp.concatenate([qg * odd, qa], axis=1)], axis=0
        )
        scores = dot_nt(keys, queries)
        top = jnp.max(scores, axis=0, keepdims=True)
        raised = jnp.exp(scores - top)
        total = jnp.sum(raised, axis=0, keepdims=True)
        weights = (raised * (1.0 / total)).astype(BF)
        probs[p, :, pl.ds(2 * tok, 2 * glob)] = weights
        mixed = dot_nn(kvt[pl.ds(at, 128), pl.ds(0, rows)], weights)
        cx[:, pl.ds(at, 128)] = jnp.transpose(jnp.where(first_head, mixed[:, :glob], mixed[:, glob:]))
        logsum = top + jnp.log(total)
        lse_t[pl.ds(2 * p, 1), :] = logsum[:, :glob]
        lse_t[pl.ds(2 * p + 1, 1), :] = logsum[:, glob:]
        return carry

    lax.fori_loop(0, pairs, glob_forward, 0, unroll=True)

    lse = jnp.transpose(lse_t[...])
    in_heads = lanes_of((glob, 128)) < HEADS
    lse = jnp.where(in_heads, lse, 0.0)
    part_a, rest = two_parts(lse)
    rest = lse - part_a.astype(F32)
    part_b = rest.astype(BF)
    part_c = rest - part_b.astype(F32)
    packed = part_a.astype(F32) + pltpu.roll(part_b.astype(F32), 16, 1) + pltpu.roll(part_c, 32, 1)
    msg1[:, pl.ds(0, width)] = cx[...].astype(BF)
    msg1[:, pl.ds(width, 128)] = packed.astype(BF)
    sends1 = []
    for k in peers:
        other = flip(k)
        at = pl.multiple_of(other * slots, slots)
        copy = remote(msg1.at[pl.ds(at, slots)], rcv1.at[k], m1s.at[k], m1r.at[k], (other, b))
        copy.start()
        sends1.append(copy)
    rcv1[0] = msg1[pl.ds(my_slots, slots), :]

    def scores_to(slot, p, mask):
        at = pl.multiple_of(p * 128, 128)
        keys = jnp.concatenate([proj[:, pl.ds(width + at, 128)], kaug[...]], axis=1)
        queries = jnp.concatenate([proj[pl.ds(0, tok), pl.ds(at, 128)] * mask, qaug[pl.ds(0, tok), :]], axis=1)
        score[slot][:, pl.ds(0, tok)] = dot_nt(keys, queries)

    def softmax_of(slot, p):
        values = score[slot][:, pl.ds(0, tok)]
        raised = jnp.exp(values - jnp.max(values, axis=0, keepdims=True))
        inverse = 1.0 / jnp.sum(raised, axis=0, keepdims=True)
        weights = raised.astype(BF)
        probs[p, :, pl.ds(slot * tok, tok)] = weights
        rl_t[pl.ds(2 * p + slot, 1), :] = inverse
        here = pl.multiple_of(p * 128 + slot * HEAD_DIM, HEAD_DIM)
        mixed = dot_nn(kvt[pl.ds(here, HEAD_DIM), pl.ds(0, rows)], weights)
        att_t[pl.ds(here, HEAD_DIM), pl.ds(0, tok)] = (mixed * inverse).astype(BF)

    def local_forward_pair(p, carry):
        scores_to(1, p, odd)
        softmax_of(0, p)
        scores_to(0, jnp.minimum(p + 1, pairs - 1), even)
        softmax_of(1, p)
        return carry

    scores_to(0, 0, even)
    lax.fori_loop(0, pairs, local_forward_pair, 0)
    att[pl.ds(0, tok), :] = jnp.transpose(att_t[:, pl.ds(0, tok)])

    head_of = lanes_of((128, width)) // HEAD_DIM
    spread_heads = jnp.where(head_of == lax.broadcasted_iota(jnp.int32, (128, width), 0), 1.0, 0.0).astype(BF)
    for copy in sends1:
        copy.wait()
    logs = []
    for k in range(n_seq):
        packed = rcv1[k, :, pl.ds(width, 128)].astype(F32)
        logs.append(packed + pltpu.roll(packed, 112, 1) + pltpu.roll(packed, 96, 1))
    high = functools.reduce(jnp.maximum, logs)
    raised = [jnp.exp(one - high) for one in logs]
    total = functools.reduce(jnp.add, raised)
    in_heads = lanes_of((slots, 128)) < HEADS
    shares = jnp.concatenate([jnp.where(in_heads, one / total, 0.0) for one in raised], axis=0)
    share_a, share_b = two_parts(shares)
    shares = dot_nn(share_a, spread_heads) + dot_nn(share_b, spread_heads)
    cx[...] = shares
    mixed = jnp.zeros((slots, width), F32)
    for k in range(n_seq):
        mixed = mixed + shares[k * slots : (k + 1) * slots] * rcv1[k, :, pl.ds(0, width)].astype(F32)
    att[pl.ds(tok, slots), :] = mixed.astype(BF)
    att_t[:, pl.ds(tok, tail)] = jnp.transpose(
        jnp.concatenate([mixed, jnp.zeros((tail - slots, width), F32)], axis=0)
    ).astype(BF)

    loads[5].wait()
    for first in range(0, width, 256):
        x2[:, pl.ds(first, 256)] = dot_nn(att[...], wo[:, pl.ds(first, 256)])
    x2[pl.ds(0, tok), :] += sec[pl.ds(0, tok), :].astype(F32)
    x2[pl.ds(tok, slots), :] += sec[pl.ds(pl.multiple_of(tok + my_slots, slots), slots), :].astype(F32)

    def second_norm(first, count):
        spread, scale = norm_stats(x2[pl.ds(first, count), :])
        n2[pl.ds(first, count), :] = (spread * scale * ffn_gain + ffn_shift).astype(BF)

    for r in range(0, tok, 128):
        second_norm(r, 128)
    second_norm(tok, slots)
    n2t[:, pl.ds(0, wide)] = jnp.transpose(n2[...])

    def d_core(i):
        return remote(gd.at[i, :, :, 1 - c], r0d.at[i], d0s.at[i], d0r.at[i], dev_c)

    def d_y(i):
        return remote(r0d.at[i, :, 1 - y], r1d.at[i], d1s.at[i], d1r.at[i], dev_y)

    def d_1(i):
        return remote(r1d.at[i, 1 - zl], r2d.at[i // 2, i % 2], d2s.at[i], d2r.at[i], dev_1)

    def d_x(h):
        return remote(r2d.at[h, 1 - x], r3d.at[h], d3s.at[h], d3r.at[h], dev_x)

    def d_2():
        return remote(r3d.at[1 - zh], r4d, d4s.at[0], d4r.at[0], dev_2)

    def do_d_y(i):
        d_core(i).wait_recv()
        r0d[i] = r0d[i] + gd[i, :, :, c]
        d_y(i).start()

    def do_d_1(i):
        d_y(i).wait_recv()
        r1d[i] = r1d[i] + r0d[i, :, y]
        d_1(i).start()

    def do_d_x(h):
        for j in range(2):
            d_1(2 * h + j).wait_recv()
            r2d[h, j] = r2d[h, j] + r1d[2 * h + j, zl]
        d_x(h).start()

    def do_d_2():
        for h in range(2):
            d_x(h).wait_recv()
            r3d[h] = r3d[h] + r2d[h, x]
        d_2().start()

    def u_core(i):
        return remote(gu.at[i, 1 - c], r0u.at[i], u0s.at[i], u0r.at[i], dev_c)

    def u_a(i, z_first):
        src, dev = (r0u.at[i, :, 1 - zl], dev_1) if z_first else (r0u.at[i, :, :, 1 - x], dev_x)
        return remote(src, r1u.at[i], u1s.at[i], u1r.at[i], dev)

    def u_b(i):
        src, dev = (r1u.at[i, :, 1 - x], dev_x) if i == 0 else (r1u.at[i, :, 1 - zl], dev_1)
        return remote(src, r2u.at[i // 2, i % 2], u2s.at[i], u2r.at[i], dev)

    def u_y(j):
        return remote(r2u.at[1 - y, j], r3u.at[j], u3s.at[j], u3r.at[j], dev_y)

    def u_2(j):
        return remote(r3u.at[j, 1 - zh], r4u.at[j], u4s.at[j], u4r.at[j], dev_2)

    def do_u_a(i):
        u_core(i).wait_recv()
        r0u[i] = r0u[i] + gu[i, c]
        if isinstance(i, int):
            u_a(i, i == 0).start()
            return

        @pl.when(i == 0)
        def _():
            u_a(i, True).start()

        @pl.when(i > 0)
        def _():
            u_a(i, False).start()

    def do_u_b(i):
        u_a(i, i == 0).wait_recv()
        r1u[i] = r1u[i] + (r0u[i, :, zl] if i == 0 else r0u[i, :, :, x])
        u_b(i).start()

    def do_u_y(j):
        for yy in range(2):
            i = 2 * yy + j
            u_b(i).wait_recv()
            r2u[yy, j] = r2u[yy, j] + r1u[i, :, x if i == 0 else zl]
        u_y(j).start()

    def do_u_2(j):
        u_y(j).wait_recv()
        r3u[j] = r3u[j] + r2u[y, j]
        u_2(j).start()

    vec[...] = jnp.zeros_like(vec)
    for i in range(n_chunk):
        for o in range(2):
            ub[pl.ds(i, 1), pl.ds(o * chunk, chunk)] = up_bias[pl.ds(piece_of(i, o) * chunk, chunk)].reshape(1, chunk)
    acc[...] = jnp.zeros_like(acc)
    gn2[...] = jnp.zeros_like(gn2)

    act = gatt
    gh = kvt
    cuts = ((0, 256, ((0, 0, 0, 256),)), (256, 256, ((0, 256, 0, 128), (1, 0, 128, 128))), (512, 256, ((1, 128, 0, 256),)))

    def hidden_at(n):
        return (hid_a, hid_b)[n % 2]

    def ffn_step(i, carry):
        for copy in stream(i):
            copy.wait()

        def up(n):
            here = pl.ds(cuts[n][0], 256)
            hidden_at(n)[...] = dot_nn(n2[...], wu[:, here]) + ub[pl.ds(i, 1), here]

        def activate(n):
            here = pl.ds(cuts[n][0], 256)
            total = jnp.zeros((1, 256), F32)
            for where, first, count in kept_rows:
                row = pl.ds(first, count)
                active, slope = gelu_pair(hidden_at(n)[row, :])
                act[row, here] = active.astype(BF)
                grad_active = jnp.concatenate(
                    [
                        gu[(i, o) + where + (slice(None),) * (5 - len(where)) + (pl.ds(at, size),)].reshape(count, size)
                        for o, at, _, size in cuts[n][2]
                    ],
                    axis=1,
                )
                grad_hidden = (slope * grad_active.astype(F32)).astype(BF)
                gh[row, here] = grad_hidden
                total = total + jnp.sum(grad_hidden.astype(F32), axis=0, keepdims=True)
            ub[pl.ds(i, 1), here] = total

        def down_terms(n):
            first, count, parts = cuts[n]
            block = dot_nn(ct_t[:, pl.ds(0, wide)], act[:, pl.ds(first, count)]).astype(BF)
            for o, at, start, size in parts:
                gd[i, o, :, :, :, pl.ds(at, size)] = block[:, start : start + size].reshape(2, 2, side, size)

        def up_terms(n):
            first, count, parts = cuts[n]
            block = dot_nn(n2t[:, pl.ds(0, wide)], gh[pl.ds(0, wide), pl.ds(first, count)]).astype(BF)
            for o, at, start, size in parts:
                gu[i, o, :, :, :, :, :, pl.ds(at, size)] = block[:, start : start + size].reshape(
                    2, 2, 2, 2, part // 2, size
                )

        up(0)
        activate(0)
        up(1)
        down_terms(0)
        activate(1)
        up(2)
        down_terms(1)
        activate(2)
        for first, count, _ in cuts:
            here = pl.ds(first, count)
            acc[:, here] += dot_nn(act[...], wd[:, here])
            gn2[:, here] += dot_nt(gh[pl.ds(0, wide), :], wu[here, :])

        @pl.when(i + 1 < n_chunk)
        def _():
            for copy in stream(i + 1):
                copy.start()

        @pl.when(i >= 1)
        def _():
            do_d_y(i - 1)
            do_u_a(i - 1)

        @pl.when(i == 3)
        def _():
            do_u_b(0)
            do_d_1(0)

        down_terms(2)
        for n in range(3):
            up_terms(n)
        d_core(i).start()
        u_core(i).start()

        return carry

    lax.fori_loop(0, n_chunk, ffn_step, 0)

    for i in range(n_chunk):
        for o in range(2):
            block = piece_of(i, o)
            vec[pl.ds(8 + block // 2, 1), pl.ds(block % 2 * chunk, chunk)] = ub[pl.ds(i, 1), pl.ds(o * chunk, chunk)]


    def second_pull(first, count):
        grad, gain_term, shift_term = norm_pull(
            x2[pl.ds(first, count), :], ffn_gain, gn2[pl.ds(first, count), :]
        )
        upstream = ct[pl.ds(first, count), :].astype(F32)
        total = upstream + grad
        acc[pl.ds(first, count), :] += x2[pl.ds(first, count), :] + down_bias
        x2[pl.ds(first, count), :] = total
        n2[pl.ds(first, count), :] = total.astype(BF)
        vec[pl.ds(4, 1), :] += gain_term
        vec[pl.ds(5, 1), :] += shift_term
        vec[pl.ds(6, 1), :] += jnp.sum(upstream, axis=0, keepdims=True)

    for r in range(0, tok, 128):
        second_pull(r, 128)
    second_pull(tok, slots)
    gatt[...] = dot_nt(n2[...], wo[...]).astype(BF)

    slot_grad = gatt[pl.ds(tok, slots), :].astype(F32)
    slot_att = att[pl.ds(tok, slots), :].astype(F32)
    head_sel = lanes_of((1, 128)) < HEADS

    def inner_aug(upstream, values):
        high, low = two_parts(upstream.astype(F32) * values)
        inner = dot_nt(high, spread_heads) + dot_nt(low, spread_heads)
        high, low = two_parts(jnp.where(head_sel, inner, 0.0))
        return (high.astype(F32) + pltpu.roll(low.astype(F32), 16, 1)).astype(BF)

    scaled = jnp.concatenate(
        [(cx[pl.ds(k * slots, slots), :] * slot_grad).astype(BF) for k in range(n_seq)], axis=0
    )
    msg1[:, pl.ds(0, width)] = scaled
    msg1[:, pl.ds(width, 128)] = inner_aug(scaled, jnp.concatenate([slot_att] * n_seq, axis=0))
    sends2 = []
    for k in peers:
        copy = remote(
            msg1.at[pl.ds(k * slots, slots)], rcv2.at[pl.ds(my_slots, slots)], m2s.at[k], m2r.at[k],
            (flip(k), b),
        )
        copy.start()
        sends2.append(copy)
    rcv2[pl.ds(my_slots, slots), :] = msg1[pl.ds(0, slots), :]
    do_d_y(3)
    do_u_a(3)
    do_d_1(1)
    do_u_b(1)

    n2t[:, pl.ds(0, tok)] = jnp.transpose(nrm[pl.ds(0, tok), :])
    n2t[:, pl.ds(tok, glob)] = jnp.transpose(nrm[pl.ds(tok, glob), :])

    outs = nrm
    outs[pl.ds(0, wide), :] = acc[...].astype(BF)
    out_copy = pltpu.make_async_copy(outs.at[pl.ds(0, tok)], o_out, osem.at[0])
    out_copy.start()
    own_out = pltpu.make_async_copy(
        outs.at[pl.ds(tok, slots)], o_gout.at[pl.ds(my_slots, slots)], osem.at[1]
    )
    own_out.start()

    scale_c = jnp.transpose(
        jnp.concatenate([rl_t[...], jnp.zeros((128 - rl_t.shape[0], tok), F32)], axis=0)
    )
    scale_a, scale_b = two_parts(scale_c)
    for r in range(0, tok, 128):
        wider = dot_nn(scale_a[r : r + 128], spread_heads) + dot_nn(scale_b[r : r + 128], spread_heads)
        scaled = (gatt[pl.ds(r, 128), :].astype(F32) * wider).astype(BF)
        gatt[pl.ds(r, 128), :] = scaled
        qaug[pl.ds(r, 128), :] = inner_aug(scaled, att[pl.ds(r, 128), :].astype(F32))
    kvt[:, pl.ds(0, rows)] = jnp.transpose(proj[:, pl.ds(width, width)])

    def chunk_at(p):
        return gu.at[p // 2, lax.rem(p, 2)]

    def put_chunk(p, value):
        gu[p // 2, lax.rem(p, 2)] = value.astype(BF).reshape(gu.shape[2:])
        q_core(p).start()

    def q_core(p):
        return remote(chunk_at(p).at[:, 1 - c], r0q.at[p], q0s.at[p], q0r.at[p], dev_c)

    def x_first(p):
        return p in (1, 7)

    def q_a(p):
        src, dev = (r0q.at[p, :, 1 - x], dev_x) if x_first(p) else (r0q.at[p, :, :, 1 - y], dev_y)
        return remote(src, r1q.at[p], q1s.at[p], q1r.at[p], dev)

    def q_b(p):
        src, dev = (r1q.at[p, :, 1 - y], dev_y) if x_first(p) else (r1q.at[p, :, 1 - x], dev_x)
        return remote(src, r2q.at[p], q2s.at[p], q2r.at[p], dev)

    def q_1(p):
        return remote(r2q.at[p], r3q.at[p], q3s.at[p], q3r.at[p], dev_1)

    def q_2(p):
        return remote(r2q.at[p, 1 - zh], r4q.at[p], q4s.at[p], q4r.at[p], dev_2)

    def take_chunk(p):
        q_core(p).wait_recv()
        r0q[p] = r0q[p] + gu[p // 2, p % 2, :, c]

    def do_q_a(*which):
        for p in which:
            take_chunk(p)
            q_a(p).start()

    def do_q_b(*which):
        for p in which:
            q_a(p).wait_recv()
            r1q[p] = r1q[p] + (r0q[p, :, x] if x_first(p) else r0q[p, :, :, y])
            q_b(p).start()

    def do_q_1(*which):
        for p in which:
            q_b(p).wait_recv()
            r2q[p] = r2q[p] + r1q[p, :, y if x_first(p) else x]

            @pl.when(zl != c)
            def _(p=p):
                q_1(p).start()

    def do_q_2(*which):
        @pl.when(zl == c)
        def _():
            for p in which:
                q_1(p).wait_recv()
                r2q[p] = r2q[p] + r3q[p]
                q_2(p).start()

    def q_plane(n):
        src = (r0q.at[5, :, 1 - x, y], r0q.at[5, :, x, 1 - y], r0q.at[5, :, 1 - x, 1 - y])[n]
        dst = (r1q.at[5, :, 0], r1q.at[5, :, 1], r2q.at[5])[n]
        return remote(src, dst, qps.at[n], qpr.at[n], (dev_x, dev_y, dev_xy)[n])

    def q_line(n):
        src = (r0q.at[5, 1 - zh, x, y], r0q.at[5, zh, x, y], r0q.at[5, 1 - zh, x, y])[n]
        dst = (r3q.at[5, 0], r3q.at[5, 1], r4q.at[5])[n]
        return remote(src, dst, qls.at[n], qlr.at[n], (dev_2, dev_1, (flip(6), b))[n])

    def do_q_plane():
        take_chunk(5)
        for n in range(3):
            q_plane(n).start()

    def do_q_line():
        for n in range(3):
            q_plane(n).wait_recv()
        total = r0q[5, :, x, y].astype(F32) + r1q[5, :, 0].astype(F32) + r1q[5, :, 1].astype(F32) + r2q[5].astype(F32)
        r0q[5, :, x, y] = total.astype(BF)

        @pl.when(zl == c)
        def _():
            q_line(0).start()

        @pl.when(zl != c)
        def _():
            q_line(1).start()
            q_line(2).start()

    def q_chunk(p):
        right = jnp.concatenate(
            [proj[:, pl.ds(pl.multiple_of(w * width + p * 128, 128), 128)] for w in range(3)], axis=1
        )
        put_chunk(p, dot_nn(n2t[...], right))

    for i in range(4):
        u_core(i).wait_send()
    for h in range(2):
        put_chunk(pairs + h, dot_nn(att_t[:, pl.ds(0, wide)], n2[:, pl.ds(h * 384, 384)]))

    minus = jnp.where(lanes_of((rows, 128)) < 32, -1.0, 0.0).astype(BF)
    factor = HEAD_DIM ** (-0.5)

    def chosen(head):
        lane = lanes_of((1, 128))
        return jnp.where((lane == head) | (lane == head + 16), 1.0, 0.0).astype(BF)

    def values_of(at):
        return jnp.concatenate([proj[:, pl.ds(2 * width + at, 128)], minus], axis=1)

    def parts_at(p):
        return acc_full.at[:, pl.ds(pl.multiple_of(lax.rem(p, 3) * 256, 256), 256)]

    def token_queries(p):
        at = pl.multiple_of(p * 128, 128)
        values = values_of(at)
        qp = proj[pl.ds(0, tok), pl.ds(at, 128)]
        gp = gatt[pl.ds(0, tok), pl.ds(at, 128)]
        ups = jnp.concatenate([gp * even_one, gp * odd_one], axis=0)
        dd = qaug[pl.ds(0, tok), :]
        inner = jnp.concatenate([dd * chosen(2 * p), dd * chosen(2 * p + 1)], axis=0)
        own = pl.ds(0, 2 * tok)
        parts_at(p)[:, 128:] = dot_nn(probs[p, :, own], ups)
        for first in range(0, 2 * tok, 256):
            right = jnp.concatenate([ups[first : first + 256], inner[first : first + 256]], axis=1)
            grad_w = dot_nt(values, right)
            here = probs[p, :, pl.ds(first, 256)].astype(F32)
            probs[p, :, pl.ds(first, 256)] = (here * grad_w).astype(BF)
        parts_at(p)[:, :128] = dot_nn(probs[p, :, own], jnp.concatenate([qp * even, qp * odd], axis=0))
        low = dot_nn(kvt[pl.ds(at, HEAD_DIM), pl.ds(0, rows)], probs[p, :, pl.ds(0, tok)])
        upper = dot_nn(
            kvt[pl.ds(pl.multiple_of(at + HEAD_DIM, HEAD_DIM), HEAD_DIM), pl.ds(0, rows)],
            probs[p, :, pl.ds(tok, tok)],
        )
        grad_q = jnp.concatenate([low, upper], axis=0) * factor
        proj[pl.ds(0, tok), pl.ds(at, 128)] = jnp.transpose(grad_q).astype(BF)

    def glob_queries(p):
        at = pl.multiple_of(p * 128, 128)
        qg = proj[pl.ds(tok, glob), pl.ds(at, 128)]
        gg = rcv2[:, pl.ds(at, 128)]
        dg = rcv2[:, pl.ds(width, 128)]
        ups = jnp.concatenate([gg * even_one, gg * odd_one], axis=0)
        inner = jnp.concatenate([dg * chosen(2 * p), dg * chosen(2 * p + 1)], axis=0)
        weights = probs[p, :, pl.ds(2 * tok, 2 * glob)]
        grad_v = parts_at(p)[:, 128:] + dot_nn(weights, ups)
        grad_w = dot_nt(values_of(at), jnp.concatenate([ups, inner], axis=1))
        grad_s = (weights.astype(F32) * grad_w).astype(BF)
        grad_k = parts_at(p)[:, :128] + dot_nn(grad_s, jnp.concatenate([qg * even, qg * odd], axis=0))
        own = dot_nn(kvt[pl.ds(at, 128), pl.ds(0, rows)], grad_s)
        own = jnp.where(first_head, own[:, :glob], own[:, glob:]) * factor
        proj[pl.ds(tok, glob), pl.ds(at, 128)] = jnp.transpose(own).astype(BF)
        proj[:, pl.ds(width + at, 128)] = grad_k.astype(BF)
        proj[:, pl.ds(2 * width + at, 128)] = grad_v.astype(BF)

    def at_steps(p, steps):
        for step, act in steps:

            @pl.when(p == step)
            def _(act=act):
                act()

    def first_pairs(p, carry):
        token_queries(p)
        return carry

    def middle_pairs(p, carry):
        token_queries(p)
        glob_queries(p - 2)
        q_chunk(p - 2)
        at_steps(p, (
            (2, lambda: (do_d_1(3), do_u_b(3), do_d_x(0))),
            (3, lambda: (do_q_a(0), do_u_y(0), do_q_b(6, 7))),
            (4, lambda: (do_q_a(1), do_d_x(1), do_u_y(1))),
            (5, lambda: (do_q_a(2), do_q_b(0), do_u_2(0), do_q_1(6, 7))),
        ))
        return carry

    def last_pairs(p, carry):
        glob_queries(p)
        q_chunk(p)
        at_steps(p, ((4, lambda: (do_q_a(3), do_q_b(1), do_d_2())), (5, lambda: (do_q_a(4), do_u_2(1), do_q_2(6, 7), do_q_1(0)))))
        return carry

    lax.fori_loop(0, 2, first_pairs, 0)
    do_d_1(2)
    do_u_b(2)
    do_q_a(6, 7)
    for copy in sends2:
        copy.wait()
    sends_o = []
    for k in peers:
        copy = remote(
            outs.at[pl.ds(tok, slots)], o_gout.at[pl.ds(my_slots, slots)], gos.at[k], gor.at[k], (flip(k), b)
        )
        copy.start()
        sends_o.append(copy)

    lax.fori_loop(2, pairs, middle_pairs, 0)
    lax.fori_loop(pairs - 2, pairs, last_pairs, 0)

    def first_pull(first):
        grad, gain_term, shift_term = norm_pull(
            sec[pl.ds(first, 128), :].astype(F32), attn_gain, gn2[pl.ds(first, 128), :]
        )
        n2[pl.ds(first, 128), :] = (grad + x2[pl.ds(first, 128), :]).astype(BF)
        vec[pl.ds(0, 1), :] += gain_term
        vec[pl.ds(1, 1), :] += shift_term

    gnm = wu
    gnm[pl.ds(0, glob), :] = dot_nt(proj[pl.ds(tok, glob), :], wq[...]).astype(BF)
    sends3 = []
    for k in (1, 2, 3):
        other = flip(k)
        for h in range(2):
            at = pl.multiple_of((4 * h + lax.rem(other, 4)) * slots, slots)
            copy = remote(
                gnm.at[pl.ds(at, slots)], rcv3.at[k - 1, h], m3s.at[2 * k - 2 + h], m3r.at[2 * k - 2 + h], (other, b)
            )
            copy.start()
            sends3.append(copy)
    do_q_plane()
    gn2[pl.ds(half, half), :] = dot_nt(proj[pl.ds(half, half), :], wq[...])
    for r in range(half, tok, 128):
        first_pull(r)
    do_q_b(2, 3)
    do_q_1(1)
    do_q_2(0)
    for copy in sends3:
        copy.wait()

    def slots_of(h):
        mine = gnm[pl.ds(pl.multiple_of((4 * h + lax.rem(s, 4)) * slots, slots), slots), :].astype(F32)
        for k in (1, 2, 3):
            mine = mine + rcv3[k - 1, h].astype(F32)
        return mine

    gsum[...] = slots_of(1 - zh).astype(BF)
    line3 = remote(gsum, rcv3b, m3s.at[6], m3r.at[6], dev_2)
    line3.start()

    gn2[pl.ds(0, half), :] = dot_nt(proj[pl.ds(0, half), :], wq[...])
    for r in range(0, half, 128):
        first_pull(r)
    keep = pltpu.make_async_copy(n2.at[pl.ds(0, half)], o_tgrad.at[pl.ds(half, half)], osem.at[2])
    keep.start()
    do_q_line()
    do_q_b(4)
    do_q_1(2, 3)
    do_q_2(1)

    line3.wait()
    grad, gain_term, shift_term = norm_pull(
        sec[pl.ds(pl.multiple_of(tok + my_slots, slots), slots), :].astype(F32),
        glob_gain,
        slots_of(zh) + rcv3b[...].astype(F32),
    )
    vec[pl.ds(2, 1), :] += gain_term
    vec[pl.ds(3, 1), :] += shift_term
    n2[pl.ds(tok, slots), :] = (grad + x2[pl.ds(tok, slots), :]).astype(BF)
    line_g = remote(n2.at[pl.ds(tok, slots)], gall, ggs_s.at[0], ggs_r.at[0], dev_2)
    line_g.start()

    share = vec.shape[1] // n_seq
    for j in range(n_seq):
        rolled = vec[pl.ds(0, 8), :]
        if j:
            rolled = pltpu.roll(rolled, vec.shape[1] - share * j, 1)
        vmsg[j, pl.ds(0, 8), :] = rolled[:, :128]
        for m in range(chunk // 128):
            vmsg[j, pl.ds(8 + m, 1), :] = vec[pl.ds(8 + j // 2, 1), pl.ds((j % 2) * chunk + m * 128, 128)]
    sends_v = []
    for k in peers:
        copy = remote(vmsg.at[flip(k)], vrcv.at[k - 1], vs.at[k], vr.at[k], (flip(k), b))
        copy.start()
        sends_v.append(copy)

    do_q_1(4)
    do_q_2(2, 3)
    back = remote(
        n2.at[pl.ds(half, half)], o_tgrad.at[pl.ds(0, half)], hs2.at[0], hr2.at[0],
        (lax.rem(s + 1, n_seq), b),
    )
    back.start()

    d_2().wait_recv()
    acc[pl.ds(96, 192), pl.ds(0, 384)] = r4d[...].astype(F32) + r3d[zh].astype(F32)
    for j in range(2):
        u_2(j).wait_recv()
    last = r4u[...].astype(F32) + r3u[:, zh].astype(F32)
    acc[pl.ds(0, 96), pl.ds(0, 384)] = last[0].reshape(96, 384)
    acc[pl.ds(0, 96), pl.ds(384, 384)] = last[1].reshape(96, 384)
    results = [
        pltpu.make_async_copy(acc.at[pl.ds(0, 96)], o_up, osem.at[4]),
        pltpu.make_async_copy(acc.at[pl.ds(96, 192), pl.ds(0, 384)], o_down, osem.at[5]),
    ]
    for copy in results:
        copy.start()

    line_g.wait()
    far_slots = pl.multiple_of(flip(4) * slots, slots)
    sends_g = []
    for n, (src, at) in enumerate(((n2.at[pl.ds(tok, slots)], my_slots), (gall, far_slots))):
        copy = pltpu.make_async_copy(src, o_ggrad.at[pl.ds(at, slots)], gsem.at[n])
        copy.start()
        sends_g.append(copy)
        for k in (1, 2, 3):
            copy = remote(
                src, o_ggrad.at[pl.ds(at, slots)], ggs_s.at[2 * k + n - 1], ggs_r.at[2 * k + n - 1], (flip(k), b)
            )
            copy.start()
            sends_g.append(copy)

    for copy in sends_v:
        copy.wait()
    vsum[0] = vmsg[s]
    for k in peers:
        vsum[0] = vsum[0] + vrcv[k - 1]
    batch_peers = (dev_c, dev_y, dev_cy)
    sends_b = []
    for n, dev in enumerate(batch_peers):
        copy = remote(vsum.at[0], vsum.at[1 + n], vbs.at[n], vbr.at[n], dev)
        copy.start()
        sends_b.append(copy)

    do_q_2(4)

    def final(n, slot):
        return remote(fmsg.at[n - 1], frcv.at[slot], fs.at[n], fr.at[n], (s, flip_b(n)))

    def flip_b(n):
        return (b, dev_c[1], dev_y[1], dev_cy[1])[n]

    @pl.when(zl == c)
    def _():
        for p in (6, 7, 0, 1, 2, 3, 4):
            q_2(p).wait_recv()
            r4q[p] = r4q[p] + r2q[p, zh]
        for n in range(3):
            q_line(n).wait_recv()
        r4q[5] = (
            r0q[5, zh, x, y].astype(F32) + r3q[5, 0].astype(F32) + r3q[5, 1].astype(F32) + r4q[5].astype(F32)
        ).astype(BF)

        def columns_of(bb):
            first = (bb * 576 - 64 * lax.rem(bb, 2)) // 128
            tiles = []
            for m in range(5):
                tile = first + m
                tiles.append(r4q[lax.rem(tile, 6), :, pl.ds(pl.multiple_of(tile // 6 * 128, 128), 128)])
            first = (bb * 192 - 64 * lax.rem(bb, 2)) // 128
            for m in range(2):
                tile = first + m
                tiles.append(r4q[pairs + tile // 3, :, pl.ds(pl.multiple_of(lax.rem(tile, 3) * 128, 128), 128)])
            return jnp.concatenate(tiles, axis=1)

        for n in (3, 2, 1):
            fmsg[n - 1] = columns_of(flip_b(n))
            final(n, y).start()
        frcv[y] = columns_of(b)

    for copy in sends_b:
        copy.wait()
    shared = vsum[0] + vsum[1] + (vsum[2] + vsum[3])
    o_vec[...] = shared[0:8, :share]
    for m in range(chunk // 128):
        o_ub[:, pl.ds(m * 128, 128)] = shared[8 + m : 9 + m, :]

    @pl.when(zl == c)
    def _():
        final(2, 1 - y).wait_recv()

    @pl.when(zl != c)
    def _():
        final(1, y).wait_recv()
        final(3, 1 - y).wait_recv()

    for yy in range(2):
        block = frcv[yy].astype(F32)
        main = block[:, :640]
        acc[pl.ds(288 + yy * 48, 48), pl.ds(0, 640)] = jnp.where(c == 1, pltpu.roll(main, 576, 1), main)
        main = block[:, 640:]
        acc[pl.ds(384 + yy * 48, 48), pl.ds(0, 256)] = jnp.where(c == 1, pltpu.roll(main, 192, 1), main)
    for copy in (
        pltpu.make_async_copy(acc.at[pl.ds(288, 96), pl.ds(0, 640)], o_qkv, osem.at[6]),
        pltpu.make_async_copy(acc.at[pl.ds(384, 96), pl.ds(0, 256)], o_wout, osem.at[7]),
    ):
        copy.start()
        results.append(copy)

    for i in range(4):
        d_core(i).wait_send()
        d_y(i).wait_send()
        d_1(i).wait_send()
        u_a(i, i == 0).wait_send()
        u_b(i).wait_send()
    for h in range(2):
        d_x(h).wait_send()
    d_2().wait_send()
    for j in range(2):
        u_y(j).wait_send()
        u_2(j).wait_send()
    for p in range(8):
        q_core(p).wait_send()
        if p != 5:
            q_a(p).wait_send()
            q_b(p).wait_send()
    for n in range(3):
        q_plane(n).wait_send()

    @pl.when(zl == c)
    def _():
        q_line(0).wait_send()
        for n in (1, 2, 3):
            final(n, y).wait_send()
        for p in (6, 7, 0, 1, 2, 3, 4):
            q_2(p).wait_send()

    @pl.when(zl != c)
    def _():
        for n in (1, 2):
            q_line(n).wait_send()
        for p in (6, 7, 0, 1, 2, 3, 4):
            q_1(p).wait_send()

    back.wait()
    keep.wait()
    out_copy.wait()
    own_out.wait()
    for copy in results:
        copy.wait()
    for copy in sends_o + sends_g:
        copy.wait()


def fits(tokens, global_states, w_qkv, w_up):
    return (
        lax.axis_size("seq") == 8
        and lax.axis_size("batch") == 4
        and tokens.shape == (1, BLOCK, HEADS * HEAD_DIM)
        and global_states.shape == (1, 128, HEADS * HEAD_DIM)
        and w_qkv.shape == (HEADS * HEAD_DIM, 3 * HEADS * HEAD_DIM)
        and w_up.shape == (HEADS * HEAD_DIM, 3072)
    )


def finish_kernel(*refs):
    ins, outs = refs[:10], refs[10:]
    for i in range(8):
        outs[i][...] = ins[i][:, : outs[i].shape[1]]
    for i in range(7):
        outs[8 + i][...] = ins[8][i, :]
    outs[15][...] = ins[9][0, :]


def fused(
    tokens, global_states, token_seg, global_seg, attn_gain, attn_shift, glob_gain, glob_shift, w_qkv, w_out,
    ffn_gain, ffn_shift, w_up, up_bias, w_down, down_bias, out_cotangent, global_cotangent,
):
    tok, width = tokens.shape[1:]
    glob = global_states.shape[1]
    hidden = w_up.shape[1]
    n_seq, n_batch = lax.axis_size("seq"), lax.axis_size("batch")
    rows, slots = tok + glob, glob // n_seq
    wide = tok + slots
    chunk, part, side = hidden // n_seq, width // n_seq, width // n_batch
    pairs = HEADS // 2
    eighth = (2, 2, 2)
    dma = pltpu.SemaphoreType.DMA

    def any_space():
        return pl.BlockSpec(memory_space=pl.ANY)

    def vmem():
        return pl.BlockSpec(memory_space=pltpu.VMEM)

    def low(*shape):
        return pltpu.VMEM(shape, BF)

    def full(*shape):
        return pltpu.VMEM(shape, F32)

    scratch = [
        low(rows, width), low(rows, width), low(rows, 3 * width), low(width, width),
        low(pairs, rows, 2 * tok + 2 * glob), low(width, tok + 128), low(wide, width), full(wide, width),
        low(wide, width), low(width, tok + 128), low(wide, width), low(width, tok + 128),
        full(rows, width), full(rows, width), low(wide, width), low(rows, 128), low(rows, 128),
        low(width, 3 * width), low(width, width), low(width, width), low(width, width),
        full(128, glob), full(16, tok), full(glob, width), low(glob, width + 128),
        low(n_seq, slots, width + 128), low(glob, width + 128),
        low(3, 2, slots, width), low(slots, width), low(slots, width), low(slots, width),
        full(16, width), full(n_seq, 16, 128), full(n_seq - 1, 16, 128), full(4, 16, 128), full(4, width),
        low(4, 2, 2, 2, side, chunk), low(4, 2, 2, side, chunk), low(4, 2, side, chunk), low(2, 2, side, chunk),
        low(2, side, chunk), low(side, chunk),
        low(4, 2, *eighth, 2, part // 2, chunk), low(4, *eighth, 2, part // 2, chunk), low(4, 2, 2, 2, part // 2, chunk),
        low(2, 2, 2, 2, part // 2, chunk), low(2, 2, 2, part // 2, chunk), low(2, 2, part // 2, chunk),
        low(8, 2, 2, 2, part // 2, chunk), low(8, 2, 2, part // 2, chunk), low(8, 2, part // 2, chunk),
        low(8, 2, part // 2, chunk), low(8, part // 2, chunk),
        low(3, part // 2, 896), low(2, part // 2, 896),
        full(wide, 256), full(wide, 256),
        dma((8,)), dma((2, 2)), dma((1,)), dma((1,)),
        *[dma((8,)) for _ in range(10)], dma((9,)), dma((9,)),
        *[dma((4,)) for _ in range(10)], *[dma((4,)) for _ in range(10)], *[dma((8,)) for _ in range(10)],
        *[dma((3,)) for _ in range(6)], dma((4,)), dma((4,)), dma((1,)), dma((1,)), dma((8,)), dma((2,)),
    ]

    results = pl.pallas_call(
        layer_kernel,
        out_shape=[
            jax.ShapeDtypeStruct((tok, width), BF),
            jax.ShapeDtypeStruct((glob, width), BF),
            jax.ShapeDtypeStruct((tok, width), BF),
            jax.ShapeDtypeStruct((glob, width), BF),
            jax.ShapeDtypeStruct((part, 640), F32),
            jax.ShapeDtypeStruct((part, 256), F32),
            jax.ShapeDtypeStruct((part, 2 * chunk), F32),
            jax.ShapeDtypeStruct((side, chunk), F32),
            jax.ShapeDtypeStruct((8, part), F32),
            jax.ShapeDtypeStruct((1, chunk), F32),
        ],
        in_specs=[any_space(), any_space(), vmem(), vmem(), vmem(), vmem(), vmem(), vmem(), any_space(), any_space(),
                  vmem(), vmem(), any_space(), vmem(), any_space(), vmem(), any_space(), any_space()],
        out_specs=[any_space()] * 8 + [vmem()] * 2,
        scratch_shapes=scratch,
        compiler_params=pltpu.CompilerParams(
            collective_id=0, has_side_effects=True, vmem_limit_bytes=64 * 1024 * 1024
        ),
        name="layer",
    )(
        tokens[0], global_states[0], token_seg, global_seg, attn_gain, attn_shift, glob_gain,
        glob_shift, w_qkv, w_out, ffn_gain, ffn_shift, w_up, up_bias, w_down, down_bias,
        out_cotangent[0], global_cotangent[0],
    )
    *large, vectors, ub = results
    columns = {4: 3 * side, 5: side}
    results = pl.pallas_call(
        finish_kernel,
        out_shape=[
            jax.ShapeDtypeStruct((one.shape[0], columns.get(i, one.shape[1])), one.dtype) for i, one in enumerate(large)
        ]
        + [jax.ShapeDtypeStruct((part,), F32)] * 7
        + [jax.ShapeDtypeStruct((chunk,), F32)],
        in_specs=[vmem()] * 10,
        out_specs=[vmem()] * 16,
        name="results",
    )(*large, vectors, ub)
    out, gout, tgrad, ggrad, g_qkv, g_out, g_up, g_down, *g_vec, g_ub = results
    return (
        out[None], gout[None], tgrad[None], ggrad[None], g_vec[0], g_vec[1], g_vec[2], g_vec[3], g_qkv, g_out,
        g_vec[4], g_vec[5], g_up, g_ub, g_down.T, g_vec[6],
    )


def local(tokens, global_states, token_seg, global_seg, *rest):
    w_qkv, w_up = rest[4], rest[8]
    way = fused if fits(tokens, global_states, w_qkv, w_up) else general
    return way(tokens, global_states, token_seg, global_seg, *rest)


def solution(mesh):
    placed = (
        P("batch", "seq", None),
        P("batch", None, None),
        P("batch", "seq"),
        P("batch", None),
        P(),
        P(),
        P(),
        P(),
        P(),
        P(),
        P(),
        P(),
        P(),
        P(),
        P(),
        P(),
        P("batch", "seq", None),
        P("batch", None, None),
    )
    return jax.shard_map(
        local,
        mesh=mesh,
        in_specs=placed,
        out_specs=(
            P("batch", "seq", None),
            P("batch", None, None),
            P("batch", "seq", None),
            P("batch", None, None),
            P("seq"),
            P("seq"),
            P("seq"),
            P("seq"),
            P("seq", "batch"),
            P("seq", "batch"),
            P("seq"),
            P("seq"),
            P("seq", "batch"),
            P("seq"),
            P("seq", "batch"),
            P("seq"),
        ),
        check_vma=False,
    )
```

```python
import functools

import jax
import jax.numpy as jnp
from jax import lax
from jax.experimental import pallas as pl
from jax.experimental.pallas import tpu as pltpu
from jax.sharding import PartitionSpec as P

HEADS = 12
HEAD_DIM = 64
BLOCK = 512


EPS = 1e-05
NEGATIVE = -1e30


def from_behind(block, axis, distance):
    devices = range(lax.axis_size(axis))
    route = [((i - distance) % len(devices), i) for i in devices]
    return lax.ppermute(block, axis, route)


def norm_rows(source, scaling, offset):
    center = jnp.mean(source, axis=-1, keepdims=True)
    spread = source - center
    variance = jnp.mean(spread * spread, axis=-1, keepdims=True)
    return spread * lax.rsqrt(variance + EPS) * scaling + offset


def norm_back(source, scaling, offset, upstream):
    _, pullback = jax.vjp(norm_rows, source, scaling, offset)
    return pullback(upstream)


def project(former, latter):
    return jnp.einsum("rsd,de->rse", former, latter, preferred_element_type=jnp.float32)


def project_back(former, latter):
    return jnp.einsum("rse,de->rsd", former, latter, preferred_element_type=jnp.float32)


def outer_sum(former, latter):
    return jnp.einsum("rsd,rse->de", former, latter, preferred_element_type=jnp.float32)


def gelu_exact(hidden):
    return jax.nn.gelu(hidden, approximate=False)


def ffn_forward(state, ffn_gain, ffn_shift, w_up, up_bias, w_down, down_bias):
    normed = norm_rows(state, ffn_gain, ffn_shift).astype(jnp.bfloat16)
    hidden = project(normed, w_up) + up_bias
    active = gelu_exact(hidden).astype(jnp.bfloat16)
    result = state + project(active, w_down) + down_bias
    return (result, (normed, hidden, active))


def ffn_backward(state, stored, upstream, ffn_gain, ffn_shift, w_up, w_down):
    normed, hidden, active = stored
    upstream_low = upstream.astype(jnp.bfloat16)
    grad_down = outer_sum(active, upstream_low)
    grad_down_bias = jnp.sum(upstream, axis=(0, 1))
    grad_active = project_back(upstream_low, w_down)
    _, gelu_pull = jax.vjp(gelu_exact, hidden)
    grad_hidden = gelu_pull(grad_active)[0].astype(jnp.bfloat16)
    grad_up = outer_sum(normed, grad_hidden)
    grad_up_bias = jnp.sum(grad_hidden.astype(jnp.float32), axis=(0, 1))
    grad_normed = project_back(grad_hidden, w_up)
    grad_state, grad_gain, grad_shift = norm_back(state, ffn_gain, ffn_shift, grad_normed)
    return (
        upstream + grad_state,
        (grad_gain, grad_shift, grad_up, grad_up_bias, grad_down, grad_down_bias),
    )


def local_scores(queries, keys_near, seg_near, keys_far, seg_far):
    scaling = HEAD_DIM ** (-0.5)
    near_scores = (
        jnp.einsum("rnqhd,rnkhd->rnhqk", queries, keys_near, preferred_element_type=jnp.float32)
        * scaling
    )
    far_scores = (
        jnp.einsum("rnqhd,rghd->rnhqg", queries, keys_far, preferred_element_type=jnp.float32)
        * scaling
    )
    near_open = (seg_near[:, :, :, None] == seg_near[:, :, None, :])[:, :, None]
    far_open = (seg_near[:, :, :, None] == seg_far[:, None, None, :])[:, :, None]
    return (jnp.where(near_open, near_scores, NEGATIVE), jnp.where(far_open, far_scores, NEGATIVE))


def local_forward(queries, keys_near, values_near, seg_near, keys_far, values_far, seg_far):
    near_scores, far_scores = local_scores(queries, keys_near, seg_near, keys_far, seg_far)
    maxima = jnp.maximum(jnp.max(near_scores, axis=-1), jnp.max(far_scores, axis=-1))
    near_exp = jnp.exp(near_scores - maxima[..., None])
    far_exp = jnp.exp(far_scores - maxima[..., None])
    totals = jnp.sum(near_exp, axis=-1) + jnp.sum(far_exp, axis=-1)
    near_weights = (near_exp / totals[..., None]).astype(jnp.bfloat16)
    far_weights = (far_exp / totals[..., None]).astype(jnp.bfloat16)
    mixed_out = jnp.einsum(
        "rnhqk,rnkhd->rnqhd", near_weights, values_near, preferred_element_type=jnp.float32
    )
    mixed_out = mixed_out + jnp.einsum(
        "rnhqg,rghd->rnqhd", far_weights, values_far, preferred_element_type=jnp.float32
    )
    return (mixed_out, maxima + jnp.log(totals))


def local_backward(
    queries, keys_near, values_near, seg_near, keys_far, values_far, seg_far, logsum, upstream
):
    scaling = HEAD_DIM ** (-0.5)
    near_scores, far_scores = local_scores(queries, keys_near, seg_near, keys_far, seg_far)
    near_weights = jnp.exp(near_scores - logsum[..., None])
    far_weights = jnp.exp(far_scores - logsum[..., None])
    near_grad = jnp.einsum(
        "rnqhd,rnkhd->rnhqk", upstream, values_near, preferred_element_type=jnp.float32
    )
    far_grad = jnp.einsum(
        "rnqhd,rghd->rnhqg", upstream, values_far, preferred_element_type=jnp.float32
    )
    row_inner = jnp.sum(near_weights * near_grad, axis=-1) + jnp.sum(
        far_weights * far_grad, axis=-1
    )
    near_score_grad = (near_weights * (near_grad - row_inner[..., None])).astype(jnp.bfloat16)
    far_score_grad = (far_weights * (far_grad - row_inner[..., None])).astype(jnp.bfloat16)
    grad_queries = jnp.einsum(
        "rnhqk,rnkhd->rnqhd", near_score_grad, keys_near, preferred_element_type=jnp.float32
    )
    grad_queries = scaling * (
        grad_queries
        + jnp.einsum(
            "rnhqg,rghd->rnqhd", far_score_grad, keys_far, preferred_element_type=jnp.float32
        )
    )
    grad_keys = scaling * jnp.einsum(
        "rnhqk,rnqhd->rnkhd", near_score_grad, queries, preferred_element_type=jnp.float32
    )
    grad_values = jnp.einsum(
        "rnhqk,rnqhd->rnkhd",
        near_weights.astype(jnp.bfloat16),
        upstream,
        preferred_element_type=jnp.float32,
    )
    grad_keys_far = scaling * jnp.einsum(
        "rnhqg,rnqhd->rghd", far_score_grad, queries, preferred_element_type=jnp.float32
    )
    grad_values_far = jnp.einsum(
        "rnhqg,rnqhd->rghd",
        far_weights.astype(jnp.bfloat16),
        upstream,
        preferred_element_type=jnp.float32,
    )
    return (grad_queries, grad_keys, grad_values, grad_keys_far, grad_values_far)


def global_scores(glob_queries, glob_keys, glob_seg, key_rows, seg_tokens):
    scaling = HEAD_DIM ** (-0.5)
    remote_scores = (
        jnp.einsum("rghd,rshd->rhgs", glob_queries, key_rows, preferred_element_type=jnp.float32)
        * scaling
    )
    own_scores = (
        jnp.einsum("rghd,rjhd->rhgj", glob_queries, glob_keys, preferred_element_type=jnp.float32)
        * scaling
    )
    remote_open = glob_seg[:, None, :, None] == seg_tokens[:, None, None, :]
    own_open = glob_seg[:, None, :, None] == glob_seg[:, None, None, :]
    return (
        jnp.where(remote_open, remote_scores, NEGATIVE),
        jnp.where(own_open, own_scores, NEGATIVE),
    )


def general(
    tokens,
    global_states,
    token_seg,
    global_seg,
    attn_gain,
    attn_shift,
    glob_gain,
    glob_shift,
    w_qkv,
    w_out,
    ffn_gain,
    ffn_shift,
    w_up,
    up_bias,
    w_down,
    down_bias,
    out_cotangent,
    global_cotangent,
):
    row_count, tok_count, model_width = tokens.shape
    glob_count = global_states.shape[1]
    half_block = BLOCK // 2
    block_count = tok_count // BLOCK
    seq_devices = lax.axis_size("seq")
    scaling = HEAD_DIM ** (-0.5)
    low_type = jnp.bfloat16
    arrived = from_behind(tokens[:, :half_block], "seq", -1)
    sectioned = jnp.concatenate([tokens[:, half_block:], arrived], axis=1).astype(jnp.float32)
    glob_state = global_states.astype(jnp.float32)
    normed = norm_rows(sectioned, attn_gain, attn_shift).astype(low_type)
    glob_normed = norm_rows(glob_state, glob_gain, glob_shift).astype(low_type)
    projected = (
        project(normed, w_qkv).astype(low_type).reshape(row_count, tok_count, 3, HEADS, HEAD_DIM)
    )
    glob_proj = (
        project(glob_normed, w_qkv)
        .astype(low_type)
        .reshape(row_count, glob_count, 3, HEADS, HEAD_DIM)
    )
    queries = projected[:, :, 0]
    key_rows = projected[:, :, 1]
    value_rows = projected[:, :, 2]
    glob_queries = glob_proj[:, :, 0]
    glob_keys = glob_proj[:, :, 1]
    glob_values = glob_proj[:, :, 2]
    block_shape = (row_count, block_count, BLOCK, HEADS, HEAD_DIM)
    block_queries = queries.reshape(block_shape)
    block_keys = key_rows.reshape(block_shape)
    block_values = value_rows.reshape(block_shape)
    block_seg = token_seg.reshape(row_count, block_count, BLOCK)
    local_out, local_logsum = local_forward(
        block_queries, block_keys, block_values, block_seg, glob_keys, glob_values, global_seg
    )
    remote_scores, own_scores = global_scores(
        glob_queries, glob_keys, global_seg, key_rows, token_seg
    )
    maxima = jnp.maximum(
        lax.pmax(jnp.max(remote_scores, axis=-1), "seq"), jnp.max(own_scores, axis=-1)
    )
    remote_total = jnp.sum(jnp.exp(remote_scores - maxima[..., None]), axis=-1)
    totals = lax.psum(remote_total, "seq") + jnp.sum(
        jnp.exp(own_scores - maxima[..., None]), axis=-1
    )
    remote_weights = (jnp.exp(remote_scores - maxima[..., None]) / totals[..., None]).astype(
        low_type
    )
    own_weights = (jnp.exp(own_scores - maxima[..., None]) / totals[..., None]).astype(low_type)
    remote_part = jnp.einsum(
        "rhgs,rshd->rghd", remote_weights, value_rows, preferred_element_type=jnp.float32
    )
    glob_out = lax.psum(remote_part, "seq")
    glob_out = glob_out + jnp.einsum(
        "rhgj,rjhd->rghd", own_weights, glob_values, preferred_element_type=jnp.float32
    )
    glob_logsum = maxima + jnp.log(totals)
    attended = local_out.reshape(row_count, tok_count, model_width).astype(low_type)
    glob_attended = glob_out.reshape(row_count, glob_count, model_width).astype(low_type)
    attn_sum = sectioned + project(attended, w_out)
    glob_sum = glob_state + project(glob_attended, w_out)
    result, stored = ffn_forward(attn_sum, ffn_gain, ffn_shift, w_up, up_bias, w_down, down_bias)
    glob_result, glob_stored = ffn_forward(
        glob_sum, ffn_gain, ffn_shift, w_up, up_bias, w_down, down_bias
    )
    grad_attn_sum, tok_ffn = ffn_backward(
        attn_sum, stored, out_cotangent.astype(jnp.float32), ffn_gain, ffn_shift, w_up, w_down
    )
    grad_glob_sum, glob_ffn = ffn_backward(
        glob_sum,
        glob_stored,
        global_cotangent.astype(jnp.float32),
        ffn_gain,
        ffn_shift,
        w_up,
        w_down,
    )
    branch_low = grad_attn_sum.astype(low_type)
    glob_branch_low = grad_glob_sum.astype(low_type)
    grad_out_all = (
        outer_sum(attended, branch_low) + outer_sum(glob_attended, glob_branch_low) / seq_devices
    )
    upstream_mix = project_back(branch_low, w_out).astype(low_type).reshape(block_shape)
    glob_upstream = (
        project_back(glob_branch_low, w_out)
        .astype(low_type)
        .reshape(row_count, glob_count, HEADS, HEAD_DIM)
    )
    remote_exact = jnp.exp(remote_scores - glob_logsum[..., None])
    own_exact = jnp.exp(own_scores - glob_logsum[..., None])
    remote_grad = jnp.einsum(
        "rghd,rshd->rhgs", glob_upstream, value_rows, preferred_element_type=jnp.float32
    )
    own_grad = jnp.einsum(
        "rghd,rjhd->rhgj", glob_upstream, glob_values, preferred_element_type=jnp.float32
    )
    row_inner = lax.psum(jnp.sum(remote_exact * remote_grad, axis=-1), "seq")
    row_inner = row_inner + jnp.sum(own_exact * own_grad, axis=-1)
    remote_score_grad = (remote_exact * (remote_grad - row_inner[..., None])).astype(low_type)
    own_score_grad = (own_exact * (own_grad - row_inner[..., None])).astype(low_type)
    remote_queries = scaling * jnp.einsum(
        "rhgs,rshd->rghd", remote_score_grad, key_rows, preferred_element_type=jnp.float32
    )
    tok_keys_extra = scaling * jnp.einsum(
        "rhgs,rghd->rshd", remote_score_grad, glob_queries, preferred_element_type=jnp.float32
    )
    tok_values_extra = jnp.einsum(
        "rhgs,rghd->rshd",
        remote_exact.astype(low_type),
        glob_upstream,
        preferred_element_type=jnp.float32,
    )
    own_queries = scaling * jnp.einsum(
        "rhgj,rjhd->rghd", own_score_grad, glob_keys, preferred_element_type=jnp.float32
    )
    own_keys = scaling * jnp.einsum(
        "rhgj,rghd->rjhd", own_score_grad, glob_queries, preferred_element_type=jnp.float32
    )
    own_values = jnp.einsum(
        "rhgj,rghd->rjhd",
        own_exact.astype(low_type),
        glob_upstream,
        preferred_element_type=jnp.float32,
    )
    grad_queries, grad_keys, grad_values, grad_keys_far, grad_values_far = local_backward(
        block_queries,
        block_keys,
        block_values,
        block_seg,
        glob_keys,
        glob_values,
        global_seg,
        local_logsum,
        upstream_mix,
    )
    far_grads = lax.psum((remote_queries, grad_keys_far, grad_values_far), "seq")
    head_shape = (row_count, tok_count, HEADS, HEAD_DIM)
    grad_projected = jnp.stack(
        [
            grad_queries.reshape(head_shape),
            grad_keys.reshape(head_shape) + tok_keys_extra,
            grad_values.reshape(head_shape) + tok_values_extra,
        ],
        axis=2,
    )
    grad_projected = grad_projected.reshape(row_count, tok_count, 3 * model_width).astype(low_type)
    glob_grad_projected = jnp.stack(
        [far_grads[0] + own_queries, far_grads[1] + own_keys, far_grads[2] + own_values], axis=2
    )
    glob_grad_projected = glob_grad_projected.reshape(
        row_count, glob_count, 3 * model_width
    ).astype(low_type)
    grad_qkv_all = (
        outer_sum(normed, grad_projected)
        + outer_sum(glob_normed, glob_grad_projected) / seq_devices
    )
    grad_normed = project_back(grad_projected, w_qkv)
    glob_grad_normed = project_back(glob_grad_projected, w_qkv)
    grad_sectioned, attn_gain_grad, attn_shift_grad = norm_back(
        sectioned, attn_gain, attn_shift, grad_normed
    )
    grad_sectioned = grad_sectioned + grad_attn_sum
    glob_grad_state, glob_gain_grad, glob_shift_grad = norm_back(
        glob_state, glob_gain, glob_shift, glob_grad_normed
    )
    global_grad = (glob_grad_state + grad_glob_sum).astype(low_type)
    grad_low = grad_sectioned.astype(low_type)
    returned = from_behind(grad_low[:, tok_count - half_block :], "seq", 1)
    token_grad = jnp.concatenate([returned, grad_low[:, : tok_count - half_block]], axis=1)
    ffn_gain_all = tok_ffn[0] + glob_ffn[0] / seq_devices
    ffn_shift_all = tok_ffn[1] + glob_ffn[1] / seq_devices
    up_all = tok_ffn[2] + glob_ffn[2] / seq_devices
    up_bias_all = tok_ffn[3] + glob_ffn[3] / seq_devices
    down_all = tok_ffn[4] + glob_ffn[4] / seq_devices
    down_bias_all = tok_ffn[5] + glob_ffn[5] / seq_devices
    glob_gain_all = glob_gain_grad / seq_devices
    glob_shift_all = glob_shift_grad / seq_devices
    mat_sums = (
        lax.psum_scatter(
            grad_qkv_all.astype(jnp.bfloat16), "batch", scatter_dimension=1, tiled=True
        ).astype(jnp.float32),
        lax.psum_scatter(
            grad_out_all.astype(jnp.bfloat16), "batch", scatter_dimension=1, tiled=True
        ).astype(jnp.float32),
        lax.psum_scatter(
            up_all.astype(jnp.bfloat16), "batch", scatter_dimension=1, tiled=True
        ).astype(jnp.float32),
        lax.psum_scatter(
            down_all.astype(jnp.bfloat16), "batch", scatter_dimension=1, tiled=True
        ).astype(jnp.float32),
    )
    vec_sums = (
        lax.psum(attn_gain_grad.astype(jnp.bfloat16), "batch").astype(jnp.float32),
        lax.psum(attn_shift_grad.astype(jnp.bfloat16), "batch").astype(jnp.float32),
        lax.psum(glob_gain_all.astype(jnp.bfloat16), "batch").astype(jnp.float32),
        lax.psum(glob_shift_all.astype(jnp.bfloat16), "batch").astype(jnp.float32),
        lax.psum(ffn_gain_all.astype(jnp.bfloat16), "batch").astype(jnp.float32),
        lax.psum(ffn_shift_all.astype(jnp.bfloat16), "batch").astype(jnp.float32),
        lax.psum(up_bias_all.astype(jnp.bfloat16), "batch").astype(jnp.float32),
        lax.psum(down_bias_all.astype(jnp.bfloat16), "batch").astype(jnp.float32),
    )
    shares = (
        lax.psum_scatter(vec_sums[0], "seq", scatter_dimension=0, tiled=True),
        lax.psum_scatter(vec_sums[1], "seq", scatter_dimension=0, tiled=True),
        lax.psum_scatter(vec_sums[2], "seq", scatter_dimension=0, tiled=True),
        lax.psum_scatter(vec_sums[3], "seq", scatter_dimension=0, tiled=True),
        lax.psum_scatter(mat_sums[0], "seq", scatter_dimension=0, tiled=True),
        lax.psum_scatter(mat_sums[1], "seq", scatter_dimension=0, tiled=True),
        lax.psum_scatter(vec_sums[4], "seq", scatter_dimension=0, tiled=True),
        lax.psum_scatter(vec_sums[5], "seq", scatter_dimension=0, tiled=True),
        lax.psum_scatter(mat_sums[2], "seq", scatter_dimension=0, tiled=True),
        lax.psum_scatter(vec_sums[6], "seq", scatter_dimension=0, tiled=True),
        lax.psum_scatter(mat_sums[3], "seq", scatter_dimension=0, tiled=True),
        lax.psum_scatter(vec_sums[7], "seq", scatter_dimension=0, tiled=True),
    )
    matrices = (shares[4], shares[5], shares[8], shares[10])
    vectors = (
        shares[0],
        shares[1],
        shares[2],
        shares[3],
        shares[6],
        shares[7],
        shares[9],
        shares[11],
    )
    return (
        result.astype(low_type),
        glob_result.astype(low_type),
        token_grad,
        global_grad,
        vectors[0],
        vectors[1],
        vectors[2],
        vectors[3],
        matrices[0],
        matrices[1],
        vectors[4],
        vectors[5],
        matrices[2],
        vectors[6],
        matrices[3],
        vectors[7],
    )


MESH = pl.DeviceIdType.MESH
BF = jnp.bfloat16
F32 = jnp.float32


def dot_nn(left, right):
    return lax.dot_general(left, right, (((1,), (0,)), ((), ())), preferred_element_type=F32)


def dot_nt(left, right):
    return lax.dot_general(left, right, (((1,), (1,)), ((), ())), preferred_element_type=F32)


def lanes_of(shape):
    return lax.broadcasted_iota(jnp.int32, shape, len(shape) - 1)


def two_parts(value):
    high = value.astype(BF)
    return high, (value - high.astype(F32)).astype(BF)


def norm_stats(value):
    center = jnp.mean(value, axis=-1, keepdims=True)
    spread = value - center
    variance = jnp.mean(spread * spread, axis=-1, keepdims=True)
    return spread, lax.rsqrt(variance + EPS)


def norm_pull(value, gain, upstream):
    spread, scale = norm_stats(value)
    unit = spread * scale
    scaled = upstream * gain
    first = jnp.mean(scaled, axis=-1, keepdims=True)
    second = jnp.mean(scaled * unit, axis=-1, keepdims=True)
    grad = scale * (scaled - first - unit * second)
    return (
        grad,
        jnp.sum(upstream * unit, axis=0, keepdims=True),
        jnp.sum(upstream, axis=0, keepdims=True),
    )


def gelu_pair(hidden):
    size = jnp.abs(hidden) * 0.7071067811865476
    step = 1.0 / (1.0 + 0.3275911 * size)
    bell = jnp.exp(-(size * size))
    series = 1.061405429 * 0.5
    for term in (-1.453152027, 1.421413741, -0.284496736, 0.254829592):
        series = series * step + term * 0.5
    tail = series * step * bell
    mass = jnp.where(hidden < 0.0, tail, 1.0 - tail)
    return hidden * mass, mass + hidden * (bell * 0.3989422804014327)


def layer_kernel(
    tokens, gstates, tseg, gseg, attn_gain, attn_shift, glob_gain, glob_shift, w_qkv, w_out,
    ffn_gain, ffn_shift, w_up, up_bias, w_down, down_bias, cotan, gcotan,
    o_out, o_gout, o_tgrad, o_ggrad, o_qkv, o_wout, o_up, o_down, o_vec, o_ub,
    sec, nrm, proj, kvt, probs, att_t, att, x2, n2, n2t, ct, ct_t, acc_full, gn2_full, gatt, qaug, kaug,
    wq, wo, wu, wd,
    lse_t, rl_t, cx, msg1, rcv1, rcv2, rcv3, rcv3b, gsum, gall, vec, vmsg, vrcv, vsum, ub,
    gd, r0d, r1d, r2d, r3d, r4d, gu, r0u, r1u, r2u, r3u, r4u, r0q, r1q, r2q, r3q, r4q, fmsg, frcv, hid_a, hid_b,
    loc, wsem, hs, hr, m1s, m1r, m2s, m2r, m3s, m3r, gos, gor, ggs_s, ggs_r, vs, vr,
    d0s, d0r, d1s, d1r, d2s, d2r, d3s, d3r, d4s, d4r,
    u0s, u0r, u1s, u1r, u2s, u2r, u3s, u3r, u4s, u4r,
    q0s, q0r, q1s, q1r, q2s, q2r, q3s, q3r, q4s, q4r,
    qps, qpr, qls, qlr, vbs, vbr, fs, fr, hs2, hr2, osem, gsem,
):
    tok, width = tokens.shape
    glob = gstates.shape[0]
    rows = tok + glob
    n_seq = lax.axis_size("seq")
    slots = glob // n_seq
    wide = tok + slots
    half = tok // 2
    pairs = HEADS // 2
    chunk = up_bias.shape[0] // n_seq
    n_chunk = up_bias.shape[0] // width
    side, part = width // 4, width // n_seq
    tail = 128

    s = lax.axis_index("seq")
    b = lax.axis_index("batch")
    x, zl, zh = s % 2, (s // 2) % 2, s // 4
    c, y = b % 2, b // 2
    dev_c, dev_y = (s, b + 1 - 2 * c), (s, b + 2 - 4 * y)
    dev_cy, dev_xy = (s, dev_y[1] + 1 - 2 * c), (s + 1 - 2 * x, dev_y[1])
    dev_x, dev_1, dev_2 = (s + 1 - 2 * x, b), (s + 2 - 4 * zl, b), (s + 4 - 8 * zh, b)

    def flip(k):
        other = s
        if k & 1:
            other = other + 1 - 2 * x
        if k & 2:
            other = other + 2 - 4 * zl
        if k & 4:
            other = other + 4 - 8 * zh
        return other

    def remote(src, dst, ss, rs, dev):
        return pltpu.make_async_remote_copy(
            src_ref=src, dst_ref=dst, send_sem=ss, recv_sem=rs, device_id=dev, device_id_type=MESH
        )

    peers = tuple(range(1, n_seq))
    acc, gn2 = acc_full.at[pl.ds(0, wide)], gn2_full.at[pl.ds(0, wide)]
    score = (acc_full, gn2_full)

    def as_row(vector):
        return vector[...].reshape(1, vector.shape[0])

    attn_gain, attn_shift, glob_gain, glob_shift, ffn_gain, ffn_shift, down_bias = (
        as_row(v) for v in (attn_gain, attn_shift, glob_gain, glob_shift, ffn_gain, ffn_shift, down_bias)
    )

    my_slots = pl.multiple_of(s * slots, slots)
    loads = [
        (tokens.at[pl.ds(half, half)], sec.at[pl.ds(0, half)]),
        (gstates, sec.at[pl.ds(tok, glob)]),
        (w_qkv, wq),
        (cotan, ct.at[pl.ds(0, tok)]),
        (gcotan.at[pl.ds(my_slots, slots)], ct.at[pl.ds(tok, slots)]),
        (w_out, wo),
    ]
    loads = [pltpu.make_async_copy(a, d, loc.at[i]) for i, (a, d) in enumerate(loads)]
    for load in loads:
        load.start()

    def piece_of(i, o):
        return 4 * (i // 2) + 2 * o + i % 2

    def stream_up(i):
        copies = []
        for o in range(2):
            at = piece_of(i, o) * chunk
            at = at if isinstance(at, int) else pl.multiple_of(at, chunk)
            copies.append(
                pltpu.make_async_copy(w_up.at[:, pl.ds(at, chunk)], wu.at[:, pl.ds(o * chunk, chunk)], wsem.at[0, o])
            )
        return copies

    def stream_down(i, to, which):
        copies = []
        for o in range(2):
            at = piece_of(i, o) * chunk
            at = at if isinstance(at, int) else pl.multiple_of(at, chunk)
            copies.append(pltpu.make_async_copy(w_down.at[pl.ds(at, chunk)], to.at[pl.ds(o * chunk, chunk)], wsem.at[which, o]))
        return copies

    def stream(i):
        return stream_up(i) + stream_down(i, wd, 1)

    for i, to in ((0, wu), (1, wd)):
        for copy in stream_down(i, to, i):
            copy.start()

    bar = pltpu.get_barrier_semaphore()
    for k in peers:
        pl.semaphore_signal(bar, inc=1, device_id=(flip(k), b), device_id_type=MESH)
    pl.semaphore_signal(bar, inc=1, device_id=dev_c, device_id_type=MESH)
    for dev in (dev_y, dev_cy, dev_xy):
        pl.semaphore_signal(bar, inc=1, device_id=dev, device_id_type=MESH)
    pl.semaphore_wait(bar, len(peers) + 4)
    halo = remote(
        tokens.at[pl.ds(0, half)], sec.at[pl.ds(half, half)], hs.at[0], hr.at[0],
        (lax.rem(s + n_seq - 1, n_seq), b),
    )
    halo.start()

    seg_row = jnp.concatenate([tseg[...], gseg[...]], axis=1)
    which = lax.broadcasted_iota(jnp.int32, (128, rows), 0)
    col = lanes_of((128, rows))
    is_glob = col >= tok
    same = which == seg_row
    q_t = jnp.where(which < 3, jnp.where(same, 1.0, 0.0), jnp.where((which == 3) & is_glob, 1.0, 0.0))
    far = jnp.where(s == 0, 0.0, NEGATIVE)
    k_t = jnp.where(which < 3, jnp.where(same, 0.0, NEGATIVE), jnp.where((which == 3) & is_glob, far, 0.0))
    qaug[...] = jnp.transpose(q_t).astype(BF)
    kaug[...] = jnp.transpose(k_t).astype(BF)

    def norm_to(first, count, gain, shift):
        for r in range(first, first + count, 128):
            spread, scale = norm_stats(sec[pl.ds(r, 128), :].astype(F32))
            nrm[pl.ds(r, 128), :] = (spread * scale * gain + shift).astype(BF)

    def project_rows(first, count):
        def step(i, carry):
            at = pl.multiple_of(i * width, width)
            proj[pl.ds(first, count), pl.ds(at, width)] = dot_nn(
                nrm[pl.ds(first, count), :], wq[:, pl.ds(at, width)]
            ).astype(BF)
            return carry

        lax.fori_loop(0, 3, step, 0)

    loads[1].wait()
    norm_to(tok, glob, glob_gain, glob_shift)
    loads[0].wait()
    norm_to(0, half, attn_gain, attn_shift)
    loads[2].wait()
    project_rows(tok, glob)
    project_rows(0, half)
    loads[3].wait()
    loads[4].wait()
    ct_t[:, pl.ds(0, wide)] = jnp.transpose(ct[...])
    kept_rows = (((0,), 0, 384), ((1, 0, 0), 384, 96), ((1, 0, 1, 0), 480, 48))
    for i in range(n_chunk):
        to = (wu, wd)[i % 2]
        for copy in stream_down(i, to, i % 2):
            copy.wait()
        for o in range(2):
            grad_active = dot_nt(ct[...], to[pl.ds(o * chunk, chunk), :]).astype(BF)
            for where, first, count in kept_rows:
                kept = gu.at[(i, o) + where]
                kept[...] = grad_active[first : first + count].reshape(kept.shape)
        if i + 2 < n_chunk:
            for copy in stream_down(i + 2, to, i % 2):
                copy.start()
    for copy in stream(0):
        copy.start()
    halo.wait()
    norm_to(half, half, attn_gain, attn_shift)
    project_rows(half, half)

    kvt[:, pl.ds(0, rows)] = jnp.transpose(proj[:, pl.ds(2 * width, width)])
    lane_p = lanes_of((1, 128))
    even = jnp.where(lane_p < HEAD_DIM, HEAD_DIM ** (-0.5), 0.0).astype(BF)
    odd = jnp.where(lane_p < HEAD_DIM, 0.0, HEAD_DIM ** (-0.5)).astype(BF)
    even_one = jnp.where(lane_p < HEAD_DIM, 1.0, 0.0).astype(BF)
    odd_one = jnp.where(lane_p < HEAD_DIM, 0.0, 1.0).astype(BF)
    first_head = lax.broadcasted_iota(jnp.int32, (128, 128), 0) < HEAD_DIM
    lse_t[...] = jnp.zeros_like(lse_t)
    rl_t[...] = jnp.zeros_like(rl_t)

    def glob_forward(p, carry):
        at = pl.multiple_of(p * 128, 128)
        keys = jnp.concatenate([proj[:, pl.ds(width + at, 128)], kaug[...]], axis=1)
        qg = proj[pl.ds(tok, glob), pl.ds(at, 128)]
        qa = qaug[pl.ds(tok, glob), :]
        queries = jnp.concatenate(
            [jnp.concatenate([qg * even, qa], axis=1), jnp.concatenate([qg * odd, qa], axis=1)], axis=0
        )
        scores = dot_nt(keys, queries)
        top = jnp.max(scores, axis=0, keepdims=True)
        raised = jnp.exp(scores - top)
        total = jnp.sum(raised, axis=0, keepdims=True)
        weights = (raised * (1.0 / total)).astype(BF)
        probs[p, :, pl.ds(2 * tok, 2 * glob)] = weights
        mixed = dot_nn(kvt[pl.ds(at, 128), pl.ds(0, rows)], weights)
        cx[:, pl.ds(at, 128)] = jnp.transpose(jnp.where(first_head, mixed[:, :glob], mixed[:, glob:]))
        logsum = top + jnp.log(total)
        lse_t[pl.ds(2 * p, 1), :] = logsum[:, :glob]
        lse_t[pl.ds(2 * p + 1, 1), :] = logsum[:, glob:]
        return carry

    lax.fori_loop(0, pairs, glob_forward, 0, unroll=True)

    lse = jnp.transpose(lse_t[...])
    in_heads = lanes_of((glob, 128)) < HEADS
    lse = jnp.where(in_heads, lse, 0.0)
    part_a, rest = two_parts(lse)
    rest = lse - part_a.astype(F32)
    part_b = rest.astype(BF)
    part_c = rest - part_b.astype(F32)
    packed = part_a.astype(F32) + pltpu.roll(part_b.astype(F32), 16, 1) + pltpu.roll(part_c, 32, 1)
    msg1[:, pl.ds(0, width)] = cx[...].astype(BF)
    msg1[:, pl.ds(width, 128)] = packed.astype(BF)
    sends1 = []
    for k in peers:
        other = flip(k)
        at = pl.multiple_of(other * slots, slots)
        copy = remote(msg1.at[pl.ds(at, slots)], rcv1.at[k], m1s.at[k], m1r.at[k], (other, b))
        copy.start()
        sends1.append(copy)
    rcv1[0] = msg1[pl.ds(my_slots, slots), :]

    def scores_to(slot, p, mask):
        at = pl.multiple_of(p * 128, 128)
        keys = jnp.concatenate([proj[:, pl.ds(width + at, 128)], kaug[...]], axis=1)
        queries = jnp.concatenate([proj[pl.ds(0, tok), pl.ds(at, 128)] * mask, qaug[pl.ds(0, tok), :]], axis=1)
        score[slot][:, pl.ds(0, tok)] = dot_nt(keys, queries)

    def softmax_of(slot, p):
        values = score[slot][:, pl.ds(0, tok)]
        raised = jnp.exp(values - jnp.max(values, axis=0, keepdims=True))
        inverse = 1.0 / jnp.sum(raised, axis=0, keepdims=True)
        weights = raised.astype(BF)
        probs[p, :, pl.ds(slot * tok, tok)] = weights
        rl_t[pl.ds(2 * p + slot, 1), :] = inverse
        here = pl.multiple_of(p * 128 + slot * HEAD_DIM, HEAD_DIM)
        mixed = dot_nn(kvt[pl.ds(here, HEAD_DIM), pl.ds(0, rows)], weights)
        att_t[pl.ds(here, HEAD_DIM), pl.ds(0, tok)] = (mixed * inverse).astype(BF)

    def local_forward_pair(p, carry):
        scores_to(1, p, odd)
        softmax_of(0, p)
        scores_to(0, jnp.minimum(p + 1, pairs - 1), even)
        softmax_of(1, p)
        return carry

    scores_to(0, 0, even)
    lax.fori_loop(0, pairs, local_forward_pair, 0)
    att[pl.ds(0, tok), :] = jnp.transpose(att_t[:, pl.ds(0, tok)])

    loads[5].wait()

    def second_norm(first, count):
        spread, scale = norm_stats(x2[pl.ds(first, count), :])
        n2[pl.ds(first, count), :] = (spread * scale * ffn_gain + ffn_shift).astype(BF)

    for first in range(0, width, 256):
        here = pl.ds(first, 256)
        x2[pl.ds(0, tok), here] = dot_nn(att[pl.ds(0, tok), :], wo[:, here]) + sec[pl.ds(0, tok), here].astype(F32)
    for r in range(0, tok, 128):
        second_norm(r, 128)

    head_of = lanes_of((128, width)) // HEAD_DIM
    spread_heads = jnp.where(head_of == lax.broadcasted_iota(jnp.int32, (128, width), 0), 1.0, 0.0).astype(BF)
    for copy in sends1:
        copy.wait()
    logs = []
    for k in range(n_seq):
        packed = rcv1[k, :, pl.ds(width, 128)].astype(F32)
        logs.append(packed + pltpu.roll(packed, 112, 1) + pltpu.roll(packed, 96, 1))
    high = functools.reduce(jnp.maximum, logs)
    raised = [jnp.exp(one - high) for one in logs]
    total = functools.reduce(jnp.add, raised)
    in_heads = lanes_of((slots, 128)) < HEADS
    shares = jnp.concatenate([jnp.where(in_heads, one / total, 0.0) for one in raised], axis=0)
    share_a, share_b = two_parts(shares)
    shares = dot_nn(share_a, spread_heads) + dot_nn(share_b, spread_heads)
    cx[...] = shares
    mixed = jnp.zeros((slots, width), F32)
    for k in range(n_seq):
        mixed = mixed + shares[k * slots : (k + 1) * slots] * rcv1[k, :, pl.ds(0, width)].astype(F32)
    att[pl.ds(tok, slots), :] = mixed.astype(BF)
    att_t[:, pl.ds(tok, tail)] = jnp.transpose(
        jnp.concatenate([mixed, jnp.zeros((tail - slots, width), F32)], axis=0)
    ).astype(BF)

    x2[pl.ds(tok, slots), :] = dot_nn(att[pl.ds(tok, slots), :], wo[...]) + sec[
        pl.ds(pl.multiple_of(tok + my_slots, slots), slots), :
    ].astype(F32)
    second_norm(tok, slots)
    n2t[:, pl.ds(0, wide)] = jnp.transpose(n2[...])

    def d_core(i):
        return remote(gd.at[i, :, :, 1 - c], r0d.at[i], d0s.at[i], d0r.at[i], dev_c)

    def d_y(i):
        return remote(r0d.at[i, :, 1 - y], r1d.at[i], d1s.at[i], d1r.at[i], dev_y)

    def d_1(i):
        return remote(r1d.at[i, 1 - zl], r2d.at[i // 2, i % 2], d2s.at[i], d2r.at[i], dev_1)

    def d_x(h):
        return remote(r2d.at[h, 1 - x], r3d.at[h], d3s.at[h], d3r.at[h], dev_x)

    def d_2():
        return remote(r3d.at[1 - zh], r4d, d4s.at[0], d4r.at[0], dev_2)

    def do_d_y(i):
        d_core(i).wait_recv()
        r0d[i] = r0d[i] + gd[i, :, :, c]
        d_y(i).start()

    def do_d_1(i):
        d_y(i).wait_recv()
        r1d[i] = r1d[i] + r0d[i, :, y]
        d_1(i).start()

    def do_d_x(h):
        for j in range(2):
            d_1(2 * h + j).wait_recv()
            r2d[h, j] = r2d[h, j] + r1d[2 * h + j, zl]
        d_x(h).start()

    def do_d_2():
        for h in range(2):
            d_x(h).wait_recv()
            r3d[h] = r3d[h] + r2d[h, x]
        d_2().start()

    def u_core(i):
        return remote(gu.at[i, 1 - c], r0u.at[i], u0s.at[i], u0r.at[i], dev_c)

    def u_a(i, z_first):
        src, dev = (r0u.at[i, :, 1 - zl], dev_1) if z_first else (r0u.at[i, :, :, 1 - x], dev_x)
        return remote(src, r1u.at[i], u1s.at[i], u1r.at[i], dev)

    def u_b(i):
        src, dev = (r1u.at[i, :, 1 - x], dev_x) if i == 0 else (r1u.at[i, :, 1 - zl], dev_1)
        return remote(src, r2u.at[i // 2, i % 2], u2s.at[i], u2r.at[i], dev)

    def u_y(j):
        return remote(r2u.at[1 - y, j], r3u.at[j], u3s.at[j], u3r.at[j], dev_y)

    def u_2(j):
        return remote(r3u.at[j, 1 - zh], r4u.at[j], u4s.at[j], u4r.at[j], dev_2)

    def do_u_a(i):
        u_core(i).wait_recv()
        r0u[i] = r0u[i] + gu[i, c]
        if isinstance(i, int):
            u_a(i, i == 0).start()
            return

        @pl.when(i == 0)
        def _():
            u_a(i, True).start()

        @pl.when(i > 0)
        def _():
            u_a(i, False).start()

    def do_u_b(i):
        u_a(i, i == 0).wait_recv()
        r1u[i] = r1u[i] + (r0u[i, :, zl] if i == 0 else r0u[i, :, :, x])
        u_b(i).start()

    def do_u_y(j):
        for yy in range(2):
            i = 2 * yy + j
            u_b(i).wait_recv()
            r2u[yy, j] = r2u[yy, j] + r1u[i, :, x if i == 0 else zl]
        u_y(j).start()

    def do_u_2(j):
        u_y(j).wait_recv()
        r3u[j] = r3u[j] + r2u[y, j]
        u_2(j).start()

    vec[...] = jnp.zeros_like(vec)
    for i in range(n_chunk):
        for o in range(2):
            ub[pl.ds(i, 1), pl.ds(o * chunk, chunk)] = up_bias[pl.ds(piece_of(i, o) * chunk, chunk)].reshape(1, chunk)
    acc[...] = jnp.zeros_like(acc)
    gn2[...] = jnp.zeros_like(gn2)

    act = gatt
    gh = kvt
    cuts = ((0, 256, ((0, 0, 0, 256),)), (256, 256, ((0, 256, 0, 128), (1, 0, 128, 128))), (512, 256, ((1, 128, 0, 256),)))

    def hidden_at(n):
        return (hid_a, hid_b)[n % 2]

    def ffn_step(i, carry):
        for copy in stream(i):
            copy.wait()

        def up(n):
            here = pl.ds(cuts[n][0], 256)
            hidden_at(n)[...] = dot_nn(n2[...], wu[:, here]) + ub[pl.ds(i, 1), here]

        def activate(n):
            here = pl.ds(cuts[n][0], 256)
            total = jnp.zeros((1, 256), F32)
            for where, first, count in kept_rows:
                row = pl.ds(first, count)
                active, slope = gelu_pair(hidden_at(n)[row, :])
                act[row, here] = active.astype(BF)
                grad_active = jnp.concatenate(
                    [
                        gu[(i, o) + where + (slice(None),) * (5 - len(where)) + (pl.ds(at, size),)].reshape(count, size)
                        for o, at, _, size in cuts[n][2]
                    ],
                    axis=1,
                )
                grad_hidden = (slope * grad_active.astype(F32)).astype(BF)
                gh[row, here] = grad_hidden
                total = total + jnp.sum(grad_hidden.astype(F32), axis=0, keepdims=True)
            ub[pl.ds(i, 1), here] = total

        def down_terms(n):
            first, count, parts = cuts[n]
            block = dot_nn(ct_t[:, pl.ds(0, wide)], act[:, pl.ds(first, count)]).astype(BF)
            for o, at, start, size in parts:
                gd[i, o, :, :, :, pl.ds(at, size)] = block[:, start : start + size].reshape(2, 2, side, size)

        def up_terms(n):
            first, count, parts = cuts[n]
            block = dot_nn(n2t[:, pl.ds(0, wide)], gh[pl.ds(0, wide), pl.ds(first, count)]).astype(BF)
            for o, at, start, size in parts:
                gu[i, o, :, :, :, :, :, pl.ds(at, size)] = block[:, start : start + size].reshape(
                    2, 2, 2, 2, part // 2, size
                )

        up(0)
        activate(0)
        up(1)
        down_terms(0)
        activate(1)
        up(2)
        down_terms(1)
        activate(2)
        for first, count, _ in cuts:
            here = pl.ds(first, count)
            acc[:, here] += dot_nn(act[...], wd[:, here])
            gn2[:, here] += dot_nt(gh[pl.ds(0, wide), :], wu[here, :])

        @pl.when(i + 1 < n_chunk)
        def _():
            for copy in stream(i + 1):
                copy.start()

        @pl.when(i >= 1)
        def _():
            do_d_y(i - 1)
            do_u_a(i - 1)

        @pl.when(i == 3)
        def _():
            do_u_b(0)
            do_d_1(0)

        down_terms(2)
        for n in range(3):
            up_terms(n)
        d_core(i).start()
        u_core(i).start()

        return carry

    lax.fori_loop(0, n_chunk, ffn_step, 0)

    for i in range(n_chunk):
        for o in range(2):
            block = piece_of(i, o)
            vec[pl.ds(8 + block // 2, 1), pl.ds(block % 2 * chunk, chunk)] = ub[pl.ds(i, 1), pl.ds(o * chunk, chunk)]


    def second_pull(first, count):
        grad, gain_term, shift_term = norm_pull(
            x2[pl.ds(first, count), :], ffn_gain, gn2[pl.ds(first, count), :]
        )
        upstream = ct[pl.ds(first, count), :].astype(F32)
        total = upstream + grad
        acc[pl.ds(first, count), :] += x2[pl.ds(first, count), :] + down_bias
        x2[pl.ds(first, count), :] = total
        n2[pl.ds(first, count), :] = total.astype(BF)
        vec[pl.ds(4, 1), :] += gain_term
        vec[pl.ds(5, 1), :] += shift_term
        vec[pl.ds(6, 1), :] += jnp.sum(upstream, axis=0, keepdims=True)

    for r in range(0, tok, 128):
        second_pull(r, 128)
    second_pull(tok, slots)
    gatt[...] = dot_nt(n2[...], wo[...]).astype(BF)

    slot_grad = gatt[pl.ds(tok, slots), :].astype(F32)
    slot_att = att[pl.ds(tok, slots), :].astype(F32)
    head_sel = lanes_of((1, 128)) < HEADS

    def inner_aug(upstream, values):
        high, low = two_parts(upstream.astype(F32) * values)
        inner = dot_nt(high, spread_heads) + dot_nt(low, spread_heads)
        high, low = two_parts(jnp.where(head_sel, inner, 0.0))
        return (high.astype(F32) + pltpu.roll(low.astype(F32), 16, 1)).astype(BF)

    scaled = jnp.concatenate(
        [(cx[pl.ds(k * slots, slots), :] * slot_grad).astype(BF) for k in range(n_seq)], axis=0
    )
    msg1[:, pl.ds(0, width)] = scaled
    msg1[:, pl.ds(width, 128)] = inner_aug(scaled, jnp.concatenate([slot_att] * n_seq, axis=0))
    sends2 = []
    for k in peers:
        copy = remote(
            msg1.at[pl.ds(k * slots, slots)], rcv2.at[pl.ds(my_slots, slots)], m2s.at[k], m2r.at[k],
            (flip(k), b),
        )
        copy.start()
        sends2.append(copy)
    rcv2[pl.ds(my_slots, slots), :] = msg1[pl.ds(0, slots), :]
    do_d_y(3)
    do_u_a(3)
    do_d_1(1)
    do_u_b(1)

    n2t[:, pl.ds(0, tok)] = jnp.transpose(nrm[pl.ds(0, tok), :])
    n2t[:, pl.ds(tok, glob)] = jnp.transpose(nrm[pl.ds(tok, glob), :])

    outs = nrm
    outs[pl.ds(0, wide), :] = acc[...].astype(BF)
    out_copy = pltpu.make_async_copy(outs.at[pl.ds(0, tok)], o_out, osem.at[0])
    out_copy.start()
    own_out = pltpu.make_async_copy(
        outs.at[pl.ds(tok, slots)], o_gout.at[pl.ds(my_slots, slots)], osem.at[1]
    )
    own_out.start()

    scale_c = jnp.transpose(
        jnp.concatenate([rl_t[...], jnp.zeros((128 - rl_t.shape[0], tok), F32)], axis=0)
    )
    scale_a, scale_b = two_parts(scale_c)
    for r in range(0, tok, 128):
        wider = dot_nn(scale_a[r : r + 128], spread_heads) + dot_nn(scale_b[r : r + 128], spread_heads)
        scaled = (gatt[pl.ds(r, 128), :].astype(F32) * wider).astype(BF)
        gatt[pl.ds(r, 128), :] = scaled
        qaug[pl.ds(r, 128), :] = inner_aug(scaled, att[pl.ds(r, 128), :].astype(F32))
    kvt[:, pl.ds(0, rows)] = jnp.transpose(proj[:, pl.ds(width, width)])

    def chunk_at(p):
        return gu.at[p // 2, lax.rem(p, 2)]

    def put_chunk(p, value):
        gu[p // 2, lax.rem(p, 2)] = value.astype(BF).reshape(gu.shape[2:])
        q_core(p).start()

    def q_core(p):
        return remote(chunk_at(p).at[:, 1 - c], r0q.at[p], q0s.at[p], q0r.at[p], dev_c)

    def x_first(p):
        return p in (1, 7)

    def q_a(p):
        src, dev = (r0q.at[p, :, 1 - x], dev_x) if x_first(p) else (r0q.at[p, :, :, 1 - y], dev_y)
        return remote(src, r1q.at[p], q1s.at[p], q1r.at[p], dev)

    def q_b(p):
        src, dev = (r1q.at[p, :, 1 - y], dev_y) if x_first(p) else (r1q.at[p, :, 1 - x], dev_x)
        return remote(src, r2q.at[p], q2s.at[p], q2r.at[p], dev)

    def q_1(p):
        return remote(r2q.at[p], r3q.at[p], q3s.at[p], q3r.at[p], dev_1)

    def q_2(p):
        return remote(r2q.at[p, 1 - zh], r4q.at[p], q4s.at[p], q4r.at[p], dev_2)

    def take_chunk(p):
        q_core(p).wait_recv()
        r0q[p] = r0q[p] + gu[p // 2, p % 2, :, c]

    def do_q_a(*which):
        for p in which:
            take_chunk(p)
            q_a(p).start()

    def do_q_b(*which):
        for p in which:
            q_a(p).wait_recv()
            r1q[p] = r1q[p] + (r0q[p, :, x] if x_first(p) else r0q[p, :, :, y])
            q_b(p).start()

    def do_q_1(*which):
        for p in which:
            q_b(p).wait_recv()
            r2q[p] = r2q[p] + r1q[p, :, y if x_first(p) else x]

            @pl.when(zl != c)
            def _(p=p):
                q_1(p).start()

    def do_q_2(*which):
        @pl.when(zl == c)
        def _():
            for p in which:
                q_1(p).wait_recv()
                r2q[p] = r2q[p] + r3q[p]
                q_2(p).start()

    def q_plane(n):
        src = (r0q.at[5, :, 1 - x, y], r0q.at[5, :, x, 1 - y], r0q.at[5, :, 1 - x, 1 - y])[n]
        dst = (r1q.at[5, :, 0], r1q.at[5, :, 1], r2q.at[5])[n]
        return remote(src, dst, qps.at[n], qpr.at[n], (dev_x, dev_y, dev_xy)[n])

    def q_line(n):
        src = (r0q.at[5, 1 - zh, x, y], r0q.at[5, zh, x, y], r0q.at[5, 1 - zh, x, y])[n]
        dst = (r3q.at[5, 0], r3q.at[5, 1], r4q.at[5])[n]
        return remote(src, dst, qls.at[n], qlr.at[n], (dev_2, dev_1, (flip(6), b))[n])

    def do_q_plane():
        take_chunk(5)
        for n in range(3):
            q_plane(n).start()

    def do_q_line():
        for n in range(3):
            q_plane(n).wait_recv()
        total = r0q[5, :, x, y].astype(F32) + r1q[5, :, 0].astype(F32) + r1q[5, :, 1].astype(F32) + r2q[5].astype(F32)
        r0q[5, :, x, y] = total.astype(BF)

        @pl.when(zl == c)
        def _():
            q_line(0).start()

        @pl.when(zl != c)
        def _():
            q_line(1).start()
            q_line(2).start()

    def q_chunk(p):
        right = jnp.concatenate(
            [proj[:, pl.ds(pl.multiple_of(w * width + p * 128, 128), 128)] for w in range(3)], axis=1
        )
        put_chunk(p, dot_nn(n2t[...], right))

    for i in range(4):
        u_core(i).wait_send()
    for h in range(2):
        put_chunk(pairs + h, dot_nn(att_t[:, pl.ds(0, wide)], n2[:, pl.ds(h * 384, 384)]))

    minus = jnp.where(lanes_of((rows, 128)) < 32, -1.0, 0.0).astype(BF)
    factor = HEAD_DIM ** (-0.5)

    def chosen(head):
        lane = lanes_of((1, 128))
        return jnp.where((lane == head) | (lane == head + 16), 1.0, 0.0).astype(BF)

    def values_of(at):
        return jnp.concatenate([proj[:, pl.ds(2 * width + at, 128)], minus], axis=1)

    def parts_at(p):
        return acc_full.at[:, pl.ds(pl.multiple_of(lax.rem(p, 3) * 256, 256), 256)]

    def token_queries(p):
        at = pl.multiple_of(p * 128, 128)
        values = values_of(at)
        qp = proj[pl.ds(0, tok), pl.ds(at, 128)]
        gp = gatt[pl.ds(0, tok), pl.ds(at, 128)]
        ups = jnp.concatenate([gp * even_one, gp * odd_one], axis=0)
        dd = qaug[pl.ds(0, tok), :]
        inner = jnp.concatenate([dd * chosen(2 * p), dd * chosen(2 * p + 1)], axis=0)
        own = pl.ds(0, 2 * tok)
        parts_at(p)[:, 128:] = dot_nn(probs[p, :, own], ups)
        for first in range(0, 2 * tok, 256):
            right = jnp.concatenate([ups[first : first + 256], inner[first : first + 256]], axis=1)
            grad_w = dot_nt(values, right)
            here = probs[p, :, pl.ds(first, 256)].astype(F32)
            probs[p, :, pl.ds(first, 256)] = (here * grad_w).astype(BF)
        parts_at(p)[:, :128] = dot_nn(probs[p, :, own], jnp.concatenate([qp * even, qp * odd], axis=0))
        low = dot_nn(kvt[pl.ds(at, HEAD_DIM), pl.ds(0, rows)], probs[p, :, pl.ds(0, tok)])
        upper = dot_nn(
            kvt[pl.ds(pl.multiple_of(at + HEAD_DIM, HEAD_DIM), HEAD_DIM), pl.ds(0, rows)],
            probs[p, :, pl.ds(tok, tok)],
        )
        grad_q = jnp.concatenate([low, upper], axis=0) * factor
        proj[pl.ds(0, tok), pl.ds(at, 128)] = jnp.transpose(grad_q).astype(BF)

    def glob_queries(p):
        at = pl.multiple_of(p * 128, 128)
        qg = proj[pl.ds(tok, glob), pl.ds(at, 128)]
        gg = rcv2[:, pl.ds(at, 128)]
        dg = rcv2[:, pl.ds(width, 128)]
        ups = jnp.concatenate([gg * even_one, gg * odd_one], axis=0)
        inner = jnp.concatenate([dg * chosen(2 * p), dg * chosen(2 * p + 1)], axis=0)
        weights = probs[p, :, pl.ds(2 * tok, 2 * glob)]
        grad_v = parts_at(p)[:, 128:] + dot_nn(weights, ups)
        grad_w = dot_nt(values_of(at), jnp.concatenate([ups, inner], axis=1))
        grad_s = (weights.astype(F32) * grad_w).astype(BF)
        grad_k = parts_at(p)[:, :128] + dot_nn(grad_s, jnp.concatenate([qg * even, qg * odd], axis=0))
        own = dot_nn(kvt[pl.ds(at, 128), pl.ds(0, rows)], grad_s)
        own = jnp.where(first_head, own[:, :glob], own[:, glob:]) * factor
        proj[pl.ds(tok, glob), pl.ds(at, 128)] = jnp.transpose(own).astype(BF)
        proj[:, pl.ds(width + at, 128)] = grad_k.astype(BF)
        proj[:, pl.ds(2 * width + at, 128)] = grad_v.astype(BF)

    def at_steps(p, steps):
        for step, act in steps:

            @pl.when(p == step)
            def _(act=act):
                act()

    def first_pairs(p, carry):
        token_queries(p)
        return carry

    def middle_pairs(p, carry):
        token_queries(p)
        glob_queries(p - 2)
        q_chunk(p - 2)
        at_steps(p, (
            (2, lambda: (do_d_1(3), do_u_b(3), do_d_x(0))),
            (3, lambda: (do_q_a(0), do_u_y(0), do_q_b(6, 7))),
            (4, lambda: (do_q_a(1), do_d_x(1), do_u_y(1))),
            (5, lambda: (do_q_a(2), do_q_b(0), do_u_2(0), do_q_1(6, 7))),
        ))
        return carry

    def last_pairs(p, carry):
        glob_queries(p)
        q_chunk(p)
        at_steps(p, ((4, lambda: (do_q_a(3), do_q_b(1), do_d_2())), (5, lambda: (do_q_a(4), do_u_2(1), do_q_2(6, 7), do_q_1(0)))))
        return carry

    lax.fori_loop(0, 2, first_pairs, 0)
    do_d_1(2)
    do_u_b(2)
    do_q_a(6, 7)
    for copy in sends2:
        copy.wait()
    sends_o = []
    for k in peers:
        copy = remote(
            outs.at[pl.ds(tok, slots)], o_gout.at[pl.ds(my_slots, slots)], gos.at[k], gor.at[k], (flip(k), b)
        )
        copy.start()
        sends_o.append(copy)

    lax.fori_loop(2, pairs, middle_pairs, 0)
    lax.fori_loop(pairs - 2, pairs, last_pairs, 0)

    def first_pull(first):
        grad, gain_term, shift_term = norm_pull(
            sec[pl.ds(first, 128), :].astype(F32), attn_gain, gn2[pl.ds(first, 128), :]
        )
        n2[pl.ds(first, 128), :] = (grad + x2[pl.ds(first, 128), :]).astype(BF)
        vec[pl.ds(0, 1), :] += gain_term
        vec[pl.ds(1, 1), :] += shift_term

    gnm = wu
    gnm[pl.ds(0, glob), :] = dot_nt(proj[pl.ds(tok, glob), :], wq[...]).astype(BF)
    sends3 = []
    for k in (1, 2, 3):
        other = flip(k)
        for h in range(2):
            at = pl.multiple_of((4 * h + lax.rem(other, 4)) * slots, slots)
            copy = remote(
                gnm.at[pl.ds(at, slots)], rcv3.at[k - 1, h], m3s.at[2 * k - 2 + h], m3r.at[2 * k - 2 + h], (other, b)
            )
            copy.start()
            sends3.append(copy)
    do_q_plane()
    gn2[pl.ds(half, half), :] = dot_nt(proj[pl.ds(half, half), :], wq[...])
    for r in range(half, tok, 128):
        first_pull(r)
    do_q_b(2, 3)
    do_q_1(1)
    do_q_2(0)
    for copy in sends3:
        copy.wait()

    quarter = half // 2
    after, after_relay = (lax.rem(s + 1, n_seq), b), (lax.rem(s + 2, n_seq), b)
    relay = ct.at[pl.ds(0, quarter)]

    def back(n):
        part_n = pl.ds(n * quarter, quarter)
        return remote(n2.at[pl.ds(half + n * quarter, quarter)], o_tgrad.at[part_n], hs2.at[n], hr2.at[n], after)

    def back_to_relay():
        return remote(n2.at[pl.ds(half + quarter, quarter)], relay, hs2.at[1], hr2.at[2], dev_x)

    def back_from_relay():
        return remote(relay, o_tgrad.at[pl.ds(quarter, quarter)], hs2.at[2], hr2.at[1], after_relay)

    def start_back():
        back(0).start()

        @pl.when(x == 0)
        def _():
            back(1).start()

        @pl.when(x == 1)
        def _():
            back_to_relay().start()

    def pass_back_on():
        @pl.when(x == 0)
        def _():
            back_to_relay().wait_recv()
            back_from_relay().start()

    def slots_of(h):
        mine = gnm[pl.ds(pl.multiple_of((4 * h + lax.rem(s, 4)) * slots, slots), slots), :].astype(F32)
        for k in (1, 2, 3):
            mine = mine + rcv3[k - 1, h].astype(F32)
        return mine

    gsum[...] = slots_of(1 - zh).astype(BF)
    line3 = remote(gsum, rcv3b, m3s.at[6], m3r.at[6], dev_2)
    line3.start()

    gn2[pl.ds(0, half), :] = dot_nt(proj[pl.ds(0, half), :], wq[...])
    for r in range(0, half, 128):
        first_pull(r)
    keep = pltpu.make_async_copy(n2.at[pl.ds(0, half)], o_tgrad.at[pl.ds(half, half)], osem.at[2])
    keep.start()
    do_q_line()
    do_q_b(4)
    do_q_1(2, 3)
    do_q_2(1)

    @pl.when(s == n_seq - 1)
    def _():
        start_back()


    line3.wait()
    grad, gain_term, shift_term = norm_pull(
        sec[pl.ds(pl.multiple_of(tok + my_slots, slots), slots), :].astype(F32),
        glob_gain,
        slots_of(zh) + rcv3b[...].astype(F32),
    )
    vec[pl.ds(2, 1), :] += gain_term
    vec[pl.ds(3, 1), :] += shift_term
    n2[pl.ds(tok, slots), :] = (grad + x2[pl.ds(tok, slots), :]).astype(BF)
    line_g = remote(n2.at[pl.ds(tok, slots)], gall, ggs_s.at[0], ggs_r.at[0], dev_2)
    line_g.start()

    share = vec.shape[1] // n_seq
    for j in range(n_seq):
        rolled = vec[pl.ds(0, 8), :]
        if j:
            rolled = pltpu.roll(rolled, vec.shape[1] - share * j, 1)
        vmsg[j, pl.ds(0, 8), :] = rolled[:, :128]
        for m in range(chunk // 128):
            vmsg[j, pl.ds(8 + m, 1), :] = vec[pl.ds(8 + j // 2, 1), pl.ds((j % 2) * chunk + m * 128, 128)]
    sends_v = []
    for k in peers:
        copy = remote(vmsg.at[flip(k)], vrcv.at[k - 1], vs.at[k], vr.at[k], (flip(k), b))
        copy.start()
        sends_v.append(copy)

    do_q_1(4)
    do_q_2(2, 3)

    d_2().wait_recv()
    acc[pl.ds(96, 192), pl.ds(0, 384)] = r4d[...].astype(F32) + r3d[zh].astype(F32)
    for j in range(2):
        u_2(j).wait_recv()
    last = r4u[...].astype(F32) + r3u[:, zh].astype(F32)
    acc[pl.ds(0, 96), pl.ds(0, 384)] = last[0].reshape(96, 384)
    acc[pl.ds(0, 96), pl.ds(384, 384)] = last[1].reshape(96, 384)
    results = [
        pltpu.make_async_copy(acc.at[pl.ds(0, 96)], o_up, osem.at[4]),
        pltpu.make_async_copy(acc.at[pl.ds(96, 192), pl.ds(0, 384)], o_down, osem.at[5]),
    ]
    for copy in results:
        copy.start()

    line_g.wait()
    far_slots = pl.multiple_of(flip(4) * slots, slots)
    sends_g = []
    for n, (src, at) in enumerate(((n2.at[pl.ds(tok, slots)], my_slots), (gall, far_slots))):
        copy = pltpu.make_async_copy(src, o_ggrad.at[pl.ds(at, slots)], gsem.at[n])
        copy.start()
        sends_g.append(copy)
        for k in (1, 2, 3):
            copy = remote(
                src, o_ggrad.at[pl.ds(at, slots)], ggs_s.at[2 * k + n - 1], ggs_r.at[2 * k + n - 1], (flip(k), b)
            )
            copy.start()
            sends_g.append(copy)

    for copy in sends_v:
        copy.wait()
    vsum[0] = vmsg[s]
    for k in peers:
        vsum[0] = vsum[0] + vrcv[k - 1]
    batch_peers = (dev_c, dev_y, dev_cy)
    sends_b = []
    for n, dev in enumerate(batch_peers):
        copy = remote(vsum.at[0], vsum.at[1 + n], vbs.at[n], vbr.at[n], dev)
        copy.start()
        sends_b.append(copy)

    do_q_2(4)

    @pl.when(s != n_seq - 1)
    def _():
        start_back()

    @pl.when(s == n_seq - 2)
    def _():
        pass_back_on()


    def final(n, slot):
        return remote(fmsg.at[n - 1], frcv.at[slot], fs.at[n], fr.at[n], (s, flip_b(n)))

    def flip_b(n):
        return (b, dev_c[1], dev_y[1], dev_cy[1])[n]

    @pl.when(zl == c)
    def _():
        for p in (6, 7, 0, 1, 2, 3, 4):
            q_2(p).wait_recv()
            r4q[p] = r4q[p] + r2q[p, zh]
        for n in range(3):
            q_line(n).wait_recv()
        r4q[5] = (
            r0q[5, zh, x, y].astype(F32) + r3q[5, 0].astype(F32) + r3q[5, 1].astype(F32) + r4q[5].astype(F32)
        ).astype(BF)

        def columns_of(bb):
            first = (bb * 576 - 64 * lax.rem(bb, 2)) // 128
            tiles = []
            for m in range(5):
                tile = first + m
                tiles.append(r4q[lax.rem(tile, 6), :, pl.ds(pl.multiple_of(tile // 6 * 128, 128), 128)])
            first = (bb * 192 - 64 * lax.rem(bb, 2)) // 128
            for m in range(2):
                tile = first + m
                tiles.append(r4q[pairs + tile // 3, :, pl.ds(pl.multiple_of(lax.rem(tile, 3) * 128, 128), 128)])
            return jnp.concatenate(tiles, axis=1)

        for n in (3, 2, 1):
            fmsg[n - 1] = columns_of(flip_b(n))
            final(n, y).start()
        frcv[y] = columns_of(b)

    @pl.when(s != n_seq - 2)
    def _():
        pass_back_on()

    for copy in sends_b:
        copy.wait()
    shared = vsum[0] + vsum[1] + (vsum[2] + vsum[3])
    o_vec[...] = shared[0:8, :share]
    for m in range(chunk // 128):
        o_ub[:, pl.ds(m * 128, 128)] = shared[8 + m : 9 + m, :]

    @pl.when(zl == c)
    def _():
        final(2, 1 - y).wait_recv()

    @pl.when(zl != c)
    def _():
        final(1, y).wait_recv()
        final(3, 1 - y).wait_recv()

    for yy in range(2):
        block = frcv[yy].astype(F32)
        main = block[:, :640]
        acc[pl.ds(288 + yy * 48, 48), pl.ds(0, 640)] = jnp.where(c == 1, pltpu.roll(main, 576, 1), main)
        main = block[:, 640:]
        acc[pl.ds(384 + yy * 48, 48), pl.ds(0, 256)] = jnp.where(c == 1, pltpu.roll(main, 192, 1), main)
    for copy in (
        pltpu.make_async_copy(acc.at[pl.ds(288, 96), pl.ds(0, 640)], o_qkv, osem.at[6]),
        pltpu.make_async_copy(acc.at[pl.ds(384, 96), pl.ds(0, 256)], o_wout, osem.at[7]),
    ):
        copy.start()
        results.append(copy)

    for i in range(4):
        d_core(i).wait_send()
        d_y(i).wait_send()
        d_1(i).wait_send()
        u_a(i, i == 0).wait_send()
        u_b(i).wait_send()
    for h in range(2):
        d_x(h).wait_send()
    d_2().wait_send()
    for j in range(2):
        u_y(j).wait_send()
        u_2(j).wait_send()
    for p in range(8):
        q_core(p).wait_send()
        if p != 5:
            q_a(p).wait_send()
            q_b(p).wait_send()
    for n in range(3):
        q_plane(n).wait_send()

    @pl.when(zl == c)
    def _():
        q_line(0).wait_send()
        for n in (1, 2, 3):
            final(n, y).wait_send()
        for p in (6, 7, 0, 1, 2, 3, 4):
            q_2(p).wait_send()

    @pl.when(zl != c)
    def _():
        for n in (1, 2):
            q_line(n).wait_send()
        for p in (6, 7, 0, 1, 2, 3, 4):
            q_1(p).wait_send()

    back(0).wait()
    back(1).wait()

    @pl.when(x == 0)
    def _():
        back_from_relay().wait_send()

    keep.wait()
    out_copy.wait()
    own_out.wait()
    for copy in results:
        copy.wait()
    for copy in sends_o + sends_g:
        copy.wait()


def fits(tokens, global_states, w_qkv, w_up):
    return (
        lax.axis_size("seq") == 8
        and lax.axis_size("batch") == 4
        and tokens.shape == (1, BLOCK, HEADS * HEAD_DIM)
        and global_states.shape == (1, 128, HEADS * HEAD_DIM)
        and w_qkv.shape == (HEADS * HEAD_DIM, 3 * HEADS * HEAD_DIM)
        and w_up.shape == (HEADS * HEAD_DIM, 3072)
    )


def finish_kernel(*refs):
    ins, outs = refs[:10], refs[10:]
    for i in range(8):
        outs[i][...] = ins[i][:, : outs[i].shape[1]]
    for i in range(7):
        outs[8 + i][...] = ins[8][i, :]
    outs[15][...] = ins[9][0, :]


def fused(
    tokens, global_states, token_seg, global_seg, attn_gain, attn_shift, glob_gain, glob_shift, w_qkv, w_out,
    ffn_gain, ffn_shift, w_up, up_bias, w_down, down_bias, out_cotangent, global_cotangent,
):
    tok, width = tokens.shape[1:]
    glob = global_states.shape[1]
    hidden = w_up.shape[1]
    n_seq, n_batch = lax.axis_size("seq"), lax.axis_size("batch")
    rows, slots = tok + glob, glob // n_seq
    wide = tok + slots
    chunk, part, side = hidden // n_seq, width // n_seq, width // n_batch
    pairs = HEADS // 2
    eighth = (2, 2, 2)
    dma = pltpu.SemaphoreType.DMA

    def any_space():
        return pl.BlockSpec(memory_space=pl.ANY)

    def vmem():
        return pl.BlockSpec(memory_space=pltpu.VMEM)

    def low(*shape):
        return pltpu.VMEM(shape, BF)

    def full(*shape):
        return pltpu.VMEM(shape, F32)

    scratch = [
        low(rows, width), low(rows, width), low(rows, 3 * width), low(width, width),
        low(pairs, rows, 2 * tok + 2 * glob), low(width, tok + 128), low(wide, width), full(wide, width),
        low(wide, width), low(width, tok + 128), low(wide, width), low(width, tok + 128),
        full(rows, width), full(rows, width), low(wide, width), low(rows, 128), low(rows, 128),
        low(width, 3 * width), low(width, width), low(width, width), low(width, width),
        full(128, glob), full(16, tok), full(glob, width), low(glob, width + 128),
        low(n_seq, slots, width + 128), low(glob, width + 128),
        low(3, 2, slots, width), low(slots, width), low(slots, width), low(slots, width),
        full(16, width), full(n_seq, 16, 128), full(n_seq - 1, 16, 128), full(4, 16, 128), full(4, width),
        low(4, 2, 2, 2, side, chunk), low(4, 2, 2, side, chunk), low(4, 2, side, chunk), low(2, 2, side, chunk),
        low(2, side, chunk), low(side, chunk),
        low(4, 2, *eighth, 2, part // 2, chunk), low(4, *eighth, 2, part // 2, chunk), low(4, 2, 2, 2, part // 2, chunk),
        low(2, 2, 2, 2, part // 2, chunk), low(2, 2, 2, part // 2, chunk), low(2, 2, part // 2, chunk),
        low(8, 2, 2, 2, part // 2, chunk), low(8, 2, 2, part // 2, chunk), low(8, 2, part // 2, chunk),
        low(8, 2, part // 2, chunk), low(8, part // 2, chunk),
        low(3, part // 2, 896), low(2, part // 2, 896),
        full(wide, 256), full(wide, 256),
        dma((8,)), dma((2, 2)), dma((1,)), dma((1,)),
        *[dma((8,)) for _ in range(10)], dma((9,)), dma((9,)),
        *[dma((4,)) for _ in range(10)], *[dma((4,)) for _ in range(10)], *[dma((8,)) for _ in range(10)],
        *[dma((3,)) for _ in range(6)], *[dma((4,)) for _ in range(4)], dma((8,)), dma((2,)),
    ]

    results = pl.pallas_call(
        layer_kernel,
        out_shape=[
            jax.ShapeDtypeStruct((tok, width), BF),
            jax.ShapeDtypeStruct((glob, width), BF),
            jax.ShapeDtypeStruct((tok, width), BF),
            jax.ShapeDtypeStruct((glob, width), BF),
            jax.ShapeDtypeStruct((part, 640), F32),
            jax.ShapeDtypeStruct((part, 256), F32),
            jax.ShapeDtypeStruct((part, 2 * chunk), F32),
            jax.ShapeDtypeStruct((side, chunk), F32),
            jax.ShapeDtypeStruct((8, part), F32),
            jax.ShapeDtypeStruct((1, chunk), F32),
        ],
        in_specs=[any_space(), any_space(), vmem(), vmem(), vmem(), vmem(), vmem(), vmem(), any_space(), any_space(),
                  vmem(), vmem(), any_space(), vmem(), any_space(), vmem(), any_space(), any_space()],
        out_specs=[any_space()] * 8 + [vmem()] * 2,
        scratch_shapes=scratch,
        compiler_params=pltpu.CompilerParams(
            collective_id=0, has_side_effects=True, vmem_limit_bytes=64 * 1024 * 1024
        ),
        name="layer",
    )(
        tokens[0], global_states[0], token_seg, global_seg, attn_gain, attn_shift, glob_gain,
        glob_shift, w_qkv, w_out, ffn_gain, ffn_shift, w_up, up_bias, w_down, down_bias,
        out_cotangent[0], global_cotangent[0],
    )
    *large, vectors, ub = results
    columns = {4: 3 * side, 5: side}
    results = pl.pallas_call(
        finish_kernel,
        out_shape=[
            jax.ShapeDtypeStruct((one.shape[0], columns.get(i, one.shape[1])), one.dtype) for i, one in enumerate(large)
        ]
        + [jax.ShapeDtypeStruct((part,), F32)] * 7
        + [jax.ShapeDtypeStruct((chunk,), F32)],
        in_specs=[vmem()] * 10,
        out_specs=[vmem()] * 16,
        name="results",
    )(*large, vectors, ub)
    out, gout, tgrad, ggrad, g_qkv, g_out, g_up, g_down, *g_vec, g_ub = results
    return (
        out[None], gout[None], tgrad[None], ggrad[None], g_vec[0], g_vec[1], g_vec[2], g_vec[3], g_qkv, g_out,
        g_vec[4], g_vec[5], g_up, g_ub, g_down.T, g_vec[6],
    )


def local(tokens, global_states, token_seg, global_seg, *rest):
    w_qkv, w_up = rest[4], rest[8]
    way = fused if fits(tokens, global_states, w_qkv, w_up) else general
    return way(tokens, global_states, token_seg, global_seg, *rest)


def solution(mesh):
    placed = (
        P("batch", "seq", None),
        P("batch", None, None),
        P("batch", "seq"),
        P("batch", None),
        P(),
        P(),
        P(),
        P(),
        P(),
        P(),
        P(),
        P(),
        P(),
        P(),
        P(),
        P(),
        P("batch", "seq", None),
        P("batch", None, None),
    )
    return jax.shard_map(
        local,
        mesh=mesh,
        in_specs=placed,
        out_specs=(
            P("batch", "seq", None),
            P("batch", None, None),
            P("batch", "seq", None),
            P("batch", None, None),
            P("seq"),
            P("seq"),
            P("seq"),
            P("seq"),
            P("seq", "batch"),
            P("seq", "batch"),
            P("seq"),
            P("seq"),
            P("seq", "batch"),
            P("seq"),
            P("seq", "batch"),
            P("seq"),
        ),
        check_vma=False,
    )
```

```python
import functools

import jax
import jax.numpy as jnp
from jax import lax
from jax.experimental import pallas as pl
from jax.experimental.pallas import tpu as pltpu
from jax.sharding import PartitionSpec as P

HEADS = 12
HEAD_DIM = 64
BLOCK = 512


EPS = 1e-05
NEGATIVE = -1e30


def from_behind(block, axis, distance):
    devices = range(lax.axis_size(axis))
    route = [((i - distance) % len(devices), i) for i in devices]
    return lax.ppermute(block, axis, route)


def norm_rows(source, scaling, offset):
    center = jnp.mean(source, axis=-1, keepdims=True)
    spread = source - center
    variance = jnp.mean(spread * spread, axis=-1, keepdims=True)
    return spread * lax.rsqrt(variance + EPS) * scaling + offset


def norm_back(source, scaling, offset, upstream):
    _, pullback = jax.vjp(norm_rows, source, scaling, offset)
    return pullback(upstream)


def project(former, latter):
    return jnp.einsum("rsd,de->rse", former, latter, preferred_element_type=jnp.float32)


def project_back(former, latter):
    return jnp.einsum("rse,de->rsd", former, latter, preferred_element_type=jnp.float32)


def outer_sum(former, latter):
    return jnp.einsum("rsd,rse->de", former, latter, preferred_element_type=jnp.float32)


def gelu_exact(hidden):
    return jax.nn.gelu(hidden, approximate=False)


def ffn_forward(state, ffn_gain, ffn_shift, w_up, up_bias, w_down, down_bias):
    normed = norm_rows(state, ffn_gain, ffn_shift).astype(jnp.bfloat16)
    hidden = project(normed, w_up) + up_bias
    active = gelu_exact(hidden).astype(jnp.bfloat16)
    result = state + project(active, w_down) + down_bias
    return (result, (normed, hidden, active))


def ffn_backward(state, stored, upstream, ffn_gain, ffn_shift, w_up, w_down):
    normed, hidden, active = stored
    upstream_low = upstream.astype(jnp.bfloat16)
    grad_down = outer_sum(active, upstream_low)
    grad_down_bias = jnp.sum(upstream, axis=(0, 1))
    grad_active = project_back(upstream_low, w_down)
    _, gelu_pull = jax.vjp(gelu_exact, hidden)
    grad_hidden = gelu_pull(grad_active)[0].astype(jnp.bfloat16)
    grad_up = outer_sum(normed, grad_hidden)
    grad_up_bias = jnp.sum(grad_hidden.astype(jnp.float32), axis=(0, 1))
    grad_normed = project_back(grad_hidden, w_up)
    grad_state, grad_gain, grad_shift = norm_back(state, ffn_gain, ffn_shift, grad_normed)
    return (
        upstream + grad_state,
        (grad_gain, grad_shift, grad_up, grad_up_bias, grad_down, grad_down_bias),
    )


def local_scores(queries, keys_near, seg_near, keys_far, seg_far):
    scaling = HEAD_DIM ** (-0.5)
    near_scores = (
        jnp.einsum("rnqhd,rnkhd->rnhqk", queries, keys_near, preferred_element_type=jnp.float32)
        * scaling
    )
    far_scores = (
        jnp.einsum("rnqhd,rghd->rnhqg", queries, keys_far, preferred_element_type=jnp.float32)
        * scaling
    )
    near_open = (seg_near[:, :, :, None] == seg_near[:, :, None, :])[:, :, None]
    far_open = (seg_near[:, :, :, None] == seg_far[:, None, None, :])[:, :, None]
    return (jnp.where(near_open, near_scores, NEGATIVE), jnp.where(far_open, far_scores, NEGATIVE))


def local_forward(queries, keys_near, values_near, seg_near, keys_far, values_far, seg_far):
    near_scores, far_scores = local_scores(queries, keys_near, seg_near, keys_far, seg_far)
    maxima = jnp.maximum(jnp.max(near_scores, axis=-1), jnp.max(far_scores, axis=-1))
    near_exp = jnp.exp(near_scores - maxima[..., None])
    far_exp = jnp.exp(far_scores - maxima[..., None])
    totals = jnp.sum(near_exp, axis=-1) + jnp.sum(far_exp, axis=-1)
    near_weights = (near_exp / totals[..., None]).astype(jnp.bfloat16)
    far_weights = (far_exp / totals[..., None]).astype(jnp.bfloat16)
    mixed_out = jnp.einsum(
        "rnhqk,rnkhd->rnqhd", near_weights, values_near, preferred_element_type=jnp.float32
    )
    mixed_out = mixed_out + jnp.einsum(
        "rnhqg,rghd->rnqhd", far_weights, values_far, preferred_element_type=jnp.float32
    )
    return (mixed_out, maxima + jnp.log(totals))


def local_backward(
    queries, keys_near, values_near, seg_near, keys_far, values_far, seg_far, logsum, upstream
):
    scaling = HEAD_DIM ** (-0.5)
    near_scores, far_scores = local_scores(queries, keys_near, seg_near, keys_far, seg_far)
    near_weights = jnp.exp(near_scores - logsum[..., None])
    far_weights = jnp.exp(far_scores - logsum[..., None])
    near_grad = jnp.einsum(
        "rnqhd,rnkhd->rnhqk", upstream, values_near, preferred_element_type=jnp.float32
    )
    far_grad = jnp.einsum(
        "rnqhd,rghd->rnhqg", upstream, values_far, preferred_element_type=jnp.float32
    )
    row_inner = jnp.sum(near_weights * near_grad, axis=-1) + jnp.sum(
        far_weights * far_grad, axis=-1
    )
    near_score_grad = (near_weights * (near_grad - row_inner[..., None])).astype(jnp.bfloat16)
    far_score_grad = (far_weights * (far_grad - row_inner[..., None])).astype(jnp.bfloat16)
    grad_queries = jnp.einsum(
        "rnhqk,rnkhd->rnqhd", near_score_grad, keys_near, preferred_element_type=jnp.float32
    )
    grad_queries = scaling * (
        grad_queries
        + jnp.einsum(
            "rnhqg,rghd->rnqhd", far_score_grad, keys_far, preferred_element_type=jnp.float32
        )
    )
    grad_keys = scaling * jnp.einsum(
        "rnhqk,rnqhd->rnkhd", near_score_grad, queries, preferred_element_type=jnp.float32
    )
    grad_values = jnp.einsum(
        "rnhqk,rnqhd->rnkhd",
        near_weights.astype(jnp.bfloat16),
        upstream,
        preferred_element_type=jnp.float32,
    )
    grad_keys_far = scaling * jnp.einsum(
        "rnhqg,rnqhd->rghd", far_score_grad, queries, preferred_element_type=jnp.float32
    )
    grad_values_far = jnp.einsum(
        "rnhqg,rnqhd->rghd",
        far_weights.astype(jnp.bfloat16),
        upstream,
        preferred_element_type=jnp.float32,
    )
    return (grad_queries, grad_keys, grad_values, grad_keys_far, grad_values_far)


def global_scores(glob_queries, glob_keys, glob_seg, key_rows, seg_tokens):
    scaling = HEAD_DIM ** (-0.5)
    remote_scores = (
        jnp.einsum("rghd,rshd->rhgs", glob_queries, key_rows, preferred_element_type=jnp.float32)
        * scaling
    )
    own_scores = (
        jnp.einsum("rghd,rjhd->rhgj", glob_queries, glob_keys, preferred_element_type=jnp.float32)
        * scaling
    )
    remote_open = glob_seg[:, None, :, None] == seg_tokens[:, None, None, :]
    own_open = glob_seg[:, None, :, None] == glob_seg[:, None, None, :]
    return (
        jnp.where(remote_open, remote_scores, NEGATIVE),
        jnp.where(own_open, own_scores, NEGATIVE),
    )


def general(
    tokens,
    global_states,
    token_seg,
    global_seg,
    attn_gain,
    attn_shift,
    glob_gain,
    glob_shift,
    w_qkv,
    w_out,
    ffn_gain,
    ffn_shift,
    w_up,
    up_bias,
    w_down,
    down_bias,
    out_cotangent,
    global_cotangent,
):
    row_count, tok_count, model_width = tokens.shape
    glob_count = global_states.shape[1]
    half_block = BLOCK // 2
    block_count = tok_count // BLOCK
    seq_devices = lax.axis_size("seq")
    scaling = HEAD_DIM ** (-0.5)
    low_type = jnp.bfloat16
    arrived = from_behind(tokens[:, :half_block], "seq", -1)
    sectioned = jnp.concatenate([tokens[:, half_block:], arrived], axis=1).astype(jnp.float32)
    glob_state = global_states.astype(jnp.float32)
    normed = norm_rows(sectioned, attn_gain, attn_shift).astype(low_type)
    glob_normed = norm_rows(glob_state, glob_gain, glob_shift).astype(low_type)
    projected = (
        project(normed, w_qkv).astype(low_type).reshape(row_count, tok_count, 3, HEADS, HEAD_DIM)
    )
    glob_proj = (
        project(glob_normed, w_qkv)
        .astype(low_type)
        .reshape(row_count, glob_count, 3, HEADS, HEAD_DIM)
    )
    queries = projected[:, :, 0]
    key_rows = projected[:, :, 1]
    value_rows = projected[:, :, 2]
    glob_queries = glob_proj[:, :, 0]
    glob_keys = glob_proj[:, :, 1]
    glob_values = glob_proj[:, :, 2]
    block_shape = (row_count, block_count, BLOCK, HEADS, HEAD_DIM)
    block_queries = queries.reshape(block_shape)
    block_keys = key_rows.reshape(block_shape)
    block_values = value_rows.reshape(block_shape)
    block_seg = token_seg.reshape(row_count, block_count, BLOCK)
    local_out, local_logsum = local_forward(
        block_queries, block_keys, block_values, block_seg, glob_keys, glob_values, global_seg
    )
    remote_scores, own_scores = global_scores(
        glob_queries, glob_keys, global_seg, key_rows, token_seg
    )
    maxima = jnp.maximum(
        lax.pmax(jnp.max(remote_scores, axis=-1), "seq"), jnp.max(own_scores, axis=-1)
    )
    remote_total = jnp.sum(jnp.exp(remote_scores - maxima[..., None]), axis=-1)
    totals = lax.psum(remote_total, "seq") + jnp.sum(
        jnp.exp(own_scores - maxima[..., None]), axis=-1
    )
    remote_weights = (jnp.exp(remote_scores - maxima[..., None]) / totals[..., None]).astype(
        low_type
    )
    own_weights = (jnp.exp(own_scores - maxima[..., None]) / totals[..., None]).astype(low_type)
    remote_part = jnp.einsum(
        "rhgs,rshd->rghd", remote_weights, value_rows, preferred_element_type=jnp.float32
    )
    glob_out = lax.psum(remote_part, "seq")
    glob_out = glob_out + jnp.einsum(
        "rhgj,rjhd->rghd", own_weights, glob_values, preferred_element_type=jnp.float32
    )
    glob_logsum = maxima + jnp.log(totals)
    attended = local_out.reshape(row_count, tok_count, model_width).astype(low_type)
    glob_attended = glob_out.reshape(row_count, glob_count, model_width).astype(low_type)
    attn_sum = sectioned + project(attended, w_out)
    glob_sum = glob_state + project(glob_attended, w_out)
    result, stored = ffn_forward(attn_sum, ffn_gain, ffn_shift, w_up, up_bias, w_down, down_bias)
    glob_result, glob_stored = ffn_forward(
        glob_sum, ffn_gain, ffn_shift, w_up, up_bias, w_down, down_bias
    )
    grad_attn_sum, tok_ffn = ffn_backward(
        attn_sum, stored, out_cotangent.astype(jnp.float32), ffn_gain, ffn_shift, w_up, w_down
    )
    grad_glob_sum, glob_ffn = ffn_backward(
        glob_sum,
        glob_stored,
        global_cotangent.astype(jnp.float32),
        ffn_gain,
        ffn_shift,
        w_up,
        w_down,
    )
    branch_low = grad_attn_sum.astype(low_type)
    glob_branch_low = grad_glob_sum.astype(low_type)
    grad_out_all = (
        outer_sum(attended, branch_low) + outer_sum(glob_attended, glob_branch_low) / seq_devices
    )
    upstream_mix = project_back(branch_low, w_out).astype(low_type).reshape(block_shape)
    glob_upstream = (
        project_back(glob_branch_low, w_out)
        .astype(low_type)
        .reshape(row_count, glob_count, HEADS, HEAD_DIM)
    )
    remote_exact = jnp.exp(remote_scores - glob_logsum[..., None])
    own_exact = jnp.exp(own_scores - glob_logsum[..., None])
    remote_grad = jnp.einsum(
        "rghd,rshd->rhgs", glob_upstream, value_rows, preferred_element_type=jnp.float32
    )
    own_grad = jnp.einsum(
        "rghd,rjhd->rhgj", glob_upstream, glob_values, preferred_element_type=jnp.float32
    )
    row_inner = lax.psum(jnp.sum(remote_exact * remote_grad, axis=-1), "seq")
    row_inner = row_inner + jnp.sum(own_exact * own_grad, axis=-1)
    remote_score_grad = (remote_exact * (remote_grad - row_inner[..., None])).astype(low_type)
    own_score_grad = (own_exact * (own_grad - row_inner[..., None])).astype(low_type)
    remote_queries = scaling * jnp.einsum(
        "rhgs,rshd->rghd", remote_score_grad, key_rows, preferred_element_type=jnp.float32
    )
    tok_keys_extra = scaling * jnp.einsum(
        "rhgs,rghd->rshd", remote_score_grad, glob_queries, preferred_element_type=jnp.float32
    )
    tok_values_extra = jnp.einsum(
        "rhgs,rghd->rshd",
        remote_exact.astype(low_type),
        glob_upstream,
        preferred_element_type=jnp.float32,
    )
    own_queries = scaling * jnp.einsum(
        "rhgj,rjhd->rghd", own_score_grad, glob_keys, preferred_element_type=jnp.float32
    )
    own_keys = scaling * jnp.einsum(
        "rhgj,rghd->rjhd", own_score_grad, glob_queries, preferred_element_type=jnp.float32
    )
    own_values = jnp.einsum(
        "rhgj,rghd->rjhd",
        own_exact.astype(low_type),
        glob_upstream,
        preferred_element_type=jnp.float32,
    )
    grad_queries, grad_keys, grad_values, grad_keys_far, grad_values_far = local_backward(
        block_queries,
        block_keys,
        block_values,
        block_seg,
        glob_keys,
        glob_values,
        global_seg,
        local_logsum,
        upstream_mix,
    )
    far_grads = lax.psum((remote_queries, grad_keys_far, grad_values_far), "seq")
    head_shape = (row_count, tok_count, HEADS, HEAD_DIM)
    grad_projected = jnp.stack(
        [
            grad_queries.reshape(head_shape),
            grad_keys.reshape(head_shape) + tok_keys_extra,
            grad_values.reshape(head_shape) + tok_values_extra,
        ],
        axis=2,
    )
    grad_projected = grad_projected.reshape(row_count, tok_count, 3 * model_width).astype(low_type)
    glob_grad_projected = jnp.stack(
        [far_grads[0] + own_queries, far_grads[1] + own_keys, far_grads[2] + own_values], axis=2
    )
    glob_grad_projected = glob_grad_projected.reshape(
        row_count, glob_count, 3 * model_width
    ).astype(low_type)
    grad_qkv_all = (
        outer_sum(normed, grad_projected)
        + outer_sum(glob_normed, glob_grad_projected) / seq_devices
    )
    grad_normed = project_back(grad_projected, w_qkv)
    glob_grad_normed = project_back(glob_grad_projected, w_qkv)
    grad_sectioned, attn_gain_grad, attn_shift_grad = norm_back(
        sectioned, attn_gain, attn_shift, grad_normed
    )
    grad_sectioned = grad_sectioned + grad_attn_sum
    glob_grad_state, glob_gain_grad, glob_shift_grad = norm_back(
        glob_state, glob_gain, glob_shift, glob_grad_normed
    )
    global_grad = (glob_grad_state + grad_glob_sum).astype(low_type)
    grad_low = grad_sectioned.astype(low_type)
    returned = from_behind(grad_low[:, tok_count - half_block :], "seq", 1)
    token_grad = jnp.concatenate([returned, grad_low[:, : tok_count - half_block]], axis=1)
    ffn_gain_all = tok_ffn[0] + glob_ffn[0] / seq_devices
    ffn_shift_all = tok_ffn[1] + glob_ffn[1] / seq_devices
    up_all = tok_ffn[2] + glob_ffn[2] / seq_devices
    up_bias_all = tok_ffn[3] + glob_ffn[3] / seq_devices
    down_all = tok_ffn[4] + glob_ffn[4] / seq_devices
    down_bias_all = tok_ffn[5] + glob_ffn[5] / seq_devices
    glob_gain_all = glob_gain_grad / seq_devices
    glob_shift_all = glob_shift_grad / seq_devices
    mat_sums = (
        lax.psum_scatter(
            grad_qkv_all.astype(jnp.bfloat16), "batch", scatter_dimension=1, tiled=True
        ).astype(jnp.float32),
        lax.psum_scatter(
            grad_out_all.astype(jnp.bfloat16), "batch", scatter_dimension=1, tiled=True
        ).astype(jnp.float32),
        lax.psum_scatter(
            up_all.astype(jnp.bfloat16), "batch", scatter_dimension=1, tiled=True
        ).astype(jnp.float32),
        lax.psum_scatter(
            down_all.astype(jnp.bfloat16), "batch", scatter_dimension=1, tiled=True
        ).astype(jnp.float32),
    )
    vec_sums = (
        lax.psum(attn_gain_grad.astype(jnp.bfloat16), "batch").astype(jnp.float32),
        lax.psum(attn_shift_grad.astype(jnp.bfloat16), "batch").astype(jnp.float32),
        lax.psum(glob_gain_all.astype(jnp.bfloat16), "batch").astype(jnp.float32),
        lax.psum(glob_shift_all.astype(jnp.bfloat16), "batch").astype(jnp.float32),
        lax.psum(ffn_gain_all.astype(jnp.bfloat16), "batch").astype(jnp.float32),
        lax.psum(ffn_shift_all.astype(jnp.bfloat16), "batch").astype(jnp.float32),
        lax.psum(up_bias_all.astype(jnp.bfloat16), "batch").astype(jnp.float32),
        lax.psum(down_bias_all.astype(jnp.bfloat16), "batch").astype(jnp.float32),
    )
    shares = (
        lax.psum_scatter(vec_sums[0], "seq", scatter_dimension=0, tiled=True),
        lax.psum_scatter(vec_sums[1], "seq", scatter_dimension=0, tiled=True),
        lax.psum_scatter(vec_sums[2], "seq", scatter_dimension=0, tiled=True),
        lax.psum_scatter(vec_sums[3], "seq", scatter_dimension=0, tiled=True),
        lax.psum_scatter(mat_sums[0], "seq", scatter_dimension=0, tiled=True),
        lax.psum_scatter(mat_sums[1], "seq", scatter_dimension=0, tiled=True),
        lax.psum_scatter(vec_sums[4], "seq", scatter_dimension=0, tiled=True),
        lax.psum_scatter(vec_sums[5], "seq", scatter_dimension=0, tiled=True),
        lax.psum_scatter(mat_sums[2], "seq", scatter_dimension=0, tiled=True),
        lax.psum_scatter(vec_sums[6], "seq", scatter_dimension=0, tiled=True),
        lax.psum_scatter(mat_sums[3], "seq", scatter_dimension=0, tiled=True),
        lax.psum_scatter(vec_sums[7], "seq", scatter_dimension=0, tiled=True),
    )
    matrices = (shares[4], shares[5], shares[8], shares[10])
    vectors = (
        shares[0],
        shares[1],
        shares[2],
        shares[3],
        shares[6],
        shares[7],
        shares[9],
        shares[11],
    )
    return (
        result.astype(low_type),
        glob_result.astype(low_type),
        token_grad,
        global_grad,
        vectors[0],
        vectors[1],
        vectors[2],
        vectors[3],
        matrices[0],
        matrices[1],
        vectors[4],
        vectors[5],
        matrices[2],
        vectors[6],
        matrices[3],
        vectors[7],
    )


MESH = pl.DeviceIdType.MESH
BF = jnp.bfloat16
F32 = jnp.float32


def dot_nn(left, right):
    return lax.dot_general(left, right, (((1,), (0,)), ((), ())), preferred_element_type=F32)


def dot_nt(left, right):
    return lax.dot_general(left, right, (((1,), (1,)), ((), ())), preferred_element_type=F32)


def lanes_of(shape):
    return lax.broadcasted_iota(jnp.int32, shape, len(shape) - 1)


def two_parts(value):
    high = value.astype(BF)
    return high, (value - high.astype(F32)).astype(BF)


def norm_stats(value):
    center = jnp.mean(value, axis=-1, keepdims=True)
    spread = value - center
    variance = jnp.mean(spread * spread, axis=-1, keepdims=True)
    return spread, lax.rsqrt(variance + EPS)


def norm_pull(value, gain, upstream):
    spread, scale = norm_stats(value)
    unit = spread * scale
    scaled = upstream * gain
    first = jnp.mean(scaled, axis=-1, keepdims=True)
    second = jnp.mean(scaled * unit, axis=-1, keepdims=True)
    grad = scale * (scaled - first - unit * second)
    return (
        grad,
        jnp.sum(upstream * unit, axis=0, keepdims=True),
        jnp.sum(upstream, axis=0, keepdims=True),
    )


def gelu_pair(hidden):
    size = jnp.abs(hidden) * 0.7071067811865476
    step = 1.0 / (1.0 + 0.3275911 * size)
    bell = jnp.exp(-(size * size))
    series = 1.061405429 * 0.5
    for term in (-1.453152027, 1.421413741, -0.284496736, 0.254829592):
        series = series * step + term * 0.5
    tail = series * step * bell
    mass = jnp.where(hidden < 0.0, tail, 1.0 - tail)
    return hidden * mass, mass + hidden * (bell * 0.3989422804014327)


def layer_kernel(
    tokens, gstates, tseg, gseg, attn_gain, attn_shift, glob_gain, glob_shift, w_qkv, w_out,
    ffn_gain, ffn_shift, w_up, up_bias, w_down, down_bias, cotan, gcotan,
    o_out, o_gout, o_tgrad, o_ggrad, o_qkv, o_wout, o_up, o_down, o_vec, o_ub,
    sec, nrm, proj, kvt, probs, att_t, att, x2, n2, n2t, ct, ct_t, acc_full, gn2_full, gatt, qaug, kaug,
    wq, wo, wu, wd,
    lse_t, rl_t, cx, msg1, rcv1, rcv2, rcv3, rcv3b, gsum, gall, vec, vmsg, vrcv, vsum, ub,
    gd, r0d, r1d, r2d, r3d, r4d, gu, r0u, r1u, r2u, r3u, r4u, r0q, r1q, r2q, r3q, r4q, fmsg, frcv, hid_a, hid_b,
    loc, wsem, hs, hr, m1s, m1r, m2s, m2r, m3s, m3r, gos, gor, ggs_s, ggs_r, vs, vr,
    d0s, d0r, d1s, d1r, d2s, d2r, d3s, d3r, d4s, d4r,
    u0s, u0r, u1s, u1r, u2s, u2r, u3s, u3r, u4s, u4r,
    q0s, q0r, q1s, q1r, q2s, q2r, q3s, q3r, q4s, q4r,
    qps, qpr, qls, qlr, vbs, vbr, fs, fr, hs2, hr2, osem, gsem,
):
    tok, width = tokens.shape
    glob = gstates.shape[0]
    rows = tok + glob
    n_seq = lax.axis_size("seq")
    slots = glob // n_seq
    wide = tok + slots
    half = tok // 2
    pairs = HEADS // 2
    chunk = up_bias.shape[0] // n_seq
    n_chunk = up_bias.shape[0] // width
    side, part = width // 4, width // n_seq
    tail = 128

    s = lax.axis_index("seq")
    b = lax.axis_index("batch")
    x, zl, zh = s % 2, (s // 2) % 2, s // 4
    c, y = b % 2, b // 2
    dev_c, dev_y = (s, b + 1 - 2 * c), (s, b + 2 - 4 * y)
    dev_cy, dev_xy = (s, dev_y[1] + 1 - 2 * c), (s + 1 - 2 * x, dev_y[1])
    dev_x, dev_1, dev_2 = (s + 1 - 2 * x, b), (s + 2 - 4 * zl, b), (s + 4 - 8 * zh, b)

    def flip(k):
        other = s
        if k & 1:
            other = other + 1 - 2 * x
        if k & 2:
            other = other + 2 - 4 * zl
        if k & 4:
            other = other + 4 - 8 * zh
        return other

    def remote(src, dst, ss, rs, dev):
        return pltpu.make_async_remote_copy(
            src_ref=src, dst_ref=dst, send_sem=ss, recv_sem=rs, device_id=dev, device_id_type=MESH
        )

    peers = tuple(range(1, n_seq))
    acc, gn2 = acc_full.at[pl.ds(0, wide)], gn2_full.at[pl.ds(0, wide)]
    score = (acc_full, gn2_full)

    def as_row(vector):
        return vector[...].reshape(1, vector.shape[0])

    attn_gain, attn_shift, glob_gain, glob_shift, ffn_gain, ffn_shift, down_bias = (
        as_row(v) for v in (attn_gain, attn_shift, glob_gain, glob_shift, ffn_gain, ffn_shift, down_bias)
    )

    my_slots = pl.multiple_of(s * slots, slots)
    loads = [
        (tokens.at[pl.ds(half, half)], sec.at[pl.ds(0, half)]),
        (gstates, sec.at[pl.ds(tok, glob)]),
        (w_qkv, wq),
        (cotan, ct.at[pl.ds(0, tok)]),
        (gcotan.at[pl.ds(my_slots, slots)], ct.at[pl.ds(tok, slots)]),
        (w_out, wo),
    ]
    loads = [pltpu.make_async_copy(a, d, loc.at[i]) for i, (a, d) in enumerate(loads)]
    for load in loads:
        load.start()

    def piece_of(i, o):
        return 4 * (i // 2) + 2 * o + i % 2

    def stream_up(i):
        copies = []
        for o in range(2):
            at = piece_of(i, o) * chunk
            at = at if isinstance(at, int) else pl.multiple_of(at, chunk)
            copies.append(
                pltpu.make_async_copy(w_up.at[:, pl.ds(at, chunk)], wu.at[:, pl.ds(o * chunk, chunk)], wsem.at[0, o])
            )
        return copies

    def stream_down(i, to, which):
        copies = []
        for o in range(2):
            at = piece_of(i, o) * chunk
            at = at if isinstance(at, int) else pl.multiple_of(at, chunk)
            copies.append(pltpu.make_async_copy(w_down.at[pl.ds(at, chunk)], to.at[pl.ds(o * chunk, chunk)], wsem.at[which, o]))
        return copies

    def stream(i):
        return stream_up(i) + stream_down(i, wd, 1)

    for i, to in ((0, wu), (1, wd)):
        for copy in stream_down(i, to, i):
            copy.start()

    bar = pltpu.get_barrier_semaphore()
    for k in peers:
        pl.semaphore_signal(bar, inc=1, device_id=(flip(k), b), device_id_type=MESH)
    pl.semaphore_signal(bar, inc=1, device_id=dev_c, device_id_type=MESH)
    for dev in (dev_y, dev_cy, dev_xy):
        pl.semaphore_signal(bar, inc=1, device_id=dev, device_id_type=MESH)
    pl.semaphore_wait(bar, len(peers) + 4)
    halo = remote(
        tokens.at[pl.ds(0, half)], sec.at[pl.ds(half, half)], hs.at[0], hr.at[0],
        (lax.rem(s + n_seq - 1, n_seq), b),
    )
    halo.start()

    seg_row = jnp.concatenate([tseg[...], gseg[...]], axis=1)
    which = lax.broadcasted_iota(jnp.int32, (128, rows), 0)
    col = lanes_of((128, rows))
    is_glob = col >= tok
    same = which == seg_row
    q_t = jnp.where(which < 3, jnp.where(same, 1.0, 0.0), jnp.where((which == 3) & is_glob, 1.0, 0.0))
    far = jnp.where(s == 0, 0.0, NEGATIVE)
    k_t = jnp.where(which < 3, jnp.where(same, 0.0, NEGATIVE), jnp.where((which == 3) & is_glob, far, 0.0))
    qaug[...] = jnp.transpose(q_t).astype(BF)
    kaug[...] = jnp.transpose(k_t).astype(BF)

    def norm_to(first, count, gain, shift):
        for r in range(first, first + count, 128):
            spread, scale = norm_stats(sec[pl.ds(r, 128), :].astype(F32))
            nrm[pl.ds(r, 128), :] = (spread * scale * gain + shift).astype(BF)

    def project_rows(first, count):
        def step(i, carry):
            at = pl.multiple_of(i * width, width)
            proj[pl.ds(first, count), pl.ds(at, width)] = dot_nn(
                nrm[pl.ds(first, count), :], wq[:, pl.ds(at, width)]
            ).astype(BF)
            return carry

        lax.fori_loop(0, 3, step, 0)

    loads[1].wait()
    norm_to(tok, glob, glob_gain, glob_shift)
    loads[0].wait()
    norm_to(0, half, attn_gain, attn_shift)
    loads[2].wait()
    project_rows(tok, glob)
    project_rows(0, half)
    loads[3].wait()
    loads[4].wait()
    ct_t[:, pl.ds(0, wide)] = jnp.transpose(ct[...])
    kept_rows = (((0,), 0, 384), ((1, 0, 0), 384, 96), ((1, 0, 1, 0), 480, 48))
    for i in range(n_chunk):
        to = (wu, wd)[i % 2]
        for copy in stream_down(i, to, i % 2):
            copy.wait()
        for o in range(2):
            grad_active = dot_nt(ct[...], to[pl.ds(o * chunk, chunk), :]).astype(BF)
            for where, first, count in kept_rows:
                kept = gu.at[(i, o) + where]
                kept[...] = grad_active[first : first + count].reshape(kept.shape)
        if i + 2 < n_chunk:
            for copy in stream_down(i + 2, to, i % 2):
                copy.start()
    for copy in stream(0):
        copy.start()
    halo.wait()
    norm_to(half, half, attn_gain, attn_shift)
    project_rows(half, half)

    kvt[:, pl.ds(0, rows)] = jnp.transpose(proj[:, pl.ds(2 * width, width)])
    lane_p = lanes_of((1, 128))
    even = jnp.where(lane_p < HEAD_DIM, HEAD_DIM ** (-0.5), 0.0).astype(BF)
    odd = jnp.where(lane_p < HEAD_DIM, 0.0, HEAD_DIM ** (-0.5)).astype(BF)
    even_one = jnp.where(lane_p < HEAD_DIM, 1.0, 0.0).astype(BF)
    odd_one = jnp.where(lane_p < HEAD_DIM, 0.0, 1.0).astype(BF)
    first_head = lax.broadcasted_iota(jnp.int32, (128, 128), 0) < HEAD_DIM
    lse_t[...] = jnp.zeros_like(lse_t)
    rl_t[...] = jnp.zeros_like(rl_t)

    def glob_forward(p, carry):
        at = pl.multiple_of(p * 128, 128)
        keys = jnp.concatenate([proj[:, pl.ds(width + at, 128)], kaug[...]], axis=1)
        qg = proj[pl.ds(tok, glob), pl.ds(at, 128)]
        qa = qaug[pl.ds(tok, glob), :]
        queries = jnp.concatenate(
            [jnp.concatenate([qg * even, qa], axis=1), jnp.concatenate([qg * odd, qa], axis=1)], axis=0
        )
        scores = dot_nt(keys, queries)
        top = jnp.max(scores, axis=0, keepdims=True)
        raised = jnp.exp(scores - top)
        total = jnp.sum(raised, axis=0, keepdims=True)
        weights = (raised * (1.0 / total)).astype(BF)
        probs[p, :, pl.ds(2 * tok, 2 * glob)] = weights
        mixed = dot_nn(kvt[pl.ds(at, 128), pl.ds(0, rows)], weights)
        cx[:, pl.ds(at, 128)] = jnp.transpose(jnp.where(first_head, mixed[:, :glob], mixed[:, glob:]))
        logsum = top + jnp.log(total)
        lse_t[pl.ds(2 * p, 1), :] = logsum[:, :glob]
        lse_t[pl.ds(2 * p + 1, 1), :] = logsum[:, glob:]
        return carry

    lax.fori_loop(0, pairs, glob_forward, 0, unroll=True)

    lse = jnp.transpose(lse_t[...])
    in_heads = lanes_of((glob, 128)) < HEADS
    lse = jnp.where(in_heads, lse, 0.0)
    part_a, rest = two_parts(lse)
    rest = lse - part_a.astype(F32)
    part_b = rest.astype(BF)
    part_c = rest - part_b.astype(F32)
    packed = part_a.astype(F32) + pltpu.roll(part_b.astype(F32), 16, 1) + pltpu.roll(part_c, 32, 1)
    msg1[:, pl.ds(0, width)] = cx[...].astype(BF)
    msg1[:, pl.ds(width, 128)] = packed.astype(BF)
    sends1 = []
    for k in peers:
        other = flip(k)
        at = pl.multiple_of(other * slots, slots)
        copy = remote(msg1.at[pl.ds(at, slots)], rcv1.at[k], m1s.at[k], m1r.at[k], (other, b))
        copy.start()
        sends1.append(copy)
    rcv1[0] = msg1[pl.ds(my_slots, slots), :]

    def scores_to(slot, p, mask):
        at = pl.multiple_of(p * 128, 128)
        keys = jnp.concatenate([proj[:, pl.ds(width + at, 128)], kaug[...]], axis=1)
        queries = jnp.concatenate([proj[pl.ds(0, tok), pl.ds(at, 128)] * mask, qaug[pl.ds(0, tok), :]], axis=1)
        score[slot][:, pl.ds(0, tok)] = dot_nt(keys, queries)

    def softmax_of(slot, p):
        values = score[slot][:, pl.ds(0, tok)]
        raised = jnp.exp(values - jnp.max(values, axis=0, keepdims=True))
        inverse = 1.0 / jnp.sum(raised, axis=0, keepdims=True)
        weights = raised.astype(BF)
        probs[p, :, pl.ds(slot * tok, tok)] = weights
        rl_t[pl.ds(2 * p + slot, 1), :] = inverse
        here = pl.multiple_of(p * 128 + slot * HEAD_DIM, HEAD_DIM)
        mixed = dot_nn(kvt[pl.ds(here, HEAD_DIM), pl.ds(0, rows)], weights)
        att_t[pl.ds(here, HEAD_DIM), pl.ds(0, tok)] = (mixed * inverse).astype(BF)

    def local_forward_pair(p, carry):
        scores_to(1, p, odd)
        softmax_of(0, p)
        scores_to(0, jnp.minimum(p + 1, pairs - 1), even)
        softmax_of(1, p)
        return carry

    scores_to(0, 0, even)
    lax.fori_loop(0, pairs, local_forward_pair, 0)
    att[pl.ds(0, tok), :] = jnp.transpose(att_t[:, pl.ds(0, tok)])

    loads[5].wait()

    def second_norm(first, count):
        spread, scale = norm_stats(x2[pl.ds(first, count), :])
        n2[pl.ds(first, count), :] = (spread * scale * ffn_gain + ffn_shift).astype(BF)

    for first in range(0, width, 256):
        here = pl.ds(first, 256)
        x2[pl.ds(0, tok), here] = dot_nn(att[pl.ds(0, tok), :], wo[:, here]) + sec[pl.ds(0, tok), here].astype(F32)
    for r in range(0, tok, 128):
        second_norm(r, 128)

    head_of = lanes_of((128, width)) // HEAD_DIM
    spread_heads = jnp.where(head_of == lax.broadcasted_iota(jnp.int32, (128, width), 0), 1.0, 0.0).astype(BF)
    for copy in sends1:
        copy.wait()
    logs = []
    for k in range(n_seq):
        packed = rcv1[k, :, pl.ds(width, 128)].astype(F32)
        logs.append(packed + pltpu.roll(packed, 112, 1) + pltpu.roll(packed, 96, 1))
    high = functools.reduce(jnp.maximum, logs)
    raised = [jnp.exp(one - high) for one in logs]
    total = functools.reduce(jnp.add, raised)
    in_heads = lanes_of((slots, 128)) < HEADS
    shares = jnp.concatenate([jnp.where(in_heads, one / total, 0.0) for one in raised], axis=0)
    share_a, share_b = two_parts(shares)
    shares = dot_nn(share_a, spread_heads) + dot_nn(share_b, spread_heads)
    cx[...] = shares
    mixed = jnp.zeros((slots, width), F32)
    for k in range(n_seq):
        mixed = mixed + shares[k * slots : (k + 1) * slots] * rcv1[k, :, pl.ds(0, width)].astype(F32)
    att[pl.ds(tok, slots), :] = mixed.astype(BF)
    att_t[:, pl.ds(tok, tail)] = jnp.transpose(
        jnp.concatenate([mixed, jnp.zeros((tail - slots, width), F32)], axis=0)
    ).astype(BF)

    x2[pl.ds(tok, slots), :] = dot_nn(att[pl.ds(tok, slots), :], wo[...]) + sec[
        pl.ds(pl.multiple_of(tok + my_slots, slots), slots), :
    ].astype(F32)
    second_norm(tok, slots)
    n2t[:, pl.ds(0, wide)] = jnp.transpose(n2[...])

    def d_core(i):
        return remote(gd.at[i, :, :, 1 - c], r0d.at[i], d0s.at[i], d0r.at[i], dev_c)

    def d_y(i):
        return remote(r0d.at[i, :, 1 - y], r1d.at[i], d1s.at[i], d1r.at[i], dev_y)

    def d_1(i):
        return remote(r1d.at[i, 1 - zl], r2d.at[i // 2, i % 2], d2s.at[i], d2r.at[i], dev_1)

    def d_x(h):
        return remote(r2d.at[h, 1 - x], r3d.at[h], d3s.at[h], d3r.at[h], dev_x)

    def d_2():
        return remote(r3d.at[1 - zh], r4d, d4s.at[0], d4r.at[0], dev_2)

    def do_d_y(i):
        d_core(i).wait_recv()
        r0d[i] = r0d[i] + gd[i, :, :, c]
        d_y(i).start()

    def do_d_1(i):
        d_y(i).wait_recv()
        r1d[i] = r1d[i] + r0d[i, :, y]
        d_1(i).start()

    def do_d_x(h):
        for j in range(2):
            d_1(2 * h + j).wait_recv()
            r2d[h, j] = r2d[h, j] + r1d[2 * h + j, zl]
        d_x(h).start()

    def do_d_2():
        for h in range(2):
            d_x(h).wait_recv()
            r3d[h] = r3d[h] + r2d[h, x]
        d_2().start()

    def u_core(i):
        return remote(gu.at[i, 1 - c], r0u.at[i], u0s.at[i], u0r.at[i], dev_c)

    def u_a(i, z_first):
        src, dev = (r0u.at[i, :, 1 - zl], dev_1) if z_first else (r0u.at[i, :, :, 1 - x], dev_x)
        return remote(src, r1u.at[i], u1s.at[i], u1r.at[i], dev)

    def u_b(i):
        src, dev = (r1u.at[i, :, 1 - x], dev_x) if i == 0 else (r1u.at[i, :, 1 - zl], dev_1)
        return remote(src, r2u.at[i // 2, i % 2], u2s.at[i], u2r.at[i], dev)

    def u_y(j):
        return remote(r2u.at[1 - y, j], r3u.at[j], u3s.at[j], u3r.at[j], dev_y)

    def u_2(j):
        return remote(r3u.at[j, 1 - zh], r4u.at[j], u4s.at[j], u4r.at[j], dev_2)

    def do_u_a(i):
        u_core(i).wait_recv()
        r0u[i] = r0u[i] + gu[i, c]
        if isinstance(i, int):
            u_a(i, i == 0).start()
            return

        @pl.when(i == 0)
        def _():
            u_a(i, True).start()

        @pl.when(i > 0)
        def _():
            u_a(i, False).start()

    def do_u_b(i):
        u_a(i, i == 0).wait_recv()
        r1u[i] = r1u[i] + (r0u[i, :, zl] if i == 0 else r0u[i, :, :, x])
        u_b(i).start()

    def do_u_y(j):
        for yy in range(2):
            i = 2 * yy + j
            u_b(i).wait_recv()
            r2u[yy, j] = r2u[yy, j] + r1u[i, :, x if i == 0 else zl]
        u_y(j).start()

    def do_u_2(j):
        u_y(j).wait_recv()
        r3u[j] = r3u[j] + r2u[y, j]
        u_2(j).start()

    vec[...] = jnp.zeros_like(vec)
    for i in range(n_chunk):
        for o in range(2):
            ub[pl.ds(i, 1), pl.ds(o * chunk, chunk)] = up_bias[pl.ds(piece_of(i, o) * chunk, chunk)].reshape(1, chunk)
    acc[...] = jnp.zeros_like(acc)
    gn2[...] = jnp.zeros_like(gn2)

    act = gatt
    gh = kvt
    cuts = ((0, 256, ((0, 0, 0, 256),)), (256, 256, ((0, 256, 0, 128), (1, 0, 128, 128))), (512, 256, ((1, 128, 0, 256),)))

    def hidden_at(n):
        return (hid_a, hid_b)[n % 2]

    def ffn_step(i, carry):
        for copy in stream(i):
            copy.wait()

        def up(n):
            here = pl.ds(cuts[n][0], 256)
            hidden_at(n)[...] = dot_nn(n2[...], wu[:, here]) + ub[pl.ds(i, 1), here]

        def activate(n):
            here = pl.ds(cuts[n][0], 256)
            total = jnp.zeros((1, 256), F32)
            for where, first, count in kept_rows:
                row = pl.ds(first, count)
                active, slope = gelu_pair(hidden_at(n)[row, :])
                act[row, here] = active.astype(BF)
                grad_active = jnp.concatenate(
                    [
                        gu[(i, o) + where + (slice(None),) * (5 - len(where)) + (pl.ds(at, size),)].reshape(count, size)
                        for o, at, _, size in cuts[n][2]
                    ],
                    axis=1,
                )
                grad_hidden = (slope * grad_active.astype(F32)).astype(BF)
                gh[row, here] = grad_hidden
                total = total + jnp.sum(grad_hidden.astype(F32), axis=0, keepdims=True)
            ub[pl.ds(i, 1), here] = total

        def down_terms(n):
            first, count, parts = cuts[n]
            block = dot_nn(ct_t[:, pl.ds(0, wide)], act[:, pl.ds(first, count)]).astype(BF)
            for o, at, start, size in parts:
                gd[i, o, :, :, :, pl.ds(at, size)] = block[:, start : start + size].reshape(2, 2, side, size)

        def up_terms(n):
            first, count, parts = cuts[n]
            block = dot_nn(n2t[:, pl.ds(0, wide)], gh[pl.ds(0, wide), pl.ds(first, count)]).astype(BF)
            for o, at, start, size in parts:
                gu[i, o, :, :, :, :, :, pl.ds(at, size)] = block[:, start : start + size].reshape(
                    2, 2, 2, 2, part // 2, size
                )

        up(0)
        activate(0)
        up(1)
        down_terms(0)
        activate(1)
        up(2)
        down_terms(1)
        activate(2)
        for first, count, _ in cuts:
            here = pl.ds(first, count)
            acc[:, here] += dot_nn(act[...], wd[:, here])
            gn2[:, here] += dot_nt(gh[pl.ds(0, wide), :], wu[here, :])

        @pl.when(i + 1 < n_chunk)
        def _():
            for copy in stream(i + 1):
                copy.start()

        @pl.when(i >= 1)
        def _():
            do_d_y(i - 1)
            do_u_a(i - 1)

        @pl.when(i == 3)
        def _():
            do_u_b(0)
            do_d_1(0)

        down_terms(2)
        for n in range(3):
            up_terms(n)
        d_core(i).start()
        u_core(i).start()

        return carry

    lax.fori_loop(0, n_chunk, ffn_step, 0)

    for i in range(n_chunk):
        for o in range(2):
            block = piece_of(i, o)
            vec[pl.ds(8 + block // 2, 1), pl.ds(block % 2 * chunk, chunk)] = ub[pl.ds(i, 1), pl.ds(o * chunk, chunk)]


    def second_pull(first, count):
        grad, gain_term, shift_term = norm_pull(
            x2[pl.ds(first, count), :], ffn_gain, gn2[pl.ds(first, count), :]
        )
        upstream = ct[pl.ds(first, count), :].astype(F32)
        total = upstream + grad
        acc[pl.ds(first, count), :] += x2[pl.ds(first, count), :] + down_bias
        x2[pl.ds(first, count), :] = total
        n2[pl.ds(first, count), :] = total.astype(BF)
        vec[pl.ds(4, 1), :] += gain_term
        vec[pl.ds(5, 1), :] += shift_term
        vec[pl.ds(6, 1), :] += jnp.sum(upstream, axis=0, keepdims=True)

    for r in range(0, tok, 128):
        second_pull(r, 128)
    second_pull(tok, slots)
    gatt[...] = dot_nt(n2[...], wo[...]).astype(BF)

    slot_grad = gatt[pl.ds(tok, slots), :].astype(F32)
    slot_att = att[pl.ds(tok, slots), :].astype(F32)
    head_sel = lanes_of((1, 128)) < HEADS

    def inner_aug(upstream, values):
        high, low = two_parts(upstream.astype(F32) * values)
        inner = dot_nt(high, spread_heads) + dot_nt(low, spread_heads)
        high, low = two_parts(jnp.where(head_sel, inner, 0.0))
        return (high.astype(F32) + pltpu.roll(low.astype(F32), 16, 1)).astype(BF)

    scaled = jnp.concatenate(
        [(cx[pl.ds(k * slots, slots), :] * slot_grad).astype(BF) for k in range(n_seq)], axis=0
    )
    msg1[:, pl.ds(0, width)] = scaled
    msg1[:, pl.ds(width, 128)] = inner_aug(scaled, jnp.concatenate([slot_att] * n_seq, axis=0))
    sends2 = []
    for k in peers:
        copy = remote(
            msg1.at[pl.ds(k * slots, slots)], rcv2.at[pl.ds(my_slots, slots)], m2s.at[k], m2r.at[k],
            (flip(k), b),
        )
        copy.start()
        sends2.append(copy)
    rcv2[pl.ds(my_slots, slots), :] = msg1[pl.ds(0, slots), :]
    do_d_y(3)
    do_u_a(3)
    do_d_1(1)
    do_u_b(1)

    n2t[:, pl.ds(0, tok)] = jnp.transpose(nrm[pl.ds(0, tok), :])
    n2t[:, pl.ds(tok, glob)] = jnp.transpose(nrm[pl.ds(tok, glob), :])

    outs = nrm
    outs[pl.ds(0, wide), :] = acc[...].astype(BF)
    out_copy = pltpu.make_async_copy(outs.at[pl.ds(0, tok)], o_out, osem.at[0])
    out_copy.start()
    own_out = pltpu.make_async_copy(
        outs.at[pl.ds(tok, slots)], o_gout.at[pl.ds(my_slots, slots)], osem.at[1]
    )
    own_out.start()

    scale_c = jnp.transpose(
        jnp.concatenate([rl_t[...], jnp.zeros((128 - rl_t.shape[0], tok), F32)], axis=0)
    )
    scale_a, scale_b = two_parts(scale_c)
    for r in range(0, tok, 128):
        wider = dot_nn(scale_a[r : r + 128], spread_heads) + dot_nn(scale_b[r : r + 128], spread_heads)
        scaled = (gatt[pl.ds(r, 128), :].astype(F32) * wider).astype(BF)
        gatt[pl.ds(r, 128), :] = scaled
        qaug[pl.ds(r, 128), :] = inner_aug(scaled, att[pl.ds(r, 128), :].astype(F32))
    kvt[:, pl.ds(0, rows)] = jnp.transpose(proj[:, pl.ds(width, width)])

    def chunk_at(p):
        return gu.at[p // 2, lax.rem(p, 2)]

    def put_chunk(p, value):
        gu[p // 2, lax.rem(p, 2)] = value.astype(BF).reshape(gu.shape[2:])
        q_core(p).start()

    def q_core(p):
        return remote(chunk_at(p).at[:, 1 - c], r0q.at[p], q0s.at[p], q0r.at[p], dev_c)

    def x_first(p):
        return p in (1, 3, 7)

    def q_a(p):
        src, dev = (r0q.at[p, :, 1 - x], dev_x) if x_first(p) else (r0q.at[p, :, :, 1 - y], dev_y)
        return remote(src, r1q.at[p], q1s.at[p], q1r.at[p], dev)

    def q_b(p):
        src, dev = (r1q.at[p, :, 1 - y], dev_y) if x_first(p) else (r1q.at[p, :, 1 - x], dev_x)
        return remote(src, r2q.at[p], q2s.at[p], q2r.at[p], dev)

    def q_1(p):
        return remote(r2q.at[p], r3q.at[p], q3s.at[p], q3r.at[p], dev_1)

    def q_2(p):
        return remote(r2q.at[p, 1 - zh], r4q.at[p], q4s.at[p], q4r.at[p], dev_2)

    def take_chunk(p):
        q_core(p).wait_recv()
        r0q[p] = r0q[p] + gu[p // 2, p % 2, :, c]

    def do_q_a(*which):
        for p in which:
            take_chunk(p)
            q_a(p).start()

    def do_q_b(*which):
        for p in which:
            q_a(p).wait_recv()
            r1q[p] = r1q[p] + (r0q[p, :, x] if x_first(p) else r0q[p, :, :, y])
            q_b(p).start()

    def do_q_1(*which):
        for p in which:
            q_b(p).wait_recv()
            r2q[p] = r2q[p] + r1q[p, :, y if x_first(p) else x]

            @pl.when(zl != c)
            def _(p=p):
                q_1(p).start()

    def do_q_2(*which):
        @pl.when(zl == c)
        def _():
            for p in which:
                q_1(p).wait_recv()
                r2q[p] = r2q[p] + r3q[p]
                q_2(p).start()

    def q_plane(n):
        src = (r0q.at[5, :, 1 - x, y], r0q.at[5, :, x, 1 - y], r0q.at[5, :, 1 - x, 1 - y])[n]
        dst = (r1q.at[5, :, 0], r1q.at[5, :, 1], r2q.at[5])[n]
        return remote(src, dst, qps.at[n], qpr.at[n], (dev_x, dev_y, dev_xy)[n])

    def q_line(n):
        src = (r0q.at[5, 1 - zh, x, y], r0q.at[5, zh, x, y], r0q.at[5, 1 - zh, x, y])[n]
        dst = (r3q.at[5, 0], r3q.at[5, 1], r4q.at[5])[n]
        return remote(src, dst, qls.at[n], qlr.at[n], (dev_2, dev_1, (flip(6), b))[n])

    def do_q_plane():
        take_chunk(5)
        for n in range(3):
            q_plane(n).start()

    def do_q_line():
        for n in range(3):
            q_plane(n).wait_recv()
        total = r0q[5, :, x, y].astype(F32) + r1q[5, :, 0].astype(F32) + r1q[5, :, 1].astype(F32) + r2q[5].astype(F32)
        r0q[5, :, x, y] = total.astype(BF)

        @pl.when(zl == c)
        def _():
            q_line(0).start()

        @pl.when(zl != c)
        def _():
            q_line(1).start()
            q_line(2).start()

    def q_chunk(p):
        right = jnp.concatenate(
            [proj[:, pl.ds(pl.multiple_of(w * width + p * 128, 128), 128)] for w in range(3)], axis=1
        )
        put_chunk(p, dot_nn(n2t[...], right))

    for i in range(4):
        u_core(i).wait_send()
    for h in range(2):
        put_chunk(pairs + h, dot_nn(att_t[:, pl.ds(0, wide)], n2[:, pl.ds(h * 384, 384)]))

    minus = jnp.where(lanes_of((rows, 128)) < 32, -1.0, 0.0).astype(BF)
    factor = HEAD_DIM ** (-0.5)

    def chosen(head):
        lane = lanes_of((1, 128))
        return jnp.where((lane == head) | (lane == head + 16), 1.0, 0.0).astype(BF)

    def values_of(at):
        return jnp.concatenate([proj[:, pl.ds(2 * width + at, 128)], minus], axis=1)

    def parts_at(p):
        return acc_full.at[:, pl.ds(pl.multiple_of(lax.rem(p, 3) * 256, 256), 256)]

    def token_queries(p):
        at = pl.multiple_of(p * 128, 128)
        values = values_of(at)
        qp = proj[pl.ds(0, tok), pl.ds(at, 128)]
        gp = gatt[pl.ds(0, tok), pl.ds(at, 128)]
        ups = jnp.concatenate([gp * even_one, gp * odd_one], axis=0)
        dd = qaug[pl.ds(0, tok), :]
        inner = jnp.concatenate([dd * chosen(2 * p), dd * chosen(2 * p + 1)], axis=0)
        own = pl.ds(0, 2 * tok)
        parts_at(p)[:, 128:] = dot_nn(probs[p, :, own], ups)
        for first in range(0, 2 * tok, 256):
            right = jnp.concatenate([ups[first : first + 256], inner[first : first + 256]], axis=1)
            grad_w = dot_nt(values, right)
            here = probs[p, :, pl.ds(first, 256)].astype(F32)
            probs[p, :, pl.ds(first, 256)] = (here * grad_w).astype(BF)
        parts_at(p)[:, :128] = dot_nn(probs[p, :, own], jnp.concatenate([qp * even, qp * odd], axis=0))
        low = dot_nn(kvt[pl.ds(at, HEAD_DIM), pl.ds(0, rows)], probs[p, :, pl.ds(0, tok)])
        upper = dot_nn(
            kvt[pl.ds(pl.multiple_of(at + HEAD_DIM, HEAD_DIM), HEAD_DIM), pl.ds(0, rows)],
            probs[p, :, pl.ds(tok, tok)],
        )
        grad_q = jnp.concatenate([low, upper], axis=0) * factor
        proj[pl.ds(0, tok), pl.ds(at, 128)] = jnp.transpose(grad_q).astype(BF)

    def glob_queries(p):
        at = pl.multiple_of(p * 128, 128)
        qg = proj[pl.ds(tok, glob), pl.ds(at, 128)]
        gg = rcv2[:, pl.ds(at, 128)]
        dg = rcv2[:, pl.ds(width, 128)]
        ups = jnp.concatenate([gg * even_one, gg * odd_one], axis=0)
        inner = jnp.concatenate([dg * chosen(2 * p), dg * chosen(2 * p + 1)], axis=0)
        weights = probs[p, :, pl.ds(2 * tok, 2 * glob)]
        grad_v = parts_at(p)[:, 128:] + dot_nn(weights, ups)
        grad_w = dot_nt(values_of(at), jnp.concatenate([ups, inner], axis=1))
        grad_s = (weights.astype(F32) * grad_w).astype(BF)
        grad_k = parts_at(p)[:, :128] + dot_nn(grad_s, jnp.concatenate([qg * even, qg * odd], axis=0))
        own = dot_nn(kvt[pl.ds(at, 128), pl.ds(0, rows)], grad_s)
        own = jnp.where(first_head, own[:, :glob], own[:, glob:]) * factor
        proj[pl.ds(tok, glob), pl.ds(at, 128)] = jnp.transpose(own).astype(BF)
        proj[:, pl.ds(width + at, 128)] = grad_k.astype(BF)
        proj[:, pl.ds(2 * width + at, 128)] = grad_v.astype(BF)

    def at_steps(p, steps):
        for step, act in steps:

            @pl.when(p == step)
            def _(act=act):
                act()

    def first_pairs(p, carry):
        token_queries(p)
        return carry

    def middle_pairs(p, carry):
        token_queries(p)
        glob_queries(p - 2)
        q_chunk(p - 2)
        at_steps(p, (
            (2, lambda: (do_d_1(3), do_u_b(3), do_d_x(0))),
            (3, lambda: (do_q_a(0), do_u_y(0), do_q_b(6, 7))),
            (4, lambda: (do_q_a(1), do_d_x(1), do_u_y(1))),
            (5, lambda: (do_q_a(2), do_q_b(0), do_u_2(0), do_q_1(6, 7))),
        ))
        return carry

    def last_pairs(p, carry):
        glob_queries(p)
        q_chunk(p)
        at_steps(p, ((4, lambda: (do_q_a(3), do_q_b(1), do_d_2())), (5, lambda: (do_q_a(4), do_u_2(1), do_q_2(6, 7), do_q_1(0)))))
        return carry

    lax.fori_loop(0, 2, first_pairs, 0)
    do_d_1(2)
    do_u_b(2)
    do_q_a(6, 7)
    for copy in sends2:
        copy.wait()
    sends_o = []
    for k in peers:
        copy = remote(
            outs.at[pl.ds(tok, slots)], o_gout.at[pl.ds(my_slots, slots)], gos.at[k], gor.at[k], (flip(k), b)
        )
        copy.start()
        sends_o.append(copy)

    lax.fori_loop(2, pairs, middle_pairs, 0)
    lax.fori_loop(pairs - 2, pairs, last_pairs, 0)

    def first_pull(first):
        grad, gain_term, shift_term = norm_pull(
            sec[pl.ds(first, 128), :].astype(F32), attn_gain, gn2[pl.ds(first, 128), :]
        )
        n2[pl.ds(first, 128), :] = (grad + x2[pl.ds(first, 128), :]).astype(BF)
        vec[pl.ds(0, 1), :] += gain_term
        vec[pl.ds(1, 1), :] += shift_term

    gnm = wu
    gnm[pl.ds(0, glob), :] = dot_nt(proj[pl.ds(tok, glob), :], wq[...]).astype(BF)
    sends3 = []
    for k in (1, 2, 3):
        other = flip(k)
        for h in range(2):
            at = pl.multiple_of((4 * h + lax.rem(other, 4)) * slots, slots)
            copy = remote(
                gnm.at[pl.ds(at, slots)], rcv3.at[k - 1, h], m3s.at[2 * k - 2 + h], m3r.at[2 * k - 2 + h], (other, b)
            )
            copy.start()
            sends3.append(copy)
    do_q_plane()
    gn2[pl.ds(half, half), :] = dot_nt(proj[pl.ds(half, half), :], wq[...])
    for r in range(half, tok, 128):
        first_pull(r)
    do_q_b(2, 3)
    do_q_1(1)
    do_q_2(0)
    for copy in sends3:
        copy.wait()

    quarter = half // 2
    after, after_relay = (lax.rem(s + 1, n_seq), b), (lax.rem(s + 2, n_seq), b)
    relay = ct.at[pl.ds(0, quarter)]

    def back(n):
        part_n = pl.ds(n * quarter, quarter)
        return remote(n2.at[pl.ds(half + n * quarter, quarter)], o_tgrad.at[part_n], hs2.at[n], hr2.at[n], after)

    def back_to_relay():
        return remote(n2.at[pl.ds(half + quarter, quarter)], relay, hs2.at[1], hr2.at[2], dev_x)

    def back_from_relay():
        return remote(relay, o_tgrad.at[pl.ds(quarter, quarter)], hs2.at[2], hr2.at[1], after_relay)

    def start_back():
        back(0).start()

        @pl.when(x == 0)
        def _():
            back(1).start()

        @pl.when(x == 1)
        def _():
            back_to_relay().start()

    def pass_back_on():
        @pl.when(x == 0)
        def _():
            back_to_relay().wait_recv()
            back_from_relay().start()

    def slots_of(h):
        mine = gnm[pl.ds(pl.multiple_of((4 * h + lax.rem(s, 4)) * slots, slots), slots), :].astype(F32)
        for k in (1, 2, 3):
            mine = mine + rcv3[k - 1, h].astype(F32)
        return mine

    gsum[...] = slots_of(1 - zh).astype(BF)
    line3 = remote(gsum, rcv3b, m3s.at[6], m3r.at[6], dev_2)
    line3.start()

    gn2[pl.ds(0, half), :] = dot_nt(proj[pl.ds(0, half), :], wq[...])
    for r in range(0, half, 128):
        first_pull(r)
    keep = pltpu.make_async_copy(n2.at[pl.ds(0, half)], o_tgrad.at[pl.ds(half, half)], osem.at[2])
    keep.start()
    do_q_line()
    do_q_b(4)
    do_q_1(2, 3)
    do_q_2(1)

    @pl.when(s == n_seq - 1)
    def _():
        start_back()


    line3.wait()
    grad, gain_term, shift_term = norm_pull(
        sec[pl.ds(pl.multiple_of(tok + my_slots, slots), slots), :].astype(F32),
        glob_gain,
        slots_of(zh) + rcv3b[...].astype(F32),
    )
    vec[pl.ds(2, 1), :] += gain_term
    vec[pl.ds(3, 1), :] += shift_term
    n2[pl.ds(tok, slots), :] = (grad + x2[pl.ds(tok, slots), :]).astype(BF)
    line_g = remote(n2.at[pl.ds(tok, slots)], gall, ggs_s.at[0], ggs_r.at[0], dev_2)
    line_g.start()

    share = vec.shape[1] // n_seq
    for j in range(n_seq):
        rolled = vec[pl.ds(0, 8), :]
        if j:
            rolled = pltpu.roll(rolled, vec.shape[1] - share * j, 1)
        vmsg[j, pl.ds(0, 8), :] = rolled[:, :128]
        for m in range(chunk // 128):
            vmsg[j, pl.ds(8 + m, 1), :] = vec[pl.ds(8 + j // 2, 1), pl.ds((j % 2) * chunk + m * 128, 128)]
    sends_v = []
    for k in peers:
        copy = remote(vmsg.at[flip(k)], vrcv.at[k - 1], vs.at[k], vr.at[k], (flip(k), b))
        copy.start()
        sends_v.append(copy)

    do_q_1(4)
    do_q_2(2, 3)

    d_2().wait_recv()
    acc[pl.ds(96, 192), pl.ds(0, 384)] = r4d[...].astype(F32) + r3d[zh].astype(F32)
    for j in range(2):
        u_2(j).wait_recv()
    last = r4u[...].astype(F32) + r3u[:, zh].astype(F32)
    acc[pl.ds(0, 96), pl.ds(0, 384)] = last[0].reshape(96, 384)
    acc[pl.ds(0, 96), pl.ds(384, 384)] = last[1].reshape(96, 384)
    results = [
        pltpu.make_async_copy(acc.at[pl.ds(0, 96)], o_up, osem.at[4]),
        pltpu.make_async_copy(acc.at[pl.ds(96, 192), pl.ds(0, 384)], o_down, osem.at[5]),
    ]
    for copy in results:
        copy.start()

    line_g.wait()
    far_slots = pl.multiple_of(flip(4) * slots, slots)
    sends_g = []
    for n, (src, at) in enumerate(((n2.at[pl.ds(tok, slots)], my_slots), (gall, far_slots))):
        copy = pltpu.make_async_copy(src, o_ggrad.at[pl.ds(at, slots)], gsem.at[n])
        copy.start()
        sends_g.append(copy)
        for k in (1, 2, 3):
            copy = remote(
                src, o_ggrad.at[pl.ds(at, slots)], ggs_s.at[2 * k + n - 1], ggs_r.at[2 * k + n - 1], (flip(k), b)
            )
            copy.start()
            sends_g.append(copy)

    for copy in sends_v:
        copy.wait()
    vsum[0] = vmsg[s]
    for k in peers:
        vsum[0] = vsum[0] + vrcv[k - 1]
    batch_peers = (dev_c, dev_y, dev_cy)
    sends_b = []
    for n, dev in enumerate(batch_peers):
        copy = remote(vsum.at[0], vsum.at[1 + n], vbs.at[n], vbr.at[n], dev)
        copy.start()
        sends_b.append(copy)

    do_q_2(4)

    @pl.when(s != n_seq - 1)
    def _():
        start_back()

    @pl.when(s == n_seq - 2)
    def _():
        pass_back_on()


    def final(n, slot):
        return remote(fmsg.at[n - 1], frcv.at[slot], fs.at[n], fr.at[n], (s, flip_b(n)))

    def flip_b(n):
        return (b, dev_c[1], dev_y[1], dev_cy[1])[n]

    @pl.when(zl == c)
    def _():
        for p in (6, 7, 0, 1, 2, 3, 4):
            q_2(p).wait_recv()
            r4q[p] = r4q[p] + r2q[p, zh]
        for n in range(3):
            q_line(n).wait_recv()
        r4q[5] = (
            r0q[5, zh, x, y].astype(F32) + r3q[5, 0].astype(F32) + r3q[5, 1].astype(F32) + r4q[5].astype(F32)
        ).astype(BF)

        def columns_of(bb):
            first = (bb * 576 - 64 * lax.rem(bb, 2)) // 128
            tiles = []
            for m in range(5):
                tile = first + m
                tiles.append(r4q[lax.rem(tile, 6), :, pl.ds(pl.multiple_of(tile // 6 * 128, 128), 128)])
            first = (bb * 192 - 64 * lax.rem(bb, 2)) // 128
            for m in range(2):
                tile = first + m
                tiles.append(r4q[pairs + tile // 3, :, pl.ds(pl.multiple_of(lax.rem(tile, 3) * 128, 128), 128)])
            return jnp.concatenate(tiles, axis=1)

        for n in (3, 2, 1):
            fmsg[n - 1] = columns_of(flip_b(n))
            final(n, y).start()
        frcv[y] = columns_of(b)

    @pl.when(s != n_seq - 2)
    def _():
        pass_back_on()

    for copy in sends_b:
        copy.wait()
    shared = vsum[0] + vsum[1] + (vsum[2] + vsum[3])
    o_vec[...] = shared[0:8, :share]
    for m in range(chunk // 128):
        o_ub[:, pl.ds(m * 128, 128)] = shared[8 + m : 9 + m, :]

    @pl.when(zl == c)
    def _():
        final(2, 1 - y).wait_recv()

    @pl.when(zl != c)
    def _():
        final(1, y).wait_recv()
        final(3, 1 - y).wait_recv()

    for yy in range(2):
        block = frcv[yy].astype(F32)
        main = block[:, :640]
        acc[pl.ds(288 + yy * 48, 48), pl.ds(0, 640)] = jnp.where(c == 1, pltpu.roll(main, 576, 1), main)
        main = block[:, 640:]
        acc[pl.ds(384 + yy * 48, 48), pl.ds(0, 256)] = jnp.where(c == 1, pltpu.roll(main, 192, 1), main)
    for copy in (
        pltpu.make_async_copy(acc.at[pl.ds(288, 96), pl.ds(0, 640)], o_qkv, osem.at[6]),
        pltpu.make_async_copy(acc.at[pl.ds(384, 96), pl.ds(0, 256)], o_wout, osem.at[7]),
    ):
        copy.start()
        results.append(copy)

    for i in range(4):
        d_core(i).wait_send()
        d_y(i).wait_send()
        d_1(i).wait_send()
        u_a(i, i == 0).wait_send()
        u_b(i).wait_send()
    for h in range(2):
        d_x(h).wait_send()
    d_2().wait_send()
    for j in range(2):
        u_y(j).wait_send()
        u_2(j).wait_send()
    for p in range(8):
        q_core(p).wait_send()
        if p != 5:
            q_a(p).wait_send()
            q_b(p).wait_send()
    for n in range(3):
        q_plane(n).wait_send()

    @pl.when(zl == c)
    def _():
        q_line(0).wait_send()
        for n in (1, 2, 3):
            final(n, y).wait_send()
        for p in (6, 7, 0, 1, 2, 3, 4):
            q_2(p).wait_send()

    @pl.when(zl != c)
    def _():
        for n in (1, 2):
            q_line(n).wait_send()
        for p in (6, 7, 0, 1, 2, 3, 4):
            q_1(p).wait_send()

    back(0).wait()
    back(1).wait()

    @pl.when(x == 0)
    def _():
        back_from_relay().wait_send()

    keep.wait()
    out_copy.wait()
    own_out.wait()
    for copy in results:
        copy.wait()
    for copy in sends_o + sends_g:
        copy.wait()


def fits(tokens, global_states, w_qkv, w_up):
    return (
        lax.axis_size("seq") == 8
        and lax.axis_size("batch") == 4
        and tokens.shape == (1, BLOCK, HEADS * HEAD_DIM)
        and global_states.shape == (1, 128, HEADS * HEAD_DIM)
        and w_qkv.shape == (HEADS * HEAD_DIM, 3 * HEADS * HEAD_DIM)
        and w_up.shape == (HEADS * HEAD_DIM, 3072)
    )


def finish_kernel(*refs):
    ins, outs = refs[:10], refs[10:]
    for i in range(8):
        outs[i][...] = ins[i][:, : outs[i].shape[1]]
    for i in range(7):
        outs[8 + i][...] = ins[8][i, :]
    outs[15][...] = ins[9][0, :]


def fused(
    tokens, global_states, token_seg, global_seg, attn_gain, attn_shift, glob_gain, glob_shift, w_qkv, w_out,
    ffn_gain, ffn_shift, w_up, up_bias, w_down, down_bias, out_cotangent, global_cotangent,
):
    tok, width = tokens.shape[1:]
    glob = global_states.shape[1]
    hidden = w_up.shape[1]
    n_seq, n_batch = lax.axis_size("seq"), lax.axis_size("batch")
    rows, slots = tok + glob, glob // n_seq
    wide = tok + slots
    chunk, part, side = hidden // n_seq, width // n_seq, width // n_batch
    pairs = HEADS // 2
    eighth = (2, 2, 2)
    dma = pltpu.SemaphoreType.DMA

    def any_space():
        return pl.BlockSpec(memory_space=pl.ANY)

    def vmem():
        return pl.BlockSpec(memory_space=pltpu.VMEM)

    def low(*shape):
        return pltpu.VMEM(shape, BF)

    def full(*shape):
        return pltpu.VMEM(shape, F32)

    scratch = [
        low(rows, width), low(rows, width), low(rows, 3 * width), low(width, width),
        low(pairs, rows, 2 * tok + 2 * glob), low(width, tok + 128), low(wide, width), full(wide, width),
        low(wide, width), low(width, tok + 128), low(wide, width), low(width, tok + 128),
        full(rows, width), full(rows, width), low(wide, width), low(rows, 128), low(rows, 128),
        low(width, 3 * width), low(width, width), low(width, width), low(width, width),
        full(128, glob), full(16, tok), full(glob, width), low(glob, width + 128),
        low(n_seq, slots, width + 128), low(glob, width + 128),
        low(3, 2, slots, width), low(slots, width), low(slots, width), low(slots, width),
        full(16, width), full(n_seq, 16, 128), full(n_seq - 1, 16, 128), full(4, 16, 128), full(4, width),
        low(4, 2, 2, 2, side, chunk), low(4, 2, 2, side, chunk), low(4, 2, side, chunk), low(2, 2, side, chunk),
        low(2, side, chunk), low(side, chunk),
        low(4, 2, *eighth, 2, part // 2, chunk), low(4, *eighth, 2, part // 2, chunk), low(4, 2, 2, 2, part // 2, chunk),
        low(2, 2, 2, 2, part // 2, chunk), low(2, 2, 2, part // 2, chunk), low(2, 2, part // 2, chunk),
        low(8, 2, 2, 2, part // 2, chunk), low(8, 2, 2, part // 2, chunk), low(8, 2, part // 2, chunk),
        low(8, 2, part // 2, chunk), low(8, part // 2, chunk),
        low(3, part // 2, 896), low(2, part // 2, 896),
        full(wide, 256), full(wide, 256),
        dma((8,)), dma((2, 2)), dma((1,)), dma((1,)),
        *[dma((8,)) for _ in range(10)], dma((9,)), dma((9,)),
        *[dma((4,)) for _ in range(10)], *[dma((4,)) for _ in range(10)], *[dma((8,)) for _ in range(10)],
        *[dma((3,)) for _ in range(6)], *[dma((4,)) for _ in range(4)], dma((8,)), dma((2,)),
    ]

    results = pl.pallas_call(
        layer_kernel,
        out_shape=[
            jax.ShapeDtypeStruct((tok, width), BF),
            jax.ShapeDtypeStruct((glob, width), BF),
            jax.ShapeDtypeStruct((tok, width), BF),
            jax.ShapeDtypeStruct((glob, width), BF),
            jax.ShapeDtypeStruct((part, 640), F32),
            jax.ShapeDtypeStruct((part, 256), F32),
            jax.ShapeDtypeStruct((part, 2 * chunk), F32),
            jax.ShapeDtypeStruct((side, chunk), F32),
            jax.ShapeDtypeStruct((8, part), F32),
            jax.ShapeDtypeStruct((1, chunk), F32),
        ],
        in_specs=[any_space(), any_space(), vmem(), vmem(), vmem(), vmem(), vmem(), vmem(), any_space(), any_space(),
                  vmem(), vmem(), any_space(), vmem(), any_space(), vmem(), any_space(), any_space()],
        out_specs=[any_space()] * 8 + [vmem()] * 2,
        scratch_shapes=scratch,
        compiler_params=pltpu.CompilerParams(
            collective_id=0, has_side_effects=True, vmem_limit_bytes=64 * 1024 * 1024
        ),
        name="layer",
    )(
        tokens[0], global_states[0], token_seg, global_seg, attn_gain, attn_shift, glob_gain,
        glob_shift, w_qkv, w_out, ffn_gain, ffn_shift, w_up, up_bias, w_down, down_bias,
        out_cotangent[0], global_cotangent[0],
    )
    *large, vectors, ub = results
    columns = {4: 3 * side, 5: side}
    results = pl.pallas_call(
        finish_kernel,
        out_shape=[
            jax.ShapeDtypeStruct((one.shape[0], columns.get(i, one.shape[1])), one.dtype) for i, one in enumerate(large)
        ]
        + [jax.ShapeDtypeStruct((part,), F32)] * 7
        + [jax.ShapeDtypeStruct((chunk,), F32)],
        in_specs=[vmem()] * 10,
        out_specs=[vmem()] * 16,
        name="results",
    )(*large, vectors, ub)
    out, gout, tgrad, ggrad, g_qkv, g_out, g_up, g_down, *g_vec, g_ub = results
    return (
        out[None], gout[None], tgrad[None], ggrad[None], g_vec[0], g_vec[1], g_vec[2], g_vec[3], g_qkv, g_out,
        g_vec[4], g_vec[5], g_up, g_ub, g_down.T, g_vec[6],
    )


def local(tokens, global_states, token_seg, global_seg, *rest):
    w_qkv, w_up = rest[4], rest[8]
    way = fused if fits(tokens, global_states, w_qkv, w_up) else general
    return way(tokens, global_states, token_seg, global_seg, *rest)


def solution(mesh):
    placed = (
        P("batch", "seq", None),
        P("batch", None, None),
        P("batch", "seq"),
        P("batch", None),
        P(),
        P(),
        P(),
        P(),
        P(),
        P(),
        P(),
        P(),
        P(),
        P(),
        P(),
        P(),
        P("batch", "seq", None),
        P("batch", None, None),
    )
    return jax.shard_map(
        local,
        mesh=mesh,
        in_specs=placed,
        out_specs=(
            P("batch", "seq", None),
            P("batch", None, None),
            P("batch", "seq", None),
            P("batch", None, None),
            P("seq"),
            P("seq"),
            P("seq"),
            P("seq"),
            P("seq", "batch"),
            P("seq", "batch"),
            P("seq"),
            P("seq"),
            P("seq", "batch"),
            P("seq"),
            P("seq", "batch"),
            P("seq"),
        ),
        check_vma=False,
    )
```
